32 devices in a mesh: expert: 8 (over z, y), tensor: 4 (over x, core).
Axes of the slice: x: 2, y: 2, z: 4, core: 2. Of those that a mesh axis runs over, the one named last changes fastest.
Arguments:
- tokens: bfloat16 [6144, 2048], P('expert'), may hold values from -6 to 6
- out_grad: bfloat16 [6144, 2048], P('expert'), may hold values from -6 to 6
- attn_gain: float32 [2048], replicated, may hold values from 0.5 to 1.5
- attn_router: float32 [2048, 8], replicated, may hold values from -0.09375 to 0.09375
- w_query: bfloat16 [2048, 2048], P(None, 'tensor'), may hold values from -0.125 to 0.125
- w_key: bfloat16 [2048, 2048], P(None, 'tensor'), may hold values from -0.125 to 0.125
- w_value: bfloat16 [2048, 2048], P(None, 'tensor'), may hold values from -0.125 to 0.125
- w_out: bfloat16 [2048, 2048], P('tensor'), may hold values from -1 to 1
- mlp_gain: float32 [2048], replicated, may hold values from 0.5 to 1.5
- mlp_router: float32 [2048, 8], replicated, may hold values from -0.09375 to 0.09375
- w_gate: bfloat16 [8, 2048, 5632], P('expert', None, 'tensor'), may hold values from -0.125 to 0.125
- w_up: bfloat16 [8, 2048, 5632], P('expert', None, 'tensor'), may hold values from -0.125 to 0.125
- w_down: bfloat16 [8, 5632, 2048], P('expert', 'tensor'), may hold values from -0.078125 to 0.078125
- deal: int32 [6144], P('expert'), may hold values from 0 to 6143, as said below
- seq_lengths: int32 [8, 3], P('expert'), may hold values from 1 to 640, 768 in all within a row
- attn_routes: int32 [6144, 2], P('expert'), may hold values from 0 to 7, all different within a row
- mlp_routes: int32 [6144, 2], P('expert'), may hold values from 0 to 7, all different within a row
- slot_order: int32 [8, 1536], P('expert'), may hold values from 0 to 1535, each once within a row
Outputs:
- mixed: bfloat16 [6144, 2048], P('expert', 'tensor')
- tokens_grad: bfloat16 [6144, 2048], P('expert', 'tensor')
- attn_gain_grad: float32 [2048], replicated
- attn_router_grad: float32 [2048, 8], replicated
- w_query_grad: float32 [2048, 2048], P(None, 'tensor')
- w_key_grad: float32 [2048, 2048], P(None, 'tensor')
- w_value_grad: float32 [2048, 2048], P(None, 'tensor')
- w_out_grad: float32 [2048, 2048], P('tensor')
- mlp_gain_grad: float32 [2048], replicated
- mlp_router_grad: float32 [2048, 8], replicated
- w_gate_grad: float32 [8, 2048, 5632], P('expert', None, 'tensor')
- w_up_grad: float32 [8, 2048, 5632], P('expert', None, 'tensor')
- w_down_grad: float32 [8, 5632, 2048], P('expert', 'tensor')
The draws below stay inside these ranges and needn't reach their ends.
Inputs may be any that keep to these rules, and one draw needn't show every extreme that they name: `deal`: each layout position occurs once. The tokens of rows s * 768 to (s + 1) * 768 - 1 that go to group g fill exactly the positions g * 768 + s * 96 to g * 768 + (s + 1) * 96 - 1, 96 of them for every s and g. `seq_lengths`: each row sums to 768; its largest length is 640. `attn_routes`: A position's two experts differ. `mlp_routes`: A position's two experts differ. `slot_order`: each row holds every number once.
All inputs are finite; a program needn't handle non-finite values.
Results may differ from the reference program's by a relative error of at most 0.018.
Values may be sent and summed in bfloat16 or wider, within the bound.
A program may use at most 320 MiB of HBM per device.

```python
import math
from functools import partial
import jax
import jax.numpy as jnp
import numpy as np
from jax import lax

D = 2048
HEAD = 128
QH = 2
AEXP = 8
KVH = 16
FFN = 5632
EXPERTS = 8
SPLIT = 1
TOK_GRP = 768
SEQS = 3
LONGEST = 640
GROUPS = 8
BUCKET = 96
TOKENS = 6144
CAP = 240
N_EXPERT = 8


def draw_deal(key, part):
    key = jax.random.fold_in(key, 11)

    def one_source(source):
        source_key = jax.random.fold_in(key, source)
        ranking = jax.random.permutation(source_key, TOK_GRP).astype(jnp.int32)
        target_group = ranking // BUCKET
        within = ranking % BUCKET
        return target_group * TOK_GRP + source * BUCKET + within
    sources = jnp.arange(GROUPS, dtype=jnp.int32)
    return jax.vmap(one_source)(sources).reshape(TOKENS).astype(jnp.int32)


def levels(key, extent, split, low, largest):
    def one(dim, shards_of):
        draws = jax.random.uniform(jax.random.fold_in(jax.random.fold_in(key, 6), dim), (shards_of,), jnp.float32, low / len(split), largest / len(split))
        return jnp.repeat(jnp.exp(draws), extent[dim] // shards_of).reshape((-1,) + (1,) * (len(extent) - dim - 1))

    factor_of = one(*split[0])
    for cut in split[1:]:
        factor_of = factor_of * one(*cut)
    return factor_of


def distinct(own_key, rows, number_of, top, lift):
    sequence = jax.random.permutation(jax.random.fold_in(own_key, 1), number_of)
    pull = sequence
    for power in range(3):
        pull = pull * pull // number_of
    pull = pull * lift // number_of
    chance = jax.random.randint(jax.random.fold_in(own_key, 2), (rows, number_of), 0, 4096) + pull
    fixed_rows = jax.random.permutation(jax.random.fold_in(own_key, 3), rows)[jnp.arange(number_of) % rows]
    chance = jnp.where(jnp.arange(rows)[:, None] == fixed_rows[None, :], 1 << 14, chance)
    score = chance * number_of + jnp.arange(number_of)
    return lax.top_k(score.astype(jnp.int32), top)[1].astype(jnp.int32)


def length_profile(count, total, limit, slope):
    portions = [(1 << 20) // math.isqrt(grade ** slope) + 1 for grade in range(2, count + 1)]
    spare, given = total - limit - (count - 1), [1] * (count - 1)
    while spare > 0:
        free = [i for i in range(count - 1) if given[i] < limit]
        whole, budget = sum([portions[i] for i in free]), spare
        for i in free:
            more = min(limit - given[i], max(1, budget * portions[i] // whole), spare)
            given[i] = given[i] + more
            spare = spare - more
    return np.array([limit] + given)


def ragged(rng, count, total, bound, slope):
    if count == 2:
        one = jax.random.randint(rng, (), max(1, total - bound), min(bound, total - 1) + 1)
        return jnp.stack([one, total - one])
    sizes = jnp.asarray(length_profile(count, total, bound, slope), jnp.int32)
    twos = (count - 1) // 2
    giver, receiver = sizes[1:1 + 2 * twos:2], sizes[2:2 + 2 * twos:2]
    margin = jnp.minimum(giver - 1, bound - receiver)
    moved = jax.random.randint(jax.random.fold_in(rng, 1), (twos,), 0, 1 << 20) % (margin + 1)
    sizes = sizes.at[1:1 + 2 * twos:2].set(giver - moved).at[2:2 + 2 * twos:2].set(receiver + moved)
    return sizes[jax.random.permutation(jax.random.fold_in(rng, 2), count)]


def bell_draw(rng, dims, scale, limit, shards=(), kind=jnp.bfloat16):
    values = scale * jax.random.normal(rng, dims, jnp.float32)
    if shards:
        values = values * levels(rng, dims, shards, -0.22, 0.18)
    return jnp.clip(values, -limit, limit).astype(kind)


def setup_inputs(seed: int = 0) -> dict:
    streams_of = jax.random.split(jax.random.key(seed), 19)
    return {
        "tokens": bell_draw(streams_of[0], (TOKENS, D), 1.0, 6.0, ((0, 8),)),
        "out_grad": bell_draw(streams_of[1], (TOKENS, D), 1.0, 6.0, ((0, 8),)),
        "attn_gain": jnp.clip(1.0 + 0.1 * jax.random.normal(streams_of[2], (D,), jnp.float32), 0.5, 1.5),
        "attn_router": bell_draw(streams_of[3], (D, AEXP), (2 * D) ** -0.5, 0.09375, (), jnp.float32),
        "w_query": bell_draw(streams_of[4], (D, KVH * HEAD), D ** -0.5, 0.125, ((1, 4),)),
        "w_key": bell_draw(streams_of[5], (D, KVH * HEAD), D ** -0.5, 0.125, ((1, 4),)),
        "w_value": bell_draw(streams_of[6], (D, KVH * HEAD), D ** -0.5, 0.125, ((1, 4),)),
        "w_out": bell_draw(streams_of[7], (KVH * HEAD, D), (QH * HEAD // 8) ** -0.5, 1.0, ((0, 4),)),
        "mlp_gain": jnp.clip(1.0 + 0.1 * jax.random.normal(streams_of[8], (D,), jnp.float32), 0.5, 1.5),
        "mlp_router": bell_draw(streams_of[9], (D, EXPERTS), (2 * D) ** -0.5, 0.09375, (), jnp.float32),
        "w_gate": bell_draw(streams_of[10], (N_EXPERT, D, FFN // SPLIT), D ** -0.5, 0.125, ((0, 8), (2, 4))),
        "w_up": bell_draw(streams_of[11], (N_EXPERT, D, FFN // SPLIT), D ** -0.5, 0.125, ((0, 8), (2, 4))),
        "w_down": bell_draw(streams_of[12], (N_EXPERT, FFN // SPLIT, D), FFN ** -0.5, 0.078125, ((0, 8), (1, 4))),
        "deal": draw_deal(jax.random.fold_in(streams_of[18], 71), 0),
        "seq_lengths": jax.vmap(lambda own: ragged(own, SEQS, TOK_GRP, LONGEST, 2))(jax.random.split(streams_of[14], GROUPS)).reshape((GROUPS, SEQS)).astype(jnp.int32),
        "attn_routes": distinct(streams_of[15], TOKENS, AEXP, 2, 2048),
        "mlp_routes": distinct(streams_of[16], TOKENS, EXPERTS, 2, 2048),
        "slot_order": jax.vmap(lambda own: jax.random.permutation(own, 2 * TOK_GRP))(jax.random.split(streams_of[17], GROUPS)).reshape((GROUPS, 2 * TOK_GRP)).astype(jnp.int32),
    }


PRECISE = lax.Precision.HIGHEST
EPSILON = 1e-06
MASKED = -1e+30

@jax.custom_vjp
def low(v):
    return lax.optimization_barrier(v.astype(jnp.bfloat16)).astype(jnp.float32)

@jax.custom_vjp
def low_back(v):
    return v

def low_keep(v):
    return (low(v), None)

def low_pass(kept, grad):
    return (grad,)

def back_keep(v):
    return (v, None)

def back_low(kept, grad):
    return (low(grad),)
low.defvjp(low_keep, low_pass)
low_back.defvjp(back_keep, back_low)

def norm_forward(values, gain):
    factor = lax.rsqrt(lax.optimization_barrier(jnp.mean(values * values, axis=-1, keepdims=True)) + EPSILON)
    return values * factor * gain

def half_turn(values):
    middle = values.shape[-1] // 2
    return jnp.concatenate([-values[..., middle:], values[..., :middle]], axis=-1)

def rotary_tables(lengths, tok_rows):
    seq_ends = jnp.cumsum(lengths).astype(jnp.int32)
    seq_starts = (seq_ends - lengths).astype(jnp.int32)
    places = jnp.arange(tok_rows, dtype=jnp.int32)
    segment = lax.optimization_barrier(jnp.sum((places[:, None] >= seq_ends[None, :]).astype(jnp.int32), axis=1)).astype(jnp.int32)
    matches = segment[:, None] == jnp.arange(lengths.shape[0], dtype=jnp.int32)[None, :]
    seq_first = lax.optimization_barrier(jnp.sum(jnp.where(matches, seq_starts[None, :], 0), axis=1)).astype(jnp.int32)
    offsets = (places - seq_first).astype(jnp.float32)
    frequency = jnp.exp(-math.log(10000.0) * jnp.arange(0, HEAD, 2, dtype=jnp.float32) / HEAD)
    angles = offsets[:, None] * frequency[None, :]
    angles = jnp.concatenate([angles, angles], axis=1)
    return (segment, jnp.cos(angles), jnp.sin(angles))

def pair_gates(logits, routes):
    columns = logits.shape[1]
    chosen_mask = (routes[:, :, None] == jnp.arange(columns, dtype=jnp.int32)[None, None, :]).astype(logits.dtype)
    picked = lax.optimization_barrier(jnp.sum(chosen_mask * logits[:, None, :], axis=2))
    return (jax.nn.softmax(picked, axis=1), chosen_mask)

def slot_table(routes, priority, expert_count, capacity):
    target = routes.reshape(-1).astype(jnp.int32)
    pair_count = target.shape[0]
    by_priority = jnp.zeros((pair_count,), jnp.int32).at[priority].set(jnp.arange(pair_count, dtype=jnp.int32))
    ranked = target[by_priority]
    matched = (ranked[:, None] == jnp.arange(expert_count, dtype=jnp.int32)[None, :]).astype(jnp.int32)
    earlier = (jnp.cumsum(matched, axis=0) - matched).astype(jnp.int32)
    ranked_slot = lax.optimization_barrier(jnp.sum(earlier * matched, axis=1)).astype(jnp.int32)
    position = ranked_slot[priority]
    return (target, position, position < capacity)

def attend_group(pieces):
    query, keys, values, segment = pieces
    places = jnp.arange(TOK_GRP, dtype=jnp.int32)
    allowed = (segment[:, None] == segment[None, :]) & (places[:, None] >= places[None, :])
    scores = jnp.einsum('qhd,khd->hqk', query, keys, precision=PRECISE) * (1.0 / math.sqrt(HEAD))
    scores = low_back(scores)
    scores = jnp.where(allowed[None], scores, MASKED)
    probs = jax.nn.softmax(scores, axis=-1)
    return jnp.einsum('hqk,khd->qhd', low(probs), values, precision=PRECISE)

def expert_apply(pieces):
    inbox, gate_w, up_w, down_w = pieces
    gate_pre = low_back(jnp.dot(inbox, gate_w, precision=PRECISE))
    up_pre = low_back(jnp.dot(inbox, up_w, precision=PRECISE))
    middle = low(jax.nn.silu(gate_pre) * up_pre)
    return low(low_back(jnp.dot(middle, down_w, precision=PRECISE)))

def reference(tokens, out_grad, attn_gain, attn_router, w_query, w_key, w_value, w_out, mlp_gain, mlp_router, w_gate, w_up, w_down, deal, seq_lengths, attn_routes, mlp_routes, slot_order):
    inverse_deal = jnp.zeros((TOKENS,), jnp.int32).at[deal].set(jnp.arange(TOKENS, dtype=jnp.int32))
    segments, cosine, sine = jax.vmap(partial(rotary_tables, tok_rows=TOK_GRP))(seq_lengths)
    cosine = cosine.reshape(TOKENS, 1, HEAD)
    sine = sine.reshape(TOKENS, 1, HEAD)
    target, position, kept = jax.vmap(partial(slot_table, expert_count=EXPERTS, capacity=CAP))(mlp_routes.reshape(GROUPS, TOK_GRP, 2), slot_order)
    group_ids = jnp.arange(GROUPS, dtype=jnp.int32)[:, None]
    sentinel = EXPERTS * GROUPS * CAP
    destination = jnp.where(kept, (target * GROUPS + group_ids) * CAP + position, sentinel).reshape(-1).astype(jnp.int32)
    pair_ids = jnp.arange(2 * TOKENS, dtype=jnp.int32)
    owner = jnp.full((sentinel + 1,), 2 * TOKENS, jnp.int32).at[destination].set(pair_ids)[:-1]
    block_units = FFN // SPLIT

    def forward(tok_in, gain_attn, router_attn, query_w, key_w, value_w, out_w, gain_mlp, router_mlp, gate_blocks, up_blocks, down_blocks):
        gate_w = gate_blocks.reshape(EXPERTS, SPLIT, D, block_units).transpose(0, 2, 1, 3).reshape(EXPERTS, D, FFN)
        up_w = up_blocks.reshape(EXPERTS, SPLIT, D, block_units).transpose(0, 2, 1, 3).reshape(EXPERTS, D, FFN)
        down_w = down_blocks.reshape(EXPERTS, FFN, D)
        resid = tok_in[inverse_deal]
        normed = norm_forward(resid, gain_attn)
        normed_low = low(normed)
        attn_gates, attn_mask = pair_gates(jnp.dot(normed, router_attn, precision=PRECISE), attn_routes)
        gate_table = lax.optimization_barrier(jnp.sum(attn_gates[:, :, None] * attn_mask, axis=1))
        query_pre = low_back(jnp.dot(normed_low, query_w, precision=PRECISE)).reshape(TOKENS, KVH, HEAD)
        key_pre = low_back(jnp.dot(normed_low, key_w, precision=PRECISE)).reshape(TOKENS, KVH, HEAD)
        values = low(low_back(jnp.dot(normed_low, value_w, precision=PRECISE))).reshape(GROUPS, TOK_GRP, KVH, HEAD)
        query = low(query_pre * cosine + half_turn(query_pre) * sine).reshape(GROUPS, TOK_GRP, KVH, HEAD)
        keys = low(key_pre * cosine + half_turn(key_pre) * sine).reshape(GROUPS, TOK_GRP, KVH, HEAD)
        heads_out = lax.map(jax.checkpoint(attend_group), (query, keys, values, segments))
        heads_low = low(low_back(heads_out.reshape(TOKENS, KVH * HEAD)))
        span = QH * HEAD
        branch = jnp.zeros((TOKENS, D), jnp.float32)
        for expert in range(AEXP):
            contrib = jnp.dot(heads_low[:, expert * span:(expert + 1) * span], out_w[expert * span:(expert + 1) * span], precision=PRECISE)
            branch = branch + gate_table[:, expert:expert + 1] * low_back(contrib)
        hidden = resid + branch
        normed_two = norm_forward(hidden, gain_mlp)
        normed_two_low = low(normed_two)
        mlp_gates = pair_gates(jnp.dot(normed_two, router_mlp, precision=PRECISE), mlp_routes)[0]
        pair_rows = low_back(normed_two_low[pair_ids // 2])
        extended = jnp.concatenate([pair_rows, jnp.zeros((1, D), jnp.float32)], axis=0)
        inboxes = extended[owner].reshape(EXPERTS, GROUPS * CAP, D)
        made = lax.map(jax.checkpoint(expert_apply), (inboxes, gate_w, up_w, down_w))
        made = jnp.concatenate([made.reshape(-1, D), jnp.zeros((1, D), jnp.float32)], axis=0)
        returned = made[destination].reshape(TOKENS, 2, D)
        result_rows = hidden + lax.optimization_barrier(jnp.sum(mlp_gates[:, :, None] * returned, axis=1))
        return result_rows[deal]
    floats = [tokens.astype(jnp.float32), attn_gain.astype(jnp.float32), attn_router.astype(jnp.float32), w_query.astype(jnp.float32), w_key.astype(jnp.float32), w_value.astype(jnp.float32), w_out.astype(jnp.float32), mlp_gain.astype(jnp.float32), mlp_router.astype(jnp.float32), w_gate.astype(jnp.float32), w_up.astype(jnp.float32), w_down.astype(jnp.float32)]
    result, pullback = jax.vjp(forward, *floats)
    gradients = pullback(out_grad.astype(jnp.float32))
    return (result.astype(jnp.bfloat16), gradients[0].astype(jnp.bfloat16), gradients[1], gradients[2], gradients[3], gradients[4], gradients[5], gradients[6], gradients[7], gradients[8], gradients[9], gradients[10], gradients[11])
```

```python
import functools
import math

import jax
import jax.numpy as jnp
from jax import lax
from jax.experimental import pallas as pl
from jax.experimental.pallas import tpu as pltpu
from jax.sharding import PartitionSpec as P

HEAD = 128
QH = 2


PRECISE = lax.Precision.HIGHEST
EPSILON = 1e-06
MASKED = -1e30


def half_turn(values):
    middle = values.shape[-1] // 2
    return jnp.concatenate([-values[..., middle:], values[..., :middle]], axis=-1)


def undo_turn(values, cosine, sine):
    return values * cosine - half_turn(values * sine)


def rotary_tables(lengths, tok_rows):
    seq_ends = jnp.cumsum(lengths)
    seq_starts = seq_ends - lengths
    places = jnp.arange(tok_rows, dtype=jnp.int32)
    segment = jnp.sum((places[:, None] >= seq_ends[None, :]).astype(jnp.int32), axis=1)
    matches = segment[:, None] == jnp.arange(lengths.shape[0], dtype=jnp.int32)[None, :]
    seq_first = jnp.sum(jnp.where(matches, seq_starts[None, :], 0), axis=1)
    offsets = (places - seq_first).astype(jnp.float32)
    frequency = jnp.exp(-math.log(10000.0) * jnp.arange(0, HEAD, 2, dtype=jnp.float32) / HEAD)
    angles = offsets[:, None] * frequency[None, :]
    angles = jnp.concatenate([angles, angles], axis=1)
    return (segment, jnp.cos(angles)[:, None, :], jnp.sin(angles)[:, None, :])


def pair_gates(logits, routes):
    columns = logits.shape[1]
    chosen_mask = (
        routes[:, :, None] == jnp.arange(columns, dtype=jnp.int32)[None, None, :]
    ).astype(jnp.float32)
    picked = jnp.sum(chosen_mask * logits[:, None, :], axis=2)
    return (jax.nn.softmax(picked, axis=1), chosen_mask)


def pair_back(gates, chosen_mask, gate_grads):
    inner = gates * (gate_grads - jnp.sum(gates * gate_grads, axis=1, keepdims=True))
    return jnp.sum(chosen_mask * inner[:, :, None], axis=1)


def slot_table(routes, priority, capacity):
    target = routes.reshape(-1)
    ahead = (target[None, :] == target[:, None]) & (priority[None, :] < priority[:, None])
    position = jnp.sum(ahead.astype(jnp.int32), axis=1)
    return (target, position, position < capacity)


def norm_stats(values, gain):
    factor = lax.rsqrt(jnp.mean(values * values, axis=1, keepdims=True) + EPSILON)
    scaled = values * factor
    return (factor, scaled, scaled * gain)


def block_scores(query, keys, segment, start, block_rows, scale):
    places = jnp.arange(keys.shape[0], dtype=jnp.int32)
    allowed = (segment[start : start + block_rows, None] == segment[None, :]) & (
        places[:, None] >= places[None, :]
    )
    raw = jnp.einsum("qhd,khd->hqk", query, keys, preferred_element_type=jnp.float32) * scale
    return jnp.where(allowed[None], raw, MASKED)


MESH = pl.DeviceIdType.MESH
MIB = 1 << 20


def flip(number, other, count):
    total, bit = 0, 1
    while bit < count:
        total = total + lax.rem(lax.div(number, bit) + lax.div(other, bit), 2) * bit
        bit *= 2
    return total


def dot_nt(left, right):
    return lax.dot_general(
        left, right, (((1,), (1,)), ((), ())), preferred_element_type=jnp.float32
    )


class Place:
    def __init__(self):
        self.groups = lax.axis_size("expert")
        self.parts = lax.axis_size("tensor")
        self.spots = self.parts // 2
        self.expert = lax.axis_index("expert")
        self.tensor = lax.axis_index("tensor")
        self.spot = lax.div(self.tensor, 2)
        self.core = lax.rem(self.tensor, 2)

    def device(self, expert, tensor):
        return {"expert": expert, "tensor": tensor}

    def across(self, step):
        return lax.rem(self.spot + step, self.spots) * 2 + self.core

    def before(self, step):
        return lax.rem(self.spot + self.spots - step, self.spots) * 2 + self.core

    def meet(self, over_expert):
        peers = [self.device(self.expert, self.spot * 2 + 1 - self.core)]
        for step in range(1, self.spots):
            peers.append(self.device(self.expert, self.across(step)))
        if over_expert:
            for step in range(1, self.groups):
                peers.append(self.device(flip(self.expert, step, self.groups), self.tensor))
        barrier = pltpu.get_barrier_semaphore()
        for peer in peers:
            pl.semaphore_signal(barrier, inc=1, device_id=peer, device_id_type=MESH)
        pl.semaphore_wait(barrier, len(peers))


def remote(source, target, send, receive, device):
    return pltpu.make_async_remote_copy(
        src_ref=source,
        dst_ref=target,
        send_sem=send,
        recv_sem=receive,
        device_id=device,
        device_id_type=MESH,
    )


class Spread:
    @staticmethod
    def scratch(chunks, spots):
        return [
            pltpu.SemaphoreType.DMA((chunks,)),
            pltpu.SemaphoreType.DMA((chunks,)),
            pltpu.SemaphoreType.DMA((chunks, max(spots - 1, 1))),
            pltpu.SemaphoreType.DMA((chunks, max(spots - 1, 1))),
            pltpu.SemaphoreType.DMA((chunks, spots)),
            pltpu.SemaphoreType.DMA((chunks, spots)),
        ]

    def __init__(self, place, source, target, sems, over_expert, sharers=1):
        self.place, self.source, self.target = place, source, target
        self.first_send, self.first_land, self.side_send, self.side_land, self.core_send, self.core_land = sems
        self.over_expert, self.sharers = over_expert, sharers
        self.width = source.shape[3]
        self.chunks = target.shape[1]

    def owner(self, chunk):
        if self.over_expert:
            return flip(self.place.expert, chunk, self.place.groups)
        return chunk

    def spot_of(self, owner, tensor):
        first = pl.multiple_of(tensor * self.width, 128)
        return self.target.at[:, owner, :, pl.ds(first, self.width)]

    def block(self, owner):
        if self.sharers == 1:
            return self.source.at[:, owner]
        return self.source.at[:, lax.div(owner, self.sharers)]

    def start(self):
        place = self.place
        own = self.owner(0)
        if not self.over_expert:
            return
        for chunk in range(1, self.chunks):
            peer = self.owner(chunk)
            remote(
                self.block(peer),
                self.spot_of(place.expert, place.tensor),
                self.first_send.at[chunk],
                self.first_land.at[chunk],
                place.device(peer, place.tensor),
            ).start()
        copy = pltpu.make_async_copy(
            self.block(own), self.spot_of(own, place.tensor), self.first_send.at[0]
        )
        copy.start()
        copy.wait()

    def first(self, chunk):
        place = self.place
        owner = self.owner(chunk)
        mine = self.spot_of(owner, place.tensor)
        if self.over_expert:

            @pl.when(chunk > 0)
            def _():
                remote(
                    self.block(owner),
                    mine,
                    self.first_send.at[chunk],
                    self.first_land.at[chunk],
                    place.device(owner, place.tensor),
                ).wait_recv()

            held = mine
        else:
            pltpu.make_async_copy(self.block(owner), mine, self.first_send.at[chunk]).start()
            held = self.block(owner)
        for step in range(1, place.spots):
            remote(
                held,
                mine,
                self.side_send.at[chunk, step - 1],
                self.side_land.at[chunk, step - 1],
                place.device(place.expert, place.across(step)),
            ).start()
        remote(
            held,
            mine,
            self.core_send.at[chunk, 0],
            self.core_land.at[chunk, 0],
            place.device(place.expert, place.spot * 2 + 1 - place.core),
        ).start()

    def second(self, chunk):
        place = self.place
        owner = self.owner(chunk)
        for step in range(1, place.spots):
            came = self.spot_of(owner, place.before(step))
            remote(
                came,
                came,
                self.side_send.at[chunk, step - 1],
                self.side_land.at[chunk, step - 1],
                place.device(place.expert, place.across(step)),
            ).wait_recv()
            remote(
                came,
                came,
                self.core_send.at[chunk, step],
                self.core_land.at[chunk, step],
                place.device(place.expert, place.spot * 2 + 1 - place.core),
            ).start()

    def third(self, chunk):
        place = self.place
        owner = self.owner(chunk)
        flipped = 1 - 2 * place.core
        for step in range(place.spots):
            came = self.spot_of(owner, place.before(step) + flipped)
            remote(
                came,
                came,
                self.core_send.at[chunk, step],
                self.core_land.at[chunk, step],
                place.device(place.expert, place.spot * 2 + 1 - place.core),
            ).wait_recv()

    def finish(self, chunk):
        place = self.place
        owner = self.owner(chunk)
        mine = self.spot_of(owner, place.tensor)
        device = place.device(place.expert, place.tensor)
        if self.over_expert:

            @pl.when(chunk > 0)
            def _():
                remote(
                    self.block(owner),
                    mine,
                    self.first_send.at[chunk],
                    self.first_land.at[chunk],
                    device,
                ).wait_send()

        else:
            pltpu.make_async_copy(self.block(owner), mine, self.first_send.at[chunk]).wait()
        for step in range(1, place.spots):
            remote(
                mine,
                mine,
                self.side_send.at[chunk, step - 1],
                self.side_land.at[chunk, step - 1],
                device,
            ).wait_send()
        for step in range(place.spots):
            remote(
                mine, mine, self.core_send.at[chunk, step], self.core_land.at[chunk, step], device
            ).wait_send()


class Collect:
    @staticmethod
    def scratch(chunks, kinds, spots, rows, width):
        return [
            pltpu.VMEM((2, kinds, spots, 2, rows, width), jnp.bfloat16),
            pltpu.VMEM((2, kinds, max(spots - 1, 1), rows, width), jnp.bfloat16),
            pltpu.VMEM((chunks, kinds, spots, rows, width), jnp.bfloat16),
            pltpu.VMEM((chunks, kinds, max(spots - 1, 1), rows, width), jnp.bfloat16),
            pltpu.SemaphoreType.DMA((chunks,)),
            pltpu.SemaphoreType.DMA((chunks,)),
            pltpu.SemaphoreType.DMA((chunks, max(spots - 1, 1))),
            pltpu.SemaphoreType.DMA((chunks, max(spots - 1, 1))),
        ]

    def __init__(self, place, refs):
        self.place = place
        self.stage, self.side, self.core_in, self.side_in = refs[:4]
        self.core_send, self.core_land, self.side_send, self.side_land = refs[4:]
        self.chunks = self.core_in.shape[0]

    def core_copy(self, chunk):
        place = self.place
        return remote(
            self.stage.at[lax.rem(chunk, 2), :, :, 1 - place.core],
            self.core_in.at[chunk],
            self.core_send.at[chunk],
            self.core_land.at[chunk],
            place.device(place.expert, place.spot * 2 + 1 - place.core),
        )

    def side_copy(self, chunk, step):
        place = self.place
        return remote(
            self.side.at[lax.rem(chunk, 2), :, step - 1],
            self.side_in.at[chunk, :, step - 1],
            self.side_send.at[chunk, step - 1],
            self.side_land.at[chunk, step - 1],
            place.device(place.expert, place.across(step)),
        )

    def free_stage(self, chunk):
        @pl.when(chunk >= 2)
        def _():
            self.core_copy(chunk - 2).wait_send()

    def first(self, chunk):
        self.core_copy(chunk).start()

    def second(self, chunk):
        place = self.place
        slot = lax.rem(chunk, 2)
        self.core_copy(chunk).wait_recv()

        @pl.when(chunk >= 2)
        def _():
            for step in range(1, place.spots):
                self.side_copy(chunk - 2, step).wait_send()

        for step in range(1, place.spots):
            there = lax.rem(place.spot + step, place.spots)
            total = self.stage[slot, :, there, place.core].astype(jnp.float32) + self.core_in[
                chunk, :, there
            ].astype(jnp.float32)
            self.side[slot, :, step - 1] = total.astype(jnp.bfloat16)
            self.side_copy(chunk, step).start()

    def third(self, chunk):
        place = self.place
        slot = lax.rem(chunk, 2)
        total = self.stage[slot, :, place.spot, place.core].astype(jnp.float32) + self.core_in[
            chunk, :, place.spot
        ].astype(jnp.float32)
        for step in range(1, place.spots):
            self.side_copy(chunk, step).wait_recv()
            total = total + self.side_in[chunk, :, step - 1].astype(jnp.float32)
        return total

    def finish(self):
        for chunk in range(max(self.chunks - 2, 0), self.chunks):
            self.core_copy(chunk).wait_send()
            for step in range(1, self.place.spots):
                self.side_copy(chunk, step).wait_send()


def when(condition, action, *args):
    pl.when(condition)(functools.partial(action, *args))


def spread_kernel(over_expert, source, target, *sems):
    place = Place()
    spread = Spread(place, source, target, sems, over_expert)
    place.meet(over_expert)
    spread.start()

    def step(turn, carry):
        when(turn < spread.chunks, spread.first, turn)
        when(turn >= 1, spread.second, turn - 1)
        return carry

    lax.fori_loop(0, spread.chunks + 1, step, 0)

    def last(turn, carry):
        spread.third(turn)
        spread.finish(turn)
        return carry

    lax.fori_loop(0, spread.chunks, last, 0)


def spread_rows(rows, over_expert, collective):
    chunks, count, width = rows.shape
    parts = lax.axis_size("tensor")
    full = pl.pallas_call(
        functools.partial(spread_kernel, over_expert),
        out_shape=jax.ShapeDtypeStruct((1, chunks, count, width * parts), rows.dtype),
        in_specs=[pl.BlockSpec(memory_space=pl.ANY)],
        out_specs=pl.BlockSpec(memory_space=pl.ANY),
        scratch_shapes=Spread.scratch(chunks, parts // 2),
        compiler_params=pltpu.CompilerParams(collective_id=collective, has_side_effects=True),
    )(rows[None])
    return full.reshape(chunks * count, width * parts)


def collect_kernel(make, operand_count, *refs):
    place = Place()
    operands = refs[:operand_count]
    result = refs[operand_count]
    collect = Collect(place, refs[operand_count + 1 :])
    place.meet(False)

    def one(chunk):
        collect.free_stage(chunk)
        slot = lax.rem(chunk, 2)
        width = result.shape[2]
        for spot in range(place.spots):
            for core in range(2):
                first = (spot * 2 + core) * width
                part = make(operands, chunk, first, width)
                collect.stage[slot, 0, spot, core] = part.astype(jnp.bfloat16)
        collect.first(chunk)

    def close(chunk):
        result[chunk] = collect.third(chunk)[0]

    def step(turn, carry):
        when(turn >= 2, close, turn - 2)
        when((turn >= 1) & (turn <= collect.chunks), collect.second, turn - 1)
        when(turn < collect.chunks, one, turn)
        return carry

    lax.fori_loop(0, collect.chunks + 2, step, 0)
    collect.finish()


def collect_rows(make, operands, chunks, rows, width, collective):
    parts = lax.axis_size("tensor")
    out = pl.pallas_call(
        functools.partial(collect_kernel, make, len(operands)),
        out_shape=jax.ShapeDtypeStruct((chunks, rows, width), jnp.float32),
        in_specs=[pl.BlockSpec(memory_space=pltpu.VMEM)] * len(operands),
        out_specs=pl.BlockSpec(memory_space=pltpu.VMEM),
        scratch_shapes=Collect.scratch(chunks, 1, parts // 2, rows, width),
        compiler_params=pltpu.CompilerParams(
            collective_id=collective, has_side_effects=True, vmem_limit_bytes=48 * MIB
        ),
    )(*operands)
    return out.reshape(chunks * rows, width)


def make_attended(span, operands, chunk, first, width):
    heads, gates, weight = operands
    total = None
    for expert in range(gates.shape[2]):
        term = gates[chunk, :, expert : expert + 1] * jnp.dot(
            heads[chunk, :, expert * span : (expert + 1) * span],
            weight[expert * span : (expert + 1) * span, first : first + width],
            preferred_element_type=jnp.float32,
        )
        total = term if total is None else total + term
    return total


def make_projected(operands, chunk, first, width):
    grads, weights = operands[:3], operands[3:]
    total = None
    for grad, weight in zip(grads, weights):
        term = dot_nt(grad[chunk], weight[first : first + width, :])
        total = term if total is None else total + term
    return total


def experts_kernel(sharers, *refs):
    (
        source, gate_hbm, up_hbm, down_hbm,
        inbox, middle_out, gate_out, up_out, returned,
        gate_w, up_w, down_w, rows, middle, gate_g, up_g, closing,
        load_sem, store_sem, back_send, back_land,
    ) = refs[:21]
    place = Place()
    spread = Spread(place, source, inbox, refs[21:27], True, sharers)
    collect = Collect(place, refs[27:])
    chunks = spread.chunks
    width = source.shape[3]
    units = gate_w.shape[1]
    tile = 704 if units % 704 == 0 else units
    loads = [
        pltpu.make_async_copy(held, kept, load_sem.at[number])
        for number, (held, kept) in enumerate(
            ((gate_hbm, gate_w), (up_hbm, up_w), (down_hbm, down_w))
        )
    ]
    for load in loads:
        load.start()
    place.meet(True)
    spread.start()

    def stores(owner):
        return [
            pltpu.make_async_copy(held, out.at[owner], store_sem.at[number])
            for number, (held, out) in enumerate(
                ((middle, middle_out), (gate_g, gate_out), (up_g, up_out))
            )
        ]

    def work(chunk):
        owner = spread.owner(chunk)
        slot = lax.rem(chunk, 2)
        spread.third(chunk)
        fetch = pltpu.make_async_copy(inbox.at[:, owner], rows, load_sem.at[3])
        fetch.start()

        @pl.when(chunk == 0)
        def _():
            for load in loads:
                load.wait()

        @pl.when(chunk > 0)
        def _():
            for store in stores(spread.owner(chunk - 1)):
                store.wait()

        collect.free_stage(chunk)
        fetch.wait()
        for first in range(0, units, tile):
            here = slice(first, first + tile)
            gate = jnp.dot(rows[0], gate_w[:, here], preferred_element_type=jnp.float32)
            up = jnp.dot(rows[0], up_w[:, here], preferred_element_type=jnp.float32)
            sig = jax.nn.sigmoid(gate)
            act = gate * sig
            middle[:, here] = (act * up).astype(jnp.bfloat16)
            grad = dot_nt(rows[1], down_w[here, :])
            gate_g[:, here] = (grad * up * sig * (1.0 + gate * (1.0 - sig))).astype(jnp.bfloat16)
            up_g[:, here] = (grad * act).astype(jnp.bfloat16)
        for store in stores(owner):
            store.start()
        for spot in range(place.spots):
            for core in range(2):
                first = (spot * 2 + core) * width
                here = slice(first, first + width)
                collect.stage[slot, 0, spot, core] = jnp.dot(
                    middle[...], down_w[:, here], preferred_element_type=jnp.float32
                ).astype(jnp.bfloat16)
                collect.stage[slot, 1, spot, core] = (
                    dot_nt(gate_g[...], gate_w[here, :]) + dot_nt(up_g[...], up_w[here, :])
                ).astype(jnp.bfloat16)
        collect.first(chunk)

    def back_copy(chunk):
        owner = spread.owner(chunk)
        return remote(
            closing.at[lax.rem(chunk, 2)],
            returned.at[:, place.expert],
            back_send.at[chunk],
            back_land.at[chunk],
            place.device(owner, place.tensor),
        )

    def close(chunk):
        slot = lax.rem(chunk, 2)
        total = collect.third(chunk)

        @pl.when(chunk >= 3)
        def _():
            back_copy(chunk - 2).wait_send()

        closing[slot] = total.astype(jnp.bfloat16)

        @pl.when(chunk > 0)
        def _():
            back_copy(chunk).start()

        @pl.when(chunk == 0)
        def _():
            own = pltpu.make_async_copy(
                closing.at[slot], returned.at[:, place.expert], back_send.at[chunk]
            )
            own.start()
            own.wait()

    def step(turn, carry):
        now = turn - 2
        when(turn < chunks, spread.first, turn)
        when((turn >= 1) & (turn <= chunks), spread.second, turn - 1)
        when(now >= 2, close, now - 2)
        when((now >= 1) & (now <= chunks), collect.second, now - 1)
        when((now >= 0) & (now < chunks), work, now)
        return carry

    lax.fori_loop(0, chunks + 4, step, 0)

    def last(turn, carry):
        spread.finish(turn)

        @pl.when(turn > 0)
        def _():
            owner = spread.owner(turn)
            remote(
                closing.at[0],
                returned.at[:, owner],
                back_send.at[turn],
                back_land.at[turn],
                place.device(owner, place.tensor),
            ).wait_recv()

        return carry

    lax.fori_loop(0, chunks, last, 0)
    for store in stores(spread.owner(chunks - 1)):
        store.wait()
    for chunk in range(max(chunks - 2, 1), chunks):
        back_copy(chunk).wait_send()
    collect.finish()


def experts(source, gate_w, up_w, down_w, sharers, collective):
    kinds, _, capacity, width = source.shape
    groups, parts = lax.axis_size("expert"), lax.axis_size("tensor")
    spots = parts // 2
    model_width, units = gate_w.shape
    low = jnp.bfloat16
    anywhere = pl.BlockSpec(memory_space=pl.ANY)
    hidden_rows = jax.ShapeDtypeStruct((groups, capacity, units), low)
    return pl.pallas_call(
        functools.partial(experts_kernel, sharers),
        out_shape=(
            jax.ShapeDtypeStruct((kinds, groups, capacity, model_width), low),
            hidden_rows,
            hidden_rows,
            hidden_rows,
            jax.ShapeDtypeStruct((kinds, groups, capacity, width), low),
        ),
        in_specs=[anywhere] * 4,
        out_specs=(anywhere,) * 5,
        scratch_shapes=[
            pltpu.VMEM((model_width, units), low),
            pltpu.VMEM((model_width, units), low),
            pltpu.VMEM((units, model_width), low),
            pltpu.VMEM((kinds, capacity, model_width), low),
            pltpu.VMEM((capacity, units), low),
            pltpu.VMEM((capacity, units), low),
            pltpu.VMEM((capacity, units), low),
            pltpu.VMEM((2, kinds, capacity, width), low),
            pltpu.SemaphoreType.DMA((4,)),
            pltpu.SemaphoreType.DMA((3,)),
            pltpu.SemaphoreType.DMA((groups,)),
            pltpu.SemaphoreType.DMA((groups,)),
        ]
        + Spread.scratch(groups, spots)
        + Collect.scratch(groups, kinds, spots, capacity, width),
        compiler_params=pltpu.CompilerParams(
            collective_id=collective, has_side_effects=True, vmem_limit_bytes=60 * MIB
        ),
    )(source, gate_w, up_w, down_w)


def to_expert(rows, group_count):
    count, width = rows.shape
    return lax.all_to_all(
        rows.reshape(group_count, count // group_count, width),
        "expert",
        split_axis=0,
        concat_axis=0,
        tiled=True,
    ).reshape(count, width)


def gather_tensor(rows):
    return lax.all_gather(rows, "tensor", axis=0)


def body(
    tokens,
    out_grad,
    attn_gain,
    attn_router,
    w_query,
    w_key,
    w_value,
    w_out,
    mlp_gain,
    mlp_router,
    w_gate,
    w_up,
    w_down,
    deal,
    seq_lengths,
    attn_routes,
    mlp_routes,
    slot_order,
):
    tok_rows, model_width = tokens.shape
    group_count = lax.axis_size("expert")
    part_count = lax.axis_size("tensor")
    group_index = lax.axis_index("expert")
    part_index = lax.axis_index("tensor")
    bucket_rows = tok_rows // group_count
    col_width = model_width // part_count
    col_first = part_index * col_width
    low = jnp.bfloat16

    def own_cols(values):
        return lax.dynamic_slice_in_dim(values, col_first, col_width, values.ndim - 1)

    deal_rank = deal // tok_rows * bucket_rows + (deal % tok_rows - group_index * bucket_rows)
    row_ids = jnp.arange(tok_rows, dtype=jnp.int32)
    deal_mask = (row_ids[:, None] == deal_rank[None, :]).astype(low)
    dealt = jnp.dot(deal_mask, own_cols(tokens), preferred_element_type=jnp.float32).astype(low)
    resid_low = spread_rows(dealt.reshape(group_count, bucket_rows, col_width), True, 0)
    grad_cols_low = to_expert(
        jnp.dot(deal_mask, own_cols(out_grad), preferred_element_type=jnp.float32).astype(low),
        group_count,
    )
    grad_cols = grad_cols_low.astype(jnp.float32)
    resid_in = resid_low.astype(jnp.float32)
    resid_cols = own_cols(resid_low).astype(jnp.float32)
    gain_one, gain_two = own_cols(attn_gain), own_cols(mlp_gain)
    router_one = lax.dynamic_slice_in_dim(attn_router, col_first, col_width, 0)
    router_two = lax.dynamic_slice_in_dim(mlp_router, col_first, col_width, 0)
    expert_count = mlp_router.shape[1]
    sharers = group_count // expert_count
    capacity = 5 * tok_rows // (2 * expert_count)
    target, position, kept = slot_table(mlp_routes, slot_order[0], capacity)
    slots = expert_count * capacity
    destination = jnp.where(kept, target * capacity + position, slots).reshape(tok_rows, 2)
    slot_ids = jnp.arange(slots, dtype=jnp.int32)
    chosen = [destination[:, way] for way in range(2)]
    to_slot = (
        (slot_ids[:, None] == chosen[0][None, :]) | (slot_ids[:, None] == chosen[1][None, :])
    ).astype(low)
    slot_grads = jnp.dot(to_slot, grad_cols_low, preferred_element_type=jnp.float32)

    segment, cosine, sine = rotary_tables(seq_lengths[0], tok_rows)
    scale = 1.0 / math.sqrt(HEAD)
    local_heads = w_query.shape[1] // HEAD
    local_experts = local_heads // QH
    span = QH * HEAD
    factor_one, scaled_one, normed_one = norm_stats(resid_in, attn_gain)
    normed_low = normed_one.astype(low)
    attn_logits = jnp.dot(normed_one, attn_router, precision=PRECISE)
    attn_gates, attn_mask = pair_gates(attn_logits, attn_routes)
    gate_table = jnp.sum(attn_gates[:, :, None] * attn_mask, axis=1)
    gate_local = lax.dynamic_slice_in_dim(gate_table, part_index * local_experts, local_experts, 1)
    query_pre = jnp.dot(normed_low, w_query, preferred_element_type=jnp.float32).reshape(
        tok_rows, local_heads, HEAD
    )
    key_pre = jnp.dot(normed_low, w_key, preferred_element_type=jnp.float32).reshape(
        tok_rows, local_heads, HEAD
    )
    values = (
        jnp.dot(normed_low, w_value, preferred_element_type=jnp.float32)
        .astype(low)
        .reshape(tok_rows, local_heads, HEAD)
    )
    query = (query_pre * cosine + half_turn(query_pre) * sine).astype(low)
    keys = (key_pre * cosine + half_turn(key_pre) * sine).astype(low)
    scores = block_scores(query, keys, segment, 0, tok_rows, scale)
    top_score = jnp.max(scores, axis=-1, keepdims=True)
    expo = jnp.exp(scores - top_score)
    totals = jnp.sum(expo, axis=-1, keepdims=True)
    probs = (expo / totals).astype(low)
    head_blocks = jnp.einsum("hqk,khd->qhd", probs, values, preferred_element_type=jnp.float32)
    log_total = top_score + jnp.log(totals)
    heads_low = head_blocks.astype(low).reshape(tok_rows, local_heads * HEAD)
    pieces, piece_rows = 4, tok_rows // 4
    attn_cols = collect_rows(
        functools.partial(make_attended, span),
        (
            heads_low.reshape(pieces, piece_rows, local_heads * HEAD),
            gate_local.reshape(pieces, piece_rows, local_experts),
            w_out,
        ),
        pieces,
        piece_rows,
        col_width,
        1,
    )
    hidden = resid_cols + attn_cols
    weighed = hidden * gain_two
    stats = jnp.concatenate(
        [
            jnp.sum(hidden * hidden, axis=1)[None, :],
            jnp.dot(weighed, router_two, precision=PRECISE).T,
        ],
        axis=0,
    )
    stats = jnp.sum(gather_tensor(stats), axis=0)
    factor_two = lax.rsqrt(stats[0] / model_width + EPSILON)[:, None]
    mlp_logits = stats[1:].T * factor_two
    scaled_two = hidden * factor_two
    normed_two = scaled_two * gain_two
    mlp_gates, mlp_mask = pair_gates(mlp_logits, mlp_routes)
    slot_rows = jnp.dot(
        to_slot, normed_two.astype(low), preferred_element_type=jnp.float32
    ).astype(low)
    slot_gates = sum(
        jnp.sum(
            jnp.where(slot_ids[:, None] == chosen[way][None, :], mlp_gates[:, way][None, :], 0.0),
            axis=1,
        )
        for way in range(2)
    )
    slot_grads = (slot_gates[:, None] * slot_grads).astype(low)
    inbox, middle, gate_grad, up_grad, returned = experts(
        jnp.stack([slot_rows, slot_grads]).reshape(2, expert_count, capacity, col_width),
        w_gate[0],
        w_up[0],
        w_down[0],
        sharers,
        2,
    )
    if sharers > 1:
        returned = (
            jnp.sum(
                returned.reshape(2, expert_count, sharers, capacity, col_width).astype(jnp.float32),
                axis=2,
            )
        ).astype(low)
    made, row_grads = returned.reshape(2, slots, col_width)
    from_slot = [(chosen[way][:, None] == slot_ids[None, :]).astype(low) for way in range(2)]
    pair_values = jnp.stack(
        [
            jnp.dot(from_slot[way], made, preferred_element_type=jnp.float32)
            for way in range(2)
        ],
        axis=1,
    )
    row_grad_sum = jnp.dot(
        from_slot[0] + from_slot[1], row_grads, preferred_element_type=jnp.float32
    )
    mixed_cols = hidden + jnp.sum(mlp_gates[:, :, None] * pair_values, axis=1)
    back_mixed = to_expert(mixed_cols.astype(low), group_count)
    weighed_two = scaled_two * gain_two
    stats = jnp.stack(
        [
            jnp.sum(pair_values[:, 0] * grad_cols, axis=1),
            jnp.sum(pair_values[:, 1] * grad_cols, axis=1),
            jnp.sum(row_grad_sum * weighed_two, axis=1),
        ]
    )
    stats = jnp.sum(gather_tensor(stats), axis=0)
    mlp_logit_grad = pair_back(mlp_gates, mlp_mask, stats[:2].T)
    norm_two_grad = row_grad_sum + jnp.dot(mlp_logit_grad, router_two.T, precision=PRECISE)
    mlp_router_grad = jnp.dot(normed_two.T, mlp_logit_grad, precision=PRECISE)
    mlp_gain_grad = jnp.sum(norm_two_grad * scaled_two, axis=0)
    mean_two = (stats[2] + jnp.sum(mlp_logit_grad * mlp_logits, axis=1)) / model_width
    hidden_grad = grad_cols + factor_two * (norm_two_grad * gain_two - scaled_two * mean_two[:, None])
    hidden_grad_low = spread_rows(
        hidden_grad.astype(low).reshape(pieces, piece_rows, col_width), False, 3
    )
    gate_wide = jnp.repeat(gate_local, span, axis=1)
    heads_float = heads_low.astype(jnp.float32)
    out_w_grad = jnp.einsum(
        "tc,td->cd",
        (heads_float * gate_wide).astype(low),
        hidden_grad_low,
        preferred_element_type=jnp.float32,
    )
    heads_plain = jnp.einsum(
        "td,cd->tc", hidden_grad_low, w_out, preferred_element_type=jnp.float32
    )
    local_gate_grad = jnp.sum(
        (heads_plain * heads_float).reshape(tok_rows, local_experts, span), axis=2
    )
    heads_grad = (heads_plain * gate_wide).astype(low).reshape(tok_rows, local_heads, HEAD)
    scores = block_scores(query, keys, segment, 0, tok_rows, scale)
    probs = jnp.exp(scores - log_total)
    value_grad = jnp.einsum(
        "hqk,qhd->khd", probs.astype(low), heads_grad, preferred_element_type=jnp.float32
    )
    prob_grad = jnp.einsum("qhd,khd->hqk", heads_grad, values, preferred_element_type=jnp.float32)
    score_grad = (
        probs * (prob_grad - jnp.sum(probs * prob_grad, axis=-1, keepdims=True))
    ).astype(low)
    query_grad = (
        jnp.einsum("hqk,khd->qhd", score_grad, keys, preferred_element_type=jnp.float32) * scale
    )
    key_grad = (
        jnp.einsum("hqk,qhd->khd", score_grad, query, preferred_element_type=jnp.float32) * scale
    )
    width = local_heads * HEAD
    query_pre_grad = undo_turn(query_grad, cosine, sine).astype(low).reshape(tok_rows, width)
    key_pre_grad = undo_turn(key_grad, cosine, sine).astype(low).reshape(tok_rows, width)
    value_pre_grad = value_grad.astype(low).reshape(tok_rows, width)
    weight_grads = [
        jnp.einsum("td,tc->dc", normed_low, grad, preferred_element_type=jnp.float32)
        for grad in (query_pre_grad, key_pre_grad, value_pre_grad)
    ]
    norm_one_cols = collect_rows(
        make_projected,
        tuple(
            grad.reshape(pieces, piece_rows, width)
            for grad in (query_pre_grad, key_pre_grad, value_pre_grad)
        )
        + (w_query, w_key, w_value),
        pieces,
        piece_rows,
        col_width,
        4,
    )
    scaled_cols = resid_cols * factor_one
    normed_cols = scaled_cols * gain_one
    stats = jnp.concatenate(
        [jnp.sum(norm_one_cols * normed_cols, axis=1)[None, :], local_gate_grad.T], axis=0
    )
    stats = gather_tensor(stats)
    gate_grads = stats[:, 1:].reshape(part_count * local_experts, tok_rows).T
    attn_pair_grad = jnp.sum(attn_mask * gate_grads[:, None, :], axis=2)
    attn_logit_grad = pair_back(attn_gates, attn_mask, attn_pair_grad)
    norm_one_grad = norm_one_cols + jnp.dot(attn_logit_grad, router_one.T, precision=PRECISE)
    attn_router_grad = jnp.dot(normed_cols.T, attn_logit_grad, precision=PRECISE)
    attn_gain_grad = jnp.sum(norm_one_grad * scaled_cols, axis=0)
    mean_one = (
        jnp.sum(stats[:, 0], axis=0) + jnp.sum(attn_logit_grad * attn_logits, axis=1)
    ) / model_width
    input_cols = hidden_grad + factor_one * (
        norm_one_grad * gain_one - scaled_cols * mean_one[:, None]
    )
    back_grad = to_expert(input_cols.astype(low), group_count)
    mixed, tokens_grad = (
        jnp.einsum("ri,rc->ic", deal_mask, back, preferred_element_type=jnp.float32).astype(low)
        for back in (back_mixed, back_grad)
    )
    out_w_grad = lax.psum(out_w_grad.astype(low), "expert").astype(jnp.float32)
    weight_grads = [
        grad.astype(jnp.float32)
        for grad in lax.psum(tuple(grad.astype(low) for grad in weight_grads), "expert")
    ]
    small = jnp.concatenate(
        [attn_gain_grad[None], attn_router_grad.T, mlp_gain_grad[None], mlp_router_grad.T], axis=0
    )
    small = gather_tensor(lax.psum(small, "expert"))
    small = small.transpose(1, 0, 2).reshape(-1, model_width)
    experts_of = attn_router.shape[1]
    rows = inbox.reshape(2, -1, model_width)
    units = middle.shape[2]
    gate_w_grad, up_w_grad = (
        jnp.einsum("sd,sf->df", rows[0], grad.reshape(-1, units), preferred_element_type=jnp.float32)
        for grad in (gate_grad, up_grad)
    )
    down_grad = jnp.einsum(
        "sf,sd->fd", middle.reshape(-1, units), rows[1], preferred_element_type=jnp.float32
    )
    return (
        mixed,
        tokens_grad,
        small[0],
        small[1 : 1 + experts_of].T,
        weight_grads[0],
        weight_grads[1],
        weight_grads[2],
        out_w_grad,
        small[1 + experts_of],
        small[2 + experts_of :].T,
        gate_w_grad[None],
        up_w_grad[None],
        down_grad[None],
    )


def solution(mesh):
    placed = (
        P("expert", None),
        P("expert", None),
        P(),
        P(),
        P(None, "tensor"),
        P(None, "tensor"),
        P(None, "tensor"),
        P("tensor", None),
        P(),
        P(),
        P("expert", None, "tensor"),
        P("expert", None, "tensor"),
        P("expert", "tensor", None),
        P("expert"),
        P("expert", None),
        P("expert", None),
        P("expert", None),
        P("expert", None),
    )
    return jax.shard_map(
        body,
        mesh=mesh,
        in_specs=placed,
        out_specs=(
            P("expert", "tensor"),
            P("expert", "tensor"),
            P(),
            P(),
            P(None, "tensor"),
            P(None, "tensor"),
            P(None, "tensor"),
            P("tensor", None),
            P(),
            P(),
            P("expert", None, "tensor"),
            P("expert", None, "tensor"),
            P("expert", "tensor", None),
        ),
        check_vma=False,
    )
```

```python
import functools
import math

import jax
import jax.numpy as jnp
from jax import lax
from jax.experimental import pallas as pl
from jax.experimental.pallas import tpu as pltpu
from jax.sharding import PartitionSpec as P

HEAD = 128
QH = 2


PRECISE = lax.Precision.HIGHEST
EPSILON = 1e-06
MASKED = -1e30


def half_turn(values):
    middle = values.shape[-1] // 2
    return jnp.concatenate([-values[..., middle:], values[..., :middle]], axis=-1)


def undo_turn(values, cosine, sine):
    return values * cosine - half_turn(values * sine)


def rotary_tables(lengths, tok_rows):
    seq_ends = jnp.cumsum(lengths)
    seq_starts = seq_ends - lengths
    places = jnp.arange(tok_rows, dtype=jnp.int32)
    segment = jnp.sum((places[:, None] >= seq_ends[None, :]).astype(jnp.int32), axis=1)
    matches = segment[:, None] == jnp.arange(lengths.shape[0], dtype=jnp.int32)[None, :]
    seq_first = jnp.sum(jnp.where(matches, seq_starts[None, :], 0), axis=1)
    offsets = (places - seq_first).astype(jnp.float32)
    frequency = jnp.exp(-math.log(10000.0) * jnp.arange(0, HEAD, 2, dtype=jnp.float32) / HEAD)
    angles = offsets[:, None] * frequency[None, :]
    angles = jnp.concatenate([angles, angles], axis=1)
    return (segment, jnp.cos(angles)[:, None, :], jnp.sin(angles)[:, None, :])


def pair_gates(logits, routes):
    columns = logits.shape[1]
    chosen_mask = (
        routes[:, :, None] == jnp.arange(columns, dtype=jnp.int32)[None, None, :]
    ).astype(jnp.float32)
    picked = jnp.sum(chosen_mask * logits[:, None, :], axis=2)
    return (jax.nn.softmax(picked, axis=1), chosen_mask)


def pair_back(gates, chosen_mask, gate_grads):
    inner = gates * (gate_grads - jnp.sum(gates * gate_grads, axis=1, keepdims=True))
    return jnp.sum(chosen_mask * inner[:, :, None], axis=1)


def slot_table(routes, priority, capacity):
    target = routes.reshape(-1)
    ahead = (target[None, :] == target[:, None]) & (priority[None, :] < priority[:, None])
    position = jnp.sum(ahead.astype(jnp.int32), axis=1)
    return (target, position, position < capacity)


def norm_stats(values, gain):
    factor = lax.rsqrt(jnp.mean(values * values, axis=1, keepdims=True) + EPSILON)
    scaled = values * factor
    return (factor, scaled, scaled * gain)


def block_scores(query, keys, segment, start, block_rows, scale):
    places = jnp.arange(keys.shape[0], dtype=jnp.int32)
    allowed = (segment[start : start + block_rows, None] == segment[None, :]) & (
        places[:, None] >= places[None, :]
    )
    raw = jnp.einsum("qhd,khd->hqk", query, keys, preferred_element_type=jnp.float32) * scale
    return jnp.where(allowed[None], raw, MASKED)


MESH = pl.DeviceIdType.MESH
MIB = 1 << 20


def flip(number, other, count):
    total, bit = 0, 1
    while bit < count:
        total = total + lax.rem(lax.div(number, bit) + lax.div(other, bit), 2) * bit
        bit *= 2
    return total


def dot_nt(left, right):
    return lax.dot_general(
        left, right, (((1,), (1,)), ((), ())), preferred_element_type=jnp.float32
    )


class Place:
    def __init__(self):
        self.groups = lax.axis_size("expert")
        self.parts = lax.axis_size("tensor")
        self.spots = self.parts // 2
        self.expert = lax.axis_index("expert")
        self.tensor = lax.axis_index("tensor")
        self.spot = lax.div(self.tensor, 2)
        self.core = lax.rem(self.tensor, 2)

    def device(self, expert, tensor):
        return {"expert": expert, "tensor": tensor}

    def across(self, step):
        return lax.rem(self.spot + step, self.spots) * 2 + self.core

    def before(self, step):
        return lax.rem(self.spot + self.spots - step, self.spots) * 2 + self.core

    def meet(self, over_expert, whole_tensor=False):
        if whole_tensor:
            peers = [self.device(self.expert, self.along(step)) for step in range(1, self.parts)]
        else:
            peers = [self.device(self.expert, self.spot * 2 + 1 - self.core)]
            for step in range(1, self.spots):
                peers.append(self.device(self.expert, self.across(step)))
        if over_expert:
            for step in range(1, self.groups):
                peers.append(self.device(flip(self.expert, step, self.groups), self.tensor))
        barrier = pltpu.get_barrier_semaphore()
        for peer in peers:
            pl.semaphore_signal(barrier, inc=1, device_id=peer, device_id_type=MESH)
        pl.semaphore_wait(barrier, len(peers))

    def along(self, step):
        return lax.rem(self.tensor + step, self.parts)


def lasting(microseconds):
    return pl.CostEstimate(
        flops=0, bytes_accessed=int(microseconds * 3_000_000), transcendentals=0
    )


def remote(source, target, send, receive, device):
    return pltpu.make_async_remote_copy(
        src_ref=source,
        dst_ref=target,
        send_sem=send,
        recv_sem=receive,
        device_id=device,
        device_id_type=MESH,
    )


class Spread:
    @staticmethod
    def scratch(chunks, spots):
        return [
            pltpu.SemaphoreType.DMA((chunks,)),
            pltpu.SemaphoreType.DMA((chunks,)),
            pltpu.SemaphoreType.DMA((chunks, max(spots - 1, 1))),
            pltpu.SemaphoreType.DMA((chunks, max(spots - 1, 1))),
            pltpu.SemaphoreType.DMA((chunks, spots)),
            pltpu.SemaphoreType.DMA((chunks, spots)),
        ]

    def __init__(self, place, source, target, sems, over_expert, sharers=1):
        self.place, self.source, self.target = place, source, target
        self.first_send, self.first_land, self.side_send, self.side_land, self.core_send, self.core_land = sems
        self.over_expert, self.sharers = over_expert, sharers
        self.width = source.shape[3]
        self.chunks = target.shape[1]

    def owner(self, chunk):
        if not self.over_expert:
            return chunk
        half, odd, pair = self.place.groups // 2, lax.rem(chunk, 2), lax.div(chunk, 2)
        even_way = jnp.minimum(chunk, 1) * half + pair
        odd_way = pair + (1 - jnp.minimum(pair, 1)) * half
        return flip(
            self.place.expert, odd * odd_way + (1 - odd) * even_way, self.place.groups
        )

    def spot_of(self, owner, tensor):
        first = pl.multiple_of(tensor * self.width, 128)
        return self.target.at[:, owner, :, pl.ds(first, self.width)]

    def block(self, owner):
        if self.sharers == 1:
            return self.source.at[:, owner]
        return self.source.at[:, lax.div(owner, self.sharers)]

    def start(self):
        place = self.place
        own = self.owner(0)
        if not self.over_expert:
            return
        for chunk in range(1, self.chunks):
            peer = self.owner(chunk)
            remote(
                self.block(peer),
                self.spot_of(place.expert, place.tensor),
                self.first_send.at[chunk],
                self.first_land.at[chunk],
                place.device(peer, place.tensor),
            ).start()
        copy = pltpu.make_async_copy(
            self.block(own), self.spot_of(own, place.tensor), self.first_send.at[0]
        )
        copy.start()
        copy.wait()

    def first(self, chunk):
        place = self.place
        owner = self.owner(chunk)
        mine = self.spot_of(owner, place.tensor)
        if self.over_expert:

            @pl.when(chunk > 0)
            def _():
                remote(
                    self.block(owner),
                    mine,
                    self.first_send.at[chunk],
                    self.first_land.at[chunk],
                    place.device(owner, place.tensor),
                ).wait_recv()

            held = mine
        else:
            pltpu.make_async_copy(self.block(owner), mine, self.first_send.at[chunk]).start()
            held = self.block(owner)
        for step in range(1, place.spots):
            remote(
                held,
                mine,
                self.side_send.at[chunk, step - 1],
                self.side_land.at[chunk, step - 1],
                place.device(place.expert, place.across(step)),
            ).start()
        remote(
            held,
            mine,
            self.core_send.at[chunk, 0],
            self.core_land.at[chunk, 0],
            place.device(place.expert, place.spot * 2 + 1 - place.core),
        ).start()

    def second(self, chunk):
        place = self.place
        owner = self.owner(chunk)
        for step in range(1, place.spots):
            came = self.spot_of(owner, place.before(step))
            remote(
                came,
                came,
                self.side_send.at[chunk, step - 1],
                self.side_land.at[chunk, step - 1],
                place.device(place.expert, place.across(step)),
            ).wait_recv()
            remote(
                came,
                came,
                self.core_send.at[chunk, step],
                self.core_land.at[chunk, step],
                place.device(place.expert, place.spot * 2 + 1 - place.core),
            ).start()

    def third(self, chunk):
        place = self.place
        owner = self.owner(chunk)
        flipped = 1 - 2 * place.core
        for step in range(place.spots):
            came = self.spot_of(owner, place.before(step) + flipped)
            remote(
                came,
                came,
                self.core_send.at[chunk, step],
                self.core_land.at[chunk, step],
                place.device(place.expert, place.spot * 2 + 1 - place.core),
            ).wait_recv()

    def finish(self, chunk):
        place = self.place
        owner = self.owner(chunk)
        mine = self.spot_of(owner, place.tensor)
        device = place.device(place.expert, place.tensor)
        if self.over_expert:

            @pl.when(chunk > 0)
            def _():
                remote(
                    self.block(owner),
                    mine,
                    self.first_send.at[chunk],
                    self.first_land.at[chunk],
                    device,
                ).wait_send()

        else:
            pltpu.make_async_copy(self.block(owner), mine, self.first_send.at[chunk]).wait()
        for step in range(1, place.spots):
            remote(
                mine,
                mine,
                self.side_send.at[chunk, step - 1],
                self.side_land.at[chunk, step - 1],
                device,
            ).wait_send()
        for step in range(place.spots):
            remote(
                mine, mine, self.core_send.at[chunk, step], self.core_land.at[chunk, step], device
            ).wait_send()


class Collect:
    @staticmethod
    def scratch(chunks, kinds, spots, rows, width):
        return [
            pltpu.VMEM((2, kinds, spots, 2, rows, width), jnp.bfloat16),
            pltpu.VMEM((2, kinds, max(spots - 1, 1), rows, width), jnp.bfloat16),
            pltpu.VMEM((chunks, kinds, spots, rows, width), jnp.bfloat16),
            pltpu.VMEM((chunks, kinds, max(spots - 1, 1), rows, width), jnp.bfloat16),
            pltpu.SemaphoreType.DMA((chunks,)),
            pltpu.SemaphoreType.DMA((chunks,)),
            pltpu.SemaphoreType.DMA((chunks, max(spots - 1, 1))),
            pltpu.SemaphoreType.DMA((chunks, max(spots - 1, 1))),
        ]

    def __init__(self, place, refs):
        self.place = place
        self.stage, self.side, self.core_in, self.side_in = refs[:4]
        self.core_send, self.core_land, self.side_send, self.side_land = refs[4:]
        self.chunks = self.core_in.shape[0]

    def core_copy(self, chunk):
        place = self.place
        return remote(
            self.stage.at[lax.rem(chunk, 2), :, :, 1 - place.core],
            self.core_in.at[chunk],
            self.core_send.at[chunk],
            self.core_land.at[chunk],
            place.device(place.expert, place.spot * 2 + 1 - place.core),
        )

    def side_copy(self, chunk, step):
        place = self.place
        return remote(
            self.side.at[lax.rem(chunk, 2), :, step - 1],
            self.side_in.at[chunk, :, step - 1],
            self.side_send.at[chunk, step - 1],
            self.side_land.at[chunk, step - 1],
            place.device(place.expert, place.across(step)),
        )

    def free_stage(self, chunk):
        @pl.when(chunk >= 2)
        def _():
            self.core_copy(chunk - 2).wait_send()

    def first(self, chunk):
        self.core_copy(chunk).start()

    def second(self, chunk):
        place = self.place
        slot = lax.rem(chunk, 2)
        self.core_copy(chunk).wait_recv()

        @pl.when(chunk >= 2)
        def _():
            for step in range(1, place.spots):
                self.side_copy(chunk - 2, step).wait_send()

        for step in range(1, place.spots):
            there = lax.rem(place.spot + step, place.spots)
            total = self.stage[slot, :, there, place.core].astype(jnp.float32) + self.core_in[
                chunk, :, there
            ].astype(jnp.float32)
            self.side[slot, :, step - 1] = total.astype(jnp.bfloat16)
            self.side_copy(chunk, step).start()

    def third(self, chunk):
        place = self.place
        slot = lax.rem(chunk, 2)
        total = self.stage[slot, :, place.spot, place.core].astype(jnp.float32) + self.core_in[
            chunk, :, place.spot
        ].astype(jnp.float32)
        for step in range(1, place.spots):
            self.side_copy(chunk, step).wait_recv()
            total = total + self.side_in[chunk, :, step - 1].astype(jnp.float32)
        return total

    def finish(self):
        for chunk in range(max(self.chunks - 2, 0), self.chunks):
            self.core_copy(chunk).wait_send()
            for step in range(1, self.place.spots):
                self.side_copy(chunk, step).wait_send()


def when(condition, action, *args):
    pl.when(condition)(functools.partial(action, *args))


def spread_kernel(over_expert, source, target, *sems):
    place = Place()
    spread = Spread(place, source, target, sems, over_expert)
    place.meet(over_expert)
    spread.start()

    def step(turn, carry):
        when(turn < spread.chunks, spread.first, turn)
        when(turn >= 1, spread.second, turn - 1)
        return carry

    lax.fori_loop(0, spread.chunks + 1, step, 0)

    def last(turn, carry):
        spread.third(turn)
        spread.finish(turn)
        return carry

    lax.fori_loop(0, spread.chunks, last, 0)


def spread_rows(rows, over_expert, collective, microseconds):
    chunks, count, width = rows.shape
    parts = lax.axis_size("tensor")
    full = pl.pallas_call(
        functools.partial(spread_kernel, over_expert),
        out_shape=jax.ShapeDtypeStruct((1, chunks, count, width * parts), rows.dtype),
        in_specs=[pl.BlockSpec(memory_space=pl.ANY)],
        out_specs=pl.BlockSpec(memory_space=pl.ANY),
        scratch_shapes=Spread.scratch(chunks, parts // 2),
        compiler_params=pltpu.CompilerParams(collective_id=collective, has_side_effects=True),
        cost_estimate=lasting(microseconds),
    )(rows[None])
    return full.reshape(chunks * count, width * parts)


def collect_kernel(make, operand_count, *refs):
    place = Place()
    operands = refs[:operand_count]
    result = refs[operand_count]
    collect = Collect(place, refs[operand_count + 1 :])
    place.meet(False)

    def one(chunk):
        collect.free_stage(chunk)
        slot = lax.rem(chunk, 2)
        width = result.shape[2]
        for spot in range(place.spots):
            for core in range(2):
                first = (spot * 2 + core) * width
                part = make(operands, chunk, first, width)
                collect.stage[slot, 0, spot, core] = part.astype(jnp.bfloat16)
        collect.first(chunk)

    def close(chunk):
        result[chunk] = collect.third(chunk)[0]

    def step(turn, carry):
        when(turn >= 2, close, turn - 2)
        when((turn >= 1) & (turn <= collect.chunks), collect.second, turn - 1)
        when(turn < collect.chunks, one, turn)
        return carry

    lax.fori_loop(0, collect.chunks + 2, step, 0)
    collect.finish()


def collect_rows(make, operands, chunks, rows, width, collective):
    parts = lax.axis_size("tensor")
    out = pl.pallas_call(
        functools.partial(collect_kernel, make, len(operands)),
        out_shape=jax.ShapeDtypeStruct((chunks, rows, width), jnp.float32),
        in_specs=[pl.BlockSpec(memory_space=pltpu.VMEM)] * len(operands),
        out_specs=pl.BlockSpec(memory_space=pltpu.VMEM),
        scratch_shapes=Collect.scratch(chunks, 1, parts // 2, rows, width),
        compiler_params=pltpu.CompilerParams(
            collective_id=collective, has_side_effects=True, vmem_limit_bytes=48 * MIB
        ),
        cost_estimate=lasting(26),
    )(*operands)
    return out.reshape(chunks * rows, width)


def make_attended(span, operands, chunk, first, width):
    heads, gates, weight = operands
    total = None
    for expert in range(gates.shape[2]):
        term = gates[chunk, :, expert : expert + 1] * jnp.dot(
            heads[chunk, :, expert * span : (expert + 1) * span],
            weight[expert * span : (expert + 1) * span, first : first + width],
            preferred_element_type=jnp.float32,
        )
        total = term if total is None else total + term
    return total


def experts_kernel(sharers, halves, piece_count, *refs):
    (source, gates, gate_hbm, up_hbm, down_hbm), refs = refs[:5], refs[5:]
    pieces, refs = refs[:piece_count], refs[piece_count:]
    (
        inbox, grads_out, middle_out, gate_out, up_out, returned,
        gate_w, up_w, down_w, rows, grads, middle, gate_g, up_g, closing, gates_in,
        load_sem, piece_sem, store_sem, back_send, back_land, mark_send, mark_land,
    ) = refs[:23]
    place = Place()
    spread = Spread(place, source, inbox, refs[23:29], True, sharers)
    collect = Collect(place, refs[29:])
    chunks = spread.chunks
    width = source.shape[3]
    units = gate_w.shape[1]
    tile = 704 if units % 704 == 0 else units
    capacity = rows.shape[0]
    loads = [
        pltpu.make_async_copy(held, kept, load_sem.at[number])
        for number, (held, kept) in enumerate(
            ((gate_hbm, gate_w), (up_hbm, up_w), (down_hbm, down_w))
        )
    ]
    for load in loads:
        load.start()
    place.meet(True)

    def mark_copy(chunk):
        peer = spread.owner(chunk)
        return remote(
            gates.at[lax.div(peer, sharers)],
            gates_in.at[place.expert],
            mark_send.at[chunk],
            mark_land.at[chunk],
            place.device(peer, place.tensor),
        )

    def mark_landed(chunk):
        peer = spread.owner(chunk)
        return remote(
            gates.at[lax.div(peer, sharers)],
            gates_in.at[peer],
            mark_send.at[chunk],
            mark_land.at[chunk],
            place.device(peer, place.tensor),
        )

    spread.start()
    for chunk in range(1, chunks):
        mark_copy(chunk).start()
    own_mark = pltpu.make_async_copy(
        gates.at[lax.div(place.expert, sharers)], gates_in.at[place.expert], mark_send.at[0]
    )
    own_mark.start()
    own_mark.wait()

    def stores(owner):
        return [
            pltpu.make_async_copy(held, out.at[owner], store_sem.at[number])
            for number, (held, out) in enumerate(
                ((middle, middle_out), (gate_g, gate_out), (up_g, up_out), (grads, grads_out))
            )
        ]

    def fetches(owner):
        copies = [pltpu.make_async_copy(inbox.at[0, owner], rows, load_sem.at[3])]
        number = 0
        for first, count in halves:
            for step in range(place.spots):
                for other in range(2):
                    tensor = place.before(step)
                    if other:
                        tensor = tensor + 1 - 2 * place.core
                    column = pl.multiple_of(tensor * width, 128)
                    copies.append(
                        pltpu.make_async_copy(
                            pieces[number].at[owner],
                            grads.at[pl.ds(first, count), pl.ds(column, width)],
                            piece_sem.at[number],
                        )
                    )
                    number += 1
        return copies

    def work(chunk):
        owner = spread.owner(chunk)
        slot = lax.rem(chunk, 2)

        @pl.when(chunk == 0)
        def _():
            for load in loads:
                load.wait()

        @pl.when(chunk > 0)
        def _():
            for store in stores(spread.owner(chunk - 1)):
                store.wait()
            mark_landed(chunk).wait_recv()

        spread.third(chunk)
        copies = fetches(owner)
        for fetch in copies:
            fetch.start()
        collect.free_stage(chunk)
        for fetch in copies:
            fetch.wait()
        wide = gates_in.shape[2]
        line = jnp.broadcast_to(gates_in[owner][:1], (capacity, wide))
        here = lax.broadcasted_iota(jnp.int32, (capacity, wide), 0) == lax.broadcasted_iota(
            jnp.int32, (capacity, wide), 1
        )
        gate_column = jnp.sum(jnp.where(here, line, 0.0), axis=1, keepdims=True)
        grads[...] = (grads[...].astype(jnp.float32) * gate_column).astype(jnp.bfloat16)
        for first in range(0, units, tile):
            here = slice(first, first + tile)
            gate = jnp.dot(rows[...], gate_w[:, here], preferred_element_type=jnp.float32)
            up = jnp.dot(rows[...], up_w[:, here], preferred_element_type=jnp.float32)
            sig = jax.nn.sigmoid(gate)
            act = gate * sig
            middle[:, here] = (act * up).astype(jnp.bfloat16)
            grad = dot_nt(grads[...], down_w[here, :])
            gate_g[:, here] = (grad * up * sig * (1.0 + gate * (1.0 - sig))).astype(jnp.bfloat16)
            up_g[:, here] = (grad * act).astype(jnp.bfloat16)
        for store in stores(owner):
            store.start()
        for spot in range(place.spots):
            for core in range(2):
                first = (spot * 2 + core) * width
                here = slice(first, first + width)
                collect.stage[slot, 0, spot, core] = jnp.dot(
                    middle[...], down_w[:, here], preferred_element_type=jnp.float32
                ).astype(jnp.bfloat16)
                collect.stage[slot, 1, spot, core] = (
                    dot_nt(gate_g[...], gate_w[here, :]) + dot_nt(up_g[...], up_w[here, :])
                ).astype(jnp.bfloat16)
        collect.first(chunk)

    def back_copy(chunk):
        owner = spread.owner(chunk)
        return remote(
            closing.at[lax.rem(chunk, 2)],
            returned.at[:, place.expert],
            back_send.at[chunk],
            back_land.at[chunk],
            place.device(owner, place.tensor),
        )

    def close(chunk):
        slot = lax.rem(chunk, 2)
        total = collect.third(chunk)

        @pl.when(chunk >= 3)
        def _():
            back_copy(chunk - 2).wait_send()

        closing[slot] = total.astype(jnp.bfloat16)

        @pl.when(chunk > 0)
        def _():
            back_copy(chunk).start()

        @pl.when(chunk == 0)
        def _():
            own = pltpu.make_async_copy(
                closing.at[slot], returned.at[:, place.expert], back_send.at[chunk]
            )
            own.start()
            own.wait()

    def step(turn, carry):
        now = turn - 2
        when(turn < chunks, spread.first, turn)
        when((turn >= 1) & (turn <= chunks), spread.second, turn - 1)
        when(now >= 2, close, now - 2)
        when((now >= 1) & (now <= chunks), collect.second, now - 1)
        when((now >= 0) & (now < chunks), work, now)
        return carry

    lax.fori_loop(0, chunks + 4, step, 0)

    def last(turn, carry):
        spread.finish(turn)

        @pl.when(turn > 0)
        def _():
            owner = spread.owner(turn)
            mark_copy(turn).wait_send()
            remote(
                closing.at[0],
                returned.at[:, owner],
                back_send.at[turn],
                back_land.at[turn],
                place.device(owner, place.tensor),
            ).wait_recv()

        return carry

    lax.fori_loop(0, chunks, last, 0)
    for store in stores(spread.owner(chunks - 1)):
        store.wait()
    for chunk in range(max(chunks - 2, 1), chunks):
        back_copy(chunk).wait_send()
    collect.finish()


def experts(source, gates, gate_w, up_w, down_w, pieces, halves, sharers, collective):
    _, capacity, width = source.shape
    groups, parts = lax.axis_size("expert"), lax.axis_size("tensor")
    spots = parts // 2
    model_width, units = gate_w.shape
    low = jnp.bfloat16
    anywhere = pl.BlockSpec(memory_space=pl.ANY)
    hidden_rows = jax.ShapeDtypeStruct((groups, capacity, units), low)
    return pl.pallas_call(
        functools.partial(experts_kernel, sharers, halves, len(pieces)),
        out_shape=(
            jax.ShapeDtypeStruct((1, groups, capacity, model_width), low),
            jax.ShapeDtypeStruct((groups, capacity, model_width), low),
            hidden_rows,
            hidden_rows,
            hidden_rows,
            jax.ShapeDtypeStruct((2, groups, capacity, width), low),
        ),
        in_specs=[anywhere] * (5 + len(pieces)),
        out_specs=(anywhere,) * 6,
        scratch_shapes=[
            pltpu.VMEM((model_width, units), low),
            pltpu.VMEM((model_width, units), low),
            pltpu.VMEM((units, model_width), low),
            pltpu.VMEM((capacity, model_width), low),
            pltpu.VMEM((capacity, model_width), low),
            pltpu.VMEM((capacity, units), low),
            pltpu.VMEM((capacity, units), low),
            pltpu.VMEM((capacity, units), low),
            pltpu.VMEM((2, 2, capacity, width), low),
            pltpu.VMEM((groups,) + gates.shape[1:], jnp.float32),
            pltpu.SemaphoreType.DMA((4,)),
            pltpu.SemaphoreType.DMA((len(pieces),)),
            pltpu.SemaphoreType.DMA((4,)),
            pltpu.SemaphoreType.DMA((groups,)),
            pltpu.SemaphoreType.DMA((groups,)),
            pltpu.SemaphoreType.DMA((groups,)),
            pltpu.SemaphoreType.DMA((groups,)),
        ]
        + Spread.scratch(groups, spots)
        + Collect.scratch(groups, 2, spots, capacity, width),
        compiler_params=pltpu.CompilerParams(
            collective_id=collective, has_side_effects=True, vmem_limit_bytes=60 * MIB
        ),
        cost_estimate=lasting(180),
    )(source[None], gates, gate_w, up_w, down_w, *pieces)


def tensor_pieces(rows):
    parts = lax.axis_size("tensor")
    spots = parts // 2
    swap = [(index, index ^ 1) for index in range(parts)]
    pieces = []
    for step in range(spots):
        came = rows
        if step:
            came = lax.ppermute(
                rows, "tensor", [(index, (index + 2 * step) % parts) for index in range(parts)]
            )
        pieces.append(came)
    return [piece for came in pieces for piece in (came, lax.ppermute(came, "tensor", swap))]


def closing_kernel(count, *refs):
    normed_t, gain, marks, hidden, scaled, routed, small_in = refs[:7]
    grads, weights, refs = refs[7 : 7 + count], refs[7 + count : 7 + 2 * count], refs[7 + 2 * count :]
    refs = refs[len(refs) - (count + 2 + 20 + 8) :]
    (
        hold, partial, stat_own, stat_in, ready, gathered, small_own, small_got, small_sum,
        ring_send, ring_land, stat_send, stat_land, back_send, back_land,
        small_send, small_land, last_send, last_land, own_sem,
    ) = refs[count + 2 : count + 22]
    summed, back, small_out = refs[:count], refs[count], refs[count + 1]
    place = Place()
    collect = Collect(place, refs[count + 22 :])
    groups, parts = place.groups, place.parts
    pieces, _, rows = collect.core_in.shape[0], None, collect.core_in.shape[3]
    width = hidden.shape[1]
    block = hold.shape[3]
    bucket = back.shape[1]
    each = rows // bucket
    place.meet(True, True)

    parity, half = lax.rem(place.expert, 2), lax.div(place.expert, 2)
    at = half + parity * (groups - 1 - 2 * half)

    def member(spot):
        spot = lax.rem(spot + groups, groups)
        high = lax.div(spot, groups // 2)
        return (1 - high) * 2 * spot + high * (2 * (groups - 1 - spot) + 1)

    ways = ((0, 1), (1, -1))

    def first_row(way, sign, step):
        spot = lax.rem(at - sign * step + 2 * groups, groups)
        return pl.multiple_of((way * groups + spot) * block, block)

    def ring_copy(step, way, sign, number, source, target):
        return remote(
            source,
            target,
            ring_send.at[step, way, number],
            ring_land.at[step, way, number],
            place.device(member(at + sign), place.tensor),
        )

    def slot(step, way, number):
        return hold.at[step, way, number]

    def spot_out(step, way, sign, number):
        return summed[number].at[pl.ds(first_row(way, sign, step), block)]

    def ring(step):
        for number in range(count):
            for way, sign in ways:

                @pl.when((step >= 1) & (step < groups))
                def _():
                    held = slot(step, way, number)
                    ring_copy(step - 1, way, sign, number, held, held).wait_recv()

                @pl.when(step >= groups)
                def _():
                    held = spot_out(step, way, sign, number)
                    ring_copy(step - 1, way, sign, number, held, held).wait_recv()

                @pl.when(step < groups)
                def _():
                    first = first_row(way, sign, step)
                    own = jnp.dot(
                        normed_t[pl.ds(first, block), :],
                        grads[number][...],
                        preferred_element_type=jnp.float32,
                    )

                    @pl.when(step == 0)
                    def _():
                        hold[0, way, number] = own.astype(jnp.bfloat16)

                    @pl.when(step > 0)
                    def _():
                        hold[step, way, number] = (
                            own + hold[step, way, number].astype(jnp.float32)
                        ).astype(jnp.bfloat16)

                @pl.when(step < groups - 1)
                def _():
                    ring_copy(
                        step, way, sign, number, slot(step, way, number), slot(step + 1, way, number)
                    ).start()

                @pl.when(step == groups - 1)
                def _():
                    held, there = slot(step, way, number), spot_out(step, way, sign, number)
                    ring_copy(step, way, sign, number, held, there).start()
                    pltpu.make_async_copy(held, there, own_sem.at[way, number]).start()

                @pl.when((step >= groups) & (step < 2 * groups - 2))
                def _():
                    held = spot_out(step, way, sign, number)
                    ring_copy(step, way, sign, number, held, held).start()

    def ring_finish(step, carry):
        for number in range(count):
            for way, sign in ways:
                held = slot(0, way, number)
                ring_copy(step, way, sign, number, held, held).wait_send()
        return carry

    def band(piece):
        return pl.ds(pl.multiple_of(piece * rows, rows), rows)

    def project(piece):
        collect.free_stage(piece)
        side = lax.rem(piece, 2)
        for spot in range(place.spots):
            for core in range(2):
                first = (spot * 2 + core) * width
                part = None
                for grad, weight in zip(grads, weights):
                    term = dot_nt(grad[band(piece), :], weight[first : first + width, :])
                    part = term if part is None else part + term
                collect.stage[side, 0, spot, core] = part.astype(jnp.bfloat16)
        collect.first(piece)

    def stat_copy(piece, step):
        return remote(
            stat_own.at[piece],
            stat_in.at[piece, step - 1],
            stat_send.at[piece, step - 1],
            stat_land.at[piece, step - 1],
            place.device(place.expert, place.along(step)),
        )

    def measure(piece):
        total = collect.third(piece)[0]
        partial[piece] = total
        inner = jnp.sum(total * scaled[band(piece), :] * gain[...], axis=1, keepdims=True)
        stat_own[piece] = jnp.broadcast_to(inner, (rows, 128))
        for step in range(1, parts):
            stat_copy(piece, step).start()

    def back_copy(target, piece, number):
        return remote(
            ready.at[piece, pl.ds(number * bucket, bucket)],
            back.at[place.expert],
            back_send.at[target],
            back_land.at[place.expert],
            place.device(target, place.tensor),
        )

    def conclude(piece):
        inner = stat_own[piece]
        for step in range(1, parts):
            stat_copy(piece, step).wait_recv()
            inner = inner + stat_in[piece, step - 1]
        mean = (inner[:, :1] + marks[band(piece), 1:2]) / (width * parts)
        grad = partial[piece] + routed[band(piece), :]
        part = scaled[band(piece), :]
        gathered[...] += jnp.sum(grad * part, axis=0, keepdims=True)
        result = hidden[band(piece), :] + marks[band(piece), 0:1] * (grad * gain[...] - part * mean)
        ready[piece] = result.astype(jnp.bfloat16)
        for number in range(each):
            target = piece * each + number

            @pl.when(target != place.expert)
            def _():
                back_copy(target, piece, number).start()

            @pl.when(target == place.expert)
            def _():
                own = pltpu.make_async_copy(
                    ready.at[piece, pl.ds(number * bucket, bucket)],
                    back.at[place.expert],
                    own_sem.at[0, count],
                )
                own.start()
                own.wait()

    def small_copy(step):
        return remote(
            small_own,
            small_got.at[step - 1],
            small_send.at[step - 1],
            small_land.at[step - 1],
            place.device(flip(place.expert, step, groups), place.tensor),
        )

    def last_copy(step, origin):
        return remote(
            small_sum,
            small_out.at[origin],
            last_send.at[step - 1],
            last_land.at[step - 1],
            place.device(place.expert, place.along(step)),
        )

    own_small = pltpu.make_async_copy(small_sum, small_out.at[place.tensor], own_sem.at[1, count])

    def small_first():
        small_own[...] = small_in[...]
        small_own[0:1, :] = gathered[...]
        for step in range(1, groups):
            small_copy(step).start()

    def small_second():
        total = small_own[...]
        for step in range(1, groups):
            small_copy(step).wait_recv()
            total = total + small_got[step - 1]
        small_sum[...] = total
        own_small.start()
        for step in range(1, parts):
            last_copy(step, place.tensor).start()

    gathered[...] = jnp.zeros_like(gathered)
    turns = max(2 * groups - 1, pieces + 5)

    def turn_step(turn, carry):
        when(turn < 2 * groups - 1, ring, turn)
        when((turn >= 3) & (turn < pieces + 3), conclude, turn - 3)
        when((turn >= 2) & (turn < pieces + 2), measure, turn - 2)
        when((turn >= 1) & (turn < pieces + 1), collect.second, turn - 1)
        when(turn < pieces, project, turn)
        when(turn == pieces + 3, small_first)
        when(turn == pieces + 4, small_second)
        return carry

    lax.fori_loop(0, turns, turn_step, 0)
    lax.fori_loop(0, 2 * groups - 2, ring_finish, 0)
    for number in range(count):
        for way, sign in ways:
            pltpu.make_async_copy(
                slot(groups - 1, way, number),
                spot_out(groups - 1, way, sign, number),
                own_sem.at[way, number],
            ).wait()
    collect.finish()
    for step in range(1, groups):
        small_copy(step).wait_send()
    own_small.wait()
    for step in range(1, parts):
        origin = lax.rem(place.tensor + parts - step, parts)
        last_copy(step, place.tensor).wait_send()
        last_copy(step, origin).wait_recv()

    def settle(piece, carry):
        for step in range(1, parts):
            stat_copy(piece, step).wait_send()
        for number in range(each):
            target = piece * each + number

            @pl.when(target != place.expert)
            def _():
                back_copy(target, piece, number).wait_send()
                remote(
                    ready.at[piece, pl.ds(number * bucket, bucket)],
                    back.at[target],
                    back_send.at[target],
                    back_land.at[target],
                    place.device(target, place.tensor),
                ).wait_recv()

        return carry

    lax.fori_loop(0, pieces, settle, 0)


def closing(normed_t, gain, marks, hidden, scaled, routed, small, grads, weights, after, pieces, collective):
    groups, parts = lax.axis_size("expert"), lax.axis_size("tensor")
    spots = parts // 2
    model_width, tokens = normed_t.shape
    columns = grads[0].shape[1]
    width = hidden.shape[1]
    count = len(grads)
    rows = tokens // pieces
    block = model_width // (2 * groups)
    low, full = jnp.bfloat16, jnp.float32
    inside = pl.BlockSpec(memory_space=pltpu.VMEM)
    anywhere = pl.BlockSpec(memory_space=pl.ANY)
    dma = pltpu.SemaphoreType.DMA
    return pl.pallas_call(
        functools.partial(closing_kernel, count),
        out_shape=(
            *(jax.ShapeDtypeStruct((model_width, columns), low) for _ in range(count)),
            jax.ShapeDtypeStruct((groups, tokens // groups, width), low),
            jax.ShapeDtypeStruct((parts,) + small.shape, full),
        ),
        in_specs=[inside] * (7 + 2 * count) + [anywhere] * len(after),
        out_specs=(anywhere,) * (count + 2),
        scratch_shapes=[
            pltpu.VMEM((groups, 2, count, block, columns), low),
            pltpu.VMEM((pieces, rows, width), full),
            pltpu.VMEM((pieces, rows, 128), full),
            pltpu.VMEM((pieces, parts - 1, rows, 128), full),
            pltpu.VMEM((pieces, rows, width), low),
            pltpu.VMEM((1, width), full),
            pltpu.VMEM(small.shape, full),
            pltpu.VMEM((groups - 1,) + small.shape, full),
            pltpu.VMEM(small.shape, full),
            dma((2 * groups - 2, 2, count)),
            dma((2 * groups - 2, 2, count)),
            dma((pieces, parts - 1)),
            dma((pieces, parts - 1)),
            dma((groups,)),
            dma((groups,)),
            dma((groups - 1,)),
            dma((groups - 1,)),
            dma((parts - 1,)),
            dma((parts - 1,)),
            dma((2, count + 1)),
        ]
        + Collect.scratch(pieces, 1, spots, rows, width),
        compiler_params=pltpu.CompilerParams(
            collective_id=collective, has_side_effects=True, vmem_limit_bytes=56 * MIB
        ),
        cost_estimate=lasting(140),
    )(normed_t, gain, marks, hidden, scaled, routed, small, *grads, *weights, *after)


def to_expert(rows, group_count):
    count, width = rows.shape
    return lax.all_to_all(
        rows.reshape(group_count, count // group_count, width),
        "expert",
        split_axis=0,
        concat_axis=0,
        tiled=True,
    ).reshape(count, width)


def side_by_side(pieces):
    parts = len(pieces)
    spots = parts // 2
    index = lax.axis_index("tensor")
    spot, core = index // 2, index % 2
    pairs = []
    for step in range(spots):
        same, other = pieces[2 * step], pieces[2 * step + 1]
        pairs.append(
            (jnp.where(core == 0, same, other), jnp.where(core == 0, other, same))
        )
    ordered = []
    for here in range(spots):
        for side in range(2):
            value = pairs[0][side]
            for step in range(1, spots):
                value = jnp.where((spot - here) % spots == step, pairs[step][side], value)
            ordered.append(value)
    return jnp.concatenate(ordered, axis=1)


def gather_tensor(rows):
    return lax.all_gather(rows, "tensor", axis=0)


def body(
    tokens,
    out_grad,
    attn_gain,
    attn_router,
    w_query,
    w_key,
    w_value,
    w_out,
    mlp_gain,
    mlp_router,
    w_gate,
    w_up,
    w_down,
    deal,
    seq_lengths,
    attn_routes,
    mlp_routes,
    slot_order,
):
    tok_rows, model_width = tokens.shape
    group_count = lax.axis_size("expert")
    part_count = lax.axis_size("tensor")
    group_index = lax.axis_index("expert")
    part_index = lax.axis_index("tensor")
    bucket_rows = tok_rows // group_count
    col_width = model_width // part_count
    col_first = part_index * col_width
    low = jnp.bfloat16

    def own_cols(values):
        return lax.dynamic_slice_in_dim(values, col_first, col_width, values.ndim - 1)

    deal_rank = deal // tok_rows * bucket_rows + (deal % tok_rows - group_index * bucket_rows)
    row_ids = jnp.arange(tok_rows, dtype=jnp.int32)
    deal_mask = (row_ids[:, None] == deal_rank[None, :]).astype(low)
    dealt = jnp.dot(deal_mask, own_cols(tokens), preferred_element_type=jnp.float32).astype(low)
    resid_low = spread_rows(dealt.reshape(group_count, bucket_rows, col_width), True, 0, 30)
    dealt_grads = jnp.dot(
        deal_mask, own_cols(out_grad), preferred_element_type=jnp.float32
    ).astype(low)
    dealt_grads, resid_low = lax.optimization_barrier((dealt_grads, resid_low))
    grad_cols_low = to_expert(dealt_grads, group_count)
    grad_cols = grad_cols_low.astype(jnp.float32)
    gain_one, gain_two = own_cols(attn_gain), own_cols(mlp_gain)
    router_one = lax.dynamic_slice_in_dim(attn_router, col_first, col_width, 0)
    router_two = lax.dynamic_slice_in_dim(mlp_router, col_first, col_width, 0)
    expert_count = mlp_router.shape[1]
    sharers = group_count // expert_count
    capacity = 5 * tok_rows // (2 * expert_count)
    target, position, kept = slot_table(mlp_routes, slot_order[0], capacity)
    slots = expert_count * capacity
    destination = jnp.where(kept, target * capacity + position, slots).reshape(tok_rows, 2)
    slot_ids = jnp.arange(slots, dtype=jnp.int32)
    chosen = [destination[:, way] for way in range(2)]
    to_slot = (
        (slot_ids[:, None] == chosen[0][None, :]) | (slot_ids[:, None] == chosen[1][None, :])
    ).astype(low)
    slot_grads = jnp.dot(to_slot, grad_cols_low, preferred_element_type=jnp.float32).astype(low)
    slot_grads = slot_grads.reshape(expert_count, capacity, col_width)
    slot_grads, resid_low = lax.optimization_barrier((slot_grads, resid_low))
    halves = ((0, capacity),)
    grad_pieces = []
    for first, count in halves:
        block = jnp.repeat(slot_grads[:, first : first + count], sharers, axis=0)
        grad_pieces.append(to_expert(block.reshape(group_count * count, col_width), group_count))

    resid_in = resid_low.astype(jnp.float32)
    resid_cols = own_cols(resid_low).astype(jnp.float32)
    segment, cosine, sine = rotary_tables(seq_lengths[0], tok_rows)
    scale = 1.0 / math.sqrt(HEAD)
    local_heads = w_query.shape[1] // HEAD
    local_experts = local_heads // QH
    span = QH * HEAD
    factor_one, scaled_one, normed_one = norm_stats(resid_in, attn_gain)
    normed_low = normed_one.astype(low)
    attn_logits = jnp.dot(normed_one, attn_router, precision=PRECISE)
    attn_gates, attn_mask = pair_gates(attn_logits, attn_routes)
    gate_table = jnp.sum(attn_gates[:, :, None] * attn_mask, axis=1)
    gate_local = lax.dynamic_slice_in_dim(gate_table, part_index * local_experts, local_experts, 1)
    query_pre = jnp.dot(normed_low, w_query, preferred_element_type=jnp.float32).reshape(
        tok_rows, local_heads, HEAD
    )
    key_pre = jnp.dot(normed_low, w_key, preferred_element_type=jnp.float32).reshape(
        tok_rows, local_heads, HEAD
    )
    values = (
        jnp.dot(normed_low, w_value, preferred_element_type=jnp.float32)
        .astype(low)
        .reshape(tok_rows, local_heads, HEAD)
    )
    query = (query_pre * cosine + half_turn(query_pre) * sine).astype(low)
    keys = (key_pre * cosine + half_turn(key_pre) * sine).astype(low)
    scores = block_scores(query, keys, segment, 0, tok_rows, scale)
    top_score = jnp.max(scores, axis=-1, keepdims=True)
    expo = jnp.exp(scores - top_score)
    totals = jnp.sum(expo, axis=-1, keepdims=True)
    probs = (expo / totals).astype(low)
    head_blocks = jnp.einsum("hqk,khd->qhd", probs, values, preferred_element_type=jnp.float32)
    log_total = top_score + jnp.log(totals)
    heads_low = head_blocks.astype(low).reshape(tok_rows, local_heads * HEAD)
    pieces, piece_rows = 4, tok_rows // 4
    attn_cols = collect_rows(
        functools.partial(make_attended, span),
        (
            heads_low.reshape(pieces, piece_rows, local_heads * HEAD),
            gate_local.reshape(pieces, piece_rows, local_experts),
            w_out,
        ),
        pieces,
        piece_rows,
        col_width,
        1,
    )
    *grad_pieces, attn_cols = lax.optimization_barrier((*grad_pieces, attn_cols))
    grad_pieces = [
        piece
        for (_, count), rows in zip(halves, grad_pieces)
        for piece in tensor_pieces(rows.reshape(group_count, count, col_width))
    ]
    hidden = resid_cols + attn_cols
    weighed = hidden * gain_two
    stats = jnp.concatenate(
        [
            jnp.sum(hidden * hidden, axis=1)[None, :],
            jnp.dot(weighed, router_two, precision=PRECISE).T,
        ],
        axis=0,
    )
    stats = jnp.sum(gather_tensor(stats), axis=0)
    factor_two = lax.rsqrt(stats[0] / model_width + EPSILON)[:, None]
    mlp_logits = stats[1:].T * factor_two
    scaled_two = hidden * factor_two
    normed_two = scaled_two * gain_two
    mlp_gates, mlp_mask = pair_gates(mlp_logits, mlp_routes)
    slot_rows = jnp.dot(
        to_slot, normed_two.astype(low), preferred_element_type=jnp.float32
    ).astype(low)
    slot_gates = sum(
        jnp.sum(
            jnp.where(slot_ids[:, None] == chosen[way][None, :], mlp_gates[:, way][None, :], 0.0),
            axis=1,
        )
        for way in range(2)
    )
    gate_lines = jnp.pad(slot_gates.reshape(expert_count, capacity), ((0, 0), (0, -capacity % 128)))
    gate_lines = jnp.broadcast_to(gate_lines[:, None, :], (expert_count, 8, gate_lines.shape[1]))
    inbox, slot_grads, middle, gate_grad, up_grad, returned = experts(
        slot_rows.reshape(expert_count, capacity, col_width),
        gate_lines,
        w_gate[0],
        w_up[0],
        w_down[0],
        grad_pieces,
        halves,
        sharers,
        2,
    )
    if sharers > 1:
        returned = (
            jnp.sum(
                returned.reshape(2, expert_count, sharers, capacity, col_width).astype(jnp.float32),
                axis=2,
            )
        ).astype(low)
    made, row_grads = returned.reshape(2, slots, col_width)
    from_slot = [(chosen[way][:, None] == slot_ids[None, :]).astype(low) for way in range(2)]
    pair_values = jnp.stack(
        [
            jnp.dot(from_slot[way], made, preferred_element_type=jnp.float32)
            for way in range(2)
        ],
        axis=1,
    )
    row_grad_sum = jnp.dot(
        from_slot[0] + from_slot[1], row_grads, preferred_element_type=jnp.float32
    )
    mixed_cols = hidden + jnp.sum(mlp_gates[:, :, None] * pair_values, axis=1)
    back_mixed = to_expert(mixed_cols.astype(low), group_count)
    weighed_two = scaled_two * gain_two
    stats = jnp.stack(
        [
            jnp.sum(pair_values[:, 0] * grad_cols, axis=1),
            jnp.sum(pair_values[:, 1] * grad_cols, axis=1),
            jnp.sum(row_grad_sum * weighed_two, axis=1),
        ]
    )
    stats = jnp.sum(gather_tensor(stats), axis=0)
    mlp_logit_grad = pair_back(mlp_gates, mlp_mask, stats[:2].T)
    norm_two_grad = row_grad_sum + jnp.dot(mlp_logit_grad, router_two.T, precision=PRECISE)
    mlp_router_grad = jnp.dot(normed_two.T, mlp_logit_grad, precision=PRECISE)
    mlp_gain_grad = jnp.sum(norm_two_grad * scaled_two, axis=0)
    mean_two = (stats[2] + jnp.sum(mlp_logit_grad * mlp_logits, axis=1)) / model_width
    hidden_grad = grad_cols + factor_two * (norm_two_grad * gain_two - scaled_two * mean_two[:, None])
    hidden_grad_low = side_by_side(tensor_pieces(hidden_grad.astype(low)))
    gate_wide = jnp.repeat(gate_local, span, axis=1)
    heads_float = heads_low.astype(jnp.float32)
    out_w_grad = jnp.einsum(
        "tc,td->cd",
        (heads_float * gate_wide).astype(low),
        hidden_grad_low,
        preferred_element_type=jnp.float32,
    )
    out_w_grad, middle, up_grad, hidden_grad_low = lax.optimization_barrier(
        (out_w_grad.astype(low), middle, up_grad, hidden_grad_low)
    )
    out_w_grad = lax.psum(out_w_grad, "expert").astype(jnp.float32)
    heads_plain = jnp.einsum(
        "td,cd->tc", hidden_grad_low, w_out, preferred_element_type=jnp.float32
    )
    gate_products = heads_plain * heads_float
    local_gate_grad = jnp.stack(
        [
            jnp.sum(gate_products[:, expert * span : (expert + 1) * span], axis=1)
            for expert in range(local_experts)
        ],
        axis=1,
    )
    heads_grad = (heads_plain * gate_wide).astype(low).reshape(tok_rows, local_heads, HEAD)
    scores = block_scores(query, keys, segment, 0, tok_rows, scale)
    probs = jnp.exp(scores - log_total)
    value_grad = jnp.einsum(
        "hqk,qhd->khd", probs.astype(low), heads_grad, preferred_element_type=jnp.float32
    )
    prob_grad = jnp.einsum("qhd,khd->hqk", heads_grad, values, preferred_element_type=jnp.float32)
    score_grad = (
        probs * (prob_grad - jnp.sum(probs * prob_grad, axis=-1, keepdims=True))
    ).astype(low)
    query_grad = (
        jnp.einsum("hqk,khd->qhd", score_grad, keys, preferred_element_type=jnp.float32) * scale
    )
    key_grad = (
        jnp.einsum("hqk,qhd->khd", score_grad, query, preferred_element_type=jnp.float32) * scale
    )
    width = local_heads * HEAD
    query_pre_grad = undo_turn(query_grad, cosine, sine).astype(low).reshape(tok_rows, width)
    key_pre_grad = undo_turn(key_grad, cosine, sine).astype(low).reshape(tok_rows, width)
    value_pre_grad = value_grad.astype(low).reshape(tok_rows, width)
    gate_grads = gather_tensor(local_gate_grad.T)
    gate_grads = gate_grads.reshape(part_count * local_experts, tok_rows).T
    attn_pair_grad = jnp.sum(attn_mask * gate_grads[:, None, :], axis=2)
    attn_logit_grad = pair_back(attn_gates, attn_mask, attn_pair_grad)
    scaled_cols = resid_cols * factor_one
    normed_cols = scaled_cols * gain_one
    attn_router_grad = jnp.dot(normed_cols.T, attn_logit_grad, precision=PRECISE)
    small = jnp.concatenate(
        [
            jnp.zeros((1, col_width), jnp.float32),
            attn_router_grad.T,
            mlp_gain_grad[None],
            mlp_router_grad.T,
        ],
        axis=0,
    )
    small = jnp.pad(small, ((0, -small.shape[0] % 8), (0, 0)))
    marks = jnp.stack(
        [factor_one[:, 0], jnp.sum(attn_logit_grad * attn_logits, axis=1)], axis=1
    )
    rows = inbox.reshape(-1, model_width)
    grad_rows = slot_grads.reshape(-1, model_width)
    units = middle.shape[2]
    gate_w_grad, up_w_grad = (
        jnp.einsum("sd,sf->df", rows, grad.reshape(-1, units), preferred_element_type=jnp.float32)
        for grad in (gate_grad, up_grad)
    )
    down_grad = jnp.einsum(
        "sf,sd->fd", middle.reshape(-1, units), grad_rows, preferred_element_type=jnp.float32
    )
    *weight_grads, back_grad, small = closing(
        normed_low.T,
        gain_one[None],
        jnp.pad(marks, ((0, 0), (0, 126))),
        hidden_grad,
        scaled_cols,
        jnp.dot(attn_logit_grad, router_one.T, precision=PRECISE),
        small,
        (query_pre_grad, key_pre_grad, value_pre_grad),
        (w_query, w_key, w_value),
        (gate_w_grad, up_w_grad, down_grad),
        pieces,
        3,
    )
    back_grad = back_grad.reshape(tok_rows, col_width)
    weight_grads = [grad.astype(jnp.float32) for grad in weight_grads]
    mixed, tokens_grad = (
        jnp.einsum("ri,rc->ic", deal_mask, back, preferred_element_type=jnp.float32).astype(low)
        for back in (back_mixed, back_grad)
    )
    small = small.transpose(1, 0, 2).reshape(-1, model_width)
    experts_of = attn_router.shape[1]
    return (
        mixed,
        tokens_grad,
        small[0],
        small[1 : 1 + experts_of].T,
        weight_grads[0],
        weight_grads[1],
        weight_grads[2],
        out_w_grad,
        small[1 + experts_of],
        small[2 + experts_of : 2 + experts_of + expert_count].T,
        gate_w_grad[None],
        up_w_grad[None],
        down_grad[None],
    )


def solution(mesh):
    placed = (
        P("expert", None),
        P("expert", None),
        P(),
        P(),
        P(None, "tensor"),
        P(None, "tensor"),
        P(None, "tensor"),
        P("tensor", None),
        P(),
        P(),
        P("expert", None, "tensor"),
        P("expert", None, "tensor"),
        P("expert", "tensor", None),
        P("expert"),
        P("expert", None),
        P("expert", None),
        P("expert", None),
        P("expert", None),
    )
    return jax.shard_map(
        body,
        mesh=mesh,
        in_specs=placed,
        out_specs=(
            P("expert", "tensor"),
            P("expert", "tensor"),
            P(),
            P(),
            P(None, "tensor"),
            P(None, "tensor"),
            P(None, "tensor"),
            P("tensor", None),
            P(),
            P(),
            P("expert", None, "tensor"),
            P("expert", None, "tensor"),
            P("expert", "tensor", None),
        ),
        check_vma=False,
    )
```

```python
import functools
import math

import jax
import jax.numpy as jnp
from jax import lax
from jax.experimental import pallas as pl
from jax.experimental.pallas import tpu as pltpu
from jax.sharding import PartitionSpec as P

HEAD = 128
QH = 2


PRECISE = lax.Precision.HIGH
EPSILON = 1e-06
MASKED = -1e30


def rotary_tables(lengths, tok_rows):
    seq_ends = jnp.cumsum(lengths)
    seq_starts = seq_ends - lengths
    places = jnp.arange(tok_rows, dtype=jnp.int32)
    segment = jnp.sum((places[:, None] >= seq_ends[None, :]).astype(jnp.int32), axis=1)
    matches = segment[:, None] == jnp.arange(lengths.shape[0], dtype=jnp.int32)[None, :]
    seq_first = jnp.sum(jnp.where(matches, seq_starts[None, :], 0), axis=1)
    offsets = (places - seq_first).astype(jnp.float32)
    frequency = jnp.exp(-math.log(10000.0) * jnp.arange(0, HEAD, 2, dtype=jnp.float32) / HEAD)
    angles = offsets[:, None] * frequency[None, :]
    angles = jnp.concatenate([angles, angles], axis=1)
    return (segment, jnp.cos(angles), jnp.sin(angles))


def pair_gates(logits, routes):
    columns = logits.shape[1]
    chosen_mask = (
        routes[:, :, None] == jnp.arange(columns, dtype=jnp.int32)[None, None, :]
    ).astype(jnp.float32)
    picked = jnp.sum(chosen_mask * logits[:, None, :], axis=2)
    return (jax.nn.softmax(picked, axis=1), chosen_mask)


def pair_back(gates, chosen_mask, gate_grads):
    inner = gates * (gate_grads - jnp.sum(gates * gate_grads, axis=1, keepdims=True))
    return jnp.sum(chosen_mask * inner[:, :, None], axis=1)


def slot_table(routes, priority, capacity):
    target = routes.reshape(-1)
    ahead = (target[None, :] == target[:, None]) & (priority[None, :] < priority[:, None])
    position = jnp.sum(ahead.astype(jnp.int32), axis=1)
    return (target, position, position < capacity)


MESH = pl.DeviceIdType.MESH
MIB = 1 << 20
AHEAD_DEAL = 2
AHEAD = 2
EARLY = 2


def flip(number, other, count):
    total, bit = 0, 1
    while bit < count:
        total = total + lax.rem(lax.div(number, bit) + lax.div(other, bit), 2) * bit
        bit *= 2
    return total


def dot_nt(left, right):
    return lax.dot_general(
        left, right, (((1,), (1,)), ((), ())), preferred_element_type=jnp.float32
    )


class Place:
    def __init__(self):
        self.groups = lax.axis_size("expert")
        self.parts = lax.axis_size("tensor")
        self.spots = self.parts // 2
        self.expert = lax.axis_index("expert")
        self.tensor = lax.axis_index("tensor")
        self.spot = lax.div(self.tensor, 2)
        self.core = lax.rem(self.tensor, 2)

    def device(self, expert, tensor):
        return {"expert": expert, "tensor": tensor}

    def across(self, step):
        return lax.rem(self.spot + step, self.spots) * 2 + self.core

    def before(self, step):
        return lax.rem(self.spot + self.spots - step, self.spots) * 2 + self.core

    def meet(self, over_expert, whole_tensor=False):
        if whole_tensor:
            peers = [self.device(self.expert, self.along(step)) for step in range(1, self.parts)]
        else:
            peers = [self.device(self.expert, self.spot * 2 + 1 - self.core)]
            for step in range(1, self.spots):
                peers.append(self.device(self.expert, self.across(step)))
        if over_expert:
            for step in range(1, self.groups):
                peers.append(self.device(flip(self.expert, step, self.groups), self.tensor))
        barrier = pltpu.get_barrier_semaphore()
        for peer in peers:
            pl.semaphore_signal(barrier, inc=1, device_id=peer, device_id_type=MESH)
        pl.semaphore_wait(barrier, len(peers))

    def along(self, step):
        return lax.rem(self.tensor + step, self.parts)


def lasting(microseconds):
    return pl.CostEstimate(
        flops=0, bytes_accessed=int(microseconds * 3_000_000), transcendentals=0
    )


def remote(source, target, send, receive, device):
    return pltpu.make_async_remote_copy(
        src_ref=source,
        dst_ref=target,
        send_sem=send,
        recv_sem=receive,
        device_id=device,
        device_id_type=MESH,
    )


class Spread:
    @staticmethod
    def scratch(chunks, spots):
        return [
            pltpu.SemaphoreType.DMA((chunks,)),
            pltpu.SemaphoreType.DMA((chunks,)),
            pltpu.SemaphoreType.DMA((chunks, max(spots - 1, 1))),
            pltpu.SemaphoreType.DMA((chunks, max(spots - 1, 1))),
            pltpu.SemaphoreType.DMA((chunks, spots)),
            pltpu.SemaphoreType.DMA((chunks, spots)),
        ]

    def __init__(self, place, source, target, sems, over_expert, sharers=1, by_group=None):
        self.place, self.source, self.target = place, source, target
        self.by_group = over_expert if by_group is None else by_group
        self.first_send, self.first_land, self.side_send, self.side_land, self.core_send, self.core_land = sems
        self.over_expert, self.sharers = over_expert, sharers
        self.width = source.shape[3]
        self.chunks = target.shape[1]

    def owner(self, chunk):
        if not self.by_group:
            return chunk
        half, odd, pair = self.place.groups // 2, lax.rem(chunk, 2), lax.div(chunk, 2)
        even_way = jnp.minimum(chunk, 1) * half + pair
        odd_way = pair + (1 - jnp.minimum(pair, 1)) * half
        return flip(
            self.place.expert, odd * odd_way + (1 - odd) * even_way, self.place.groups
        )

    def spot_of(self, owner, tensor):
        first = pl.multiple_of(tensor * self.width, 128)
        return self.target.at[:, owner, :, pl.ds(first, self.width)]

    def block(self, owner):
        if self.sharers == 1:
            return self.source.at[:, owner]
        return self.source.at[:, lax.div(owner, self.sharers)]

    def send(self, chunk):
        place = self.place
        peer = self.owner(chunk)
        remote(
            self.block(peer),
            self.spot_of(place.expert, place.tensor),
            self.first_send.at[chunk],
            self.first_land.at[chunk],
            place.device(peer, place.tensor),
        ).start()

    def start(self, ahead):
        place = self.place
        own = self.owner(0)
        if not self.over_expert:
            return
        for chunk in range(1, min(ahead + 1, self.chunks)):
            self.send(chunk)
        copy = pltpu.make_async_copy(
            self.block(own), self.spot_of(own, place.tensor), self.first_send.at[0]
        )
        copy.start()
        copy.wait()

    def first(self, chunk):
        place = self.place
        owner = self.owner(chunk)
        mine = self.spot_of(owner, place.tensor)
        if self.over_expert:

            @pl.when(chunk > 0)
            def _():
                remote(
                    self.block(owner),
                    mine,
                    self.first_send.at[chunk],
                    self.first_land.at[chunk],
                    place.device(owner, place.tensor),
                ).wait_recv()

            held = mine
        else:
            pltpu.make_async_copy(self.block(owner), mine, self.first_send.at[chunk]).start()
            held = self.block(owner)
        for step in range(1, place.spots):
            remote(
                held,
                mine,
                self.side_send.at[chunk, step - 1],
                self.side_land.at[chunk, step - 1],
                place.device(place.expert, place.across(step)),
            ).start()
        remote(
            held,
            mine,
            self.core_send.at[chunk, 0],
            self.core_land.at[chunk, 0],
            place.device(place.expert, place.spot * 2 + 1 - place.core),
        ).start()

    def second(self, chunk):
        place = self.place
        owner = self.owner(chunk)
        for step in range(1, place.spots):
            came = self.spot_of(owner, place.before(step))
            remote(
                came,
                came,
                self.side_send.at[chunk, step - 1],
                self.side_land.at[chunk, step - 1],
                place.device(place.expert, place.across(step)),
            ).wait_recv()
            remote(
                came,
                came,
                self.core_send.at[chunk, step],
                self.core_land.at[chunk, step],
                place.device(place.expert, place.spot * 2 + 1 - place.core),
            ).start()

    def third(self, chunk):
        place = self.place
        owner = self.owner(chunk)
        flipped = 1 - 2 * place.core
        if not self.over_expert:
            mine = self.spot_of(owner, place.tensor)
            pltpu.make_async_copy(self.block(owner), mine, self.first_send.at[chunk]).wait()
        for step in range(place.spots):
            came = self.spot_of(owner, place.before(step) + flipped)
            remote(
                came,
                came,
                self.core_send.at[chunk, step],
                self.core_land.at[chunk, step],
                place.device(place.expert, place.spot * 2 + 1 - place.core),
            ).wait_recv()

    def finish(self, chunk):
        place = self.place
        owner = self.owner(chunk)
        mine = self.spot_of(owner, place.tensor)
        device = place.device(place.expert, place.tensor)
        if self.over_expert:

            @pl.when(chunk > 0)
            def _():
                remote(
                    self.block(owner),
                    mine,
                    self.first_send.at[chunk],
                    self.first_land.at[chunk],
                    device,
                ).wait_send()

        for step in range(1, place.spots):
            remote(
                mine,
                mine,
                self.side_send.at[chunk, step - 1],
                self.side_land.at[chunk, step - 1],
                device,
            ).wait_send()
        for step in range(place.spots):
            remote(
                mine, mine, self.core_send.at[chunk, step], self.core_land.at[chunk, step], device
            ).wait_send()


class Collect:
    @staticmethod
    def scratch(chunks, kinds, spots, rows, width, slots=2):
        return [
            pltpu.VMEM((slots, kinds, spots, 2, rows, width), jnp.bfloat16),
            pltpu.VMEM((slots, kinds, max(spots - 1, 1), rows, width), jnp.bfloat16),
            pltpu.VMEM((chunks, kinds, spots, rows, width), jnp.bfloat16),
            pltpu.VMEM((chunks, kinds, max(spots - 1, 1), rows, width), jnp.bfloat16),
            pltpu.SemaphoreType.DMA((chunks,)),
            pltpu.SemaphoreType.DMA((chunks,)),
            pltpu.SemaphoreType.DMA((chunks, max(spots - 1, 1))),
            pltpu.SemaphoreType.DMA((chunks, max(spots - 1, 1))),
        ]

    def __init__(self, place, refs):
        self.place = place
        self.stage, self.side, self.core_in, self.side_in = refs[:4]
        self.core_send, self.core_land, self.side_send, self.side_land = refs[4:]
        self.chunks = self.core_in.shape[0]
        self.slots = self.stage.shape[0]

    def core_copy(self, chunk):
        place = self.place
        return remote(
            self.stage.at[lax.rem(chunk, self.slots), :, :, 1 - place.core],
            self.core_in.at[chunk],
            self.core_send.at[chunk],
            self.core_land.at[chunk],
            place.device(place.expert, place.spot * 2 + 1 - place.core),
        )

    def side_copy(self, chunk, step):
        place = self.place
        return remote(
            self.side.at[lax.rem(chunk, self.slots), :, step - 1],
            self.side_in.at[chunk, :, step - 1],
            self.side_send.at[chunk, step - 1],
            self.side_land.at[chunk, step - 1],
            place.device(place.expert, place.across(step)),
        )

    def free_stage(self, chunk):
        @pl.when(chunk >= self.slots)
        def _():
            self.core_copy(chunk - self.slots).wait_send()

    def first(self, chunk):
        self.core_copy(chunk).start()

    def second(self, chunk):
        place = self.place
        slot = lax.rem(chunk, self.slots)
        self.core_copy(chunk).wait_recv()

        @pl.when(chunk >= self.slots)
        def _():
            for step in range(1, place.spots):
                self.side_copy(chunk - self.slots, step).wait_send()

        for step in range(1, place.spots):
            there = lax.rem(place.spot + step, place.spots)
            total = self.stage[slot, :, there, place.core].astype(jnp.float32) + self.core_in[
                chunk, :, there
            ].astype(jnp.float32)
            self.side[slot, :, step - 1] = total.astype(jnp.bfloat16)
            self.side_copy(chunk, step).start()

    def third(self, chunk):
        place = self.place
        slot = lax.rem(chunk, self.slots)
        total = self.stage[slot, :, place.spot, place.core].astype(jnp.float32) + self.core_in[
            chunk, :, place.spot
        ].astype(jnp.float32)
        for step in range(1, place.spots):
            self.side_copy(chunk, step).wait_recv()
            total = total + self.side_in[chunk, :, step - 1].astype(jnp.float32)
        return total

    def finish(self):
        for chunk in range(max(self.chunks - self.slots, 0), self.chunks):
            self.core_copy(chunk).wait_send()
            for step in range(1, self.place.spots):
                self.side_copy(chunk, step).wait_send()


def when(condition, action, *args):
    pl.when(condition)(functools.partial(action, *args))


def spread_kernel(over_expert, source, target, *sems):
    place = Place()
    spread = Spread(place, source, target, sems, over_expert)
    place.meet(over_expert)
    spread.start(AHEAD_DEAL)

    def step(turn, carry):
        when(turn < spread.chunks, spread.first, turn)
        if over_expert:
            when(turn + 1 + AHEAD_DEAL < spread.chunks, spread.send, turn + 1 + AHEAD_DEAL)
        when(turn >= 1, spread.second, turn - 1)
        return carry

    lax.fori_loop(0, spread.chunks + 1, step, 0)

    def last(turn, carry):
        spread.third(turn)
        spread.finish(turn)
        return carry

    lax.fori_loop(0, spread.chunks, last, 0)


def spread_rows(rows, over_expert, collective, microseconds):
    chunks, count, width = rows.shape
    parts = lax.axis_size("tensor")
    full = pl.pallas_call(
        functools.partial(spread_kernel, over_expert),
        out_shape=jax.ShapeDtypeStruct((1, chunks, count, width * parts), rows.dtype),
        in_specs=[pl.BlockSpec(memory_space=pl.ANY)],
        out_specs=pl.BlockSpec(memory_space=pl.ANY),
        scratch_shapes=Spread.scratch(chunks, parts // 2),
        compiler_params=pltpu.CompilerParams(collective_id=collective, has_side_effects=True),
        cost_estimate=lasting(microseconds),
    )(rows[None])
    return full.reshape(chunks * count, width * parts)


def collect_kernel(make, operand_count, *refs):
    place = Place()
    operands = refs[:operand_count]
    result = refs[operand_count]
    collect = Collect(place, refs[operand_count + 1 :])
    place.meet(False)

    def one(chunk):
        collect.free_stage(chunk)
        slot = lax.rem(chunk, 2)
        width = result.shape[2]
        for spot in range(place.spots):
            for core in range(2):
                first = (spot * 2 + core) * width
                part = make(operands, chunk, first, width)
                collect.stage[slot, 0, spot, core] = part.astype(jnp.bfloat16)
        collect.first(chunk)

    def close(chunk):
        result[chunk] = collect.third(chunk)[0]

    def step(turn, carry):
        when(turn >= 2, close, turn - 2)
        when((turn >= 1) & (turn <= collect.chunks), collect.second, turn - 1)
        when(turn < collect.chunks, one, turn)
        return carry

    lax.fori_loop(0, collect.chunks + 2, step, 0)
    collect.finish()


def collect_rows(make, operands, chunks, rows, width, collective):
    parts = lax.axis_size("tensor")
    out = pl.pallas_call(
        functools.partial(collect_kernel, make, len(operands)),
        out_shape=jax.ShapeDtypeStruct((chunks, rows, width), jnp.float32),
        in_specs=[pl.BlockSpec(memory_space=pltpu.VMEM)] * len(operands),
        out_specs=pl.BlockSpec(memory_space=pltpu.VMEM),
        scratch_shapes=Collect.scratch(chunks, 1, parts // 2, rows, width),
        compiler_params=pltpu.CompilerParams(
            collective_id=collective, has_side_effects=True, vmem_limit_bytes=48 * MIB
        ),
        cost_estimate=lasting(26),
    )(*operands)
    return out.reshape(chunks * rows, width)


def make_attended(span, operands, chunk, first, width):
    heads, gates, weight = operands
    total = None
    for expert in range(gates.shape[2]):
        term = gates[chunk, :, expert : expert + 1] * jnp.dot(
            heads[chunk, :, expert * span : (expert + 1) * span],
            weight[expert * span : (expert + 1) * span, first : first + width],
            preferred_element_type=jnp.float32,
        )
        total = term if total is None else total + term
    return total


def experts_kernel(sharers, *refs):
    (
        source, source_grads, gates, gate_hbm, up_hbm, down_hbm,
        inbox, inbox_grads, grads_out, middle_out, gate_out, up_out, returned,
        gate_w, up_w, down_w, rows, grads, middle, gate_g, up_g, closing, gates_in,
        load_sem, store_sem, back_send, back_land, mark_send, mark_land,
    ) = refs[:29]
    place = Place()
    spread = Spread(place, source, inbox, refs[29:35], True, sharers)
    spread_grads = Spread(place, source_grads, inbox_grads, refs[35:41], False, by_group=True)
    collect = Collect(place, refs[41:])
    chunks = spread.chunks
    width = source.shape[3]
    units = gate_w.shape[1]
    tile = 704 if units % 704 == 0 else units
    capacity = rows.shape[0]
    loads = [
        pltpu.make_async_copy(held, kept, load_sem.at[number])
        for number, (held, kept) in enumerate(
            ((gate_hbm, gate_w), (up_hbm, up_w), (down_hbm, down_w))
        )
    ]
    for load in loads:
        load.start()
    place.meet(True)

    def mark_copy(chunk):
        peer = spread.owner(chunk)
        return remote(
            gates.at[lax.div(peer, sharers)],
            gates_in.at[place.expert],
            mark_send.at[chunk],
            mark_land.at[chunk],
            place.device(peer, place.tensor),
        )

    def mark_landed(chunk):
        peer = spread.owner(chunk)
        return remote(
            gates.at[lax.div(peer, sharers)],
            gates_in.at[peer],
            mark_send.at[chunk],
            mark_land.at[chunk],
            place.device(peer, place.tensor),
        )

    spread.start(AHEAD)
    for chunk in range(1, chunks):
        mark_copy(chunk).start()
    own_mark = pltpu.make_async_copy(
        gates.at[lax.div(place.expert, sharers)], gates_in.at[place.expert], mark_send.at[0]
    )
    own_mark.start()
    own_mark.wait()
    for chunk in range(EARLY):
        spread_grads.first(chunk)

    def stores(owner):
        return [
            pltpu.make_async_copy(held, out.at[owner], store_sem.at[number])
            for number, (held, out) in enumerate(
                ((middle, middle_out), (gate_g, gate_out), (up_g, up_out), (grads, grads_out))
            )
        ]

    def fetches(owner):
        return [
            pltpu.make_async_copy(inbox.at[0, owner], rows, load_sem.at[3]),
            pltpu.make_async_copy(inbox_grads.at[0, owner], grads, load_sem.at[4]),
        ]

    def work(chunk):
        owner = spread.owner(chunk)

        @pl.when(chunk == 0)
        def _():
            for load in loads:
                load.wait()

        @pl.when(chunk > 0)
        def _():
            for store in stores(spread.owner(chunk - 1)):
                store.wait()
            mark_landed(chunk).wait_recv()

        spread.third(chunk)
        spread_grads.third(chunk)
        copies = fetches(owner)
        for fetch in copies:
            fetch.start()
        for fetch in copies:
            fetch.wait()
        wide = gates_in.shape[2]
        line = jnp.broadcast_to(gates_in[owner][:1], (capacity, wide))
        here = lax.broadcasted_iota(jnp.int32, (capacity, wide), 0) == lax.broadcasted_iota(
            jnp.int32, (capacity, wide), 1
        )
        gate_column = jnp.sum(jnp.where(here, line, 0.0), axis=1, keepdims=True)
        grads[...] = (grads[...].astype(jnp.float32) * gate_column).astype(jnp.bfloat16)
        for first in range(0, units, tile):
            here = slice(first, first + tile)
            gate = jnp.dot(rows[...], gate_w[:, here], preferred_element_type=jnp.float32)
            up = jnp.dot(rows[...], up_w[:, here], preferred_element_type=jnp.float32)
            sig = jax.nn.sigmoid(gate)
            act = gate * sig
            middle[:, here] = (act * up).astype(jnp.bfloat16)
            grad = dot_nt(grads[...], down_w[here, :])
            gate_g[:, here] = (grad * up * sig * (1.0 + gate * (1.0 - sig))).astype(jnp.bfloat16)
            up_g[:, here] = (grad * act).astype(jnp.bfloat16)
        for store in stores(owner):
            store.start()
        made, fed = 2 * chunk, 2 * chunk + 1
        when(chunk >= 1, collect.second, made - 1)
        when(chunk >= 1, close, made - 2)
        collect.free_stage(made)
        for spot in range(place.spots):
            for core in range(2):
                first = (spot * 2 + core) * width
                here = slice(first, first + width)
                collect.stage[lax.rem(made, 4), 0, spot, core] = jnp.dot(
                    middle[...], down_w[:, here], preferred_element_type=jnp.float32
                ).astype(jnp.bfloat16)
        collect.first(made)
        collect.free_stage(fed)
        for spot in range(place.spots):
            for core in range(2):
                first = (spot * 2 + core) * width
                here = slice(first, first + width)
                collect.stage[lax.rem(fed, 4), 0, spot, core] = (
                    dot_nt(gate_g[...], gate_w[here, :]) + dot_nt(up_g[...], up_w[here, :])
                ).astype(jnp.bfloat16)
        collect.first(fed)
        collect.second(made)
        when(chunk >= 1, close, made - 1)

    def back_copy(item, owner=None):
        peer = spread.owner(lax.div(item, 2))
        return remote(
            closing.at[lax.rem(item, 4)],
            returned.at[lax.rem(item, 2), place.expert if owner is None else owner],
            back_send.at[item],
            back_land.at[item],
            place.device(peer, place.tensor),
        )

    def close(item):
        slot = lax.rem(item, 4)
        total = collect.third(item)[0]

        @pl.when(item >= 6)
        def _():
            back_copy(item - 4).wait_send()

        closing[slot] = total.astype(jnp.bfloat16)

        @pl.when(item >= 2)
        def _():
            back_copy(item).start()

        @pl.when(item < 2)
        def _():
            own = pltpu.make_async_copy(
                closing.at[slot],
                returned.at[lax.rem(item, 2), place.expert],
                back_send.at[item],
            )
            own.start()
            own.wait()

    def step(turn, carry):
        now = turn - 2
        when(turn < chunks, spread.first, turn)
        when(turn + 1 + AHEAD < chunks, spread.send, turn + 1 + AHEAD)
        when((turn >= 1) & (turn <= chunks), spread.second, turn - 1)
        when(turn + EARLY < chunks, spread_grads.first, turn + EARLY)
        when((turn >= 1) & (turn <= chunks), spread_grads.second, turn - 1)
        when(now >= 0, work, now)
        return carry

    lax.fori_loop(0, chunks + 2, step, 0)
    items = 2 * chunks
    collect.second(items - 1)
    close(items - 2)
    close(items - 1)

    def last(turn, carry):
        spread.finish(turn)
        spread_grads.finish(turn)

        @pl.when(turn > 0)
        def _():
            mark_copy(turn).wait_send()
            for item in (2 * turn, 2 * turn + 1):
                back_copy(item, spread.owner(turn)).wait_recv()

        return carry

    lax.fori_loop(0, chunks, last, 0)
    for store in stores(spread.owner(chunks - 1)):
        store.wait()
    for item in range(max(items - 4, 2), items):
        back_copy(item).wait_send()
    collect.finish()


def experts(source, source_grads, gates, gate_w, up_w, down_w, sharers, collective):
    _, capacity, width = source.shape
    groups, parts = lax.axis_size("expert"), lax.axis_size("tensor")
    spots = parts // 2
    model_width, units = gate_w.shape
    low = jnp.bfloat16
    anywhere = pl.BlockSpec(memory_space=pl.ANY)
    hidden_rows = jax.ShapeDtypeStruct((groups, capacity, units), low)
    return pl.pallas_call(
        functools.partial(experts_kernel, sharers),
        out_shape=(
            jax.ShapeDtypeStruct((1, groups, capacity, model_width), low),
            jax.ShapeDtypeStruct((1, groups, capacity, model_width), low),
            jax.ShapeDtypeStruct((groups, capacity, model_width), low),
            hidden_rows,
            hidden_rows,
            hidden_rows,
            jax.ShapeDtypeStruct((2, groups, capacity, width), low),
        ),
        in_specs=[anywhere] * 6,
        out_specs=(anywhere,) * 7,
        scratch_shapes=[
            pltpu.VMEM((model_width, units), low),
            pltpu.VMEM((model_width, units), low),
            pltpu.VMEM((units, model_width), low),
            pltpu.VMEM((capacity, model_width), low),
            pltpu.VMEM((capacity, model_width), low),
            pltpu.VMEM((capacity, units), low),
            pltpu.VMEM((capacity, units), low),
            pltpu.VMEM((capacity, units), low),
            pltpu.VMEM((4, capacity, width), low),
            pltpu.VMEM((groups,) + gates.shape[1:], jnp.float32),
            pltpu.SemaphoreType.DMA((5,)),
            pltpu.SemaphoreType.DMA((4,)),
            pltpu.SemaphoreType.DMA((2 * groups,)),
            pltpu.SemaphoreType.DMA((2 * groups,)),
            pltpu.SemaphoreType.DMA((groups,)),
            pltpu.SemaphoreType.DMA((groups,)),
        ]
        + Spread.scratch(groups, spots)
        + Spread.scratch(groups, spots)
        + Collect.scratch(2 * groups, 1, spots, capacity, width, 4),
        compiler_params=pltpu.CompilerParams(
            collective_id=collective, has_side_effects=True, vmem_limit_bytes=60 * MIB
        ),
        cost_estimate=lasting(180),
    )(source[None], source_grads[None], gates, gate_w, up_w, down_w)


def across_spots(rows):
    parts = lax.axis_size("tensor")
    pairs = [
        [(index, (index + 2 * step) % parts) for index in range(parts)]
        for step in range(parts // 2)
    ]
    return [rows] + [lax.ppermute(rows, "tensor", pair) for pair in pairs[1:]]


def across_cores(pieces):
    swap = [(index, index ^ 1) for index in range(lax.axis_size("tensor"))]
    return [part for piece in pieces for part in (piece, lax.ppermute(piece, "tensor", swap))]


def closing_kernel(count, *refs):
    normed_t, gain, marks, hidden, scaled, routed, small_in = refs[:7]
    grads, weights, refs = refs[7 : 7 + count], refs[7 + count : 7 + 2 * count], refs[7 + 2 * count :]
    refs = refs[len(refs) - (count + 2 + 20 + 8) :]
    (
        hold, partial, stat_own, stat_in, ready, gathered, small_own, small_got, small_sum,
        ring_send, ring_land, stat_send, stat_land, back_send, back_land,
        small_send, small_land, last_send, last_land, own_sem,
    ) = refs[count + 2 : count + 22]
    summed, back, small_out = refs[:count], refs[count], refs[count + 1]
    place = Place()
    collect = Collect(place, refs[count + 22 :])
    groups, parts = place.groups, place.parts
    pieces, _, rows = collect.core_in.shape[0], None, collect.core_in.shape[3]
    width = hidden.shape[1]
    block = hold.shape[3]
    bucket = back.shape[1]
    each = rows // bucket
    place.meet(True, True)

    parity, half = lax.rem(place.expert, 2), lax.div(place.expert, 2)
    at = half + parity * (groups - 1 - 2 * half)

    def member(spot):
        spot = lax.rem(spot + groups, groups)
        high = lax.div(spot, groups // 2)
        return (1 - high) * 2 * spot + high * (2 * (groups - 1 - spot) + 1)

    ways = ((0, 1), (1, -1))

    def first_row(way, sign, step):
        spot = lax.rem(at - sign * step + 2 * groups, groups)
        return pl.multiple_of((way * groups + spot) * block, block)

    def ring_copy(step, way, sign, number, source, target):
        return remote(
            source,
            target,
            ring_send.at[step, way, number],
            ring_land.at[step, way, number],
            place.device(member(at + sign), place.tensor),
        )

    def slot(step, way, number):
        return hold.at[step, way, number]

    def spot_out(step, way, sign, number):
        return summed[number].at[pl.ds(first_row(way, sign, step), block)]

    def ring(step):
        for number in range(count):
            for way, sign in ways:

                @pl.when((step >= 1) & (step < groups))
                def _():
                    held = slot(step, way, number)
                    ring_copy(step - 1, way, sign, number, held, held).wait_recv()

                @pl.when(step >= groups)
                def _():
                    held = spot_out(step, way, sign, number)
                    ring_copy(step - 1, way, sign, number, held, held).wait_recv()

                @pl.when(step < groups)
                def _():
                    first = first_row(way, sign, step)
                    own = jnp.dot(
                        normed_t[pl.ds(first, block), :],
                        grads[number][...],
                        preferred_element_type=jnp.float32,
                    )

                    @pl.when(step == 0)
                    def _():
                        hold[0, way, number] = own.astype(jnp.bfloat16)

                    @pl.when(step > 0)
                    def _():
                        hold[step, way, number] = (
                            own + hold[step, way, number].astype(jnp.float32)
                        ).astype(jnp.bfloat16)

                @pl.when(step < groups - 1)
                def _():
                    ring_copy(
                        step, way, sign, number, slot(step, way, number), slot(step + 1, way, number)
                    ).start()

                @pl.when(step == groups - 1)
                def _():
                    held, there = slot(step, way, number), spot_out(step, way, sign, number)
                    ring_copy(step, way, sign, number, held, there).start()
                    pltpu.make_async_copy(held, there, own_sem.at[way, number]).start()

                @pl.when((step >= groups) & (step < 2 * groups - 2))
                def _():
                    held = spot_out(step, way, sign, number)
                    ring_copy(step, way, sign, number, held, held).start()

    def ring_finish(step, carry):
        for number in range(count):
            for way, sign in ways:
                held = slot(0, way, number)
                ring_copy(step, way, sign, number, held, held).wait_send()
        return carry

    def band(piece):
        return pl.ds(pl.multiple_of(piece * rows, rows), rows)

    def project(piece):
        collect.free_stage(piece)
        side = lax.rem(piece, 2)
        for spot in range(place.spots):
            for core in range(2):
                first = (spot * 2 + core) * width
                part = None
                for grad, weight in zip(grads, weights):
                    term = dot_nt(grad[band(piece), :], weight[first : first + width, :])
                    part = term if part is None else part + term
                collect.stage[side, 0, spot, core] = part.astype(jnp.bfloat16)
        collect.first(piece)

    def stat_copy(piece, step):
        return remote(
            stat_own.at[piece],
            stat_in.at[piece, step - 1],
            stat_send.at[piece, step - 1],
            stat_land.at[piece, step - 1],
            place.device(place.expert, place.along(step)),
        )

    def measure(piece):
        total = collect.third(piece)[0]
        partial[piece] = total
        inner = jnp.sum(total * scaled[band(piece), :] * gain[...], axis=1, keepdims=True)
        stat_own[piece] = jnp.broadcast_to(inner, (rows, 128))
        for step in range(1, parts):
            stat_copy(piece, step).start()

    def back_copy(target, piece, number):
        return remote(
            ready.at[piece, pl.ds(number * bucket, bucket)],
            back.at[place.expert],
            back_send.at[target],
            back_land.at[place.expert],
            place.device(target, place.tensor),
        )

    def conclude(piece):
        inner = stat_own[piece]
        for step in range(1, parts):
            stat_copy(piece, step).wait_recv()
            inner = inner + stat_in[piece, step - 1]
        mean = (inner[:, :1] + marks[band(piece), 1:2]) / (width * parts)
        grad = partial[piece] + routed[band(piece), :]
        part = scaled[band(piece), :]
        gathered[...] += jnp.sum(grad * part, axis=0, keepdims=True)
        result = hidden[band(piece), :] + marks[band(piece), 0:1] * (grad * gain[...] - part * mean)
        ready[piece] = result.astype(jnp.bfloat16)
        for number in range(each):
            target = piece * each + number

            @pl.when(target != place.expert)
            def _():
                back_copy(target, piece, number).start()

            @pl.when(target == place.expert)
            def _():
                own = pltpu.make_async_copy(
                    ready.at[piece, pl.ds(number * bucket, bucket)],
                    back.at[place.expert],
                    own_sem.at[0, count],
                )
                own.start()
                own.wait()

    def small_copy(step):
        return remote(
            small_own,
            small_got.at[step - 1],
            small_send.at[step - 1],
            small_land.at[step - 1],
            place.device(flip(place.expert, step, groups), place.tensor),
        )

    def last_copy(step, origin):
        return remote(
            small_sum,
            small_out.at[origin],
            last_send.at[step - 1],
            last_land.at[step - 1],
            place.device(place.expert, place.along(step)),
        )

    own_small = pltpu.make_async_copy(small_sum, small_out.at[place.tensor], own_sem.at[1, count])

    def small_first():
        small_own[...] = small_in[...]
        small_own[0:1, :] = gathered[...]
        for step in range(1, groups):
            small_copy(step).start()

    def small_second():
        total = small_own[...]
        for step in range(1, groups):
            small_copy(step).wait_recv()
            total = total + small_got[step - 1]
        small_sum[...] = total
        own_small.start()
        for step in range(1, parts):
            last_copy(step, place.tensor).start()

    gathered[...] = jnp.zeros_like(gathered)
    turns = max(2 * groups - 1, pieces + 5)

    def turn_step(turn, carry):
        when(turn < 2 * groups - 1, ring, turn)
        when((turn >= 3) & (turn < pieces + 3), conclude, turn - 3)
        when((turn >= 2) & (turn < pieces + 2), measure, turn - 2)
        when((turn >= 1) & (turn < pieces + 1), collect.second, turn - 1)
        when(turn < pieces, project, turn)
        when(turn == pieces + 3, small_first)
        when(turn == pieces + 4, small_second)
        return carry

    lax.fori_loop(0, turns, turn_step, 0)
    lax.fori_loop(0, 2 * groups - 2, ring_finish, 0)
    for number in range(count):
        for way, sign in ways:
            pltpu.make_async_copy(
                slot(groups - 1, way, number),
                spot_out(groups - 1, way, sign, number),
                own_sem.at[way, number],
            ).wait()
    collect.finish()
    for step in range(1, groups):
        small_copy(step).wait_send()
    own_small.wait()
    for step in range(1, parts):
        origin = lax.rem(place.tensor + parts - step, parts)
        last_copy(step, place.tensor).wait_send()
        last_copy(step, origin).wait_recv()

    def settle(piece, carry):
        for step in range(1, parts):
            stat_copy(piece, step).wait_send()
        for number in range(each):
            target = piece * each + number

            @pl.when(target != place.expert)
            def _():
                back_copy(target, piece, number).wait_send()
                remote(
                    ready.at[piece, pl.ds(number * bucket, bucket)],
                    back.at[target],
                    back_send.at[target],
                    back_land.at[target],
                    place.device(target, place.tensor),
                ).wait_recv()

        return carry

    lax.fori_loop(0, pieces, settle, 0)


def closing(normed_t, gain, marks, hidden, scaled, routed, small, grads, weights, after, pieces, collective):
    groups, parts = lax.axis_size("expert"), lax.axis_size("tensor")
    spots = parts // 2
    model_width, tokens = normed_t.shape
    columns = grads[0].shape[1]
    width = hidden.shape[1]
    count = len(grads)
    rows = tokens // pieces
    block = model_width // (2 * groups)
    low, full = jnp.bfloat16, jnp.float32
    inside = pl.BlockSpec(memory_space=pltpu.VMEM)
    anywhere = pl.BlockSpec(memory_space=pl.ANY)
    dma = pltpu.SemaphoreType.DMA
    return pl.pallas_call(
        functools.partial(closing_kernel, count),
        out_shape=(
            *(jax.ShapeDtypeStruct((model_width, columns), low) for _ in range(count)),
            jax.ShapeDtypeStruct((groups, tokens // groups, width), low),
            jax.ShapeDtypeStruct((parts,) + small.shape, full),
        ),
        in_specs=[inside] * (7 + 2 * count) + [anywhere] * len(after),
        out_specs=(anywhere,) * (count + 2),
        scratch_shapes=[
            pltpu.VMEM((groups, 2, count, block, columns), low),
            pltpu.VMEM((pieces, rows, width), full),
            pltpu.VMEM((pieces, rows, 128), full),
            pltpu.VMEM((pieces, parts - 1, rows, 128), full),
            pltpu.VMEM((pieces, rows, width), low),
            pltpu.VMEM((1, width), full),
            pltpu.VMEM(small.shape, full),
            pltpu.VMEM((groups - 1,) + small.shape, full),
            pltpu.VMEM(small.shape, full),
            dma((2 * groups - 2, 2, count)),
            dma((2 * groups - 2, 2, count)),
            dma((pieces, parts - 1)),
            dma((pieces, parts - 1)),
            dma((groups,)),
            dma((groups,)),
            dma((groups - 1,)),
            dma((groups - 1,)),
            dma((parts - 1,)),
            dma((parts - 1,)),
            dma((2, count + 1)),
        ]
        + Collect.scratch(pieces, 1, spots, rows, width),
        compiler_params=pltpu.CompilerParams(
            collective_id=collective, has_side_effects=True, vmem_limit_bytes=56 * MIB
        ),
        cost_estimate=lasting(140),
    )(normed_t, gain, marks, hidden, scaled, routed, small, *grads, *weights, *after)


def dot_tn(left, right):
    return lax.dot_general(
        left, right, (((0,), (0,)), ((), ())), preferred_element_type=jnp.float32
    )


def bands(tokens):
    size = 256 if tokens % 256 == 0 else tokens
    return [(first, size) for first in range(0, tokens, size)]


def masked_scores(query, keys, segment_column, segment_row, first, size, column):
    last = first + size
    rows = slice(first, last)
    scores = dot_nt(query[rows, column], keys[:last, column]) * (1.0 / math.sqrt(HEAD))
    place = lax.broadcasted_iota(jnp.int32, (size, last), 0) + first
    other = lax.broadcasted_iota(jnp.int32, (size, last), 1)
    allowed = (segment_column[rows, :] == segment_row[:, :last]) & (place >= other)
    return jnp.where(allowed, scores, MASKED)


def attend_kernel(
    resid, gain, router, w_query, w_key, w_value, cosine, sine, segment_column, segment_row,
    normed, normed_t, factor, logits, query, keys, values, heads, log_total,
):
    tokens, columns = query.shape
    low = jnp.bfloat16
    for first, size in bands(tokens):
        rows = slice(first, first + size)
        value = resid[rows, :].astype(jnp.float32)
        scale = lax.rsqrt(jnp.mean(value * value, axis=1, keepdims=True) + EPSILON)
        value = value * scale * gain[...]
        high = value.astype(low)
        rest = (value - high.astype(jnp.float32)).astype(low)
        factor[rows, :] = scale
        normed[rows, :] = high
        normed_t[:, rows] = high.T
        logits[rows, :] = jnp.dot(
            high, router[...], preferred_element_type=jnp.float32
        ) + jnp.dot(rest, router[...], preferred_element_type=jnp.float32)
        values[rows, :] = jnp.dot(
            high, w_value[...], preferred_element_type=jnp.float32
        ).astype(low)
        for weight, out in ((w_query, query), (w_key, keys)):
            flat = jnp.dot(high, weight[...], preferred_element_type=jnp.float32)
            for head in range(columns // HEAD):
                column = slice(head * HEAD, (head + 1) * HEAD)
                part = flat[:, column]
                turned = pltpu.roll(part, HEAD // 2, 1)
                out[rows, column] = (part * cosine[rows, :] + turned * sine[rows, :]).astype(low)
    for head in range(columns // HEAD):
        column = slice(head * HEAD, (head + 1) * HEAD)
        for first, size in bands(tokens):
            last = first + size
            rows = slice(first, last)
            scores = masked_scores(query, keys, segment_column, segment_row, first, size, column)
            top = jnp.max(scores, axis=1, keepdims=True)
            expo = jnp.exp(scores - top)
            total = jnp.sum(expo, axis=1, keepdims=True)
            probs = (expo / total).astype(low)
            heads[rows, column] = jnp.dot(
                probs, values[:last, column], preferred_element_type=jnp.float32
            ).astype(low)
            log_total[rows, head : head + 1] = top + jnp.log(total)


def attend(resid, gain, router, weights, cosine, sine, segment):
    tokens, model_width = resid.shape
    columns = weights[0].shape[1]
    low, full = jnp.bfloat16, jnp.float32
    block = jax.ShapeDtypeStruct((tokens, columns), low)
    inside = pl.BlockSpec(memory_space=pltpu.VMEM)
    return pl.pallas_call(
        attend_kernel,
        out_shape=(
            jax.ShapeDtypeStruct((tokens, model_width), low),
            jax.ShapeDtypeStruct((model_width, tokens), low),
            jax.ShapeDtypeStruct((tokens, 1), full),
            jax.ShapeDtypeStruct((tokens, router.shape[1]), full),
            block,
            block,
            block,
            block,
            jax.ShapeDtypeStruct((tokens, columns // HEAD), full),
        ),
        in_specs=[inside] * 10,
        out_specs=(inside,) * 9,
        compiler_params=pltpu.CompilerParams(vmem_limit_bytes=56 * MIB),
        cost_estimate=lasting(20),
    )(resid, gain, router, *weights, cosine, sine, segment[:, None], segment[None, :])


def attend_back_kernel(
    grads, w_out, gates, heads, query, keys, values, log_total, cosine, sine,
    segment_column, segment_row,
    query_grad, key_grad, value_grad, gate_grad, weight_grad,
    heads_grad, gated, key_sum, value_sum,
):
    tokens, columns = query.shape
    low = jnp.bfloat16
    span = columns // gates.shape[1]
    scale = 1.0 / math.sqrt(HEAD)
    for first, size in bands(tokens):
        rows = slice(first, first + size)
        plain = dot_nt(grads[rows, :], w_out[...])
        for expert in range(gates.shape[1]):
            column = slice(expert * span, (expert + 1) * span)
            gate = gates[rows, expert : expert + 1]
            head = heads[rows, column].astype(jnp.float32)
            gate_grad[rows, expert : expert + 1] = jnp.sum(
                plain[:, column] * head, axis=1, keepdims=True
            )
            heads_grad[rows, column] = (plain[:, column] * gate).astype(low)
            gated[rows, column] = (head * gate).astype(low)
    weight_grad[...] = dot_tn(gated[...], grads[...]).astype(low)

    def unturn(value, rows):
        turned = pltpu.roll(value * sine[rows, :], HEAD // 2, 1)
        return value * cosine[rows, :] + turned

    for head in range(columns // HEAD):
        column = slice(head * HEAD, (head + 1) * HEAD)
        for first, size in bands(tokens):
            last = first + size
            rows = slice(first, last)
            scores = masked_scores(query, keys, segment_column, segment_row, first, size, column)
            probs = jnp.exp(scores - log_total[rows, head : head + 1])
            value_part = dot_tn(probs.astype(low), heads_grad[rows, column])
            prob_grad = dot_nt(heads_grad[rows, column], values[:last, column])
            score_grad = (
                probs * (prob_grad - jnp.sum(probs * prob_grad, axis=1, keepdims=True))
            ).astype(low)
            query_grad[rows, column] = unturn(
                jnp.dot(score_grad, keys[:last, column], preferred_element_type=jnp.float32)
                * scale,
                rows,
            ).astype(low)
            key_part = dot_tn(score_grad, query[rows, column])
            if first:
                value_sum[:first, :] += value_part[:first]
                key_sum[:first, :] += key_part[:first]
            value_sum[rows, :] = value_part[first:]
            key_sum[rows, :] = key_part[first:]
        whole = slice(0, tokens)
        key_grad[:, column] = unturn(key_sum[...] * scale, whole).astype(low)
        value_grad[:, column] = value_sum[...].astype(low)


def attend_back(grads, w_out, gates, heads, query, keys, values, log_total, cosine, sine, segment):
    tokens, model_width = grads.shape
    columns = query.shape[1]
    low, full = jnp.bfloat16, jnp.float32
    block = jax.ShapeDtypeStruct((tokens, columns), low)
    inside = pl.BlockSpec(memory_space=pltpu.VMEM)
    return pl.pallas_call(
        attend_back_kernel,
        out_shape=(
            block,
            block,
            block,
            jax.ShapeDtypeStruct(gates.shape, full),
            jax.ShapeDtypeStruct(w_out.shape, low),
        ),
        in_specs=[inside] * 12,
        out_specs=(inside,) * 5,
        scratch_shapes=[
            pltpu.VMEM((tokens, columns), low),
            pltpu.VMEM((tokens, columns), low),
            pltpu.VMEM((tokens, HEAD), full),
            pltpu.VMEM((tokens, HEAD), full),
        ],
        compiler_params=pltpu.CompilerParams(vmem_limit_bytes=56 * MIB),
        cost_estimate=lasting(25),
    )(
        grads, w_out, gates, heads, query, keys, values, log_total, cosine, sine,
        segment[:, None], segment[None, :],
    )


def to_expert(rows, group_count):
    count, width = rows.shape
    return lax.all_to_all(
        rows.reshape(group_count, count // group_count, width),
        "expert",
        split_axis=0,
        concat_axis=0,
        tiled=True,
    ).reshape(count, width)


def side_by_side(pieces):
    parts = len(pieces)
    spots = parts // 2
    index = lax.axis_index("tensor")
    spot, core = index // 2, index % 2
    pairs = []
    for step in range(spots):
        same, other = pieces[2 * step], pieces[2 * step + 1]
        pairs.append(
            (jnp.where(core == 0, same, other), jnp.where(core == 0, other, same))
        )
    ordered = []
    for here in range(spots):
        for side in range(2):
            value = pairs[0][side]
            for step in range(1, spots):
                value = jnp.where((spot - here) % spots == step, pairs[step][side], value)
            ordered.append(value)
    return jnp.concatenate(ordered, axis=1)


def gather_tensor(rows):
    return lax.all_gather(rows, "tensor", axis=0)


def body(
    tokens,
    out_grad,
    attn_gain,
    attn_router,
    w_query,
    w_key,
    w_value,
    w_out,
    mlp_gain,
    mlp_router,
    w_gate,
    w_up,
    w_down,
    deal,
    seq_lengths,
    attn_routes,
    mlp_routes,
    slot_order,
):
    tok_rows, model_width = tokens.shape
    group_count = lax.axis_size("expert")
    part_count = lax.axis_size("tensor")
    group_index = lax.axis_index("expert")
    part_index = lax.axis_index("tensor")
    bucket_rows = tok_rows // group_count
    col_width = model_width // part_count
    col_first = part_index * col_width
    low = jnp.bfloat16

    def own_cols(values):
        return lax.dynamic_slice_in_dim(values, col_first, col_width, values.ndim - 1)

    deal_rank = deal // tok_rows * bucket_rows + (deal % tok_rows - group_index * bucket_rows)
    row_ids = jnp.arange(tok_rows, dtype=jnp.int32)
    deal_mask = (row_ids[:, None] == deal_rank[None, :]).astype(low)
    dealt = jnp.dot(deal_mask, own_cols(tokens), preferred_element_type=jnp.float32).astype(low)
    resid_low = spread_rows(dealt.reshape(group_count, bucket_rows, col_width), True, 0, 30)
    dealt_grads = jnp.dot(
        deal_mask, own_cols(out_grad), preferred_element_type=jnp.float32
    ).astype(low)
    dealt_grads, resid_low = lax.optimization_barrier((dealt_grads, resid_low))
    grad_cols_low = to_expert(dealt_grads, group_count)
    gain_one, gain_two = own_cols(attn_gain), own_cols(mlp_gain)
    router_one = lax.dynamic_slice_in_dim(attn_router, col_first, col_width, 0)
    router_two = lax.dynamic_slice_in_dim(mlp_router, col_first, col_width, 0)
    expert_count = mlp_router.shape[1]
    sharers = group_count // expert_count
    capacity = 5 * tok_rows // (2 * expert_count)
    target, position, kept = slot_table(mlp_routes, slot_order[0], capacity)
    slots = expert_count * capacity
    destination = jnp.where(kept, target * capacity + position, slots).reshape(tok_rows, 2)
    slot_ids = jnp.arange(slots, dtype=jnp.int32)
    chosen = [destination[:, way] for way in range(2)]
    to_slot = (
        (slot_ids[:, None] == chosen[0][None, :]) | (slot_ids[:, None] == chosen[1][None, :])
    ).astype(low)
    resid_cols = own_cols(resid_low).astype(jnp.float32)
    segment, cosine, sine = rotary_tables(seq_lengths[0], tok_rows)
    sign = jnp.where(jnp.arange(HEAD) < HEAD // 2, -1.0, 1.0)
    local_heads = w_query.shape[1] // HEAD
    local_experts = local_heads // QH
    span = QH * HEAD
    experts_of = attn_router.shape[1]
    router_high = lax.reduce_precision(attn_router, 8, 7)
    router_parts = jnp.concatenate([router_high, attn_router - router_high], axis=1).astype(low)
    router_parts = jnp.pad(router_parts, ((0, 0), (0, -router_parts.shape[1] % 128)))
    normed_low, normed_t, factor_one, logit_parts, query, keys, values, heads_low, log_total = (
        attend(
            resid_low,
            attn_gain[None],
            router_parts,
            (w_query, w_key, w_value),
            cosine,
            sine * sign,
            segment,
        )
    )
    attn_logits = logit_parts[:, :experts_of] + logit_parts[:, experts_of : 2 * experts_of]
    attn_gates, attn_mask = pair_gates(attn_logits, attn_routes)
    gate_table = jnp.sum(attn_gates[:, :, None] * attn_mask, axis=1)
    gate_local = lax.dynamic_slice_in_dim(gate_table, part_index * local_experts, local_experts, 1)
    grad_cols_low, heads_low = lax.optimization_barrier((grad_cols_low, heads_low))
    grad_cols = grad_cols_low.astype(jnp.float32)
    slot_grads = jnp.dot(to_slot, grad_cols_low, preferred_element_type=jnp.float32).astype(low)
    slot_grads = jnp.repeat(slot_grads.reshape(expert_count, capacity, col_width), sharers, axis=0)
    slot_grads = to_expert(slot_grads.reshape(group_count * capacity, col_width), group_count)
    pieces, piece_rows = 4, tok_rows // 4
    attn_cols = collect_rows(
        functools.partial(make_attended, span),
        (
            heads_low.reshape(pieces, piece_rows, local_heads * HEAD),
            gate_local.reshape(pieces, piece_rows, local_experts),
            w_out,
        ),
        pieces,
        piece_rows,
        col_width,
        1,
    )
    hidden = resid_cols + attn_cols
    weighed = hidden * gain_two
    stats = jnp.concatenate(
        [
            jnp.sum(hidden * hidden, axis=1)[None, :],
            jnp.dot(weighed, router_two, precision=PRECISE).T,
        ],
        axis=0,
    )
    stats = jnp.sum(gather_tensor(stats), axis=0)
    factor_two = lax.rsqrt(stats[0] / model_width + EPSILON)[:, None]
    mlp_logits = stats[1:].T * factor_two
    scaled_two = hidden * factor_two
    normed_two = scaled_two * gain_two
    mlp_gates, mlp_mask = pair_gates(mlp_logits, mlp_routes)
    slot_rows = jnp.dot(
        to_slot, normed_two.astype(low), preferred_element_type=jnp.float32
    ).astype(low)
    slot_gates = sum(
        jnp.sum(
            jnp.where(slot_ids[:, None] == chosen[way][None, :], mlp_gates[:, way][None, :], 0.0),
            axis=1,
        )
        for way in range(2)
    )
    gate_lines = jnp.pad(slot_gates.reshape(expert_count, capacity), ((0, 0), (0, -capacity % 128)))
    gate_lines = jnp.broadcast_to(gate_lines[:, None, :], (expert_count, 8, gate_lines.shape[1]))
    inbox, _, slot_grads, middle, gate_grad, up_grad, returned = experts(
        slot_rows.reshape(expert_count, capacity, col_width),
        slot_grads.reshape(group_count, capacity, col_width),
        gate_lines,
        w_gate[0],
        w_up[0],
        w_down[0],
        sharers,
        2,
    )
    if sharers > 1:
        returned = (
            jnp.sum(
                returned.reshape(2, expert_count, sharers, capacity, col_width).astype(jnp.float32),
                axis=2,
            )
        ).astype(low)
    made, row_grads = returned.reshape(2, slots, col_width)
    from_slot = [(chosen[way][:, None] == slot_ids[None, :]).astype(low) for way in range(2)]
    pair_values = jnp.stack(
        [
            jnp.dot(from_slot[way], made, preferred_element_type=jnp.float32)
            for way in range(2)
        ],
        axis=1,
    )
    row_grad_sum = jnp.dot(
        from_slot[0] + from_slot[1], row_grads, preferred_element_type=jnp.float32
    )
    mixed_cols = hidden + jnp.sum(mlp_gates[:, :, None] * pair_values, axis=1)
    back_mixed = to_expert(mixed_cols.astype(low), group_count)
    weighed_two = scaled_two * gain_two
    stats = jnp.stack(
        [
            jnp.sum(pair_values[:, 0] * grad_cols, axis=1),
            jnp.sum(pair_values[:, 1] * grad_cols, axis=1),
            jnp.sum(row_grad_sum * weighed_two, axis=1),
        ]
    )
    stats = jnp.sum(gather_tensor(stats), axis=0)
    mlp_logit_grad = pair_back(mlp_gates, mlp_mask, stats[:2].T)
    norm_two_grad = row_grad_sum + jnp.dot(mlp_logit_grad, router_two.T, precision=PRECISE)
    mlp_router_grad = jnp.dot(normed_two.T, mlp_logit_grad, precision=PRECISE)
    mlp_gain_grad = jnp.sum(norm_two_grad * scaled_two, axis=0)
    mean_two = (stats[2] + jnp.sum(mlp_logit_grad * mlp_logits, axis=1)) / model_width
    hidden_grad = grad_cols + factor_two * (norm_two_grad * gain_two - scaled_two * mean_two[:, None])
    rows = inbox.reshape(-1, model_width)
    grad_rows = slot_grads.reshape(-1, model_width)
    units = middle.shape[2]

    def rows_product(left, right):
        return jnp.einsum("sa,sb->ab", left, right, preferred_element_type=jnp.float32)

    hidden_pieces = across_spots(hidden_grad.astype(low))
    gate_w_grad = rows_product(rows, gate_grad.reshape(-1, units))
    *hidden_pieces, gate_w_grad = lax.optimization_barrier((*hidden_pieces, gate_w_grad))
    hidden_grad_low = side_by_side(across_cores(hidden_pieces))
    query_pre_grad, key_pre_grad, value_pre_grad, local_gate_grad, out_w_grad = attend_back(
        hidden_grad_low,
        w_out,
        gate_local,
        heads_low,
        query,
        keys,
        values,
        log_total,
        cosine,
        sine * sign,
        segment,
    )
    out_w_grad, middle, up_grad = lax.optimization_barrier((out_w_grad, middle, up_grad))
    out_w_grad = lax.psum(out_w_grad, "expert").astype(jnp.float32)
    gate_grads = gather_tensor(local_gate_grad.T)
    gate_grads = gate_grads.reshape(part_count * local_experts, tok_rows).T
    attn_pair_grad = jnp.sum(attn_mask * gate_grads[:, None, :], axis=2)
    attn_logit_grad = pair_back(attn_gates, attn_mask, attn_pair_grad)
    scaled_cols = resid_cols * factor_one
    normed_cols = scaled_cols * gain_one
    attn_router_grad = jnp.dot(normed_cols.T, attn_logit_grad, precision=PRECISE)
    small = jnp.concatenate(
        [
            jnp.zeros((1, col_width), jnp.float32),
            attn_router_grad.T,
            mlp_gain_grad[None],
            mlp_router_grad.T,
        ],
        axis=0,
    )
    small = jnp.pad(small, ((0, -small.shape[0] % 8), (0, 0)))
    marks = jnp.stack(
        [factor_one[:, 0], jnp.sum(attn_logit_grad * attn_logits, axis=1)], axis=1
    )
    up_w_grad = rows_product(rows, up_grad.reshape(-1, units))
    down_grad = rows_product(middle.reshape(-1, units), grad_rows)
    *weight_grads, back_grad, small = closing(
        normed_t,
        gain_one[None],
        jnp.pad(marks, ((0, 0), (0, 126))),
        hidden_grad,
        scaled_cols,
        jnp.dot(attn_logit_grad, router_one.T, precision=PRECISE),
        small,
        (query_pre_grad, key_pre_grad, value_pre_grad),
        (w_query, w_key, w_value),
        (gate_w_grad, up_w_grad, down_grad),
        pieces,
        3,
    )
    back_grad = back_grad.reshape(tok_rows, col_width)
    weight_grads = [grad.astype(jnp.float32) for grad in weight_grads]
    mixed, tokens_grad = (
        jnp.einsum("ri,rc->ic", deal_mask, back, preferred_element_type=jnp.float32).astype(low)
        for back in (back_mixed, back_grad)
    )
    small = small.transpose(1, 0, 2).reshape(-1, model_width)
    return (
        mixed,
        tokens_grad,
        small[0],
        small[1 : 1 + experts_of].T,
        weight_grads[0],
        weight_grads[1],
        weight_grads[2],
        out_w_grad,
        small[1 + experts_of],
        small[2 + experts_of : 2 + experts_of + expert_count].T,
        gate_w_grad[None],
        up_w_grad[None],
        down_grad[None],
    )


def solution(mesh):
    placed = (
        P("expert", None),
        P("expert", None),
        P(),
        P(),
        P(None, "tensor"),
        P(None, "tensor"),
        P(None, "tensor"),
        P("tensor", None),
        P(),
        P(),
        P("expert", None, "tensor"),
        P("expert", None, "tensor"),
        P("expert", "tensor", None),
        P("expert"),
        P("expert", None),
        P("expert", None),
        P("expert", None),
        P("expert", None),
    )
    return jax.shard_map(
        body,
        mesh=mesh,
        in_specs=placed,
        out_specs=(
            P("expert", "tensor"),
            P("expert", "tensor"),
            P(),
            P(),
            P(None, "tensor"),
            P(None, "tensor"),
            P(None, "tensor"),
            P("tensor", None),
            P(),
            P(),
            P("expert", None, "tensor"),
            P("expert", None, "tensor"),
            P("expert", "tensor", None),
        ),
        check_vma=False,
    )
```

```python
import functools
import math

import jax
import jax.numpy as jnp
from jax import lax
from jax.experimental import pallas as pl
from jax.experimental.pallas import tpu as pltpu
from jax.sharding import PartitionSpec as P

HEAD = 128
QH = 2


PRECISE = lax.Precision.HIGH
EPSILON = 1e-06
MASKED = -1e30


def rotary_tables(lengths, tok_rows):
    seq_ends = jnp.cumsum(lengths)
    seq_starts = seq_ends - lengths
    places = jnp.arange(tok_rows, dtype=jnp.int32)
    segment = jnp.sum((places[:, None] >= seq_ends[None, :]).astype(jnp.int32), axis=1)
    matches = segment[:, None] == jnp.arange(lengths.shape[0], dtype=jnp.int32)[None, :]
    seq_first = jnp.sum(jnp.where(matches, seq_starts[None, :], 0), axis=1)
    offsets = (places - seq_first).astype(jnp.float32)
    frequency = jnp.exp(-math.log(10000.0) * jnp.arange(0, HEAD, 2, dtype=jnp.float32) / HEAD)
    angles = offsets[:, None] * frequency[None, :]
    angles = jnp.concatenate([angles, angles], axis=1)
    return (segment, jnp.cos(angles), jnp.sin(angles))


def pair_gates(logits, routes):
    columns = logits.shape[1]
    chosen_mask = (
        routes[:, :, None] == jnp.arange(columns, dtype=jnp.int32)[None, None, :]
    ).astype(jnp.float32)
    picked = jnp.sum(chosen_mask * logits[:, None, :], axis=2)
    return (jax.nn.softmax(picked, axis=1), chosen_mask)


def pair_back(gates, chosen_mask, gate_grads):
    inner = gates * (gate_grads - jnp.sum(gates * gate_grads, axis=1, keepdims=True))
    return jnp.sum(chosen_mask * inner[:, :, None], axis=1)


def slot_table(routes, priority, capacity):
    target = routes.reshape(-1)
    ahead = (target[None, :] == target[:, None]) & (priority[None, :] < priority[:, None])
    position = jnp.sum(ahead.astype(jnp.int32), axis=1)
    return (target, position, position < capacity)


MESH = pl.DeviceIdType.MESH
MIB = 1 << 20
AHEAD_DEAL = 2
AHEAD = 2
EARLY = 2


def flip(number, other, count):
    total, bit = 0, 1
    while bit < count:
        total = total + lax.rem(lax.div(number, bit) + lax.div(other, bit), 2) * bit
        bit *= 2
    return total


def dot_nt(left, right):
    return lax.dot_general(
        left, right, (((1,), (1,)), ((), ())), preferred_element_type=jnp.float32
    )


class Place:
    def __init__(self):
        self.groups = lax.axis_size("expert")
        self.parts = lax.axis_size("tensor")
        self.spots = self.parts // 2
        self.expert = lax.axis_index("expert")
        self.tensor = lax.axis_index("tensor")
        self.spot = lax.div(self.tensor, 2)
        self.core = lax.rem(self.tensor, 2)

    def device(self, expert, tensor):
        return {"expert": expert, "tensor": tensor}

    def across(self, step):
        return lax.rem(self.spot + step, self.spots) * 2 + self.core

    def before(self, step):
        return lax.rem(self.spot + self.spots - step, self.spots) * 2 + self.core

    def meet(self, over_expert, whole_tensor=False):
        if whole_tensor:
            peers = [self.device(self.expert, self.along(step)) for step in range(1, self.parts)]
        else:
            peers = [self.device(self.expert, self.spot * 2 + 1 - self.core)]
            for step in range(1, self.spots):
                peers.append(self.device(self.expert, self.across(step)))
        if over_expert:
            for step in range(1, self.groups):
                peers.append(self.device(flip(self.expert, step, self.groups), self.tensor))
        barrier = pltpu.get_barrier_semaphore()
        for peer in peers:
            pl.semaphore_signal(barrier, inc=1, device_id=peer, device_id_type=MESH)
        pl.semaphore_wait(barrier, len(peers))

    def along(self, step):
        return lax.rem(self.tensor + step, self.parts)


def lasting(microseconds):
    return pl.CostEstimate(
        flops=0, bytes_accessed=int(microseconds * 3_000_000), transcendentals=0
    )


def remote(source, target, send, receive, device):
    return pltpu.make_async_remote_copy(
        src_ref=source,
        dst_ref=target,
        send_sem=send,
        recv_sem=receive,
        device_id=device,
        device_id_type=MESH,
    )


class Spread:
    @staticmethod
    def scratch(chunks, spots):
        return [
            pltpu.SemaphoreType.DMA((chunks,)),
            pltpu.SemaphoreType.DMA((chunks,)),
            pltpu.SemaphoreType.DMA((chunks, max(spots - 1, 1))),
            pltpu.SemaphoreType.DMA((chunks, max(spots - 1, 1))),
            pltpu.SemaphoreType.DMA((chunks, spots)),
            pltpu.SemaphoreType.DMA((chunks, spots)),
        ]

    def __init__(self, place, source, target, sems, over_expert, sharers=1, by_group=None):
        self.place, self.source, self.target = place, source, target
        self.by_group = over_expert if by_group is None else by_group
        self.first_send, self.first_land, self.side_send, self.side_land, self.core_send, self.core_land = sems
        self.over_expert, self.sharers = over_expert, sharers
        self.width = source.shape[3]
        self.chunks = target.shape[1]

    def owner(self, chunk):
        if not self.by_group:
            return chunk
        half, odd, pair = self.place.groups // 2, lax.rem(chunk, 2), lax.div(chunk, 2)
        even_way = jnp.minimum(chunk, 1) * half + pair
        odd_way = pair + (1 - jnp.minimum(pair, 1)) * half
        return flip(
            self.place.expert, odd * odd_way + (1 - odd) * even_way, self.place.groups
        )

    def spot_of(self, owner, tensor):
        first = pl.multiple_of(tensor * self.width, 128)
        return self.target.at[:, owner, :, pl.ds(first, self.width)]

    def block(self, owner):
        if self.sharers == 1:
            return self.source.at[:, owner]
        return self.source.at[:, lax.div(owner, self.sharers)]

    def send(self, chunk):
        place = self.place
        peer = self.owner(chunk)
        remote(
            self.block(peer),
            self.spot_of(place.expert, place.tensor),
            self.first_send.at[chunk],
            self.first_land.at[chunk],
            place.device(peer, place.tensor),
        ).start()

    def start(self, ahead):
        place = self.place
        own = self.owner(0)
        if not self.over_expert:
            return
        for chunk in range(1, min(ahead + 1, self.chunks)):
            self.send(chunk)
        copy = pltpu.make_async_copy(
            self.block(own), self.spot_of(own, place.tensor), self.first_send.at[0]
        )
        copy.start()
        copy.wait()

    def first(self, chunk):
        place = self.place
        owner = self.owner(chunk)
        mine = self.spot_of(owner, place.tensor)
        if self.over_expert:

            @pl.when(chunk > 0)
            def _():
                remote(
                    self.block(owner),
                    mine,
                    self.first_send.at[chunk],
                    self.first_land.at[chunk],
                    place.device(owner, place.tensor),
                ).wait_recv()

            held = mine
        else:
            pltpu.make_async_copy(self.block(owner), mine, self.first_send.at[chunk]).start()
            held = self.block(owner)
        for step in range(1, place.spots):
            remote(
                held,
                mine,
                self.side_send.at[chunk, step - 1],
                self.side_land.at[chunk, step - 1],
                place.device(place.expert, place.across(step)),
            ).start()
        remote(
            held,
            mine,
            self.core_send.at[chunk, 0],
            self.core_land.at[chunk, 0],
            place.device(place.expert, place.spot * 2 + 1 - place.core),
        ).start()

    def second(self, chunk):
        place = self.place
        owner = self.owner(chunk)
        for step in range(1, place.spots):
            came = self.spot_of(owner, place.before(step))
            remote(
                came,
                came,
                self.side_send.at[chunk, step - 1],
                self.side_land.at[chunk, step - 1],
                place.device(place.expert, place.across(step)),
            ).wait_recv()
            remote(
                came,
                came,
                self.core_send.at[chunk, step],
                self.core_land.at[chunk, step],
                place.device(place.expert, place.spot * 2 + 1 - place.core),
            ).start()

    def third(self, chunk):
        place = self.place
        owner = self.owner(chunk)
        flipped = 1 - 2 * place.core
        if not self.over_expert:
            mine = self.spot_of(owner, place.tensor)
            pltpu.make_async_copy(self.block(owner), mine, self.first_send.at[chunk]).wait()
        for step in range(place.spots):
            came = self.spot_of(owner, place.before(step) + flipped)
            remote(
                came,
                came,
                self.core_send.at[chunk, step],
                self.core_land.at[chunk, step],
                place.device(place.expert, place.spot * 2 + 1 - place.core),
            ).wait_recv()

    def finish(self, chunk):
        place = self.place
        owner = self.owner(chunk)
        mine = self.spot_of(owner, place.tensor)
        device = place.device(place.expert, place.tensor)
        if self.over_expert:

            @pl.when(chunk > 0)
            def _():
                remote(
                    self.block(owner),
                    mine,
                    self.first_send.at[chunk],
                    self.first_land.at[chunk],
                    device,
                ).wait_send()

        for step in range(1, place.spots):
            remote(
                mine,
                mine,
                self.side_send.at[chunk, step - 1],
                self.side_land.at[chunk, step - 1],
                device,
            ).wait_send()
        for step in range(place.spots):
            remote(
                mine, mine, self.core_send.at[chunk, step], self.core_land.at[chunk, step], device
            ).wait_send()


class Collect:
    @staticmethod
    def scratch(chunks, kinds, spots, rows, width, slots=2):
        return [
            pltpu.VMEM((slots, kinds, spots, 2, rows, width), jnp.bfloat16),
            pltpu.VMEM((slots, kinds, max(spots - 1, 1), rows, width), jnp.bfloat16),
            pltpu.VMEM((chunks, kinds, spots, rows, width), jnp.bfloat16),
            pltpu.VMEM((chunks, kinds, max(spots - 1, 1), rows, width), jnp.bfloat16),
            pltpu.SemaphoreType.DMA((chunks,)),
            pltpu.SemaphoreType.DMA((chunks,)),
            pltpu.SemaphoreType.DMA((chunks, max(spots - 1, 1))),
            pltpu.SemaphoreType.DMA((chunks, max(spots - 1, 1))),
        ]

    def __init__(self, place, refs):
        self.place = place
        self.stage, self.side, self.core_in, self.side_in = refs[:4]
        self.core_send, self.core_land, self.side_send, self.side_land = refs[4:]
        self.chunks = self.core_in.shape[0]
        self.slots = self.stage.shape[0]

    def core_copy(self, chunk):
        place = self.place
        return remote(
            self.stage.at[lax.rem(chunk, self.slots), :, :, 1 - place.core],
            self.core_in.at[chunk],
            self.core_send.at[chunk],
            self.core_land.at[chunk],
            place.device(place.expert, place.spot * 2 + 1 - place.core),
        )

    def side_copy(self, chunk, step):
        place = self.place
        return remote(
            self.side.at[lax.rem(chunk, self.slots), :, step - 1],
            self.side_in.at[chunk, :, step - 1],
            self.side_send.at[chunk, step - 1],
            self.side_land.at[chunk, step - 1],
            place.device(place.expert, place.across(step)),
        )

    def free_stage(self, chunk):
        @pl.when(chunk >= self.slots)
        def _():
            self.core_copy(chunk - self.slots).wait_send()

    def first(self, chunk):
        self.core_copy(chunk).start()

    def second(self, chunk):
        place = self.place
        slot = lax.rem(chunk, self.slots)
        self.core_copy(chunk).wait_recv()

        @pl.when(chunk >= self.slots)
        def _():
            for step in range(1, place.spots):
                self.side_copy(chunk - self.slots, step).wait_send()

        for step in range(1, place.spots):
            there = lax.rem(place.spot + step, place.spots)
            total = self.stage[slot, :, there, place.core].astype(jnp.float32) + self.core_in[
                chunk, :, there
            ].astype(jnp.float32)
            self.side[slot, :, step - 1] = total.astype(jnp.bfloat16)
            self.side_copy(chunk, step).start()

    def third(self, chunk):
        place = self.place
        slot = lax.rem(chunk, self.slots)
        total = self.stage[slot, :, place.spot, place.core].astype(jnp.float32) + self.core_in[
            chunk, :, place.spot
        ].astype(jnp.float32)
        for step in range(1, place.spots):
            self.side_copy(chunk, step).wait_recv()
            total = total + self.side_in[chunk, :, step - 1].astype(jnp.float32)
        return total

    def finish(self):
        for chunk in range(max(self.chunks - self.slots, 0), self.chunks):
            self.core_copy(chunk).wait_send()
            for step in range(1, self.place.spots):
                self.side_copy(chunk, step).wait_send()


def when(condition, action, *args):
    pl.when(condition)(functools.partial(action, *args))


def spread_kernel(over_expert, source, target, *sems):
    place = Place()
    spread = Spread(place, source, target, sems, over_expert)
    place.meet(over_expert)
    spread.start(AHEAD_DEAL)

    def step(turn, carry):
        when(turn < spread.chunks, spread.first, turn)
        if over_expert:
            when(turn + 1 + AHEAD_DEAL < spread.chunks, spread.send, turn + 1 + AHEAD_DEAL)
        when(turn >= 1, spread.second, turn - 1)
        return carry

    lax.fori_loop(0, spread.chunks + 1, step, 0)

    def last(turn, carry):
        spread.third(turn)
        spread.finish(turn)
        return carry

    lax.fori_loop(0, spread.chunks, last, 0)


def spread_rows(rows, over_expert, collective, microseconds):
    chunks, count, width = rows.shape
    parts = lax.axis_size("tensor")
    full = pl.pallas_call(
        functools.partial(spread_kernel, over_expert),
        out_shape=jax.ShapeDtypeStruct((1, chunks, count, width * parts), rows.dtype),
        in_specs=[pl.BlockSpec(memory_space=pl.ANY)],
        out_specs=pl.BlockSpec(memory_space=pl.ANY),
        scratch_shapes=Spread.scratch(chunks, parts // 2),
        compiler_params=pltpu.CompilerParams(collective_id=collective, has_side_effects=True),
        cost_estimate=lasting(microseconds),
    )(rows[None])
    return full.reshape(chunks * count, width * parts)


def collect_kernel(make, operand_count, *refs):
    place = Place()
    operands = refs[:operand_count]
    result = refs[operand_count]
    collect = Collect(place, refs[operand_count + 1 :])
    place.meet(False)

    def one(chunk):
        collect.free_stage(chunk)
        slot = lax.rem(chunk, 2)
        width = result.shape[2]
        for spot in range(place.spots):
            for core in range(2):
                first = (spot * 2 + core) * width
                part = make(operands, chunk, first, width)
                collect.stage[slot, 0, spot, core] = part.astype(jnp.bfloat16)
        collect.first(chunk)

    def close(chunk):
        result[chunk] = collect.third(chunk)[0]

    def step(turn, carry):
        when(turn >= 2, close, turn - 2)
        when((turn >= 1) & (turn <= collect.chunks), collect.second, turn - 1)
        when(turn < collect.chunks, one, turn)
        return carry

    lax.fori_loop(0, collect.chunks + 2, step, 0)
    collect.finish()


def collect_rows(make, operands, chunks, rows, width, collective):
    parts = lax.axis_size("tensor")
    out = pl.pallas_call(
        functools.partial(collect_kernel, make, len(operands)),
        out_shape=jax.ShapeDtypeStruct((chunks, rows, width), jnp.float32),
        in_specs=[pl.BlockSpec(memory_space=pltpu.VMEM)] * len(operands),
        out_specs=pl.BlockSpec(memory_space=pltpu.VMEM),
        scratch_shapes=Collect.scratch(chunks, 1, parts // 2, rows, width),
        compiler_params=pltpu.CompilerParams(
            collective_id=collective, has_side_effects=True, vmem_limit_bytes=48 * MIB
        ),
        cost_estimate=lasting(26),
    )(*operands)
    return out.reshape(chunks * rows, width)


def make_attended(span, operands, chunk, first, width):
    heads, gates, weight = operands
    total = None
    for expert in range(gates.shape[2]):
        term = gates[chunk, :, expert : expert + 1] * jnp.dot(
            heads[chunk, :, expert * span : (expert + 1) * span],
            weight[expert * span : (expert + 1) * span, first : first + width],
            preferred_element_type=jnp.float32,
        )
        total = term if total is None else total + term
    return total


def experts_kernel(sharers, *refs):
    (
        source, source_grads, gates, gate_hbm, up_hbm, down_hbm,
        inbox, inbox_grads, grads_out, middle_out, gate_out, up_out, returned,
        gate_w, up_w, down_w, rows, grads, middle, gate_g, up_g, closing, gates_in,
        load_sem, store_sem, back_send, back_land, mark_send, mark_land,
    ) = refs[:29]
    place = Place()
    spread = Spread(place, source, inbox, refs[29:35], True, sharers)
    spread_grads = Spread(place, source_grads, inbox_grads, refs[35:41], False, by_group=True)
    collect = Collect(place, refs[41:])
    chunks = spread.chunks
    width = source.shape[3]
    units = gate_w.shape[1]
    tile = 704 if units % 704 == 0 else units
    capacity = rows.shape[0]
    loads = [
        pltpu.make_async_copy(held, kept, load_sem.at[number])
        for number, (held, kept) in enumerate(
            ((gate_hbm, gate_w), (up_hbm, up_w), (down_hbm, down_w))
        )
    ]
    for load in loads:
        load.start()
    place.meet(True)

    def mark_copy(chunk):
        peer = spread.owner(chunk)
        return remote(
            gates.at[lax.div(peer, sharers)],
            gates_in.at[place.expert],
            mark_send.at[chunk],
            mark_land.at[chunk],
            place.device(peer, place.tensor),
        )

    def mark_landed(chunk):
        peer = spread.owner(chunk)
        return remote(
            gates.at[lax.div(peer, sharers)],
            gates_in.at[peer],
            mark_send.at[chunk],
            mark_land.at[chunk],
            place.device(peer, place.tensor),
        )

    spread.start(AHEAD)
    for chunk in range(1, chunks):
        mark_copy(chunk).start()
    own_mark = pltpu.make_async_copy(
        gates.at[lax.div(place.expert, sharers)], gates_in.at[place.expert], mark_send.at[0]
    )
    own_mark.start()
    own_mark.wait()
    for chunk in range(EARLY):
        spread_grads.first(chunk)

    def stores(owner):
        return [
            pltpu.make_async_copy(held, out.at[owner], store_sem.at[number])
            for number, (held, out) in enumerate(
                ((middle, middle_out), (gate_g, gate_out), (up_g, up_out), (grads, grads_out))
            )
        ]

    def fetches(owner):
        return [
            pltpu.make_async_copy(inbox.at[0, owner], rows, load_sem.at[3]),
            pltpu.make_async_copy(inbox_grads.at[0, owner], grads, load_sem.at[4]),
        ]

    def work(chunk):
        owner = spread.owner(chunk)

        @pl.when(chunk == 0)
        def _():
            for load in loads:
                load.wait()

        @pl.when(chunk > 0)
        def _():
            for store in stores(spread.owner(chunk - 1)):
                store.wait()
            mark_landed(chunk).wait_recv()

        spread.third(chunk)
        spread_grads.third(chunk)
        copies = fetches(owner)
        for fetch in copies:
            fetch.start()
        for fetch in copies:
            fetch.wait()
        wide = gates_in.shape[2]
        line = jnp.broadcast_to(gates_in[owner][:1], (capacity, wide))
        here = lax.broadcasted_iota(jnp.int32, (capacity, wide), 0) == lax.broadcasted_iota(
            jnp.int32, (capacity, wide), 1
        )
        gate_column = jnp.sum(jnp.where(here, line, 0.0), axis=1, keepdims=True)
        grads[...] = (grads[...].astype(jnp.float32) * gate_column).astype(jnp.bfloat16)
        for first in range(0, units, tile):
            here = slice(first, first + tile)
            gate = jnp.dot(rows[...], gate_w[:, here], preferred_element_type=jnp.float32)
            up = jnp.dot(rows[...], up_w[:, here], preferred_element_type=jnp.float32)
            sig = jax.nn.sigmoid(gate)
            act = gate * sig
            middle[:, here] = (act * up).astype(jnp.bfloat16)
            grad = dot_nt(grads[...], down_w[here, :])
            gate_g[:, here] = (grad * up * sig * (1.0 + gate * (1.0 - sig))).astype(jnp.bfloat16)
            up_g[:, here] = (grad * act).astype(jnp.bfloat16)
        for store in stores(owner):
            store.start()
        made, fed = 2 * chunk, 2 * chunk + 1
        when(chunk >= 1, collect.second, made - 1)
        when(chunk >= 1, close, made - 2)
        collect.free_stage(made)
        for spot in range(place.spots):
            for core in range(2):
                first = (spot * 2 + core) * width
                here = slice(first, first + width)
                collect.stage[lax.rem(made, 4), 0, spot, core] = jnp.dot(
                    middle[...], down_w[:, here], preferred_element_type=jnp.float32
                ).astype(jnp.bfloat16)
        collect.first(made)
        collect.free_stage(fed)
        for spot in range(place.spots):
            for core in range(2):
                first = (spot * 2 + core) * width
                here = slice(first, first + width)
                collect.stage[lax.rem(fed, 4), 0, spot, core] = (
                    dot_nt(gate_g[...], gate_w[here, :]) + dot_nt(up_g[...], up_w[here, :])
                ).astype(jnp.bfloat16)
        collect.first(fed)
        collect.second(made)
        when(chunk >= 1, close, made - 1)

    def back_copy(item, owner=None):
        peer = spread.owner(lax.div(item, 2))
        return remote(
            closing.at[lax.rem(item, 4)],
            returned.at[lax.rem(item, 2), place.expert if owner is None else owner],
            back_send.at[item],
            back_land.at[item],
            place.device(peer, place.tensor),
        )

    def close(item):
        slot = lax.rem(item, 4)
        total = collect.third(item)[0]

        @pl.when(item >= 6)
        def _():
            back_copy(item - 4).wait_send()

        closing[slot] = total.astype(jnp.bfloat16)

        @pl.when(item >= 2)
        def _():
            back_copy(item).start()

        @pl.when(item < 2)
        def _():
            own = pltpu.make_async_copy(
                closing.at[slot],
                returned.at[lax.rem(item, 2), place.expert],
                back_send.at[item],
            )
            own.start()
            own.wait()

    def step(turn, carry):
        now = turn - 2
        when(turn < chunks, spread.first, turn)
        when(turn + 1 + AHEAD < chunks, spread.send, turn + 1 + AHEAD)
        when((turn >= 1) & (turn <= chunks), spread.second, turn - 1)
        when(turn + EARLY < chunks, spread_grads.first, turn + EARLY)
        when((turn >= 1) & (turn <= chunks), spread_grads.second, turn - 1)
        when(now >= 0, work, now)
        return carry

    lax.fori_loop(0, chunks + 2, step, 0)
    items = 2 * chunks
    collect.second(items - 1)
    close(items - 2)
    close(items - 1)

    def last(turn, carry):
        spread.finish(turn)
        spread_grads.finish(turn)

        @pl.when(turn > 0)
        def _():
            mark_copy(turn).wait_send()
            for item in (2 * turn, 2 * turn + 1):
                back_copy(item, spread.owner(turn)).wait_recv()

        return carry

    lax.fori_loop(0, chunks, last, 0)
    for store in stores(spread.owner(chunks - 1)):
        store.wait()
    for item in range(max(items - 4, 2), items):
        back_copy(item).wait_send()
    collect.finish()


def experts(source, source_grads, gates, gate_w, up_w, down_w, sharers, collective):
    _, capacity, width = source.shape
    groups, parts = lax.axis_size("expert"), lax.axis_size("tensor")
    spots = parts // 2
    model_width, units = gate_w.shape
    low = jnp.bfloat16
    anywhere = pl.BlockSpec(memory_space=pl.ANY)
    hidden_rows = jax.ShapeDtypeStruct((groups, capacity, units), low)
    return pl.pallas_call(
        functools.partial(experts_kernel, sharers),
        out_shape=(
            jax.ShapeDtypeStruct((1, groups, capacity, model_width), low),
            jax.ShapeDtypeStruct((1, groups, capacity, model_width), low),
            jax.ShapeDtypeStruct((groups, capacity, model_width), low),
            hidden_rows,
            hidden_rows,
            hidden_rows,
            jax.ShapeDtypeStruct((2, groups, capacity, width), low),
        ),
        in_specs=[anywhere] * 6,
        out_specs=(anywhere,) * 7,
        scratch_shapes=[
            pltpu.VMEM((model_width, units), low),
            pltpu.VMEM((model_width, units), low),
            pltpu.VMEM((units, model_width), low),
            pltpu.VMEM((capacity, model_width), low),
            pltpu.VMEM((capacity, model_width), low),
            pltpu.VMEM((capacity, units), low),
            pltpu.VMEM((capacity, units), low),
            pltpu.VMEM((capacity, units), low),
            pltpu.VMEM((4, capacity, width), low),
            pltpu.VMEM((groups,) + gates.shape[1:], jnp.float32),
            pltpu.SemaphoreType.DMA((5,)),
            pltpu.SemaphoreType.DMA((4,)),
            pltpu.SemaphoreType.DMA((2 * groups,)),
            pltpu.SemaphoreType.DMA((2 * groups,)),
            pltpu.SemaphoreType.DMA((groups,)),
            pltpu.SemaphoreType.DMA((groups,)),
        ]
        + Spread.scratch(groups, spots)
        + Spread.scratch(groups, spots)
        + Collect.scratch(2 * groups, 1, spots, capacity, width, 4),
        compiler_params=pltpu.CompilerParams(
            collective_id=collective, has_side_effects=True, vmem_limit_bytes=60 * MIB
        ),
        cost_estimate=lasting(180),
    )(source[None], source_grads[None], gates, gate_w, up_w, down_w)


class Exchange:
    @staticmethod
    def scratch(pieces, parts, rows, lanes):
        wide = (rows + 127) // 128 * 128
        return [
            pltpu.VMEM((pieces, lanes, wide), jnp.float32),
            pltpu.VMEM((pieces, parts - 1, lanes, wide), jnp.float32),
            pltpu.SemaphoreType.DMA((pieces, parts - 1)),
            pltpu.SemaphoreType.DMA((pieces, parts - 1)),
        ]

    def __init__(self, place, refs):
        self.place = place
        self.own, self.got, self.sent, self.landed = refs

    def copy(self, piece, step):
        return remote(
            self.own.at[piece],
            self.got.at[piece, step - 1],
            self.sent.at[piece, step - 1],
            self.landed.at[piece, step - 1],
            self.place.device(self.place.expert, self.place.along(step)),
        )

    def start(self, piece, values):
        _, lanes, wide = self.own.shape
        rows = values.shape[0]
        if rows < wide:
            blank = jnp.zeros((wide - rows, 128), jnp.float32)
            values = jnp.concatenate([values, blank], axis=0)
        self.own[piece] = values.T[:lanes]
        for step in range(1, self.place.parts):
            self.copy(piece, step).start()

    def total(self, piece, rows):
        _, lanes, wide = self.own.shape
        total = self.own[piece]
        for step in range(1, self.place.parts):
            self.copy(piece, step).wait_recv()
            total = total + self.got[piece, step - 1]
        blank = jnp.zeros((128 - lanes, wide), jnp.float32)
        return jnp.concatenate([total, blank], axis=0).T[:rows]

    def finish(self, piece):
        for step in range(1, self.place.parts):
            self.copy(piece, step).wait_send()


def closing_kernel(jobs, *refs):
    (
        normed_t, gain, marks, small_in, query_grad, key_grad, value_grad, gated_t, hidden_grads,
        hidden_hbm, scaled_hbm, routed_hbm, query_hbm, key_hbm, value_hbm,
    ), refs = refs[:15], refs[15:]
    grads = (query_grad, key_grad, value_grad)
    count = len(grads)
    lefts, rights, refs = refs[:3], refs[3:6], refs[6:]
    summed, back, small_out, products, refs = refs[:4], refs[4], refs[5], refs[6:9], refs[9:]
    (
        hold, hold_out, partial, ready, gathered, small_own, small_got, small_sum,
        hidden, scaled, routed, w_query, w_key, w_value, right, left, product,
        ring_send, ring_land, back_send, back_land,
        small_send, small_land, last_send, last_land, own_sem, load_sem, job_sem,
    ) = refs[:28]
    weights = (w_query, w_key, w_value)
    place = Place()
    exchange = Exchange(place, refs[28:32])
    collect = Collect(place, refs[32:])
    groups, parts = place.groups, place.parts
    pieces, rows = collect.core_in.shape[0], collect.core_in.shape[3]
    width = hidden.shape[1]
    block = hold.shape[3]
    bucket = back.shape[1]
    each = rows // bucket
    loads = [
        pltpu.make_async_copy(held, kept, load_sem.at[number])
        for number, (held, kept) in enumerate(
            (
                (query_hbm, w_query), (key_hbm, w_key), (value_hbm, w_value),
                (hidden_hbm, hidden), (scaled_hbm, scaled), (routed_hbm, routed),
            )
        )
    ]
    for load in loads:
        load.start()
    place.meet(True, True)

    parity, half = lax.rem(place.expert, 2), lax.div(place.expert, 2)
    at = half + parity * (groups - 1 - 2 * half)

    def member(spot):
        spot = lax.rem(spot + groups, groups)
        high = lax.div(spot, groups // 2)
        return (1 - high) * 2 * spot + high * (2 * (groups - 1 - spot) + 1)

    ways = ((0, 1), (1, -1))

    def first_row(way, sign, step):
        spot = lax.rem(at - sign * step + 2 * groups, groups)
        return pl.multiple_of((way * groups + spot) * block, block)

    def ring_copy(step, way, sign, number, source, target):
        return remote(
            source,
            target,
            ring_send.at[step, way, number],
            ring_land.at[step, way, number],
            place.device(member(at + sign), place.tensor),
        )

    out_rows, out_columns = hold_out.shape[2:]

    def first_column(sign, step):
        spot = lax.rem(at - sign * step + 2 * groups, groups)
        return pl.multiple_of(spot * out_columns, 128)

    def slot(step, way, number):
        if number == count:
            return hold_out.at[step, way]
        return hold.at[step, way, number]

    def spot_out(step, way, sign, number):
        if number == count:
            return summed[number].at[
                pl.ds(way * out_rows, out_rows), pl.ds(first_column(sign, step), out_columns)
            ]
        return summed[number].at[pl.ds(first_row(way, sign, step), block)]

    def own_part(step, way, sign, number):
        if number == count:
            return jnp.dot(
                gated_t[way * out_rows : (way + 1) * out_rows, :],
                hidden_grads[:, pl.ds(first_column(sign, step), out_columns)],
                preferred_element_type=jnp.float32,
            )
        return jnp.dot(
            normed_t[pl.ds(first_row(way, sign, step), block), :],
            grads[number][...],
            preferred_element_type=jnp.float32,
        )

    def ring(step):
        for number in range(count + 1):
            for way, sign in ways:

                @pl.when((step >= 1) & (step < groups))
                def _():
                    held = slot(step, way, number)
                    ring_copy(step - 1, way, sign, number, held, held).wait_recv()

                @pl.when(step >= groups)
                def _():
                    held = spot_out(step, way, sign, number)
                    ring_copy(step - 1, way, sign, number, held, held).wait_recv()

                @pl.when(step < groups)
                def _():
                    own = own_part(step, way, sign, number)
                    held = slot(step, way, number)

                    @pl.when(step == 0)
                    def _():
                        held[...] = own.astype(jnp.bfloat16)

                    @pl.when(step > 0)
                    def _():
                        held[...] = (own + held[...].astype(jnp.float32)).astype(jnp.bfloat16)

                @pl.when(step < groups - 1)
                def _():
                    ring_copy(
                        step, way, sign, number, slot(step, way, number), slot(step + 1, way, number)
                    ).start()

                @pl.when(step == groups - 1)
                def _():
                    held, there = slot(step, way, number), spot_out(step, way, sign, number)
                    ring_copy(step, way, sign, number, held, there).start()
                    pltpu.make_async_copy(held, there, own_sem.at[way, number]).start()

                @pl.when((step >= groups) & (step < 2 * groups - 2))
                def _():
                    held = spot_out(step, way, sign, number)
                    ring_copy(step, way, sign, number, held, held).start()

    def ring_finish(step, carry):
        for number in range(count + 1):
            for way, sign in ways:
                held = slot(0, way, number)
                ring_copy(step, way, sign, number, held, held).wait_send()
        return carry

    def band(piece):
        return pl.ds(pl.multiple_of(piece * rows, rows), rows)

    def project(piece):
        collect.free_stage(piece)
        side = lax.rem(piece, 2)
        for spot in range(place.spots):
            for core in range(2):
                first = (spot * 2 + core) * width
                part = None
                for grad, weight in zip(grads, weights):
                    term = dot_nt(grad[band(piece), :], weight[first : first + width, :])
                    part = term if part is None else part + term
                collect.stage[side, 0, spot, core] = part.astype(jnp.bfloat16)
        collect.first(piece)

    def measure(piece):
        total = collect.third(piece)[0]
        partial[piece] = total
        inner = jnp.sum(total * scaled[band(piece), :] * gain[...], axis=1, keepdims=True)
        exchange.start(piece, jnp.broadcast_to(inner, (rows, 128)))

    def back_copy(target, piece, number):
        return remote(
            ready.at[piece, pl.ds(number * bucket, bucket)],
            back.at[place.expert],
            back_send.at[target],
            back_land.at[place.expert],
            place.device(target, place.tensor),
        )

    def conclude(piece):
        inner = exchange.total(piece, rows)
        mean = (inner[:, :1] + marks[band(piece), 1:2]) / (width * parts)
        grad = partial[piece] + routed[band(piece), :]
        part = scaled[band(piece), :]
        gathered[...] += jnp.sum(grad * part, axis=0, keepdims=True)
        result = hidden[band(piece), :] + marks[band(piece), 0:1] * (grad * gain[...] - part * mean)
        ready[piece] = result.astype(jnp.bfloat16)
        for number in range(each):
            target = piece * each + number

            @pl.when(target != place.expert)
            def _():
                back_copy(target, piece, number).start()

            @pl.when(target == place.expert)
            def _():
                own = pltpu.make_async_copy(
                    ready.at[piece, pl.ds(number * bucket, bucket)],
                    back.at[place.expert],
                    own_sem.at[0, count + 1],
                )
                own.start()
                own.wait()

    def small_copy(step):
        return remote(
            small_own,
            small_got.at[step - 1],
            small_send.at[step - 1],
            small_land.at[step - 1],
            place.device(flip(place.expert, step, groups), place.tensor),
        )

    def last_copy(step, origin):
        return remote(
            small_sum,
            small_out.at[origin],
            last_send.at[step - 1],
            last_land.at[step - 1],
            place.device(place.expert, place.along(step)),
        )

    own_small = pltpu.make_async_copy(small_sum, small_out.at[place.tensor], own_sem.at[1, count + 1])

    def small_first():
        small_own[...] = small_in[...]
        small_own[0:1, :] = gathered[...]
        for step in range(1, groups):
            small_copy(step).start()

    def small_second():
        total = small_own[...]
        for step in range(1, groups):
            small_copy(step).wait_recv()
            total = total + small_got[step - 1]
        small_sum[...] = total
        own_small.start()
        for step in range(1, parts):
            last_copy(step, place.tensor).start()

    gathered[...] = jnp.zeros_like(gathered)
    turns = max(2 * groups - 1, pieces + 5)
    tiles = sum(job[0] for job in jobs)
    each_turn = -(-tiles // turns)

    def job_of(number, first, action):
        start = 0
        for index, (many, size, wide) in enumerate(jobs):
            when(
                (number >= start) & (number < start + many),
                functools.partial(action, index, size, wide),
                number - start,
            )
            start += many

    def right_copy(index, wide):
        return pltpu.make_async_copy(rights[index], right.at[:, pl.ds(0, wide)], job_sem.at[4])

    def left_copy(index, size, tile, side):
        first = pl.multiple_of(tile * size, 128)
        return pltpu.make_async_copy(
            lefts[index].at[:, pl.ds(first, size)],
            left.at[side, :, pl.ds(0, size)],
            job_sem.at[side],
        )

    def product_copy(index, size, wide, tile, side):
        first = pl.multiple_of(tile * size, 8)
        return pltpu.make_async_copy(
            product.at[side, pl.ds(0, size), pl.ds(0, wide)],
            products[index].at[pl.ds(first, size)],
            job_sem.at[2 + side],
        )

    def multiply(number):
        side = lax.rem(number, 2)

        def fetch_next(index, size, wide, tile):
            left_copy(index, size, tile, 1 - side).start()

        def stored(index, size, wide, tile):
            product_copy(index, size, wide, tile, side).wait()

        def work(index, size, wide, tile):
            @pl.when(tile == 0)
            def _():
                right_copy(index, wide).start()
                right_copy(index, wide).wait()

            left_copy(index, size, tile, side).wait()
            value = dot_tn(left[side, :, :size], right[:, :wide])
            product[side, :size, :wide] = value
            product_copy(index, size, wide, tile, side).start()

        job_of(number + 1, None, fetch_next)
        job_of(number - 2, None, stored)
        job_of(number, None, work)

    left_copy(0, jobs[0][1], 0, 0).start()

    def turn_step(turn, carry):
        when(turn < 2 * groups - 1, ring, turn)

        @pl.when(turn == 0)
        def _():
            for load in loads:
                load.wait()

        when((turn >= 3) & (turn < pieces + 3), conclude, turn - 3)
        when((turn >= 2) & (turn < pieces + 2), measure, turn - 2)
        when((turn >= 1) & (turn < pieces + 1), collect.second, turn - 1)
        when(turn < pieces, project, turn)
        when(turn == pieces + 3, small_first)
        when(turn == pieces + 4, small_second)
        lax.fori_loop(
            turn * each_turn,
            jnp.minimum((turn + 1) * each_turn, tiles),
            lambda number, held: (multiply(number), held)[1],
            0,
        )
        return carry

    lax.fori_loop(0, turns, turn_step, 0)
    for number in (tiles - 2, tiles - 1):
        index, tile = 0, number
        while tile >= jobs[index][0]:
            tile -= jobs[index][0]
            index += 1
        product_copy(index, jobs[index][1], jobs[index][2], tile, number % 2).wait()
    lax.fori_loop(0, 2 * groups - 2, ring_finish, 0)
    for number in range(count + 1):
        for way, sign in ways:
            pltpu.make_async_copy(
                slot(groups - 1, way, number),
                spot_out(groups - 1, way, sign, number),
                own_sem.at[way, number],
            ).wait()
    collect.finish()
    for step in range(1, groups):
        small_copy(step).wait_send()
    own_small.wait()
    for step in range(1, parts):
        origin = lax.rem(place.tensor + parts - step, parts)
        last_copy(step, place.tensor).wait_send()
        last_copy(step, origin).wait_recv()

    def settle(piece, carry):
        exchange.finish(piece)
        for number in range(each):
            target = piece * each + number

            @pl.when(target != place.expert)
            def _():
                back_copy(target, piece, number).wait_send()
                remote(
                    ready.at[piece, pl.ds(number * bucket, bucket)],
                    back.at[target],
                    back_send.at[target],
                    back_land.at[target],
                    place.device(target, place.tensor),
                ).wait_recv()

        return carry

    lax.fori_loop(0, pieces, settle, 0)


def closing(
    normed_t, gain, marks, small, grads, gated_t, hidden_grads, hidden, scaled, routed, weights,
    lefts, rights, pieces, collective,
):
    groups, parts = lax.axis_size("expert"), lax.axis_size("tensor")
    spots = parts // 2
    model_width, tokens = normed_t.shape
    columns = grads[0].shape[1]
    width = hidden.shape[1]
    count = len(grads)
    rows = tokens // pieces
    block = model_width // (2 * groups)
    low, full = jnp.bfloat16, jnp.float32
    inside = pl.BlockSpec(memory_space=pltpu.VMEM)
    anywhere = pl.BlockSpec(memory_space=pl.ANY)
    dma = pltpu.SemaphoreType.DMA
    jobs = []
    for left, right in zip(lefts, rights):
        jobs.append((left.shape[1] // 128, 128, right.shape[1]))
    depth = lefts[0].shape[0]
    tile = max(job[1] for job in jobs)
    wide = max(job[2] for job in jobs)
    return pl.pallas_call(
        functools.partial(closing_kernel, tuple(jobs)),
        out_shape=(
            *(jax.ShapeDtypeStruct((model_width, columns), low) for _ in range(count)),
            jax.ShapeDtypeStruct((columns, model_width), low),
            jax.ShapeDtypeStruct((groups, tokens // groups, width), low),
            jax.ShapeDtypeStruct((parts,) + small.shape, full),
            *(
                jax.ShapeDtypeStruct((left.shape[1], right.shape[1]), full)
                for left, right in zip(lefts, rights)
            ),
        ),
        in_specs=[inside] * 9 + [anywhere] * 12,
        out_specs=(anywhere,) * 9,
        scratch_shapes=[
            pltpu.VMEM((groups, 2, count, block, columns), low),
            pltpu.VMEM((groups, 2, columns // 2, model_width // groups), low),
            pltpu.VMEM((pieces, rows, width), full),
            pltpu.VMEM((pieces, rows, width), low),
            pltpu.VMEM((1, width), full),
            pltpu.VMEM(small.shape, full),
            pltpu.VMEM((groups - 1,) + small.shape, full),
            pltpu.VMEM(small.shape, full),
            pltpu.VMEM((tokens, width), full),
            pltpu.VMEM((tokens, width), full),
            pltpu.VMEM((tokens, width), full),
            *(pltpu.VMEM(weight.shape, low) for weight in weights),
            pltpu.VMEM((depth, wide), low),
            pltpu.VMEM((2, depth, tile), low),
            pltpu.VMEM((2, tile, wide), full),
            dma((2 * groups - 2, 2, count + 1)),
            dma((2 * groups - 2, 2, count + 1)),
            dma((groups,)),
            dma((groups,)),
            dma((groups - 1,)),
            dma((groups - 1,)),
            dma((parts - 1,)),
            dma((parts - 1,)),
            dma((2, count + 2)),
            dma((6,)),
            dma((5,)),
        ]
        + Exchange.scratch(pieces, parts, rows, 8)
        + Collect.scratch(pieces, 1, spots, rows, width),
        compiler_params=pltpu.CompilerParams(
            collective_id=collective, has_side_effects=True, vmem_limit_bytes=60 * MIB
        ),
        cost_estimate=lasting(200),
    )(
        normed_t, gain, marks, small, *grads, gated_t, hidden_grads, hidden, scaled, routed, *weights,
        *lefts, *rights,
    )


def precise_dot(left, right):
    return jnp.dot(
        left, right, precision=lax.Precision.HIGHEST, preferred_element_type=jnp.float32
    )


def settle_kernel(
    came, picks, gates, logits, factor, hidden, grads, gain, router_t,
    mixed, hidden_grad, gathered, router_grad, gain_grad,
    row_grads, ready, *refs,
):
    place = Place()
    exchange = Exchange(place, refs[:4])
    pieces, rows, width = row_grads.shape
    spread = Spread(place, ready, gathered, refs[4:], False)
    slots, experts_of = came.shape[1], logits.shape[1]
    low = jnp.bfloat16
    place.meet(False, True)
    router_grad[...] = jnp.zeros_like(router_grad)
    gain_grad[...] = jnp.zeros_like(gain_grad)

    def band(piece):
        return pl.ds(pl.multiple_of(piece * rows, rows), rows)

    def scaled_of(piece):
        return hidden[band(piece), :] * factor[band(piece), :]

    def gather(piece):
        here = band(piece)
        numbers = lax.broadcasted_iota(jnp.int32, (rows, slots), 1)
        chosen = [(picks[here, way : way + 1] == numbers).astype(low) for way in range(2)]
        result = hidden[here, :]
        grad = grads[here, :].astype(jnp.float32)
        lane = lax.broadcasted_iota(jnp.int32, (rows, 128), 1)
        stats = jnp.zeros((rows, 128), jnp.float32)
        for way in range(2):
            value = jnp.dot(chosen[way], came[0], preferred_element_type=jnp.float32)
            result = result + gates[here, way : way + 1] * value
            stats = jnp.where(lane == way, jnp.sum(value * grad, axis=1, keepdims=True), stats)
        mixed[here, :] = result.astype(low)
        total = jnp.dot(chosen[0] + chosen[1], came[1], preferred_element_type=jnp.float32)
        row_grads[piece] = total
        inner = jnp.sum(total * scaled_of(piece) * gain[...], axis=1, keepdims=True)
        exchange.start(piece, jnp.where(lane == 2, inner, stats))

    def settle(piece):
        here = band(piece)
        stats = exchange.total(piece, rows)
        gate = [gates[here, way : way + 1] for way in range(2)]
        shared = gate[0] * stats[:, :1] + gate[1] * stats[:, 1:2]
        names = lax.broadcasted_iota(jnp.int32, (rows, experts_of), 1)
        logit_grad = jnp.zeros((rows, experts_of), jnp.float32)
        for way in range(2):
            term = gate[way] * (stats[:, way : way + 1] - shared)
            logit_grad = logit_grad + jnp.where(picks[here, 2 + way : 3 + way] == names, term, 0.0)
        mean = (
            stats[:, 2:3] + jnp.sum(logit_grad * logits[here, :], axis=1, keepdims=True)
        ) / (width * place.parts)
        scaled = scaled_of(piece)
        grad = row_grads[piece] + precise_dot(logit_grad, router_t[...])
        gain_grad[...] += jnp.sum(grad * scaled, axis=0, keepdims=True)
        router_grad[...] += lax.dot_general(
            logit_grad,
            scaled * gain[...],
            (((0,), (0,)), ((), ())),
            precision=lax.Precision.HIGHEST,
            preferred_element_type=jnp.float32,
        )
        result = grads[here, :].astype(jnp.float32) + factor[here, :] * (
            grad * gain[...] - scaled * mean
        )
        hidden_grad[here, :] = result
        ready[0, piece] = result.astype(low)
        spread.first(piece)

    def step(turn, carry):
        when(turn < pieces, gather, turn)
        when((turn >= 2) & (turn <= pieces + 1), settle, turn - 2)
        when(turn >= 3, spread.second, turn - 3)
        return carry

    lax.fori_loop(0, pieces + 3, step, 0)

    def last(piece, carry):
        spread.third(piece)
        spread.finish(piece)
        exchange.finish(piece)
        return carry

    lax.fori_loop(0, pieces, last, 0)


def settle(came, picks, gates, logits, factor, hidden, grads, gain, router_t, pieces, collective):
    parts = lax.axis_size("tensor")
    tokens, width = hidden.shape
    rows = tokens // pieces
    low, full = jnp.bfloat16, jnp.float32
    inside = pl.BlockSpec(memory_space=pltpu.VMEM)
    return pl.pallas_call(
        settle_kernel,
        out_shape=(
            jax.ShapeDtypeStruct((tokens, width), low),
            jax.ShapeDtypeStruct((tokens, width), full),
            jax.ShapeDtypeStruct((1, pieces, rows, width * parts), low),
            jax.ShapeDtypeStruct(router_t.shape, full),
            jax.ShapeDtypeStruct((1, width), full),
        ),
        in_specs=[inside] * 9,
        out_specs=(inside, inside, pl.BlockSpec(memory_space=pl.ANY), inside, inside),
        scratch_shapes=[
            pltpu.VMEM((pieces, rows, width), full),
            pltpu.VMEM((1, pieces, rows, width), low),
        ]
        + Exchange.scratch(pieces, parts, rows, 8)
        + Spread.scratch(pieces, parts // 2),
        compiler_params=pltpu.CompilerParams(
            collective_id=collective, has_side_effects=True, vmem_limit_bytes=48 * MIB
        ),
        cost_estimate=lasting(30),
    )(came, picks, gates, logits, factor, hidden, grads, gain, router_t)


def dot_tn(left, right):
    return lax.dot_general(
        left, right, (((0,), (0,)), ((), ())), preferred_element_type=jnp.float32
    )


def bands(tokens):
    size = 256 if tokens % 256 == 0 else tokens
    return [(first, size) for first in range(0, tokens, size)]


def masked_scores(query, keys, segment_column, segment_row, first, size, column):
    last = first + size
    rows = slice(first, last)
    scores = dot_nt(query[rows, column], keys[:last, column]) * (1.0 / math.sqrt(HEAD))
    place = lax.broadcasted_iota(jnp.int32, (size, last), 0) + first
    other = lax.broadcasted_iota(jnp.int32, (size, last), 1)
    allowed = (segment_column[rows, :] == segment_row[:, :last]) & (place >= other)
    return jnp.where(allowed, scores, MASKED)


def attend_kernel(
    resid, gain, router, w_query, w_key, w_value, cosine, sine, segment_column, segment_row,
    normed, normed_t, factor, logits, query, keys, values, heads, log_total,
):
    tokens, columns = query.shape
    low = jnp.bfloat16
    for first, size in bands(tokens):
        rows = slice(first, first + size)
        value = resid[rows, :].astype(jnp.float32)
        scale = lax.rsqrt(jnp.mean(value * value, axis=1, keepdims=True) + EPSILON)
        value = value * scale * gain[...]
        high = value.astype(low)
        rest = (value - high.astype(jnp.float32)).astype(low)
        factor[rows, :] = scale
        normed[rows, :] = high
        normed_t[:, rows] = high.T
        logits[rows, :] = jnp.dot(
            high, router[...], preferred_element_type=jnp.float32
        ) + jnp.dot(rest, router[...], preferred_element_type=jnp.float32)
        values[rows, :] = jnp.dot(
            high, w_value[...], preferred_element_type=jnp.float32
        ).astype(low)
        for weight, out in ((w_query, query), (w_key, keys)):
            flat = jnp.dot(high, weight[...], preferred_element_type=jnp.float32)
            for head in range(columns // HEAD):
                column = slice(head * HEAD, (head + 1) * HEAD)
                part = flat[:, column]
                turned = pltpu.roll(part, HEAD // 2, 1)
                out[rows, column] = (part * cosine[rows, :] + turned * sine[rows, :]).astype(low)
    for head in range(columns // HEAD):
        column = slice(head * HEAD, (head + 1) * HEAD)
        for first, size in bands(tokens):
            last = first + size
            rows = slice(first, last)
            scores = masked_scores(query, keys, segment_column, segment_row, first, size, column)
            top = jnp.max(scores, axis=1, keepdims=True)
            expo = jnp.exp(scores - top)
            total = jnp.sum(expo, axis=1, keepdims=True)
            probs = (expo / total).astype(low)
            heads[rows, column] = jnp.dot(
                probs, values[:last, column], preferred_element_type=jnp.float32
            ).astype(low)
            log_total[rows, head : head + 1] = top + jnp.log(total)


def attend(resid, gain, router, weights, cosine, sine, segment):
    tokens, model_width = resid.shape
    columns = weights[0].shape[1]
    low, full = jnp.bfloat16, jnp.float32
    block = jax.ShapeDtypeStruct((tokens, columns), low)
    inside = pl.BlockSpec(memory_space=pltpu.VMEM)
    return pl.pallas_call(
        attend_kernel,
        out_shape=(
            jax.ShapeDtypeStruct((tokens, model_width), low),
            jax.ShapeDtypeStruct((model_width, tokens), low),
            jax.ShapeDtypeStruct((tokens, 1), full),
            jax.ShapeDtypeStruct((tokens, router.shape[1]), full),
            block,
            block,
            block,
            block,
            jax.ShapeDtypeStruct((tokens, columns // HEAD), full),
        ),
        in_specs=[inside] * 10,
        out_specs=(inside,) * 9,
        compiler_params=pltpu.CompilerParams(vmem_limit_bytes=56 * MIB),
        cost_estimate=lasting(20),
    )(resid, gain, router, *weights, cosine, sine, segment[:, None], segment[None, :])


def attend_back_kernel(
    grads, w_out, gates, heads, query, keys, values, log_total, cosine, sine,
    segment_column, segment_row,
    query_grad, key_grad, value_grad, gate_grad, gated_t,
    heads_grad, key_sum, value_sum,
):
    tokens, columns = query.shape
    low = jnp.bfloat16
    span = columns // gates.shape[1]
    scale = 1.0 / math.sqrt(HEAD)
    for first, size in bands(tokens):
        rows = slice(first, first + size)
        plain = dot_nt(grads[rows, :], w_out[...])
        for expert in range(gates.shape[1]):
            column = slice(expert * span, (expert + 1) * span)
            gate = gates[rows, expert : expert + 1]
            head = heads[rows, column].astype(jnp.float32)
            gate_grad[rows, expert : expert + 1] = jnp.sum(
                plain[:, column] * head, axis=1, keepdims=True
            )
            heads_grad[rows, column] = (plain[:, column] * gate).astype(low)
            gated_t[column, rows] = (head * gate).T.astype(low)

    def unturn(value, rows):
        turned = pltpu.roll(value * sine[rows, :], HEAD // 2, 1)
        return value * cosine[rows, :] + turned

    for head in range(columns // HEAD):
        column = slice(head * HEAD, (head + 1) * HEAD)
        for first, size in bands(tokens):
            last = first + size
            rows = slice(first, last)
            scores = masked_scores(query, keys, segment_column, segment_row, first, size, column)
            probs = jnp.exp(scores - log_total[rows, head : head + 1])
            value_part = dot_tn(probs.astype(low), heads_grad[rows, column])
            prob_grad = dot_nt(heads_grad[rows, column], values[:last, column])
            score_grad = (
                probs * (prob_grad - jnp.sum(probs * prob_grad, axis=1, keepdims=True))
            ).astype(low)
            query_grad[rows, column] = unturn(
                jnp.dot(score_grad, keys[:last, column], preferred_element_type=jnp.float32)
                * scale,
                rows,
            ).astype(low)
            key_part = dot_tn(score_grad, query[rows, column])
            if first:
                value_sum[:first, :] += value_part[:first]
                key_sum[:first, :] += key_part[:first]
            value_sum[rows, :] = value_part[first:]
            key_sum[rows, :] = key_part[first:]
        whole = slice(0, tokens)
        key_grad[:, column] = unturn(key_sum[...] * scale, whole).astype(low)
        value_grad[:, column] = value_sum[...].astype(low)


def attend_back(grads, w_out, gates, heads, query, keys, values, log_total, cosine, sine, segment):
    tokens, model_width = grads.shape
    columns = query.shape[1]
    low, full = jnp.bfloat16, jnp.float32
    block = jax.ShapeDtypeStruct((tokens, columns), low)
    inside = pl.BlockSpec(memory_space=pltpu.VMEM)
    return pl.pallas_call(
        attend_back_kernel,
        out_shape=(
            block,
            block,
            block,
            jax.ShapeDtypeStruct(gates.shape, full),
            jax.ShapeDtypeStruct((columns, tokens), low),
        ),
        in_specs=[inside] * 12,
        out_specs=(inside,) * 5,
        scratch_shapes=[
            pltpu.VMEM((tokens, columns), low),
            pltpu.VMEM((tokens, HEAD), full),
            pltpu.VMEM((tokens, HEAD), full),
        ],
        compiler_params=pltpu.CompilerParams(vmem_limit_bytes=56 * MIB),
        cost_estimate=lasting(25),
    )(
        grads, w_out, gates, heads, query, keys, values, log_total, cosine, sine,
        segment[:, None], segment[None, :],
    )


def to_expert(rows, group_count):
    count, width = rows.shape
    return lax.all_to_all(
        rows.reshape(group_count, count // group_count, width),
        "expert",
        split_axis=0,
        concat_axis=0,
        tiled=True,
    ).reshape(count, width)


def gather_tensor(rows):
    return lax.all_gather(rows, "tensor", axis=0)


def body(
    tokens,
    out_grad,
    attn_gain,
    attn_router,
    w_query,
    w_key,
    w_value,
    w_out,
    mlp_gain,
    mlp_router,
    w_gate,
    w_up,
    w_down,
    deal,
    seq_lengths,
    attn_routes,
    mlp_routes,
    slot_order,
):
    tok_rows, model_width = tokens.shape
    group_count = lax.axis_size("expert")
    part_count = lax.axis_size("tensor")
    group_index = lax.axis_index("expert")
    part_index = lax.axis_index("tensor")
    bucket_rows = tok_rows // group_count
    col_width = model_width // part_count
    col_first = part_index * col_width
    low = jnp.bfloat16

    def own_cols(values):
        return lax.dynamic_slice_in_dim(values, col_first, col_width, values.ndim - 1)

    deal_rank = deal // tok_rows * bucket_rows + (deal % tok_rows - group_index * bucket_rows)
    row_ids = jnp.arange(tok_rows, dtype=jnp.int32)
    deal_mask = (row_ids[:, None] == deal_rank[None, :]).astype(low)
    dealt = jnp.dot(deal_mask, own_cols(tokens), preferred_element_type=jnp.float32).astype(low)
    resid_low = spread_rows(dealt.reshape(group_count, bucket_rows, col_width), True, 0, 30)
    dealt_grads = jnp.dot(
        deal_mask, own_cols(out_grad), preferred_element_type=jnp.float32
    ).astype(low)
    dealt_grads, resid_low = lax.optimization_barrier((dealt_grads, resid_low))
    grad_cols_low = to_expert(dealt_grads, group_count)
    gain_one, gain_two = own_cols(attn_gain), own_cols(mlp_gain)
    router_one = lax.dynamic_slice_in_dim(attn_router, col_first, col_width, 0)
    router_two = lax.dynamic_slice_in_dim(mlp_router, col_first, col_width, 0)
    expert_count = mlp_router.shape[1]
    sharers = group_count // expert_count
    capacity = 5 * tok_rows // (2 * expert_count)
    target, position, kept = slot_table(mlp_routes, slot_order[0], capacity)
    slots = expert_count * capacity
    destination = jnp.where(kept, target * capacity + position, slots).reshape(tok_rows, 2)
    slot_ids = jnp.arange(slots, dtype=jnp.int32)
    chosen = [destination[:, way] for way in range(2)]
    to_slot = (
        (slot_ids[:, None] == chosen[0][None, :]) | (slot_ids[:, None] == chosen[1][None, :])
    ).astype(low)
    resid_cols = own_cols(resid_low).astype(jnp.float32)
    segment, cosine, sine = rotary_tables(seq_lengths[0], tok_rows)
    sign = jnp.where(jnp.arange(HEAD) < HEAD // 2, -1.0, 1.0)
    local_heads = w_query.shape[1] // HEAD
    local_experts = local_heads // QH
    span = QH * HEAD
    experts_of = attn_router.shape[1]
    router_high = lax.reduce_precision(attn_router, 8, 7)
    router_parts = jnp.concatenate([router_high, attn_router - router_high], axis=1).astype(low)
    router_parts = jnp.pad(router_parts, ((0, 0), (0, -router_parts.shape[1] % 128)))
    normed_low, normed_t, factor_one, logit_parts, query, keys, values, heads_low, log_total = (
        attend(
            resid_low,
            attn_gain[None],
            router_parts,
            (w_query, w_key, w_value),
            cosine,
            sine * sign,
            segment,
        )
    )
    attn_logits = logit_parts[:, :experts_of] + logit_parts[:, experts_of : 2 * experts_of]
    attn_gates, attn_mask = pair_gates(attn_logits, attn_routes)
    gate_table = jnp.sum(attn_gates[:, :, None] * attn_mask, axis=1)
    gate_local = lax.dynamic_slice_in_dim(gate_table, part_index * local_experts, local_experts, 1)
    grad_cols_low, heads_low = lax.optimization_barrier((grad_cols_low, heads_low))
    slot_grads = jnp.dot(to_slot, grad_cols_low, preferred_element_type=jnp.float32).astype(low)
    slot_grads = jnp.repeat(slot_grads.reshape(expert_count, capacity, col_width), sharers, axis=0)
    slot_grads = to_expert(slot_grads.reshape(group_count * capacity, col_width), group_count)
    pieces, piece_rows = 4, tok_rows // 4
    attn_cols = collect_rows(
        functools.partial(make_attended, span),
        (
            heads_low.reshape(pieces, piece_rows, local_heads * HEAD),
            gate_local.reshape(pieces, piece_rows, local_experts),
            w_out,
        ),
        pieces,
        piece_rows,
        col_width,
        1,
    )
    hidden = resid_cols + attn_cols
    weighed = hidden * gain_two
    stats = jnp.concatenate(
        [
            jnp.sum(hidden * hidden, axis=1)[None, :],
            jnp.dot(weighed, router_two, precision=PRECISE).T,
        ],
        axis=0,
    )
    stats = jnp.sum(gather_tensor(stats), axis=0)
    factor_two = lax.rsqrt(stats[0] / model_width + EPSILON)[:, None]
    mlp_logits = stats[1:].T * factor_two
    scaled_two = hidden * factor_two
    normed_two = scaled_two * gain_two
    mlp_gates, _ = pair_gates(mlp_logits, mlp_routes)
    slot_rows = jnp.dot(
        to_slot, normed_two.astype(low), preferred_element_type=jnp.float32
    ).astype(low)
    slot_gates = sum(
        jnp.sum(
            jnp.where(slot_ids[:, None] == chosen[way][None, :], mlp_gates[:, way][None, :], 0.0),
            axis=1,
        )
        for way in range(2)
    )
    gate_lines = jnp.pad(slot_gates.reshape(expert_count, capacity), ((0, 0), (0, -capacity % 128)))
    gate_lines = jnp.broadcast_to(gate_lines[:, None, :], (expert_count, 8, gate_lines.shape[1]))
    inbox, _, slot_grads, middle, gate_grad, up_grad, returned = experts(
        slot_rows.reshape(expert_count, capacity, col_width),
        slot_grads.reshape(group_count, capacity, col_width),
        gate_lines,
        w_gate[0],
        w_up[0],
        w_down[0],
        sharers,
        2,
    )
    if sharers > 1:
        returned = (
            jnp.sum(
                returned.reshape(2, expert_count, sharers, capacity, col_width).astype(jnp.float32),
                axis=2,
            )
        ).astype(low)
    mixed_cols, hidden_grad, hidden_grad_low, mlp_router_grad, mlp_gain_grad = settle(
        returned.reshape(2, slots, col_width),
        jnp.concatenate([destination, mlp_routes], axis=1),
        mlp_gates,
        mlp_logits,
        factor_two,
        hidden,
        grad_cols_low,
        gain_two[None],
        router_two.T,
        pieces,
        4,
    )
    back_mixed = to_expert(mixed_cols, group_count)
    hidden_grad_low = hidden_grad_low.reshape(tok_rows, model_width)
    query_pre_grad, key_pre_grad, value_pre_grad, local_gate_grad, gated_t = attend_back(
        hidden_grad_low,
        w_out,
        gate_local,
        heads_low,
        query,
        keys,
        values,
        log_total,
        cosine,
        sine * sign,
        segment,
    )
    gate_grads = gather_tensor(local_gate_grad.T)
    gate_grads = gate_grads.reshape(part_count * local_experts, tok_rows).T
    attn_pair_grad = jnp.sum(attn_mask * gate_grads[:, None, :], axis=2)
    attn_logit_grad = pair_back(attn_gates, attn_mask, attn_pair_grad)
    scaled_cols = resid_cols * factor_one
    normed_cols = scaled_cols * gain_one
    attn_router_grad = jnp.dot(normed_cols.T, attn_logit_grad, precision=PRECISE)
    small = jnp.concatenate(
        [
            jnp.zeros((1, col_width), jnp.float32),
            attn_router_grad.T,
            mlp_gain_grad,
            mlp_router_grad,
        ],
        axis=0,
    )
    small = jnp.pad(small, ((0, -small.shape[0] % 8), (0, 0)))
    marks = jnp.stack(
        [factor_one[:, 0], jnp.sum(attn_logit_grad * attn_logits, axis=1)], axis=1
    )
    rows = inbox.reshape(-1, model_width)
    units = middle.shape[2]
    middle, gate_grad, up_grad = (
        jnp.pad(values.reshape(-1, units), ((0, 0), (0, -units % 128)))
        for values in (middle, gate_grad, up_grad)
    )
    *weight_grads, back_grad, small, gate_w_grad, up_w_grad, down_grad = closing(
        normed_t,
        gain_one[None],
        jnp.pad(marks, ((0, 0), (0, 126))),
        small,
        (query_pre_grad, key_pre_grad, value_pre_grad),
        gated_t,
        hidden_grad_low,
        hidden_grad,
        scaled_cols,
        jnp.dot(attn_logit_grad, router_one.T, precision=PRECISE),
        (w_query, w_key, w_value),
        (rows, rows, middle),
        (gate_grad, up_grad, slot_grads.reshape(-1, model_width)),
        pieces,
        3,
    )
    back_grad = back_grad.reshape(tok_rows, col_width)
    weight_grads = [grad.astype(jnp.float32) for grad in weight_grads]
    mixed, tokens_grad = (
        jnp.einsum("ri,rc->ic", deal_mask, back, preferred_element_type=jnp.float32).astype(low)
        for back in (back_mixed, back_grad)
    )
    small = small.transpose(1, 0, 2).reshape(-1, model_width)
    return (
        mixed,
        tokens_grad,
        small[0],
        small[1 : 1 + experts_of].T,
        weight_grads[0],
        weight_grads[1],
        weight_grads[2],
        weight_grads[3],
        small[1 + experts_of],
        small[2 + experts_of : 2 + experts_of + expert_count].T,
        gate_w_grad[None, :, :units],
        up_w_grad[None, :, :units],
        down_grad[None, :units],
    )


def solution(mesh):
    placed = (
        P("expert", None),
        P("expert", None),
        P(),
        P(),
        P(None, "tensor"),
        P(None, "tensor"),
        P(None, "tensor"),
        P("tensor", None),
        P(),
        P(),
        P("expert", None, "tensor"),
        P("expert", None, "tensor"),
        P("expert", "tensor", None),
        P("expert"),
        P("expert", None),
        P("expert", None),
        P("expert", None),
        P("expert", None),
    )
    return jax.shard_map(
        body,
        mesh=mesh,
        in_specs=placed,
        out_specs=(
            P("expert", "tensor"),
            P("expert", "tensor"),
            P(),
            P(),
            P(None, "tensor"),
            P(None, "tensor"),
            P(None, "tensor"),
            P("tensor", None),
            P(),
            P(),
            P("expert", None, "tensor"),
            P("expert", None, "tensor"),
            P("expert", "tensor", None),
        ),
        check_vma=False,
    )
```

```python
import functools
import math

import jax
import jax.numpy as jnp
from jax import lax
from jax.experimental import pallas as pl
from jax.experimental.pallas import tpu as pltpu
from jax.sharding import PartitionSpec as P

HEAD = 128
QH = 2


PRECISE = lax.Precision.HIGH
EPSILON = 1e-06
MASKED = -1e30


def rotary_tables(lengths, tok_rows):
    seq_ends = jnp.cumsum(lengths)
    seq_starts = seq_ends - lengths
    places = jnp.arange(tok_rows, dtype=jnp.int32)
    segment = jnp.sum((places[:, None] >= seq_ends[None, :]).astype(jnp.int32), axis=1)
    matches = segment[:, None] == jnp.arange(lengths.shape[0], dtype=jnp.int32)[None, :]
    seq_first = jnp.sum(jnp.where(matches, seq_starts[None, :], 0), axis=1)
    offsets = (places - seq_first).astype(jnp.float32)
    frequency = jnp.exp(-math.log(10000.0) * jnp.arange(0, HEAD, 2, dtype=jnp.float32) / HEAD)
    angles = offsets[:, None] * frequency[None, :]
    angles = jnp.concatenate([angles, angles], axis=1)
    return (segment, jnp.cos(angles), jnp.sin(angles))


def pair_gates(logits, routes):
    columns = logits.shape[1]
    chosen_mask = (
        routes[:, :, None] == jnp.arange(columns, dtype=jnp.int32)[None, None, :]
    ).astype(jnp.float32)
    picked = jnp.sum(chosen_mask * logits[:, None, :], axis=2)
    return (jax.nn.softmax(picked, axis=1), chosen_mask)


def slot_table(routes, priority, capacity):
    target = routes.reshape(-1)
    ahead = (target[None, :] == target[:, None]) & (priority[None, :] < priority[:, None])
    position = jnp.sum(ahead.astype(jnp.int32), axis=1)
    return (target, position, position < capacity)


MESH = pl.DeviceIdType.MESH
MIB = 1 << 20
AHEAD_DEAL = 2
AHEAD = 2
EARLY = 2


def flip(number, other, count):
    total, bit = 0, 1
    while bit < count:
        total = total + lax.rem(lax.div(number, bit) + lax.div(other, bit), 2) * bit
        bit *= 2
    return total


def dot_nt(left, right):
    return lax.dot_general(
        left, right, (((1,), (1,)), ((), ())), preferred_element_type=jnp.float32
    )


class Place:
    def __init__(self):
        self.groups = lax.axis_size("expert")
        self.parts = lax.axis_size("tensor")
        self.spots = self.parts // 2
        self.expert = lax.axis_index("expert")
        self.tensor = lax.axis_index("tensor")
        self.spot = lax.div(self.tensor, 2)
        self.core = lax.rem(self.tensor, 2)

    def device(self, expert, tensor):
        return {"expert": expert, "tensor": tensor}

    def across(self, step):
        return lax.rem(self.spot + step, self.spots) * 2 + self.core

    def before(self, step):
        return lax.rem(self.spot + self.spots - step, self.spots) * 2 + self.core

    def meet(self, over_expert, whole_tensor=False):
        if whole_tensor:
            peers = [self.device(self.expert, self.along(step)) for step in range(1, self.parts)]
        else:
            peers = [self.device(self.expert, self.spot * 2 + 1 - self.core)]
            for step in range(1, self.spots):
                peers.append(self.device(self.expert, self.across(step)))
        if over_expert:
            for step in range(1, self.groups):
                peers.append(self.device(flip(self.expert, step, self.groups), self.tensor))
        barrier = pltpu.get_barrier_semaphore()
        for peer in peers:
            pl.semaphore_signal(barrier, inc=1, device_id=peer, device_id_type=MESH)
        pl.semaphore_wait(barrier, len(peers))

    def along(self, step):
        return lax.rem(self.tensor + step, self.parts)


def lasting(microseconds):
    return pl.CostEstimate(
        flops=0, bytes_accessed=int(microseconds * 3_000_000), transcendentals=0
    )


def remote(source, target, send, receive, device):
    return pltpu.make_async_remote_copy(
        src_ref=source,
        dst_ref=target,
        send_sem=send,
        recv_sem=receive,
        device_id=device,
        device_id_type=MESH,
    )


class Spread:
    @staticmethod
    def scratch(chunks, spots):
        return [
            pltpu.SemaphoreType.DMA((chunks,)),
            pltpu.SemaphoreType.DMA((chunks,)),
            pltpu.SemaphoreType.DMA((chunks, max(spots - 1, 1))),
            pltpu.SemaphoreType.DMA((chunks, max(spots - 1, 1))),
            pltpu.SemaphoreType.DMA((chunks, spots)),
            pltpu.SemaphoreType.DMA((chunks, spots)),
        ]

    def __init__(self, place, source, target, sems, over_expert, sharers=1, by_group=None):
        self.place, self.source, self.target = place, source, target
        self.by_group = over_expert if by_group is None else by_group
        self.first_send, self.first_land, self.side_send, self.side_land, self.core_send, self.core_land = sems
        self.over_expert, self.sharers = over_expert, sharers
        self.width = source.shape[3]
        self.chunks = target.shape[1]

    def owner(self, chunk):
        if not self.by_group:
            return chunk
        half, odd, pair = self.place.groups // 2, lax.rem(chunk, 2), lax.div(chunk, 2)
        even_way = jnp.minimum(chunk, 1) * half + pair
        odd_way = pair + (1 - jnp.minimum(pair, 1)) * half
        return flip(
            self.place.expert, odd * odd_way + (1 - odd) * even_way, self.place.groups
        )

    def spot_of(self, owner, tensor):
        first = pl.multiple_of(tensor * self.width, 128)
        return self.target.at[:, owner, :, pl.ds(first, self.width)]

    def block(self, owner):
        if self.sharers == 1:
            return self.source.at[:, owner]
        return self.source.at[:, lax.div(owner, self.sharers)]

    def send(self, chunk):
        place = self.place
        peer = self.owner(chunk)
        remote(
            self.block(peer),
            self.spot_of(place.expert, place.tensor),
            self.first_send.at[chunk],
            self.first_land.at[chunk],
            place.device(peer, place.tensor),
        ).start()

    def start(self, ahead):
        place = self.place
        own = self.owner(0)
        if not self.over_expert:
            return
        for chunk in range(1, min(ahead + 1, self.chunks)):
            self.send(chunk)
        copy = pltpu.make_async_copy(
            self.block(own), self.spot_of(own, place.tensor), self.first_send.at[0]
        )
        copy.start()
        copy.wait()

    def first(self, chunk):
        place = self.place
        owner = self.owner(chunk)
        mine = self.spot_of(owner, place.tensor)
        if self.over_expert:

            @pl.when(chunk > 0)
            def _():
                remote(
                    self.block(owner),
                    mine,
                    self.first_send.at[chunk],
                    self.first_land.at[chunk],
                    place.device(owner, place.tensor),
                ).wait_recv()

            held = mine
        else:
            pltpu.make_async_copy(self.block(owner), mine, self.first_send.at[chunk]).start()
            held = self.block(owner)
        for step in range(1, place.spots):
            remote(
                held,
                mine,
                self.side_send.at[chunk, step - 1],
                self.side_land.at[chunk, step - 1],
                place.device(place.expert, place.across(step)),
            ).start()
        remote(
            held,
            mine,
            self.core_send.at[chunk, 0],
            self.core_land.at[chunk, 0],
            place.device(place.expert, place.spot * 2 + 1 - place.core),
        ).start()

    def second(self, chunk):
        place = self.place
        owner = self.owner(chunk)
        for step in range(1, place.spots):
            came = self.spot_of(owner, place.before(step))
            remote(
                came,
                came,
                self.side_send.at[chunk, step - 1],
                self.side_land.at[chunk, step - 1],
                place.device(place.expert, place.across(step)),
            ).wait_recv()
            remote(
                came,
                came,
                self.core_send.at[chunk, step],
                self.core_land.at[chunk, step],
                place.device(place.expert, place.spot * 2 + 1 - place.core),
            ).start()

    def third(self, chunk):
        place = self.place
        owner = self.owner(chunk)
        flipped = 1 - 2 * place.core
        if not self.over_expert:
            mine = self.spot_of(owner, place.tensor)
            pltpu.make_async_copy(self.block(owner), mine, self.first_send.at[chunk]).wait()
        for step in range(place.spots):
            came = self.spot_of(owner, place.before(step) + flipped)
            remote(
                came,
                came,
                self.core_send.at[chunk, step],
                self.core_land.at[chunk, step],
                place.device(place.expert, place.spot * 2 + 1 - place.core),
            ).wait_recv()

    def finish(self, chunk):
        place = self.place
        owner = self.owner(chunk)
        mine = self.spot_of(owner, place.tensor)
        device = place.device(place.expert, place.tensor)
        if self.over_expert:

            @pl.when(chunk > 0)
            def _():
                remote(
                    self.block(owner),
                    mine,
                    self.first_send.at[chunk],
                    self.first_land.at[chunk],
                    device,
                ).wait_send()

        for step in range(1, place.spots):
            remote(
                mine,
                mine,
                self.side_send.at[chunk, step - 1],
                self.side_land.at[chunk, step - 1],
                device,
            ).wait_send()
        for step in range(place.spots):
            remote(
                mine, mine, self.core_send.at[chunk, step], self.core_land.at[chunk, step], device
            ).wait_send()


class Collect:
    @staticmethod
    def scratch(chunks, kinds, spots, rows, width, slots=2):
        return [
            pltpu.VMEM((slots, kinds, spots, 2, rows, width), jnp.bfloat16),
            pltpu.VMEM((slots, kinds, max(spots - 1, 1), rows, width), jnp.bfloat16),
            pltpu.VMEM((chunks, kinds, spots, rows, width), jnp.bfloat16),
            pltpu.VMEM((chunks, kinds, max(spots - 1, 1), rows, width), jnp.bfloat16),
            pltpu.SemaphoreType.DMA((chunks,)),
            pltpu.SemaphoreType.DMA((chunks,)),
            pltpu.SemaphoreType.DMA((chunks, max(spots - 1, 1))),
            pltpu.SemaphoreType.DMA((chunks, max(spots - 1, 1))),
        ]

    def __init__(self, place, refs):
        self.place = place
        self.stage, self.side, self.core_in, self.side_in = refs[:4]
        self.core_send, self.core_land, self.side_send, self.side_land = refs[4:]
        self.chunks = self.core_in.shape[0]
        self.slots = self.stage.shape[0]

    def core_copy(self, chunk):
        place = self.place
        return remote(
            self.stage.at[lax.rem(chunk, self.slots), :, :, 1 - place.core],
            self.core_in.at[chunk],
            self.core_send.at[chunk],
            self.core_land.at[chunk],
            place.device(place.expert, place.spot * 2 + 1 - place.core),
        )

    def side_copy(self, chunk, step):
        place = self.place
        return remote(
            self.side.at[lax.rem(chunk, self.slots), :, step - 1],
            self.side_in.at[chunk, :, step - 1],
            self.side_send.at[chunk, step - 1],
            self.side_land.at[chunk, step - 1],
            place.device(place.expert, place.across(step)),
        )

    def free_stage(self, chunk):
        @pl.when(chunk >= self.slots)
        def _():
            self.core_copy(chunk - self.slots).wait_send()

    def first(self, chunk):
        self.core_copy(chunk).start()

    def second(self, chunk):
        place = self.place
        slot = lax.rem(chunk, self.slots)
        self.core_copy(chunk).wait_recv()

        @pl.when(chunk >= self.slots)
        def _():
            for step in range(1, place.spots):
                self.side_copy(chunk - self.slots, step).wait_send()

        for step in range(1, place.spots):
            there = lax.rem(place.spot + step, place.spots)
            total = self.stage[slot, :, there, place.core].astype(jnp.float32) + self.core_in[
                chunk, :, there
            ].astype(jnp.float32)
            self.side[slot, :, step - 1] = total.astype(jnp.bfloat16)
            self.side_copy(chunk, step).start()

    def third(self, chunk):
        place = self.place
        slot = lax.rem(chunk, self.slots)
        total = self.stage[slot, :, place.spot, place.core].astype(jnp.float32) + self.core_in[
            chunk, :, place.spot
        ].astype(jnp.float32)
        for step in range(1, place.spots):
            self.side_copy(chunk, step).wait_recv()
            total = total + self.side_in[chunk, :, step - 1].astype(jnp.float32)
        return total

    def finish(self):
        for chunk in range(max(self.chunks - self.slots, 0), self.chunks):
            self.core_copy(chunk).wait_send()
            for step in range(1, self.place.spots):
                self.side_copy(chunk, step).wait_send()


def when(condition, action, *args):
    pl.when(condition)(functools.partial(action, *args))


def spread_kernel(over_expert, source, target, *sems):
    place = Place()
    spread = Spread(place, source, target, sems, over_expert)
    place.meet(over_expert)
    spread.start(AHEAD_DEAL)

    def step(turn, carry):
        when(turn < spread.chunks, spread.first, turn)
        if over_expert:
            when(turn + 1 + AHEAD_DEAL < spread.chunks, spread.send, turn + 1 + AHEAD_DEAL)
        when(turn >= 1, spread.second, turn - 1)
        return carry

    lax.fori_loop(0, spread.chunks + 1, step, 0)

    def last(turn, carry):
        spread.third(turn)
        spread.finish(turn)
        return carry

    lax.fori_loop(0, spread.chunks, last, 0)


def spread_rows(rows, over_expert, collective, microseconds):
    chunks, count, width = rows.shape
    parts = lax.axis_size("tensor")
    full = pl.pallas_call(
        functools.partial(spread_kernel, over_expert),
        out_shape=jax.ShapeDtypeStruct((1, chunks, count, width * parts), rows.dtype),
        in_specs=[pl.BlockSpec(memory_space=pl.ANY)],
        out_specs=pl.BlockSpec(memory_space=pl.ANY),
        scratch_shapes=Spread.scratch(chunks, parts // 2),
        compiler_params=pltpu.CompilerParams(collective_id=collective, has_side_effects=True),
        cost_estimate=lasting(microseconds),
    )(rows[None])
    return full.reshape(chunks * count, width * parts)


def collect_kernel(make, operand_count, *refs):
    place = Place()
    operands = refs[:operand_count]
    result = refs[operand_count]
    collect = Collect(place, refs[operand_count + 1 :])
    place.meet(False)

    def one(chunk):
        collect.free_stage(chunk)
        slot = lax.rem(chunk, 2)
        width = result.shape[2]
        for spot in range(place.spots):
            for core in range(2):
                first = (spot * 2 + core) * width
                part = make(operands, chunk, first, width)
                collect.stage[slot, 0, spot, core] = part.astype(jnp.bfloat16)
        collect.first(chunk)

    def close(chunk):
        result[chunk] = collect.third(chunk)[0]

    def step(turn, carry):
        when(turn >= 2, close, turn - 2)
        when((turn >= 1) & (turn <= collect.chunks), collect.second, turn - 1)
        when(turn < collect.chunks, one, turn)
        return carry

    lax.fori_loop(0, collect.chunks + 2, step, 0)
    collect.finish()


def collect_rows(make, operands, chunks, rows, width, collective):
    parts = lax.axis_size("tensor")
    out = pl.pallas_call(
        functools.partial(collect_kernel, make, len(operands)),
        out_shape=jax.ShapeDtypeStruct((chunks, rows, width), jnp.float32),
        in_specs=[pl.BlockSpec(memory_space=pltpu.VMEM)] * len(operands),
        out_specs=pl.BlockSpec(memory_space=pltpu.VMEM),
        scratch_shapes=Collect.scratch(chunks, 1, parts // 2, rows, width),
        compiler_params=pltpu.CompilerParams(
            collective_id=collective, has_side_effects=True, vmem_limit_bytes=48 * MIB
        ),
        cost_estimate=lasting(26),
    )(*operands)
    return out.reshape(chunks * rows, width)


def make_attended(span, operands, chunk, first, width):
    heads, gates, weight = operands
    total = None
    for expert in range(gates.shape[2]):
        term = gates[chunk, :, expert : expert + 1] * jnp.dot(
            heads[chunk, :, expert * span : (expert + 1) * span],
            weight[expert * span : (expert + 1) * span, first : first + width],
            preferred_element_type=jnp.float32,
        )
        total = term if total is None else total + term
    return total


def experts_kernel(sharers, *refs):
    (
        source, source_grads, gates, gate_hbm, up_hbm, down_hbm,
        inbox, inbox_grads, grads_out, middle_out, gate_out, up_out, returned,
        gate_w, up_w, down_w, rows, grads, middle, gate_g, up_g, closing, gates_in,
        load_sem, store_sem, back_send, back_land, mark_send, mark_land,
    ) = refs[:29]
    place = Place()
    spread = Spread(place, source, inbox, refs[29:35], True, sharers)
    spread_grads = Spread(place, source_grads, inbox_grads, refs[35:41], False, by_group=True)
    collect = Collect(place, refs[41:])
    chunks = spread.chunks
    width = source.shape[3]
    units = gate_w.shape[1]
    tile = 704 if units % 704 == 0 else units
    capacity = rows.shape[0]
    loads = [
        pltpu.make_async_copy(held, kept, load_sem.at[number])
        for number, (held, kept) in enumerate(
            ((gate_hbm, gate_w), (up_hbm, up_w), (down_hbm, down_w))
        )
    ]
    for load in loads:
        load.start()
    place.meet(True)

    def mark_copy(chunk):
        peer = spread.owner(chunk)
        return remote(
            gates.at[lax.div(peer, sharers)],
            gates_in.at[place.expert],
            mark_send.at[chunk],
            mark_land.at[chunk],
            place.device(peer, place.tensor),
        )

    def mark_landed(chunk):
        peer = spread.owner(chunk)
        return remote(
            gates.at[lax.div(peer, sharers)],
            gates_in.at[peer],
            mark_send.at[chunk],
            mark_land.at[chunk],
            place.device(peer, place.tensor),
        )

    spread.start(AHEAD)
    for chunk in range(1, chunks):
        mark_copy(chunk).start()
    own_mark = pltpu.make_async_copy(
        gates.at[lax.div(place.expert, sharers)], gates_in.at[place.expert], mark_send.at[0]
    )
    own_mark.start()
    own_mark.wait()
    for chunk in range(EARLY):
        spread_grads.first(chunk)

    def stores(owner):
        return [
            pltpu.make_async_copy(held, out.at[owner], store_sem.at[number])
            for number, (held, out) in enumerate(
                ((middle, middle_out), (gate_g, gate_out), (up_g, up_out), (grads, grads_out))
            )
        ]

    def fetches(owner):
        return [
            pltpu.make_async_copy(inbox.at[0, owner], rows, load_sem.at[3]),
            pltpu.make_async_copy(inbox_grads.at[0, owner], grads, load_sem.at[4]),
        ]

    def work(chunk):
        owner = spread.owner(chunk)

        @pl.when(chunk == 0)
        def _():
            for load in loads:
                load.wait()

        @pl.when(chunk > 0)
        def _():
            for store in stores(spread.owner(chunk - 1)):
                store.wait()
            mark_landed(chunk).wait_recv()

        spread.third(chunk)
        spread_grads.third(chunk)
        copies = fetches(owner)
        for fetch in copies:
            fetch.start()
        for fetch in copies:
            fetch.wait()
        wide = gates_in.shape[2]
        line = jnp.broadcast_to(gates_in[owner][:1], (capacity, wide))
        here = lax.broadcasted_iota(jnp.int32, (capacity, wide), 0) == lax.broadcasted_iota(
            jnp.int32, (capacity, wide), 1
        )
        gate_column = jnp.sum(jnp.where(here, line, 0.0), axis=1, keepdims=True)
        grads[...] = (grads[...].astype(jnp.float32) * gate_column).astype(jnp.bfloat16)
        for first in range(0, units, tile):
            here = slice(first, first + tile)
            gate = jnp.dot(rows[...], gate_w[:, here], preferred_element_type=jnp.float32)
            up = jnp.dot(rows[...], up_w[:, here], preferred_element_type=jnp.float32)
            sig = jax.nn.sigmoid(gate)
            act = gate * sig
            middle[:, here] = (act * up).astype(jnp.bfloat16)
            grad = dot_nt(grads[...], down_w[here, :])
            gate_g[:, here] = (grad * up * sig * (1.0 + gate * (1.0 - sig))).astype(jnp.bfloat16)
            up_g[:, here] = (grad * act).astype(jnp.bfloat16)
        for store in stores(owner):
            store.start()
        made, fed = 2 * chunk, 2 * chunk + 1
        when(chunk >= 1, collect.second, made - 1)
        when(chunk >= 1, close, made - 2)
        collect.free_stage(made)
        for spot in range(place.spots):
            for core in range(2):
                first = (spot * 2 + core) * width
                here = slice(first, first + width)
                collect.stage[lax.rem(made, 4), 0, spot, core] = jnp.dot(
                    middle[...], down_w[:, here], preferred_element_type=jnp.float32
                ).astype(jnp.bfloat16)
        collect.first(made)
        collect.free_stage(fed)
        for spot in range(place.spots):
            for core in range(2):
                first = (spot * 2 + core) * width
                here = slice(first, first + width)
                collect.stage[lax.rem(fed, 4), 0, spot, core] = (
                    dot_nt(gate_g[...], gate_w[here, :]) + dot_nt(up_g[...], up_w[here, :])
                ).astype(jnp.bfloat16)
        collect.first(fed)
        collect.second(made)
        when(chunk >= 1, close, made - 1)

    def back_copy(item, owner=None):
        peer = spread.owner(lax.div(item, 2))
        return remote(
            closing.at[lax.rem(item, 4)],
            returned.at[lax.rem(item, 2), place.expert if owner is None else owner],
            back_send.at[item],
            back_land.at[item],
            place.device(peer, place.tensor),
        )

    def close(item):
        slot = lax.rem(item, 4)
        total = collect.third(item)[0]

        @pl.when(item >= 6)
        def _():
            back_copy(item - 4).wait_send()

        closing[slot] = total.astype(jnp.bfloat16)

        @pl.when(item >= 2)
        def _():
            back_copy(item).start()

        @pl.when(item < 2)
        def _():
            own = pltpu.make_async_copy(
                closing.at[slot],
                returned.at[lax.rem(item, 2), place.expert],
                back_send.at[item],
            )
            own.start()
            own.wait()

    def step(turn, carry):
        now = turn - 2
        when(turn < chunks, spread.first, turn)
        when(turn + 1 + AHEAD < chunks, spread.send, turn + 1 + AHEAD)
        when((turn >= 1) & (turn <= chunks), spread.second, turn - 1)
        when(turn + EARLY < chunks, spread_grads.first, turn + EARLY)
        when((turn >= 1) & (turn <= chunks), spread_grads.second, turn - 1)
        when(now >= 0, work, now)
        return carry

    lax.fori_loop(0, chunks + 2, step, 0)
    items = 2 * chunks
    collect.second(items - 1)
    close(items - 2)
    close(items - 1)

    def last(turn, carry):
        spread.finish(turn)
        spread_grads.finish(turn)

        @pl.when(turn > 0)
        def _():
            mark_copy(turn).wait_send()
            for item in (2 * turn, 2 * turn + 1):
                back_copy(item, spread.owner(turn)).wait_recv()

        return carry

    lax.fori_loop(0, chunks, last, 0)
    for store in stores(spread.owner(chunks - 1)):
        store.wait()
    for item in range(max(items - 4, 2), items):
        back_copy(item).wait_send()
    collect.finish()


def experts(source, source_grads, gates, gate_w, up_w, down_w, sharers, collective):
    _, capacity, width = source.shape
    groups, parts = lax.axis_size("expert"), lax.axis_size("tensor")
    spots = parts // 2
    model_width, units = gate_w.shape
    low = jnp.bfloat16
    anywhere = pl.BlockSpec(memory_space=pl.ANY)
    hidden_rows = jax.ShapeDtypeStruct((groups, capacity, units), low)
    return pl.pallas_call(
        functools.partial(experts_kernel, sharers),
        out_shape=(
            jax.ShapeDtypeStruct((1, groups, capacity, model_width), low),
            jax.ShapeDtypeStruct((1, groups, capacity, model_width), low),
            jax.ShapeDtypeStruct((groups, capacity, model_width), low),
            hidden_rows,
            hidden_rows,
            hidden_rows,
            jax.ShapeDtypeStruct((2, groups, capacity, width), low),
        ),
        in_specs=[anywhere] * 6,
        out_specs=(anywhere,) * 7,
        scratch_shapes=[
            pltpu.VMEM((model_width, units), low),
            pltpu.VMEM((model_width, units), low),
            pltpu.VMEM((units, model_width), low),
            pltpu.VMEM((capacity, model_width), low),
            pltpu.VMEM((capacity, model_width), low),
            pltpu.VMEM((capacity, units), low),
            pltpu.VMEM((capacity, units), low),
            pltpu.VMEM((capacity, units), low),
            pltpu.VMEM((4, capacity, width), low),
            pltpu.VMEM((groups,) + gates.shape[1:], jnp.float32),
            pltpu.SemaphoreType.DMA((5,)),
            pltpu.SemaphoreType.DMA((4,)),
            pltpu.SemaphoreType.DMA((2 * groups,)),
            pltpu.SemaphoreType.DMA((2 * groups,)),
            pltpu.SemaphoreType.DMA((groups,)),
            pltpu.SemaphoreType.DMA((groups,)),
        ]
        + Spread.scratch(groups, spots)
        + Spread.scratch(groups, spots)
        + Collect.scratch(2 * groups, 1, spots, capacity, width, 4),
        compiler_params=pltpu.CompilerParams(
            collective_id=collective, has_side_effects=True, vmem_limit_bytes=60 * MIB
        ),
        cost_estimate=lasting(180),
    )(source[None], source_grads[None], gates, gate_w, up_w, down_w)


class Return:
    @staticmethod
    def scratch(pieces, rows, width, groups):
        return [
            pltpu.VMEM((pieces, rows, width), jnp.bfloat16),
            pltpu.SemaphoreType.DMA((groups,)),
            pltpu.SemaphoreType.DMA((groups,)),
            pltpu.SemaphoreType.DMA,
        ]

    def __init__(self, place, back, refs):
        self.place, self.back = place, back
        self.ready, self.sent, self.landed, self.kept = refs
        self.bucket = back.shape[1]
        self.each = self.ready.shape[1] // self.bucket

    def block(self, piece, number):
        return self.ready.at[piece, pl.ds(number * self.bucket, self.bucket)]

    def copy(self, piece, number, index):
        target = piece * self.each + number
        return remote(
            self.block(piece, number),
            self.back.at[index],
            self.sent.at[target],
            self.landed.at[index],
            self.place.device(target, self.place.tensor),
        )

    def start(self, piece, values):
        place = self.place
        self.ready[piece] = values
        for number in range(self.each):
            target = piece * self.each + number

            @pl.when(target != place.expert)
            def _():
                self.copy(piece, number, place.expert).start()

            @pl.when(target == place.expert)
            def _():
                own = pltpu.make_async_copy(
                    self.block(piece, number), self.back.at[place.expert], self.kept
                )
                own.start()
                own.wait()

    def finish(self, piece):
        for number in range(self.each):
            target = piece * self.each + number

            @pl.when(target != self.place.expert)
            def _():
                self.copy(piece, number, self.place.expert).wait_send()
                self.copy(piece, number, target).wait_recv()


def pair_grad(gates, gate_grads, names, count):
    shared = gates[0] * gate_grads[0] + gates[1] * gate_grads[1]
    lane = lax.broadcasted_iota(jnp.int32, (gates[0].shape[0], count), 1)
    return sum(
        jnp.where(name == lane, gate * (grad - shared), 0.0)
        for gate, grad, name in zip(gates, gate_grads, names)
    )


def precise_dot(left, right, contract=(1, 0)):
    return lax.dot_general(
        left,
        right,
        (((contract[0],), (contract[1],)), ((), ())),
        precision=lax.Precision.HIGHEST,
        preferred_element_type=jnp.float32,
    )


class Exchange:
    @staticmethod
    def scratch(pieces, parts, rows, lanes):
        wide = (rows + 127) // 128 * 128
        return [
            pltpu.VMEM((pieces, lanes, wide), jnp.float32),
            pltpu.VMEM((pieces, parts - 1, lanes, wide), jnp.float32),
            pltpu.SemaphoreType.DMA((pieces, parts - 1)),
            pltpu.SemaphoreType.DMA((pieces, parts - 1)),
        ]

    def __init__(self, place, refs):
        self.place = place
        self.own, self.got, self.sent, self.landed = refs

    def copy(self, piece, step):
        return remote(
            self.own.at[piece],
            self.got.at[piece, step - 1],
            self.sent.at[piece, step - 1],
            self.landed.at[piece, step - 1],
            self.place.device(self.place.expert, self.place.along(step)),
        )

    def start(self, piece, values):
        _, lanes, wide = self.own.shape
        rows = values.shape[0]
        if rows < wide:
            blank = jnp.zeros((wide - rows, 128), jnp.float32)
            values = jnp.concatenate([values, blank], axis=0)
        self.own[piece] = values.T[:lanes]
        for step in range(1, self.place.parts):
            self.copy(piece, step).start()

    def total(self, piece, rows):
        _, lanes, wide = self.own.shape
        total = self.own[piece]
        for step in range(1, self.place.parts):
            self.copy(piece, step).wait_recv()
            total = total + self.got[piece, step - 1]
        blank = jnp.zeros((128 - lanes, wide), jnp.float32)
        return jnp.concatenate([total, blank], axis=0).T[:rows]

    def finish(self, piece):
        for step in range(1, self.place.parts):
            self.copy(piece, step).wait_send()


def closing_kernel(jobs, *refs):
    (
        normed_t, gain, factor, gates, routes, logits, gate_grads, router_t, gain_two, router_two,
        query_grad, key_grad, value_grad, gated_t, hidden_grads,
        hidden_hbm, resid_hbm, query_hbm, key_hbm, value_hbm,
    ), refs = refs[:20], refs[20:]
    grads = (query_grad, key_grad, value_grad)
    count = len(grads)
    lefts, rights, refs = refs[:3], refs[3:6], refs[6:]
    summed, back, small_out, products, refs = refs[:4], refs[4], refs[5], refs[6:9], refs[9:]
    (
        hold, hold_out, partial, small_own, small_got, small_sum,
        hidden, resid, w_query, w_key, w_value, right, left, product,
        ring_send, ring_land, small_send, small_land, last_send, last_land,
        own_sem, load_sem, job_sem,
    ) = refs[:23]
    weights = (w_query, w_key, w_value)
    place = Place()
    exchange, of_gates = Exchange(place, refs[23:27]), Exchange(place, refs[27:31])
    giving = Return(place, back, refs[31:35])
    collect = Collect(place, refs[35:])
    groups, parts = place.groups, place.parts
    pieces, rows = collect.core_in.shape[0], collect.core_in.shape[3]
    width = hidden.shape[1]
    block = hold.shape[3]
    experts_of = logits.shape[1]
    loads = [
        pltpu.make_async_copy(held, kept, load_sem.at[number])
        for number, (held, kept) in enumerate(
            (
                (query_hbm, w_query), (key_hbm, w_key), (value_hbm, w_value),
                (hidden_hbm, hidden), (resid_hbm, resid),
            )
        )
    ]
    for load in loads:
        load.start()
    place.meet(True, True)

    parity, half = lax.rem(place.expert, 2), lax.div(place.expert, 2)
    at = half + parity * (groups - 1 - 2 * half)

    def member(spot):
        spot = lax.rem(spot + groups, groups)
        high = lax.div(spot, groups // 2)
        return (1 - high) * 2 * spot + high * (2 * (groups - 1 - spot) + 1)

    ways = ((0, 1), (1, -1))

    def first_row(way, sign, step):
        spot = lax.rem(at - sign * step + 2 * groups, groups)
        return pl.multiple_of((way * groups + spot) * block, block)

    def ring_copy(step, way, sign, number, source, target):
        return remote(
            source,
            target,
            ring_send.at[step, way, number],
            ring_land.at[step, way, number],
            place.device(member(at + sign), place.tensor),
        )

    out_rows, out_columns = hold_out.shape[2:]

    def first_column(sign, step):
        spot = lax.rem(at - sign * step + 2 * groups, groups)
        return pl.multiple_of(spot * out_columns, 128)

    def slot(step, way, number):
        if number == count:
            return hold_out.at[step, way]
        return hold.at[step, way, number]

    def spot_out(step, way, sign, number):
        if number == count:
            return summed[number].at[
                pl.ds(way * out_rows, out_rows), pl.ds(first_column(sign, step), out_columns)
            ]
        return summed[number].at[pl.ds(first_row(way, sign, step), block)]

    def own_part(step, way, sign, number):
        if number == count:
            return jnp.dot(
                gated_t[way * out_rows : (way + 1) * out_rows, :],
                hidden_grads[:, pl.ds(first_column(sign, step), out_columns)],
                preferred_element_type=jnp.float32,
            )
        return jnp.dot(
            normed_t[pl.ds(first_row(way, sign, step), block), :],
            grads[number][...],
            preferred_element_type=jnp.float32,
        )

    def ring(step):
        for number in range(count + 1):
            for way, sign in ways:

                @pl.when((step >= 1) & (step < groups))
                def _():
                    held = slot(step, way, number)
                    ring_copy(step - 1, way, sign, number, held, held).wait_recv()

                @pl.when(step >= groups)
                def _():
                    held = spot_out(step, way, sign, number)
                    ring_copy(step - 1, way, sign, number, held, held).wait_recv()

                @pl.when(step < groups)
                def _():
                    own = own_part(step, way, sign, number)
                    held = slot(step, way, number)

                    @pl.when(step == 0)
                    def _():
                        held[...] = own.astype(jnp.bfloat16)

                    @pl.when(step > 0)
                    def _():
                        held[...] = (own + held[...].astype(jnp.float32)).astype(jnp.bfloat16)

                @pl.when(step < groups - 1)
                def _():
                    ring_copy(
                        step, way, sign, number, slot(step, way, number), slot(step + 1, way, number)
                    ).start()

                @pl.when(step == groups - 1)
                def _():
                    held, there = slot(step, way, number), spot_out(step, way, sign, number)
                    ring_copy(step, way, sign, number, held, there).start()
                    pltpu.make_async_copy(held, there, own_sem.at[way, number]).start()

                @pl.when((step >= groups) & (step < 2 * groups - 2))
                def _():
                    held = spot_out(step, way, sign, number)
                    ring_copy(step, way, sign, number, held, held).start()

    def ring_finish(step, carry):
        for number in range(count + 1):
            for way, sign in ways:
                held = slot(0, way, number)
                ring_copy(step, way, sign, number, held, held).wait_send()
        return carry

    def band(piece):
        return pl.ds(pl.multiple_of(piece * rows, rows), rows)

    def project(piece):
        collect.free_stage(piece)
        side = lax.rem(piece, 2)
        for spot in range(place.spots):
            for core in range(2):
                first = (spot * 2 + core) * width
                part = None
                for grad, weight in zip(grads, weights):
                    term = dot_nt(grad[band(piece), :], weight[first : first + width, :])
                    part = term if part is None else part + term
                collect.stage[side, 0, spot, core] = part.astype(jnp.bfloat16)
        collect.first(piece)

    def scaled_of(piece):
        return resid[band(piece), :].astype(jnp.float32) * factor[band(piece), :]

    def tell(piece):
        lane = lax.broadcasted_iota(jnp.int32, (rows, 128), 1)
        values = jnp.zeros((rows, 128), jnp.float32)
        held = gate_grads.shape[1]
        for number in range(held):
            column = gate_grads[band(piece), number : number + 1]
            values = jnp.where(lane == place.tensor * held + number, column, values)
        of_gates.start(piece, values)

    def measure(piece):
        total = collect.third(piece)[0]
        partial[piece] = total
        inner = jnp.sum(total * scaled_of(piece) * gain[...], axis=1, keepdims=True)
        exchange.start(piece, jnp.broadcast_to(inner, (rows, 128)))

    def conclude(piece):
        here = band(piece)
        every = of_gates.total(piece, rows)[:, :experts_of]
        lane = lax.broadcasted_iota(jnp.int32, (rows, experts_of), 1)
        names = [routes[here, way : way + 1] for way in range(2)]
        logit_grad = pair_grad(
            [gates[here, way : way + 1] for way in range(2)],
            [
                jnp.sum(jnp.where(name == lane, every, 0.0), axis=1, keepdims=True)
                for name in names
            ],
            names,
            experts_of,
        )
        inner = exchange.total(piece, rows)[:, :1] + jnp.sum(
            logit_grad * logits[here, :], axis=1, keepdims=True
        )
        mean = inner / (width * parts)
        scaled = scaled_of(piece)
        grad = partial[piece] + precise_dot(logit_grad, router_t[...])
        small_own[0:1, :] += jnp.sum(grad * scaled, axis=0, keepdims=True)
        small_own[1 : 1 + experts_of, :] += precise_dot(logit_grad, scaled * gain[...], (0, 0))
        result = hidden[here, :] + factor[here, :] * (grad * gain[...] - scaled * mean)
        giving.start(piece, result.astype(jnp.bfloat16))

    def small_copy(step):
        return remote(
            small_own,
            small_got.at[step - 1],
            small_send.at[step - 1],
            small_land.at[step - 1],
            place.device(flip(place.expert, step, groups), place.tensor),
        )

    def last_copy(step, origin):
        return remote(
            small_sum,
            small_out.at[origin],
            last_send.at[step - 1],
            last_land.at[step - 1],
            place.device(place.expert, place.along(step)),
        )

    own_small = pltpu.make_async_copy(small_sum, small_out.at[place.tensor], own_sem.at[0, count + 1])

    def small_first():
        first = 1 + experts_of
        small_own[first : first + 1, :] = gain_two[...]
        small_own[first + 1 : first + 1 + router_two.shape[0], :] = router_two[...]
        for step in range(1, groups):
            small_copy(step).start()

    def small_second():
        total = small_own[...]
        for step in range(1, groups):
            small_copy(step).wait_recv()
            total = total + small_got[step - 1]
        small_sum[...] = total
        own_small.start()
        for step in range(1, parts):
            last_copy(step, place.tensor).start()

    small_own[...] = jnp.zeros_like(small_own)
    turns = max(2 * groups - 1, pieces + 5)
    tiles = sum(job[0] for job in jobs)
    each_turn = -(-tiles // turns)

    def job_of(number, first, action):
        start = 0
        for index, (many, size, wide) in enumerate(jobs):
            when(
                (number >= start) & (number < start + many),
                functools.partial(action, index, size, wide),
                number - start,
            )
            start += many

    def right_copy(index, wide):
        return pltpu.make_async_copy(rights[index], right.at[:, pl.ds(0, wide)], job_sem.at[4])

    def left_copy(index, size, tile, side):
        first = pl.multiple_of(tile * size, 128)
        return pltpu.make_async_copy(
            lefts[index].at[:, pl.ds(first, size)],
            left.at[side, :, pl.ds(0, size)],
            job_sem.at[side],
        )

    def product_copy(index, size, wide, tile, side):
        first = pl.multiple_of(tile * size, 8)
        return pltpu.make_async_copy(
            product.at[side, pl.ds(0, size), pl.ds(0, wide)],
            products[index].at[pl.ds(first, size)],
            job_sem.at[2 + side],
        )

    def multiply(number):
        side = lax.rem(number, 2)

        def fetch_next(index, size, wide, tile):
            left_copy(index, size, tile, 1 - side).start()

        def stored(index, size, wide, tile):
            product_copy(index, size, wide, tile, side).wait()

        def work(index, size, wide, tile):
            @pl.when(tile == 0)
            def _():
                right_copy(index, wide).start()
                right_copy(index, wide).wait()

            left_copy(index, size, tile, side).wait()
            product[side, :size, :wide] = dot_tn(left[side, :, :size], right[:, :wide]).astype(
                jnp.bfloat16
            )
            product_copy(index, size, wide, tile, side).start()

        job_of(number + 1, None, fetch_next)
        job_of(number - 2, None, stored)
        job_of(number, None, work)

    left_copy(0, jobs[0][1], 0, 0).start()

    def turn_step(turn, carry):
        when(turn < 2 * groups - 1, ring, turn)

        @pl.when(turn == 0)
        def _():
            for load in loads:
                load.wait()

        when((turn >= 3) & (turn < pieces + 3), conclude, turn - 3)
        when((turn >= 2) & (turn < pieces + 2), measure, turn - 2)
        when((turn >= 1) & (turn < pieces + 1), collect.second, turn - 1)
        when(turn < pieces, project, turn)
        when(turn < pieces, tell, turn)
        when(turn == pieces + 3, small_first)
        when(turn == pieces + 4, small_second)
        lax.fori_loop(
            turn * each_turn,
            jnp.minimum((turn + 1) * each_turn, tiles),
            lambda number, held: (multiply(number), held)[1],
            0,
        )
        return carry

    lax.fori_loop(0, turns, turn_step, 0)
    for number in (tiles - 2, tiles - 1):
        index, tile = 0, number
        while tile >= jobs[index][0]:
            tile -= jobs[index][0]
            index += 1
        product_copy(index, jobs[index][1], jobs[index][2], tile, number % 2).wait()
    lax.fori_loop(0, 2 * groups - 2, ring_finish, 0)
    for number in range(count + 1):
        for way, sign in ways:
            pltpu.make_async_copy(
                slot(groups - 1, way, number),
                spot_out(groups - 1, way, sign, number),
                own_sem.at[way, number],
            ).wait()
    collect.finish()
    for step in range(1, groups):
        small_copy(step).wait_send()
    own_small.wait()
    for step in range(1, parts):
        origin = lax.rem(place.tensor + parts - step, parts)
        last_copy(step, place.tensor).wait_send()
        last_copy(step, origin).wait_recv()

    def settle(piece, carry):
        exchange.finish(piece)
        of_gates.finish(piece)
        giving.finish(piece)
        return carry

    lax.fori_loop(0, pieces, settle, 0)


def closing(
    normed_t, columns_in, grads, gated_t, hidden_grads, hidden, resid, weights,
    lefts, rights, pieces, collective,
):
    groups, parts = lax.axis_size("expert"), lax.axis_size("tensor")
    spots = parts // 2
    model_width, tokens = normed_t.shape
    columns = grads[0].shape[1]
    width = hidden.shape[1]
    count = len(grads)
    small = jax.ShapeDtypeStruct(
        ((2 + columns_in[4].shape[1] + columns_in[-1].shape[0] + 7) // 8 * 8, width), jnp.float32
    )
    rows = tokens // pieces
    block = model_width // (2 * groups)
    low, full = jnp.bfloat16, jnp.float32
    inside = pl.BlockSpec(memory_space=pltpu.VMEM)
    anywhere = pl.BlockSpec(memory_space=pl.ANY)
    dma = pltpu.SemaphoreType.DMA
    jobs = []
    for left, right in zip(lefts, rights):
        jobs.append((left.shape[1] // 128, 128, right.shape[1]))
    depth = lefts[0].shape[0]
    tile = max(job[1] for job in jobs)
    wide = max(job[2] for job in jobs)
    return pl.pallas_call(
        functools.partial(closing_kernel, tuple(jobs)),
        out_shape=(
            *(jax.ShapeDtypeStruct((model_width, columns), low) for _ in range(count)),
            jax.ShapeDtypeStruct((columns, model_width), low),
            jax.ShapeDtypeStruct((groups, tokens // groups, width), low),
            jax.ShapeDtypeStruct((parts,) + small.shape, full),
            *(
                jax.ShapeDtypeStruct((left.shape[1], right.shape[1]), low)
                for left, right in zip(lefts, rights)
            ),
        ),
        in_specs=[inside] * 15 + [anywhere] * 11,
        out_specs=(anywhere,) * 9,
        scratch_shapes=[
            pltpu.VMEM((groups, 2, count, block, columns), low),
            pltpu.VMEM((groups, 2, columns // 2, model_width // groups), low),
            pltpu.VMEM((pieces, rows, width), full),
            pltpu.VMEM(small.shape, full),
            pltpu.VMEM((groups - 1,) + small.shape, full),
            pltpu.VMEM(small.shape, full),
            pltpu.VMEM((tokens, width), full),
            pltpu.VMEM((tokens, width), low),
            *(pltpu.VMEM(weight.shape, low) for weight in weights),
            pltpu.VMEM((depth, wide), low),
            pltpu.VMEM((2, depth, tile), low),
            pltpu.VMEM((2, tile, wide), low),
            dma((2 * groups - 2, 2, count + 1)),
            dma((2 * groups - 2, 2, count + 1)),
            dma((groups - 1,)),
            dma((groups - 1,)),
            dma((parts - 1,)),
            dma((parts - 1,)),
            dma((2, count + 2)),
            dma((5,)),
            dma((5,)),
        ]
        + Exchange.scratch(pieces, parts, rows, 8)
        + Exchange.scratch(pieces, parts, rows, (columns_in[4].shape[1] + 7) // 8 * 8)
        + Return.scratch(pieces, rows, width, groups)
        + Collect.scratch(pieces, 1, spots, rows, width),
        compiler_params=pltpu.CompilerParams(
            collective_id=collective, has_side_effects=True, vmem_limit_bytes=60 * MIB
        ),
        cost_estimate=lasting(200),
    )(
        normed_t, *columns_in, *grads, gated_t, hidden_grads, hidden, resid, *weights,
        *lefts, *rights,
    )


def settle_kernel(
    came, picks, gates, logits, factor, hidden, grads, gain, router_t,
    back, hidden_grad, gathered, router_grad, gain_grad,
    row_grads, ready, *refs,
):
    place = Place()
    exchange = Exchange(place, refs[:4])
    giving = Return(place, back, refs[4:8])
    pieces, rows, width = row_grads.shape
    spread = Spread(place, ready, gathered, refs[8:], False)
    slots, experts_of = came.shape[1], logits.shape[1]
    low = jnp.bfloat16
    place.meet(True, True)
    router_grad[...] = jnp.zeros_like(router_grad)
    gain_grad[...] = jnp.zeros_like(gain_grad)

    def band(piece):
        return pl.ds(pl.multiple_of(piece * rows, rows), rows)

    def scaled_of(piece):
        return hidden[band(piece), :] * factor[band(piece), :]

    def gather(piece):
        here = band(piece)
        numbers = lax.broadcasted_iota(jnp.int32, (rows, slots), 1)
        chosen = [(picks[here, way : way + 1] == numbers).astype(low) for way in range(2)]
        result = hidden[here, :]
        grad = grads[here, :].astype(jnp.float32)
        lane = lax.broadcasted_iota(jnp.int32, (rows, 128), 1)
        stats = jnp.zeros((rows, 128), jnp.float32)
        for way in range(2):
            value = jnp.dot(chosen[way], came[0], preferred_element_type=jnp.float32)
            result = result + gates[here, way : way + 1] * value
            stats = jnp.where(lane == way, jnp.sum(value * grad, axis=1, keepdims=True), stats)
        total = jnp.dot(chosen[0] + chosen[1], came[1], preferred_element_type=jnp.float32)
        row_grads[piece] = total
        inner = jnp.sum(total * scaled_of(piece) * gain[...], axis=1, keepdims=True)
        exchange.start(piece, jnp.where(lane == 2, inner, stats))
        giving.start(piece, result.astype(low))

    def settle(piece):
        here = band(piece)
        stats = exchange.total(piece, rows)
        logit_grad = pair_grad(
            [gates[here, way : way + 1] for way in range(2)],
            [stats[:, way : way + 1] for way in range(2)],
            [picks[here, 2 + way : 3 + way] for way in range(2)],
            experts_of,
        )
        mean = (
            stats[:, 2:3] + jnp.sum(logit_grad * logits[here, :], axis=1, keepdims=True)
        ) / (width * place.parts)
        scaled = scaled_of(piece)
        grad = row_grads[piece] + precise_dot(logit_grad, router_t[...])
        gain_grad[...] += jnp.sum(grad * scaled, axis=0, keepdims=True)
        router_grad[...] += precise_dot(logit_grad, scaled * gain[...], (0, 0))
        result = grads[here, :].astype(jnp.float32) + factor[here, :] * (
            grad * gain[...] - scaled * mean
        )
        hidden_grad[here, :] = result
        ready[0, piece] = result.astype(low)
        spread.first(piece)

    def step(turn, carry):
        when(turn < pieces, gather, turn)
        when((turn >= 2) & (turn <= pieces + 1), settle, turn - 2)
        when(turn >= 3, spread.second, turn - 3)
        return carry

    lax.fori_loop(0, pieces + 3, step, 0)

    def last(piece, carry):
        spread.third(piece)
        spread.finish(piece)
        exchange.finish(piece)
        giving.finish(piece)
        return carry

    lax.fori_loop(0, pieces, last, 0)


def settle(came, picks, gates, logits, factor, hidden, grads, gain, router_t, pieces, collective):
    groups, parts = lax.axis_size("expert"), lax.axis_size("tensor")
    tokens, width = hidden.shape
    rows = tokens // pieces
    low, full = jnp.bfloat16, jnp.float32
    inside = pl.BlockSpec(memory_space=pltpu.VMEM)
    anywhere = pl.BlockSpec(memory_space=pl.ANY)
    return pl.pallas_call(
        settle_kernel,
        out_shape=(
            jax.ShapeDtypeStruct((groups, tokens // groups, width), low),
            jax.ShapeDtypeStruct((tokens, width), full),
            jax.ShapeDtypeStruct((1, pieces, rows, width * parts), low),
            jax.ShapeDtypeStruct(router_t.shape, full),
            jax.ShapeDtypeStruct((1, width), full),
        ),
        in_specs=[inside] * 9,
        out_specs=(anywhere, inside, anywhere, inside, inside),
        scratch_shapes=[
            pltpu.VMEM((pieces, rows, width), full),
            pltpu.VMEM((1, pieces, rows, width), low),
        ]
        + Exchange.scratch(pieces, parts, rows, 8)
        + Return.scratch(pieces, rows, width, groups)
        + Spread.scratch(pieces, parts // 2),
        compiler_params=pltpu.CompilerParams(
            collective_id=collective, has_side_effects=True, vmem_limit_bytes=48 * MIB
        ),
        cost_estimate=lasting(30),
    )(came, picks, gates, logits, factor, hidden, grads, gain, router_t)


def dot_tn(left, right):
    return lax.dot_general(
        left, right, (((0,), (0,)), ((), ())), preferred_element_type=jnp.float32
    )


def bands(tokens):
    size = 256 if tokens % 256 == 0 else tokens
    return [(first, size) for first in range(0, tokens, size)]


def masked_scores(query, keys, segment_column, segment_row, first, size, column):
    last = first + size
    rows = slice(first, last)
    scores = dot_nt(query[rows, column], keys[:last, column]) * (1.0 / math.sqrt(HEAD))
    place = lax.broadcasted_iota(jnp.int32, (size, last), 0) + first
    other = lax.broadcasted_iota(jnp.int32, (size, last), 1)
    allowed = (segment_column[rows, :] == segment_row[:, :last]) & (place >= other)
    return jnp.where(allowed, scores, MASKED)


def attend_kernel(
    resid, gain, router, w_query, w_key, w_value, cosine, sine, segment_column, segment_row,
    normed, normed_t, factor, logits, query, keys, values, heads, log_total,
):
    tokens, columns = query.shape
    low = jnp.bfloat16
    for first, size in bands(tokens):
        rows = slice(first, first + size)
        value = resid[rows, :].astype(jnp.float32)
        scale = lax.rsqrt(jnp.mean(value * value, axis=1, keepdims=True) + EPSILON)
        value = value * scale * gain[...]
        high = value.astype(low)
        rest = (value - high.astype(jnp.float32)).astype(low)
        factor[rows, :] = scale
        normed[rows, :] = high
        normed_t[:, rows] = high.T
        logits[rows, :] = jnp.dot(
            high, router[...], preferred_element_type=jnp.float32
        ) + jnp.dot(rest, router[...], preferred_element_type=jnp.float32)
        values[rows, :] = jnp.dot(
            high, w_value[...], preferred_element_type=jnp.float32
        ).astype(low)
        for weight, out in ((w_query, query), (w_key, keys)):
            flat = jnp.dot(high, weight[...], preferred_element_type=jnp.float32)
            for head in range(columns // HEAD):
                column = slice(head * HEAD, (head + 1) * HEAD)
                part = flat[:, column]
                turned = pltpu.roll(part, HEAD // 2, 1)
                out[rows, column] = (part * cosine[rows, :] + turned * sine[rows, :]).astype(low)
    for head in range(columns // HEAD):
        column = slice(head * HEAD, (head + 1) * HEAD)
        for first, size in bands(tokens):
            last = first + size
            rows = slice(first, last)
            scores = masked_scores(query, keys, segment_column, segment_row, first, size, column)
            top = jnp.max(scores, axis=1, keepdims=True)
            expo = jnp.exp(scores - top)
            total = jnp.sum(expo, axis=1, keepdims=True)
            probs = (expo / total).astype(low)
            heads[rows, column] = jnp.dot(
                probs, values[:last, column], preferred_element_type=jnp.float32
            ).astype(low)
            log_total[rows, head : head + 1] = top + jnp.log(total)


def attend(resid, gain, router, weights, cosine, sine, segment):
    tokens, model_width = resid.shape
    columns = weights[0].shape[1]
    low, full = jnp.bfloat16, jnp.float32
    block = jax.ShapeDtypeStruct((tokens, columns), low)
    inside = pl.BlockSpec(memory_space=pltpu.VMEM)
    return pl.pallas_call(
        attend_kernel,
        out_shape=(
            jax.ShapeDtypeStruct((tokens, model_width), low),
            jax.ShapeDtypeStruct((model_width, tokens), low),
            jax.ShapeDtypeStruct((tokens, 1), full),
            jax.ShapeDtypeStruct((tokens, router.shape[1]), full),
            block,
            block,
            block,
            block,
            jax.ShapeDtypeStruct((tokens, columns // HEAD), full),
        ),
        in_specs=[inside] * 10,
        out_specs=(inside,) * 9,
        compiler_params=pltpu.CompilerParams(vmem_limit_bytes=56 * MIB),
        cost_estimate=lasting(20),
    )(resid, gain, router, *weights, cosine, sine, segment[:, None], segment[None, :])


def attend_back_kernel(
    grads, w_out, gates, heads, query, keys, values, log_total, cosine, sine,
    segment_column, segment_row,
    query_grad, key_grad, value_grad, gate_grad, gated_t,
    heads_grad, key_sum, value_sum,
):
    tokens, columns = query.shape
    low = jnp.bfloat16
    span = columns // gates.shape[1]
    scale = 1.0 / math.sqrt(HEAD)
    for first, size in bands(tokens):
        rows = slice(first, first + size)
        plain = dot_nt(grads[rows, :], w_out[...])
        for expert in range(gates.shape[1]):
            column = slice(expert * span, (expert + 1) * span)
            gate = gates[rows, expert : expert + 1]
            head = heads[rows, column].astype(jnp.float32)
            gate_grad[rows, expert : expert + 1] = jnp.sum(
                plain[:, column] * head, axis=1, keepdims=True
            )
            heads_grad[rows, column] = (plain[:, column] * gate).astype(low)
            gated_t[column, rows] = (head * gate).T.astype(low)

    def unturn(value, rows):
        turned = pltpu.roll(value * sine[rows, :], HEAD // 2, 1)
        return value * cosine[rows, :] + turned

    for head in range(columns // HEAD):
        column = slice(head * HEAD, (head + 1) * HEAD)
        for first, size in bands(tokens):
            last = first + size
            rows = slice(first, last)
            scores = masked_scores(query, keys, segment_column, segment_row, first, size, column)
            probs = jnp.exp(scores - log_total[rows, head : head + 1])
            value_part = dot_tn(probs.astype(low), heads_grad[rows, column])
            prob_grad = dot_nt(heads_grad[rows, column], values[:last, column])
            score_grad = (
                probs * (prob_grad - jnp.sum(probs * prob_grad, axis=1, keepdims=True))
            ).astype(low)
            query_grad[rows, column] = unturn(
                jnp.dot(score_grad, keys[:last, column], preferred_element_type=jnp.float32)
                * scale,
                rows,
            ).astype(low)
            key_part = dot_tn(score_grad, query[rows, column])
            if first:
                value_sum[:first, :] += value_part[:first]
                key_sum[:first, :] += key_part[:first]
            value_sum[rows, :] = value_part[first:]
            key_sum[rows, :] = key_part[first:]
        whole = slice(0, tokens)
        key_grad[:, column] = unturn(key_sum[...] * scale, whole).astype(low)
        value_grad[:, column] = value_sum[...].astype(low)


def attend_back(grads, w_out, gates, heads, query, keys, values, log_total, cosine, sine, segment):
    tokens, model_width = grads.shape
    columns = query.shape[1]
    low, full = jnp.bfloat16, jnp.float32
    block = jax.ShapeDtypeStruct((tokens, columns), low)
    inside = pl.BlockSpec(memory_space=pltpu.VMEM)
    return pl.pallas_call(
        attend_back_kernel,
        out_shape=(
            block,
            block,
            block,
            jax.ShapeDtypeStruct(gates.shape, full),
            jax.ShapeDtypeStruct((columns, tokens), low),
        ),
        in_specs=[inside] * 12,
        out_specs=(inside,) * 5,
        scratch_shapes=[
            pltpu.VMEM((tokens, columns), low),
            pltpu.VMEM((tokens, HEAD), full),
            pltpu.VMEM((tokens, HEAD), full),
        ],
        compiler_params=pltpu.CompilerParams(vmem_limit_bytes=56 * MIB),
        cost_estimate=lasting(25),
    )(
        grads, w_out, gates, heads, query, keys, values, log_total, cosine, sine,
        segment[:, None], segment[None, :],
    )


def to_expert(rows, group_count):
    count, width = rows.shape
    return lax.all_to_all(
        rows.reshape(group_count, count // group_count, width),
        "expert",
        split_axis=0,
        concat_axis=0,
        tiled=True,
    ).reshape(count, width)


def gather_tensor(rows):
    return lax.all_gather(rows, "tensor", axis=0)


def body(
    tokens,
    out_grad,
    attn_gain,
    attn_router,
    w_query,
    w_key,
    w_value,
    w_out,
    mlp_gain,
    mlp_router,
    w_gate,
    w_up,
    w_down,
    deal,
    seq_lengths,
    attn_routes,
    mlp_routes,
    slot_order,
):
    tok_rows, model_width = tokens.shape
    group_count = lax.axis_size("expert")
    part_count = lax.axis_size("tensor")
    group_index = lax.axis_index("expert")
    part_index = lax.axis_index("tensor")
    bucket_rows = tok_rows // group_count
    col_width = model_width // part_count
    col_first = part_index * col_width
    low = jnp.bfloat16

    def own_cols(values):
        return lax.dynamic_slice_in_dim(values, col_first, col_width, values.ndim - 1)

    deal_rank = deal // tok_rows * bucket_rows + (deal % tok_rows - group_index * bucket_rows)
    row_ids = jnp.arange(tok_rows, dtype=jnp.int32)
    deal_mask = (row_ids[:, None] == deal_rank[None, :]).astype(low)
    dealt = jnp.dot(deal_mask, own_cols(tokens), preferred_element_type=jnp.float32).astype(low)
    resid_low = spread_rows(dealt.reshape(group_count, bucket_rows, col_width), True, 0, 30)
    dealt_grads = jnp.dot(
        deal_mask, own_cols(out_grad), preferred_element_type=jnp.float32
    ).astype(low)
    dealt_grads, resid_low = lax.optimization_barrier((dealt_grads, resid_low))
    grad_cols_low = to_expert(dealt_grads, group_count)
    gain_one, gain_two = own_cols(attn_gain), own_cols(mlp_gain)
    router_one = lax.dynamic_slice_in_dim(attn_router, col_first, col_width, 0)
    router_two = lax.dynamic_slice_in_dim(mlp_router, col_first, col_width, 0)
    expert_count = mlp_router.shape[1]
    sharers = group_count // expert_count
    capacity = 5 * tok_rows // (2 * expert_count)
    target, position, kept = slot_table(mlp_routes, slot_order[0], capacity)
    slots = expert_count * capacity
    destination = jnp.where(kept, target * capacity + position, slots).reshape(tok_rows, 2)
    slot_ids = jnp.arange(slots, dtype=jnp.int32)
    chosen = [destination[:, way] for way in range(2)]
    to_slot = (
        (slot_ids[:, None] == chosen[0][None, :]) | (slot_ids[:, None] == chosen[1][None, :])
    ).astype(low)
    resid_cols = own_cols(resid_low).astype(jnp.float32)
    segment, cosine, sine = rotary_tables(seq_lengths[0], tok_rows)
    sign = jnp.where(jnp.arange(HEAD) < HEAD // 2, -1.0, 1.0)
    local_heads = w_query.shape[1] // HEAD
    local_experts = local_heads // QH
    span = QH * HEAD
    experts_of = attn_router.shape[1]
    router_high = lax.reduce_precision(attn_router, 8, 7)
    router_parts = jnp.concatenate([router_high, attn_router - router_high], axis=1).astype(low)
    router_parts = jnp.pad(router_parts, ((0, 0), (0, -router_parts.shape[1] % 128)))
    normed_low, normed_t, factor_one, logit_parts, query, keys, values, heads_low, log_total = (
        attend(
            resid_low,
            attn_gain[None],
            router_parts,
            (w_query, w_key, w_value),
            cosine,
            sine * sign,
            segment,
        )
    )
    attn_logits = logit_parts[:, :experts_of] + logit_parts[:, experts_of : 2 * experts_of]
    attn_gates, attn_mask = pair_gates(attn_logits, attn_routes)
    gate_table = jnp.sum(attn_gates[:, :, None] * attn_mask, axis=1)
    gate_local = lax.dynamic_slice_in_dim(gate_table, part_index * local_experts, local_experts, 1)
    grad_cols_low, heads_low = lax.optimization_barrier((grad_cols_low, heads_low))
    slot_grads = jnp.dot(to_slot, grad_cols_low, preferred_element_type=jnp.float32).astype(low)
    slot_grads = jnp.repeat(slot_grads.reshape(expert_count, capacity, col_width), sharers, axis=0)
    slot_grads = to_expert(slot_grads.reshape(group_count * capacity, col_width), group_count)
    pieces, piece_rows = 4, tok_rows // 4
    attn_cols = collect_rows(
        functools.partial(make_attended, span),
        (
            heads_low.reshape(pieces, piece_rows, local_heads * HEAD),
            gate_local.reshape(pieces, piece_rows, local_experts),
            w_out,
        ),
        pieces,
        piece_rows,
        col_width,
        1,
    )
    hidden = resid_cols + attn_cols
    weighed = hidden * gain_two
    stats = jnp.concatenate(
        [
            jnp.sum(hidden * hidden, axis=1)[None, :],
            jnp.dot(weighed, router_two, precision=PRECISE).T,
        ],
        axis=0,
    )
    stats = jnp.sum(gather_tensor(stats), axis=0)
    factor_two = lax.rsqrt(stats[0] / model_width + EPSILON)[:, None]
    mlp_logits = stats[1:].T * factor_two
    scaled_two = hidden * factor_two
    normed_two = scaled_two * gain_two
    mlp_gates, _ = pair_gates(mlp_logits, mlp_routes)
    slot_rows = jnp.dot(
        to_slot, normed_two.astype(low), preferred_element_type=jnp.float32
    ).astype(low)
    slot_gates = sum(
        jnp.sum(
            jnp.where(slot_ids[:, None] == chosen[way][None, :], mlp_gates[:, way][None, :], 0.0),
            axis=1,
        )
        for way in range(2)
    )
    gate_lines = jnp.pad(slot_gates.reshape(expert_count, capacity), ((0, 0), (0, -capacity % 128)))
    gate_lines = jnp.broadcast_to(gate_lines[:, None, :], (expert_count, 8, gate_lines.shape[1]))
    inbox, _, slot_grads, middle, gate_grad, up_grad, returned = experts(
        slot_rows.reshape(expert_count, capacity, col_width),
        slot_grads.reshape(group_count, capacity, col_width),
        gate_lines,
        w_gate[0],
        w_up[0],
        w_down[0],
        sharers,
        2,
    )
    if sharers > 1:
        returned = (
            jnp.sum(
                returned.reshape(2, expert_count, sharers, capacity, col_width).astype(jnp.float32),
                axis=2,
            )
        ).astype(low)
    back_mixed, hidden_grad, hidden_grad_low, mlp_router_grad, mlp_gain_grad = settle(
        returned.reshape(2, slots, col_width),
        jnp.concatenate([destination, mlp_routes], axis=1),
        mlp_gates,
        mlp_logits,
        factor_two,
        hidden,
        grad_cols_low,
        gain_two[None],
        router_two.T,
        pieces,
        4,
    )
    back_mixed = back_mixed.reshape(tok_rows, col_width)
    hidden_grad_low = hidden_grad_low.reshape(tok_rows, model_width)
    query_pre_grad, key_pre_grad, value_pre_grad, local_gate_grad, gated_t = attend_back(
        hidden_grad_low,
        w_out,
        gate_local,
        heads_low,
        query,
        keys,
        values,
        log_total,
        cosine,
        sine * sign,
        segment,
    )
    rows = inbox.reshape(-1, model_width)
    units = middle.shape[2]
    middle, gate_grad, up_grad = (
        jnp.pad(values.reshape(-1, units), ((0, 0), (0, -units % 128)))
        for values in (middle, gate_grad, up_grad)
    )
    *weight_grads, back_grad, small, gate_w_grad, up_w_grad, down_grad = closing(
        normed_t,
        (
            gain_one[None],
            factor_one,
            attn_gates,
            attn_routes,
            attn_logits,
            local_gate_grad,
            router_one.T,
            mlp_gain_grad,
            mlp_router_grad,
        ),
        (query_pre_grad, key_pre_grad, value_pre_grad),
        gated_t,
        hidden_grad_low,
        hidden_grad,
        own_cols(resid_low),
        (w_query, w_key, w_value),
        (rows, rows, middle),
        (gate_grad, up_grad, slot_grads.reshape(-1, model_width)),
        pieces,
        3,
    )
    back_grad = back_grad.reshape(tok_rows, col_width)
    weight_grads = [grad.astype(jnp.float32) for grad in weight_grads]
    mixed, tokens_grad = (
        jnp.einsum("ri,rc->ic", deal_mask, back, preferred_element_type=jnp.float32).astype(low)
        for back in (back_mixed, back_grad)
    )
    small = small.transpose(1, 0, 2).reshape(-1, model_width)
    return (
        mixed,
        tokens_grad,
        small[0],
        small[1 : 1 + experts_of].T,
        weight_grads[0],
        weight_grads[1],
        weight_grads[2],
        weight_grads[3],
        small[1 + experts_of],
        small[2 + experts_of : 2 + experts_of + expert_count].T,
        gate_w_grad[None, :, :units].astype(jnp.float32),
        up_w_grad[None, :, :units].astype(jnp.float32),
        down_grad[None, :units].astype(jnp.float32),
    )


def solution(mesh):
    placed = (
        P("expert", None),
        P("expert", None),
        P(),
        P(),
        P(None, "tensor"),
        P(None, "tensor"),
        P(None, "tensor"),
        P("tensor", None),
        P(),
        P(),
        P("expert", None, "tensor"),
        P("expert", None, "tensor"),
        P("expert", "tensor", None),
        P("expert"),
        P("expert", None),
        P("expert", None),
        P("expert", None),
        P("expert", None),
    )
    return jax.shard_map(
        body,
        mesh=mesh,
        in_specs=placed,
        out_specs=(
            P("expert", "tensor"),
            P("expert", "tensor"),
            P(),
            P(),
            P(None, "tensor"),
            P(None, "tensor"),
            P(None, "tensor"),
            P("tensor", None),
            P(),
            P(),
            P("expert", None, "tensor"),
            P("expert", None, "tensor"),
            P("expert", "tensor", None),
        ),
        check_vma=False,
    )
```

```python
import functools
import math

import jax
import jax.numpy as jnp
import numpy as np
from jax import lax
from jax.experimental import pallas as pl
from jax.experimental.pallas import tpu as pltpu
from jax.sharding import PartitionSpec as P

HEAD = 128
QH = 2


EPSILON = 1e-06
MASKED = -1e30


def rotary_tables(tokens):
    frequency = np.exp(-math.log(10000.0) * np.arange(0, HEAD, 2, dtype=np.float32) / HEAD)
    angles = np.arange(tokens, dtype=np.float32)[:, None] * frequency.astype(np.float32)[None, :]
    angles = np.concatenate([angles, angles], axis=1).astype(np.float64)
    return jnp.asarray(np.cos(angles), jnp.float32), jnp.asarray(np.sin(angles), jnp.float32)


MESH = pl.DeviceIdType.MESH
MIB = 1 << 20
AHEAD_DEAL = 2
AHEAD = 2
FRONT = 3
SQUARES = 8
ROUTES, ROUTES_TWO, SLOTS = 0, 2, 4


def flip(number, other, count):
    total, bit = 0, 1
    while bit < count:
        total = total + lax.rem(lax.div(number, bit) + lax.div(other, bit), 2) * bit
        bit *= 2
    return total


def dot_nt(left, right):
    return lax.dot_general(
        left, right, (((1,), (1,)), ((), ())), preferred_element_type=jnp.float32
    )


class Place:
    def __init__(self):
        self.groups = lax.axis_size("expert")
        self.parts = lax.axis_size("tensor")
        self.spots = self.parts // 2
        self.expert = lax.axis_index("expert")
        self.tensor = lax.axis_index("tensor")
        self.spot = lax.div(self.tensor, 2)
        self.core = lax.rem(self.tensor, 2)

    def device(self, expert, tensor):
        return {"expert": expert, "tensor": tensor}

    def across(self, step):
        return lax.rem(self.spot + step, self.spots) * 2 + self.core

    def before(self, step):
        return lax.rem(self.spot + self.spots - step, self.spots) * 2 + self.core

    def meet(self, over_expert, whole_tensor=False):
        if whole_tensor:
            peers = [self.device(self.expert, self.along(step)) for step in range(1, self.parts)]
        else:
            peers = [self.device(self.expert, self.spot * 2 + 1 - self.core)]
            for step in range(1, self.spots):
                peers.append(self.device(self.expert, self.across(step)))
        if over_expert:
            for step in range(1, self.groups):
                peers.append(self.device(flip(self.expert, step, self.groups), self.tensor))
        barrier = pltpu.get_barrier_semaphore()
        for peer in peers:
            pl.semaphore_signal(barrier, inc=1, device_id=peer, device_id_type=MESH)
        pl.semaphore_wait(barrier, len(peers))

    def along(self, step):
        return lax.rem(self.tensor + step, self.parts)


def lasting(microseconds):
    return pl.CostEstimate(
        flops=0, bytes_accessed=int(microseconds * 3_000_000), transcendentals=0
    )


def remote(source, target, send, receive, device):
    return pltpu.make_async_remote_copy(
        src_ref=source,
        dst_ref=target,
        send_sem=send,
        recv_sem=receive,
        device_id=device,
        device_id_type=MESH,
    )


class Spread:
    @staticmethod
    def scratch(chunks, spots):
        return [
            pltpu.SemaphoreType.DMA((chunks,)),
            pltpu.SemaphoreType.DMA((chunks,)),
            pltpu.SemaphoreType.DMA((chunks, max(spots - 1, 1))),
            pltpu.SemaphoreType.DMA((chunks, max(spots - 1, 1))),
            pltpu.SemaphoreType.DMA((chunks, spots)),
            pltpu.SemaphoreType.DMA((chunks, spots)),
        ]

    def __init__(self, place, source, target, sems, over_expert, sharers=1, by_group=None):
        self.place, self.source, self.target = place, source, target
        self.by_group = over_expert if by_group is None else by_group
        self.first_send, self.first_land, self.side_send, self.side_land, self.core_send, self.core_land = sems
        self.over_expert, self.sharers = over_expert, sharers
        self.width = source.shape[3]
        self.chunks = target.shape[1]

    def owner(self, chunk):
        if not self.by_group:
            return chunk
        half, odd, pair = self.place.groups // 2, lax.rem(chunk, 2), lax.div(chunk, 2)
        even_way = jnp.minimum(chunk, 1) * half + pair
        odd_way = pair + (1 - jnp.minimum(pair, 1)) * half
        return flip(
            self.place.expert, odd * odd_way + (1 - odd) * even_way, self.place.groups
        )

    def spot_of(self, owner, tensor):
        first = pl.multiple_of(tensor * self.width, 128)
        return self.target.at[:, owner, :, pl.ds(first, self.width)]

    def block(self, owner):
        if self.sharers == 1:
            return self.source.at[:, owner]
        return self.source.at[:, lax.div(owner, self.sharers)]

    def send(self, chunk):
        place = self.place
        peer = self.owner(chunk)
        remote(
            self.block(peer),
            self.spot_of(place.expert, place.tensor),
            self.first_send.at[chunk],
            self.first_land.at[chunk],
            place.device(peer, place.tensor),
        ).start()

    def start(self, ahead):
        place = self.place
        own = self.owner(0)
        if not self.over_expert:
            return
        for chunk in range(1, min(ahead + 1, self.chunks)):
            self.send(chunk)
        copy = pltpu.make_async_copy(
            self.block(own), self.spot_of(own, place.tensor), self.first_send.at[0]
        )
        copy.start()
        copy.wait()

    def first(self, chunk):
        place = self.place
        owner = self.owner(chunk)
        mine = self.spot_of(owner, place.tensor)
        if self.over_expert:

            @pl.when(chunk > 0)
            def _():
                remote(
                    self.block(owner),
                    mine,
                    self.first_send.at[chunk],
                    self.first_land.at[chunk],
                    place.device(owner, place.tensor),
                ).wait_recv()

            held = mine
        else:
            pltpu.make_async_copy(self.block(owner), mine, self.first_send.at[chunk]).start()
            held = self.block(owner)
        for step in range(1, place.spots):
            remote(
                held,
                mine,
                self.side_send.at[chunk, step - 1],
                self.side_land.at[chunk, step - 1],
                place.device(place.expert, place.across(step)),
            ).start()
        remote(
            held,
            mine,
            self.core_send.at[chunk, 0],
            self.core_land.at[chunk, 0],
            place.device(place.expert, place.spot * 2 + 1 - place.core),
        ).start()

    def second(self, chunk):
        place = self.place
        owner = self.owner(chunk)
        for step in range(1, place.spots):
            came = self.spot_of(owner, place.before(step))
            remote(
                came,
                came,
                self.side_send.at[chunk, step - 1],
                self.side_land.at[chunk, step - 1],
                place.device(place.expert, place.across(step)),
            ).wait_recv()
            remote(
                came,
                came,
                self.core_send.at[chunk, step],
                self.core_land.at[chunk, step],
                place.device(place.expert, place.spot * 2 + 1 - place.core),
            ).start()

    def third(self, chunk):
        place = self.place
        owner = self.owner(chunk)
        flipped = 1 - 2 * place.core
        if not self.over_expert:
            mine = self.spot_of(owner, place.tensor)
            pltpu.make_async_copy(self.block(owner), mine, self.first_send.at[chunk]).wait()
        for step in range(place.spots):
            came = self.spot_of(owner, place.before(step) + flipped)
            remote(
                came,
                came,
                self.core_send.at[chunk, step],
                self.core_land.at[chunk, step],
                place.device(place.expert, place.spot * 2 + 1 - place.core),
            ).wait_recv()

    def finish(self, chunk):
        place = self.place
        owner = self.owner(chunk)
        mine = self.spot_of(owner, place.tensor)
        device = place.device(place.expert, place.tensor)
        if self.over_expert:

            @pl.when(chunk > 0)
            def _():
                remote(
                    self.block(owner),
                    mine,
                    self.first_send.at[chunk],
                    self.first_land.at[chunk],
                    device,
                ).wait_send()

        for step in range(1, place.spots):
            remote(
                mine,
                mine,
                self.side_send.at[chunk, step - 1],
                self.side_land.at[chunk, step - 1],
                device,
            ).wait_send()
        for step in range(place.spots):
            remote(
                mine, mine, self.core_send.at[chunk, step], self.core_land.at[chunk, step], device
            ).wait_send()


class Collect:
    @staticmethod
    def scratch(chunks, kinds, spots, rows, width, slots=2):
        return [
            pltpu.VMEM((slots, kinds, spots, 2, rows, width), jnp.bfloat16),
            pltpu.VMEM((slots, kinds, max(spots - 1, 1), rows, width), jnp.bfloat16),
            pltpu.VMEM((chunks, kinds, spots, rows, width), jnp.bfloat16),
            pltpu.VMEM((chunks, kinds, max(spots - 1, 1), rows, width), jnp.bfloat16),
            pltpu.SemaphoreType.DMA((chunks,)),
            pltpu.SemaphoreType.DMA((chunks,)),
            pltpu.SemaphoreType.DMA((chunks, max(spots - 1, 1))),
            pltpu.SemaphoreType.DMA((chunks, max(spots - 1, 1))),
        ]

    def __init__(self, place, refs):
        self.place = place
        self.stage, self.side, self.core_in, self.side_in = refs[:4]
        self.core_send, self.core_land, self.side_send, self.side_land = refs[4:]
        self.chunks = self.core_in.shape[0]
        self.slots = self.stage.shape[0]

    def core_copy(self, chunk):
        place = self.place
        return remote(
            self.stage.at[lax.rem(chunk, self.slots), :, :, 1 - place.core],
            self.core_in.at[chunk],
            self.core_send.at[chunk],
            self.core_land.at[chunk],
            place.device(place.expert, place.spot * 2 + 1 - place.core),
        )

    def side_copy(self, chunk, step):
        place = self.place
        return remote(
            self.side.at[lax.rem(chunk, self.slots), :, step - 1],
            self.side_in.at[chunk, :, step - 1],
            self.side_send.at[chunk, step - 1],
            self.side_land.at[chunk, step - 1],
            place.device(place.expert, place.across(step)),
        )

    def free_stage(self, chunk):
        @pl.when(chunk >= self.slots)
        def _():
            self.core_copy(chunk - self.slots).wait_send()

    def first(self, chunk):
        self.core_copy(chunk).start()

    def second(self, chunk):
        place = self.place
        slot = lax.rem(chunk, self.slots)
        self.core_copy(chunk).wait_recv()

        @pl.when(chunk >= self.slots)
        def _():
            for step in range(1, place.spots):
                self.side_copy(chunk - self.slots, step).wait_send()

        for step in range(1, place.spots):
            there = lax.rem(place.spot + step, place.spots)
            total = self.stage[slot, :, there, place.core].astype(jnp.float32) + self.core_in[
                chunk, :, there
            ].astype(jnp.float32)
            self.side[slot, :, step - 1] = total.astype(jnp.bfloat16)
            self.side_copy(chunk, step).start()

    def third(self, chunk):
        place = self.place
        slot = lax.rem(chunk, self.slots)
        total = self.stage[slot, :, place.spot, place.core].astype(jnp.float32) + self.core_in[
            chunk, :, place.spot
        ].astype(jnp.float32)
        for step in range(1, place.spots):
            self.side_copy(chunk, step).wait_recv()
            total = total + self.side_in[chunk, :, step - 1].astype(jnp.float32)
        return total

    def finish(self):
        for chunk in range(max(self.chunks - self.slots, 0), self.chunks):
            self.core_copy(chunk).wait_send()
            for step in range(1, self.place.spots):
                self.side_copy(chunk, step).wait_send()


def when(condition, action, *args):
    pl.when(condition)(functools.partial(action, *args))


def columns_of(rows):
    blank = jnp.zeros((128 - rows.shape[0], rows.shape[1]), jnp.float32)
    return jnp.concatenate([rows, blank], axis=0).T


def deal_kernel(
    capacity, experts_of, tokens, out_grad, ranks, rows_in,
    full, dealt_grads, marks, mark_rows,
    held, sending, slots, load_sem, *sems,
):
    place = Place()
    count, width = held.shape[1:]
    groups, bucket, _ = dealt_grads.shape
    low = jnp.bfloat16
    own = pl.ds(pl.multiple_of(place.tensor * width, 128), width)
    loads = [
        pltpu.make_async_copy(source.at[:, own], held.at[number], load_sem.at[number])
        for number, source in enumerate((tokens, out_grad))
    ]
    for load in loads:
        load.start()
    spread = Spread(place, sending, full, sems, True)
    place.meet(True)

    def dealt(number, group):
        rank = lax.broadcasted_iota(jnp.int32, (bucket, count), 0) + group * bucket
        chosen = (ranks[...] == rank).astype(low)
        return jnp.dot(chosen, held[number], preferred_element_type=jnp.float32).astype(low)

    loads[0].wait()
    for group in range(groups):
        sending[0, group] = dealt(0, group)
    spread.start(AHEAD_DEAL)

    def number_slots():
        rows = rows_in[...].astype(jnp.float32)
        columns = columns_of(rows)
        lane = lax.broadcasted_iota(jnp.int32, (count, 128), 1)
        found = jnp.zeros((count, 128), jnp.float32)
        for way in range(2):
            target = columns[:, ROUTES_TWO + way : ROUTES_TWO + way + 1]
            order = columns[:, 4 + way : 5 + way]
            position = jnp.zeros((count, 1), jnp.float32)
            for other in range(2):
                earlier = (rows[ROUTES_TWO + other : ROUTES_TWO + other + 1] == target) & (
                    rows[4 + other : 5 + other] < order
                )
                position = position + jnp.sum(
                    jnp.where(earlier, 1.0, 0.0), axis=1, keepdims=True
                )
            slot = jnp.where(
                position < capacity, target * capacity + position, experts_of * capacity
            )
            marks[:, SLOTS + way : SLOTS + way + 1] = slot.astype(jnp.int32)
            found = jnp.where(lane == way, slot, found)
        marks[:, :SLOTS] = columns[:, :SLOTS].astype(jnp.int32)
        slots[...] = found
        mark_rows[...] = slots[...].T[:8].astype(jnp.int32)

    def deal_grads():
        loads[1].wait()
        for group in range(groups):
            dealt_grads[group] = dealt(1, group)

    def step(turn, carry):
        when(turn < spread.chunks, spread.first, turn)
        when(turn + 1 + AHEAD_DEAL < spread.chunks, spread.send, turn + 1 + AHEAD_DEAL)
        when(turn >= 1, spread.second, turn - 1)
        when(turn == 1, deal_grads)
        when(turn == 2, number_slots)
        return carry

    lax.fori_loop(0, spread.chunks + 1, step, 0)

    def last(turn, carry):
        spread.third(turn)
        spread.finish(turn)
        return carry

    lax.fori_loop(0, spread.chunks, last, 0)


def deal_rows(tokens, out_grad, ranks, rows_in, capacity, experts_of, collective):
    groups, parts = lax.axis_size("expert"), lax.axis_size("tensor")
    count, model_width = tokens.shape
    width, bucket = model_width // parts, count // groups
    low = tokens.dtype
    inside = pl.BlockSpec(memory_space=pltpu.VMEM)
    anywhere = pl.BlockSpec(memory_space=pl.ANY)
    return pl.pallas_call(
        functools.partial(deal_kernel, capacity, experts_of),
        out_shape=(
            jax.ShapeDtypeStruct((1, groups, bucket, model_width), low),
            jax.ShapeDtypeStruct((groups, bucket, width), low),
            jax.ShapeDtypeStruct((count, 8), jnp.int32),
            jax.ShapeDtypeStruct((8, count), jnp.int32),
        ),
        in_specs=[anywhere] * 2 + [inside] * 2,
        out_specs=(anywhere,) + (inside,) * 3,
        scratch_shapes=[
            pltpu.VMEM((2, count, width), low),
            pltpu.VMEM((1, groups, bucket, width), low),
            pltpu.VMEM((count, 128), jnp.float32),
            pltpu.SemaphoreType.DMA((2,)),
        ]
        + Spread.scratch(groups, parts // 2),
        compiler_params=pltpu.CompilerParams(
            collective_id=collective, has_side_effects=True, vmem_limit_bytes=40 * MIB
        ),
        cost_estimate=lasting(35),
    )(tokens, out_grad, ranks, rows_in)


def experts_kernel(sharers, *refs):
    (
        source, source_grads, gates, gate_hbm, up_hbm, down_hbm, early_grads,
        inbox, inbox_grads, grads_out, middle_out, gate_out, up_out, returned,
        gate_w, up_w, down_w, rows, grads, middle, gate_g, up_g, closing, gates_in,
        load_sem, store_sem, back_send, back_land, mark_send, mark_land,
    ) = refs[:30]
    place = Place()
    spread = Spread(place, source, inbox, refs[30:36], True, sharers)
    spread_grads = Spread(place, source_grads, inbox_grads, refs[36:42], True, sharers)
    collect = Collect(place, refs[42:])
    chunks = spread.chunks
    width = source.shape[3]
    units = gate_w.shape[1]
    tile = 704 if units % 704 == 0 else units
    capacity = rows.shape[0]
    loads = [
        pltpu.make_async_copy(held, kept, load_sem.at[number])
        for number, (held, kept) in enumerate(
            ((gate_hbm, gate_w), (up_hbm, up_w), (down_hbm, down_w))
        )
    ]
    for load in loads:
        load.start()
    place.meet(True)

    def mark_copy(chunk):
        peer = spread.owner(chunk)
        return remote(
            gates.at[lax.div(peer, sharers)],
            gates_in.at[place.expert],
            mark_send.at[chunk],
            mark_land.at[chunk],
            place.device(peer, place.tensor),
        )

    def mark_landed(chunk):
        peer = spread.owner(chunk)
        return remote(
            gates.at[lax.div(peer, sharers)],
            gates_in.at[peer],
            mark_send.at[chunk],
            mark_land.at[chunk],
            place.device(peer, place.tensor),
        )

    spread.start(AHEAD)
    for chunk in range(1, chunks):
        mark_copy(chunk).start()
    own_mark = pltpu.make_async_copy(
        gates.at[lax.div(place.expert, sharers)], gates_in.at[place.expert], mark_send.at[0]
    )
    own_mark.start()
    own_mark.wait()
    early = min(FRONT, chunks)
    for chunk in range(early, min(AHEAD + 1, chunks)):
        spread_grads.send(chunk)

    def stores(owner):
        return [
            pltpu.make_async_copy(held, out.at[owner], store_sem.at[number])
            for number, (held, out) in enumerate(
                ((middle, middle_out), (gate_g, gate_out), (up_g, up_out), (grads, grads_out))
            )
        ]

    def fetches(owner):
        return [
            pltpu.make_async_copy(inbox.at[0, owner], rows, load_sem.at[3]),
            pltpu.make_async_copy(early_grads.at[0, owner], grads, load_sem.at[4]),
            pltpu.make_async_copy(inbox_grads.at[0, owner], grads, load_sem.at[4]),
        ]

    def work(chunk):
        owner = spread.owner(chunk)

        @pl.when(chunk == 0)
        def _():
            for load in loads:
                load.wait()

        @pl.when(chunk > 0)
        def _():
            for store in stores(spread.owner(chunk - 1)):
                store.wait()
            mark_landed(chunk).wait_recv()

        spread.third(chunk)
        when(chunk >= early, spread_grads.third, chunk)
        fetch, fetch_early, fetch_late = fetches(owner)
        fetch.start()
        when(chunk < early, fetch_early.start)
        when(chunk >= early, fetch_late.start)
        fetch.wait()
        fetch_early.wait()
        wide = gates_in.shape[2]
        line = jnp.broadcast_to(gates_in[owner][:1], (capacity, wide))
        here = lax.broadcasted_iota(jnp.int32, (capacity, wide), 0) == lax.broadcasted_iota(
            jnp.int32, (capacity, wide), 1
        )
        gate_column = jnp.sum(jnp.where(here, line, 0.0), axis=1, keepdims=True)
        grads[...] = (grads[...].astype(jnp.float32) * gate_column).astype(jnp.bfloat16)
        for first in range(0, units, tile):
            here = slice(first, first + tile)
            gate = jnp.dot(rows[...], gate_w[:, here], preferred_element_type=jnp.float32)
            up = jnp.dot(rows[...], up_w[:, here], preferred_element_type=jnp.float32)
            sig = jax.nn.sigmoid(gate)
            act = gate * sig
            middle[:, here] = (act * up).astype(jnp.bfloat16)
            grad = dot_nt(grads[...], down_w[here, :])
            gate_g[:, here] = (grad * up * sig * (1.0 + gate * (1.0 - sig))).astype(jnp.bfloat16)
            up_g[:, here] = (grad * act).astype(jnp.bfloat16)
        for store in stores(owner):
            store.start()
        made, fed = 2 * chunk, 2 * chunk + 1
        when(chunk >= 1, collect.second, made - 1)
        when(chunk >= 1, close, made - 2)
        collect.free_stage(made)
        for spot in range(place.spots):
            for core in range(2):
                first = (spot * 2 + core) * width
                here = slice(first, first + width)
                collect.stage[lax.rem(made, 4), 0, spot, core] = jnp.dot(
                    middle[...], down_w[:, here], preferred_element_type=jnp.float32
                ).astype(jnp.bfloat16)
        collect.first(made)
        collect.free_stage(fed)
        for spot in range(place.spots):
            for core in range(2):
                first = (spot * 2 + core) * width
                here = slice(first, first + width)
                collect.stage[lax.rem(fed, 4), 0, spot, core] = (
                    dot_nt(gate_g[...], gate_w[here, :]) + dot_nt(up_g[...], up_w[here, :])
                ).astype(jnp.bfloat16)
        collect.first(fed)
        collect.second(made)
        when(chunk >= 1, close, made - 1)

    def back_copy(item, owner=None):
        peer = spread.owner(lax.div(item, 2))
        return remote(
            closing.at[lax.rem(item, 4)],
            returned.at[lax.rem(item, 2), place.expert if owner is None else owner],
            back_send.at[item],
            back_land.at[item],
            place.device(peer, place.tensor),
        )

    def close(item):
        slot = lax.rem(item, 4)
        total = collect.third(item)[0]

        @pl.when(item >= 6)
        def _():
            back_copy(item - 4).wait_send()

        closing[slot] = total.astype(jnp.bfloat16)

        @pl.when(item >= 2)
        def _():
            back_copy(item).start()

        @pl.when(item < 2)
        def _():
            own = pltpu.make_async_copy(
                closing.at[slot],
                returned.at[lax.rem(item, 2), place.expert],
                back_send.at[item],
            )
            own.start()
            own.wait()

    def send_grads(chunk):
        when(chunk >= early, spread_grads.send, chunk)

    def step(turn, carry):
        now = turn - 2
        when(turn < chunks, spread.first, turn)
        when(turn + 1 + AHEAD < chunks, spread.send, turn + 1 + AHEAD)
        when((turn >= 1) & (turn <= chunks), spread.second, turn - 1)
        when((turn >= early - 1 - AHEAD) & (turn + 1 + AHEAD < chunks), send_grads, turn + 1 + AHEAD)
        when((turn >= early) & (turn < chunks), spread_grads.first, turn)
        when((turn > early) & (turn <= chunks), spread_grads.second, turn - 1)
        when(now >= 0, work, now)
        return carry

    lax.fori_loop(0, chunks + 2, step, 0)
    items = 2 * chunks
    collect.second(items - 1)
    close(items - 2)
    close(items - 1)

    def last(turn, carry):
        spread.finish(turn)
        when(turn >= early, spread_grads.finish, turn)

        @pl.when(turn > 0)
        def _():
            mark_copy(turn).wait_send()
            for item in (2 * turn, 2 * turn + 1):
                back_copy(item, spread.owner(turn)).wait_recv()

        return carry

    lax.fori_loop(0, chunks, last, 0)
    for store in stores(spread.owner(chunks - 1)):
        store.wait()
    for item in range(max(items - 4, 2), items):
        back_copy(item).wait_send()
    collect.finish()


def experts(source, source_grads, early_grads, gates, gate_w, up_w, down_w, sharers, collective):
    _, capacity, width = source.shape
    groups, parts = lax.axis_size("expert"), lax.axis_size("tensor")
    spots = parts // 2
    model_width, units = gate_w.shape
    low = jnp.bfloat16
    anywhere = pl.BlockSpec(memory_space=pl.ANY)
    hidden_rows = jax.ShapeDtypeStruct((groups, capacity, units), low)
    return pl.pallas_call(
        functools.partial(experts_kernel, sharers),
        out_shape=(
            jax.ShapeDtypeStruct((1, groups, capacity, model_width), low),
            jax.ShapeDtypeStruct((1, groups, capacity, model_width), low),
            jax.ShapeDtypeStruct((groups, capacity, model_width), low),
            hidden_rows,
            hidden_rows,
            hidden_rows,
            jax.ShapeDtypeStruct((2, groups, capacity, width), low),
        ),
        in_specs=[anywhere] * 7,
        out_specs=(anywhere,) * 7,
        scratch_shapes=[
            pltpu.VMEM((model_width, units), low),
            pltpu.VMEM((model_width, units), low),
            pltpu.VMEM((units, model_width), low),
            pltpu.VMEM((capacity, model_width), low),
            pltpu.VMEM((capacity, model_width), low),
            pltpu.VMEM((capacity, units), low),
            pltpu.VMEM((capacity, units), low),
            pltpu.VMEM((capacity, units), low),
            pltpu.VMEM((4, capacity, width), low),
            pltpu.VMEM((groups,) + gates.shape[1:], jnp.float32),
            pltpu.SemaphoreType.DMA((5,)),
            pltpu.SemaphoreType.DMA((4,)),
            pltpu.SemaphoreType.DMA((2 * groups,)),
            pltpu.SemaphoreType.DMA((2 * groups,)),
            pltpu.SemaphoreType.DMA((groups,)),
            pltpu.SemaphoreType.DMA((groups,)),
        ]
        + Spread.scratch(groups, spots)
        + Spread.scratch(groups, spots)
        + Collect.scratch(2 * groups, 1, spots, capacity, width, 4),
        compiler_params=pltpu.CompilerParams(
            collective_id=collective, has_side_effects=True, vmem_limit_bytes=60 * MIB
        ),
        cost_estimate=lasting(180),
    )(source[None], source_grads[None], gates, gate_w, up_w, down_w, early_grads)


class Return:
    @staticmethod
    def scratch(pieces, rows, width, groups):
        return [
            pltpu.VMEM((pieces, rows, width), jnp.bfloat16),
            pltpu.SemaphoreType.DMA((groups,)),
            pltpu.SemaphoreType.DMA((groups,)),
            pltpu.SemaphoreType.DMA,
        ]

    def __init__(self, place, back, refs):
        self.place, self.back = place, back
        self.ready, self.sent, self.landed, self.kept = refs
        self.bucket = back.shape[1]
        self.each = self.ready.shape[1] // self.bucket

    def block(self, piece, number):
        return self.ready.at[piece, pl.ds(number * self.bucket, self.bucket)]

    def copy(self, piece, number, index):
        target = piece * self.each + number
        return remote(
            self.block(piece, number),
            self.back.at[index],
            self.sent.at[target],
            self.landed.at[index],
            self.place.device(target, self.place.tensor),
        )

    def start(self, piece, values):
        place = self.place
        self.ready[piece] = values
        for number in range(self.each):
            target = piece * self.each + number

            @pl.when(target != place.expert)
            def _():
                self.copy(piece, number, place.expert).start()

            @pl.when(target == place.expert)
            def _():
                own = pltpu.make_async_copy(
                    self.block(piece, number), self.back.at[place.expert], self.kept
                )
                own.start()
                own.wait()

    def finish(self, piece):
        for number in range(self.each):
            target = piece * self.each + number

            @pl.when(target != self.place.expert)
            def _():
                self.copy(piece, number, self.place.expert).wait_send()
                self.copy(piece, number, target).wait_recv()


def pair_grad(gates, gate_grads, names, count):
    shared = gates[0] * gate_grads[0] + gates[1] * gate_grads[1]
    lane = lax.broadcasted_iota(jnp.int32, (gates[0].shape[0], count), 1)
    return sum(
        jnp.where(name == lane, gate * (grad - shared), 0.0)
        for gate, grad, name in zip(gates, gate_grads, names)
    )


def precise_dot(left, right, contract=(1, 0)):
    return lax.dot_general(
        left,
        right,
        (((contract[0],), (contract[1],)), ((), ())),
        precision=lax.Precision.HIGHEST,
        preferred_element_type=jnp.float32,
    )


class Exchange:
    @staticmethod
    def scratch(pieces, parts, rows, lanes):
        wide = (rows + 127) // 128 * 128
        return [
            pltpu.VMEM((pieces, lanes, wide), jnp.float32),
            pltpu.VMEM((pieces, parts - 1, lanes, wide), jnp.float32),
            pltpu.SemaphoreType.DMA((pieces, parts - 1)),
            pltpu.SemaphoreType.DMA((pieces, parts - 1)),
        ]

    def __init__(self, place, refs):
        self.place = place
        self.own, self.got, self.sent, self.landed = refs

    def copy(self, piece, step):
        return remote(
            self.own.at[piece],
            self.got.at[piece, step - 1],
            self.sent.at[piece, step - 1],
            self.landed.at[piece, step - 1],
            self.place.device(self.place.expert, self.place.along(step)),
        )

    def start(self, piece, values):
        _, lanes, wide = self.own.shape
        rows = values.shape[0]
        if rows < wide:
            blank = jnp.zeros((wide - rows, 128), jnp.float32)
            values = jnp.concatenate([values, blank], axis=0)
        self.own[piece] = values.T[:lanes]
        for step in range(1, self.place.parts):
            self.copy(piece, step).start()

    def total(self, piece, rows):
        _, lanes, wide = self.own.shape
        total = self.own[piece]
        for step in range(1, self.place.parts):
            self.copy(piece, step).wait_recv()
            total = total + self.got[piece, step - 1]
        blank = jnp.zeros((128 - lanes, wide), jnp.float32)
        return jnp.concatenate([total, blank], axis=0).T[:rows]

    def finish(self, piece):
        for step in range(1, self.place.parts):
            self.copy(piece, step).wait_send()


def closing_kernel(jobs, *refs):
    (
        normed_t, gain, factor, gates, marks, logits, gate_grads, router_t, gain_two, router_two,
        query_grad, key_grad, value_grad, gated_t, hidden_grads,
        hidden_hbm, resid_hbm, query_hbm, key_hbm, value_hbm,
    ), refs = refs[:20], refs[20:]
    grads = (query_grad, key_grad, value_grad)
    count = len(grads)
    lefts, rights, refs = refs[:3], refs[3:6], refs[6:]
    summed, back, small_out, products, refs = refs[:4], refs[4], refs[5], refs[6:9], refs[9:]
    (
        hold, hold_out, partial, small_own, small_got, small_sum,
        hidden, resid, w_query, w_key, w_value, right, left, product,
        ring_send, ring_land, small_send, small_land, last_send, last_land,
        own_sem, load_sem, job_sem,
    ) = refs[:23]
    weights = (w_query, w_key, w_value)
    place = Place()
    exchange, of_gates = Exchange(place, refs[23:27]), Exchange(place, refs[27:31])
    giving = Return(place, back, refs[31:35])
    collect = Collect(place, refs[35:])
    groups, parts = place.groups, place.parts
    pieces, rows = collect.core_in.shape[0], collect.core_in.shape[3]
    width = hidden.shape[1]
    block = hold.shape[3]
    experts_of = logits.shape[1]
    own_columns = pl.ds(pl.multiple_of(place.tensor * width, 128), width)
    loads = [
        pltpu.make_async_copy(held, kept, load_sem.at[number])
        for number, (held, kept) in enumerate(
            (
                (query_hbm, w_query), (key_hbm, w_key), (value_hbm, w_value),
                (hidden_hbm, hidden), (resid_hbm.at[:, own_columns], resid),
            )
        )
    ]
    for load in loads:
        load.start()
    place.meet(True, True)

    parity, half = lax.rem(place.expert, 2), lax.div(place.expert, 2)
    at = half + parity * (groups - 1 - 2 * half)

    def member(spot):
        spot = lax.rem(spot + groups, groups)
        high = lax.div(spot, groups // 2)
        return (1 - high) * 2 * spot + high * (2 * (groups - 1 - spot) + 1)

    ways = ((0, 1), (1, -1))

    def first_row(way, sign, step):
        spot = lax.rem(at - sign * step + 2 * groups, groups)
        return pl.multiple_of((way * groups + spot) * block, block)

    def ring_copy(step, way, sign, number, source, target):
        return remote(
            source,
            target,
            ring_send.at[step, way, number],
            ring_land.at[step, way, number],
            place.device(member(at + sign), place.tensor),
        )

    out_rows, out_columns = hold_out.shape[2:]

    def first_column(sign, step):
        spot = lax.rem(at - sign * step + 2 * groups, groups)
        return pl.multiple_of(spot * out_columns, 128)

    def slot(step, way, number):
        if number == count:
            return hold_out.at[step, way]
        return hold.at[step, way, number]

    def spot_out(step, way, sign, number):
        if number == count:
            return summed[number].at[
                pl.ds(way * out_rows, out_rows), pl.ds(first_column(sign, step), out_columns)
            ]
        return summed[number].at[pl.ds(first_row(way, sign, step), block)]

    def own_part(step, way, sign, number):
        if number == count:
            return jnp.dot(
                gated_t[way * out_rows : (way + 1) * out_rows, :],
                hidden_grads[:, pl.ds(first_column(sign, step), out_columns)],
                preferred_element_type=jnp.float32,
            )
        return jnp.dot(
            normed_t[pl.ds(first_row(way, sign, step), block), :],
            grads[number][...],
            preferred_element_type=jnp.float32,
        )

    def ring(step):
        for number in range(count + 1):
            for way, sign in ways:

                @pl.when((step >= 1) & (step < groups))
                def _():
                    held = slot(step, way, number)
                    ring_copy(step - 1, way, sign, number, held, held).wait_recv()

                @pl.when(step >= groups)
                def _():
                    held = spot_out(step, way, sign, number)
                    ring_copy(step - 1, way, sign, number, held, held).wait_recv()

                @pl.when(step < groups)
                def _():
                    own = own_part(step, way, sign, number)
                    held = slot(step, way, number)

                    @pl.when(step == 0)
                    def _():
                        held[...] = own.astype(jnp.bfloat16)

                    @pl.when(step > 0)
                    def _():
                        held[...] = (own + held[...].astype(jnp.float32)).astype(jnp.bfloat16)

                @pl.when(step < groups - 1)
                def _():
                    ring_copy(
                        step, way, sign, number, slot(step, way, number), slot(step + 1, way, number)
                    ).start()

                @pl.when(step == groups - 1)
                def _():
                    held, there = slot(step, way, number), spot_out(step, way, sign, number)
                    ring_copy(step, way, sign, number, held, there).start()
                    pltpu.make_async_copy(held, there, own_sem.at[way, number]).start()

                @pl.when((step >= groups) & (step < 2 * groups - 2))
                def _():
                    held = spot_out(step, way, sign, number)
                    ring_copy(step, way, sign, number, held, held).start()

    def ring_finish(step, carry):
        for number in range(count + 1):
            for way, sign in ways:
                held = slot(0, way, number)
                ring_copy(step, way, sign, number, held, held).wait_send()
        return carry

    def band(piece):
        return pl.ds(pl.multiple_of(piece * rows, rows), rows)

    def project(piece):
        collect.free_stage(piece)
        side = lax.rem(piece, 2)
        for spot in range(place.spots):
            for core in range(2):
                first = (spot * 2 + core) * width
                part = None
                for grad, weight in zip(grads, weights):
                    term = dot_nt(grad[band(piece), :], weight[first : first + width, :])
                    part = term if part is None else part + term
                collect.stage[side, 0, spot, core] = part.astype(jnp.bfloat16)
        collect.first(piece)

    def scaled_of(piece):
        return resid[band(piece), :].astype(jnp.float32) * factor[band(piece), :]

    def tell(piece):
        lane = lax.broadcasted_iota(jnp.int32, (rows, 128), 1)
        values = jnp.zeros((rows, 128), jnp.float32)
        held = gate_grads.shape[1]
        for number in range(held):
            column = gate_grads[band(piece), number : number + 1]
            values = jnp.where(lane == place.tensor * held + number, column, values)
        of_gates.start(piece, values)

    def measure(piece):
        total = collect.third(piece)[0]
        partial[piece] = total
        inner = jnp.sum(total * scaled_of(piece) * gain[...], axis=1, keepdims=True)
        exchange.start(piece, jnp.broadcast_to(inner, (rows, 128)))

    def conclude(piece):
        here = band(piece)
        every = of_gates.total(piece, rows)[:, :experts_of]
        lane = lax.broadcasted_iota(jnp.int32, (rows, experts_of), 1)
        names = [marks[here, ROUTES + way : ROUTES + way + 1] for way in range(2)]
        logit_grad = pair_grad(
            [gates[here, way : way + 1] for way in range(2)],
            [
                jnp.sum(jnp.where(name == lane, every, 0.0), axis=1, keepdims=True)
                for name in names
            ],
            names,
            experts_of,
        )
        inner = exchange.total(piece, rows)[:, :1] + jnp.sum(
            logit_grad * logits[here, :], axis=1, keepdims=True
        )
        mean = inner / (width * parts)
        scaled = scaled_of(piece)
        grad = partial[piece] + precise_dot(logit_grad, router_t[...])
        small_own[0:1, :] += jnp.sum(grad * scaled, axis=0, keepdims=True)
        small_own[1 : 1 + experts_of, :] += precise_dot(logit_grad, scaled * gain[...], (0, 0))
        result = hidden[here, :] + factor[here, :] * (grad * gain[...] - scaled * mean)
        giving.start(piece, result.astype(jnp.bfloat16))

    def small_copy(step):
        return remote(
            small_own,
            small_got.at[step - 1],
            small_send.at[step - 1],
            small_land.at[step - 1],
            place.device(flip(place.expert, step, groups), place.tensor),
        )

    def last_copy(step, origin):
        return remote(
            small_sum,
            small_out.at[origin],
            last_send.at[step - 1],
            last_land.at[step - 1],
            place.device(place.expert, place.along(step)),
        )

    own_small = pltpu.make_async_copy(small_sum, small_out.at[place.tensor], own_sem.at[0, count + 1])

    def small_first():
        first = 1 + experts_of
        small_own[first : first + 1, :] = gain_two[...]
        small_own[first + 1 : first + 1 + router_two.shape[0], :] = router_two[...]
        for step in range(1, groups):
            small_copy(step).start()

    def small_second():
        total = small_own[...]
        for step in range(1, groups):
            small_copy(step).wait_recv()
            total = total + small_got[step - 1]
        small_sum[...] = total
        own_small.start()
        for step in range(1, parts):
            last_copy(step, place.tensor).start()

    small_own[...] = jnp.zeros_like(small_own)
    turns = max(2 * groups - 1, pieces + 5)
    tiles = sum(job[0] for job in jobs)
    each_turn = -(-tiles // turns)

    def job_of(number, first, action):
        start = 0
        for index, (many, size, wide) in enumerate(jobs):
            when(
                (number >= start) & (number < start + many),
                functools.partial(action, index, size, wide),
                number - start,
            )
            start += many

    def right_copy(index, wide):
        return pltpu.make_async_copy(rights[index], right.at[:, pl.ds(0, wide)], job_sem.at[4])

    def left_copy(index, size, tile, side):
        first = pl.multiple_of(tile * size, 128)
        return pltpu.make_async_copy(
            lefts[index].at[:, pl.ds(first, size)],
            left.at[side, :, pl.ds(0, size)],
            job_sem.at[side],
        )

    def product_copy(index, size, wide, tile, side):
        first = pl.multiple_of(tile * size, 8)
        return pltpu.make_async_copy(
            product.at[side, pl.ds(0, size), pl.ds(0, wide)],
            products[index].at[pl.ds(first, size)],
            job_sem.at[2 + side],
        )

    def multiply(number):
        side = lax.rem(number, 2)

        def fetch_next(index, size, wide, tile):
            left_copy(index, size, tile, 1 - side).start()

        def stored(index, size, wide, tile):
            product_copy(index, size, wide, tile, side).wait()

        def work(index, size, wide, tile):
            @pl.when(tile == 0)
            def _():
                right_copy(index, wide).start()
                right_copy(index, wide).wait()

            left_copy(index, size, tile, side).wait()
            product[side, :size, :wide] = dot_tn(left[side, :, :size], right[:, :wide]).astype(
                jnp.bfloat16
            )
            product_copy(index, size, wide, tile, side).start()

        job_of(number + 1, None, fetch_next)
        job_of(number - 2, None, stored)
        job_of(number, None, work)

    left_copy(0, jobs[0][1], 0, 0).start()

    def turn_step(turn, carry):
        when(turn < 2 * groups - 1, ring, turn)

        @pl.when(turn == 0)
        def _():
            for load in loads:
                load.wait()

        when((turn >= 3) & (turn < pieces + 3), conclude, turn - 3)
        when((turn >= 2) & (turn < pieces + 2), measure, turn - 2)
        when((turn >= 1) & (turn < pieces + 1), collect.second, turn - 1)
        when(turn < pieces, project, turn)
        when(turn < pieces, tell, turn)
        when(turn == pieces + 3, small_first)
        when(turn == pieces + 4, small_second)
        lax.fori_loop(
            turn * each_turn,
            jnp.minimum((turn + 1) * each_turn, tiles),
            lambda number, held: (multiply(number), held)[1],
            0,
        )
        return carry

    lax.fori_loop(0, turns, turn_step, 0)
    for number in (tiles - 2, tiles - 1):
        index, tile = 0, number
        while tile >= jobs[index][0]:
            tile -= jobs[index][0]
            index += 1
        product_copy(index, jobs[index][1], jobs[index][2], tile, number % 2).wait()
    lax.fori_loop(0, 2 * groups - 2, ring_finish, 0)
    for number in range(count + 1):
        for way, sign in ways:
            pltpu.make_async_copy(
                slot(groups - 1, way, number),
                spot_out(groups - 1, way, sign, number),
                own_sem.at[way, number],
            ).wait()
    collect.finish()
    for step in range(1, groups):
        small_copy(step).wait_send()
    own_small.wait()
    for step in range(1, parts):
        origin = lax.rem(place.tensor + parts - step, parts)
        last_copy(step, place.tensor).wait_send()
        last_copy(step, origin).wait_recv()

    def settle(piece, carry):
        exchange.finish(piece)
        of_gates.finish(piece)
        giving.finish(piece)
        return carry

    lax.fori_loop(0, pieces, settle, 0)


def closing(
    normed_t, columns_in, grads, gated_t, hidden_grads, hidden, resid, weights,
    lefts, rights, pieces, collective,
):
    groups, parts = lax.axis_size("expert"), lax.axis_size("tensor")
    spots = parts // 2
    model_width, tokens = normed_t.shape
    columns = grads[0].shape[1]
    width = hidden.shape[1]
    count = len(grads)
    small = jax.ShapeDtypeStruct(
        ((2 + columns_in[4].shape[1] + columns_in[-1].shape[0] + 7) // 8 * 8, width), jnp.float32
    )
    rows = tokens // pieces
    block = model_width // (2 * groups)
    low, full = jnp.bfloat16, jnp.float32
    inside = pl.BlockSpec(memory_space=pltpu.VMEM)
    anywhere = pl.BlockSpec(memory_space=pl.ANY)
    dma = pltpu.SemaphoreType.DMA
    jobs = []
    for left, right in zip(lefts, rights):
        jobs.append((left.shape[1] // 128, 128, right.shape[1]))
    depth = lefts[0].shape[0]
    tile = max(job[1] for job in jobs)
    wide = max(job[2] for job in jobs)
    return pl.pallas_call(
        functools.partial(closing_kernel, tuple(jobs)),
        out_shape=(
            *(jax.ShapeDtypeStruct((model_width, columns), low) for _ in range(count)),
            jax.ShapeDtypeStruct((columns, model_width), low),
            jax.ShapeDtypeStruct((groups, tokens // groups, width), low),
            jax.ShapeDtypeStruct((parts,) + small.shape, full),
            *(
                jax.ShapeDtypeStruct((left.shape[1], right.shape[1]), low)
                for left, right in zip(lefts, rights)
            ),
        ),
        in_specs=[inside] * 15 + [anywhere] * 11,
        out_specs=(anywhere,) * 9,
        scratch_shapes=[
            pltpu.VMEM((groups, 2, count, block, columns), low),
            pltpu.VMEM((groups, 2, columns // 2, model_width // groups), low),
            pltpu.VMEM((pieces, rows, width), full),
            pltpu.VMEM(small.shape, full),
            pltpu.VMEM((groups - 1,) + small.shape, full),
            pltpu.VMEM(small.shape, full),
            pltpu.VMEM((tokens, width), full),
            pltpu.VMEM((tokens, width), low),
            *(pltpu.VMEM(weight.shape, low) for weight in weights),
            pltpu.VMEM((depth, wide), low),
            pltpu.VMEM((2, depth, tile), low),
            pltpu.VMEM((2, tile, wide), low),
            dma((2 * groups - 2, 2, count + 1)),
            dma((2 * groups - 2, 2, count + 1)),
            dma((groups - 1,)),
            dma((groups - 1,)),
            dma((parts - 1,)),
            dma((parts - 1,)),
            dma((2, count + 2)),
            dma((5,)),
            dma((5,)),
        ]
        + Exchange.scratch(pieces, parts, rows, 8)
        + Exchange.scratch(pieces, parts, rows, (columns_in[4].shape[1] + 7) // 8 * 8)
        + Return.scratch(pieces, rows, width, groups)
        + Collect.scratch(pieces, 1, spots, rows, width),
        compiler_params=pltpu.CompilerParams(
            collective_id=collective, has_side_effects=True, vmem_limit_bytes=60 * MIB
        ),
        cost_estimate=lasting(200),
    )(
        normed_t, *columns_in, *grads, gated_t, hidden_grads, hidden, resid, *weights,
        *lefts, *rights,
    )


def settle_kernel(
    came, marks, gates, logits, factor, hidden, grads, gain, router_t,
    back, hidden_grad, gathered, router_grad, gain_grad,
    row_grads, ready, *refs,
):
    place = Place()
    exchange = Exchange(place, refs[:4])
    giving = Return(place, back, refs[4:8])
    pieces, rows, width = row_grads.shape
    spread = Spread(place, ready, gathered, refs[8:], False)
    slots, experts_of = came.shape[1], logits.shape[1]
    low = jnp.bfloat16
    place.meet(True, True)
    router_grad[...] = jnp.zeros_like(router_grad)
    gain_grad[...] = jnp.zeros_like(gain_grad)

    def band(piece):
        return pl.ds(pl.multiple_of(piece * rows, rows), rows)

    def scaled_of(piece):
        return hidden[band(piece), :] * factor[band(piece), :]

    def gather(piece):
        here = band(piece)
        numbers = lax.broadcasted_iota(jnp.int32, (rows, slots), 1)
        chosen = [(marks[here, SLOTS + way : SLOTS + way + 1] == numbers).astype(low) for way in range(2)]
        result = hidden[here, :]
        grad = grads[here, :].astype(jnp.float32)
        lane = lax.broadcasted_iota(jnp.int32, (rows, 128), 1)
        stats = jnp.zeros((rows, 128), jnp.float32)
        for way in range(2):
            value = jnp.dot(chosen[way], came[0], preferred_element_type=jnp.float32)
            result = result + gates[here, way : way + 1] * value
            stats = jnp.where(lane == way, jnp.sum(value * grad, axis=1, keepdims=True), stats)
        total = jnp.dot(chosen[0] + chosen[1], came[1], preferred_element_type=jnp.float32)
        row_grads[piece] = total
        inner = jnp.sum(total * scaled_of(piece) * gain[...], axis=1, keepdims=True)
        exchange.start(piece, jnp.where(lane == 2, inner, stats))
        giving.start(piece, result.astype(low))

    def settle(piece):
        here = band(piece)
        stats = exchange.total(piece, rows)
        logit_grad = pair_grad(
            [gates[here, way : way + 1] for way in range(2)],
            [stats[:, way : way + 1] for way in range(2)],
            [marks[here, ROUTES_TWO + way : ROUTES_TWO + way + 1] for way in range(2)],
            experts_of,
        )
        mean = (
            stats[:, 2:3] + jnp.sum(logit_grad * logits[here, :], axis=1, keepdims=True)
        ) / (width * place.parts)
        scaled = scaled_of(piece)
        grad = row_grads[piece] + precise_dot(logit_grad, router_t[...])
        gain_grad[...] += jnp.sum(grad * scaled, axis=0, keepdims=True)
        router_grad[...] += precise_dot(logit_grad, scaled * gain[...], (0, 0))
        result = grads[here, :].astype(jnp.float32) + factor[here, :] * (
            grad * gain[...] - scaled * mean
        )
        hidden_grad[here, :] = result
        ready[0, piece] = result.astype(low)
        spread.first(piece)

    def step(turn, carry):
        when(turn < pieces, gather, turn)
        when((turn >= 2) & (turn <= pieces + 1), settle, turn - 2)
        when(turn >= 3, spread.second, turn - 3)
        return carry

    lax.fori_loop(0, pieces + 3, step, 0)

    def last(piece, carry):
        spread.third(piece)
        spread.finish(piece)
        exchange.finish(piece)
        giving.finish(piece)
        return carry

    lax.fori_loop(0, pieces, last, 0)


def settle(came, marks, gates, logits, factor, hidden, grads, gain, router_t, pieces, collective):
    groups, parts = lax.axis_size("expert"), lax.axis_size("tensor")
    tokens, width = hidden.shape
    rows = tokens // pieces
    low, full = jnp.bfloat16, jnp.float32
    inside = pl.BlockSpec(memory_space=pltpu.VMEM)
    anywhere = pl.BlockSpec(memory_space=pl.ANY)
    return pl.pallas_call(
        settle_kernel,
        out_shape=(
            jax.ShapeDtypeStruct((groups, tokens // groups, width), low),
            jax.ShapeDtypeStruct((tokens, width), full),
            jax.ShapeDtypeStruct((1, pieces, rows, width * parts), low),
            jax.ShapeDtypeStruct(router_t.shape, full),
            jax.ShapeDtypeStruct((1, width), full),
        ),
        in_specs=[inside] * 9,
        out_specs=(anywhere, inside, anywhere, inside, inside),
        scratch_shapes=[
            pltpu.VMEM((pieces, rows, width), full),
            pltpu.VMEM((1, pieces, rows, width), low),
        ]
        + Exchange.scratch(pieces, parts, rows, 8)
        + Return.scratch(pieces, rows, width, groups)
        + Spread.scratch(pieces, parts // 2),
        compiler_params=pltpu.CompilerParams(
            collective_id=collective, has_side_effects=True, vmem_limit_bytes=48 * MIB
        ),
        cost_estimate=lasting(30),
    )(came, marks, gates, logits, factor, hidden, grads, gain, router_t)


def dot_tn(left, right):
    return lax.dot_general(
        left, right, (((0,), (0,)), ((), ())), preferred_element_type=jnp.float32
    )


def bands(tokens):
    size = 256 if tokens % 256 == 0 else tokens
    return [(first, size) for first in range(0, tokens, size)]


def sequence_starts(lengths):
    starts = [0]
    for number in range(lengths.shape[1] - 1):
        starts.append(starts[-1] + lengths[0, number])
    return starts


def masked_scores(query, keys, lengths, first, size, column):
    last = first + size
    scores = dot_nt(query[first:last, column], keys[:last, column]) * (1.0 / math.sqrt(HEAD))
    place = lax.broadcasted_iota(jnp.int32, (size, 1), 0) + first
    start = jnp.zeros((size, 1), jnp.int32)
    for value in sequence_starts(lengths)[1:]:
        start = jnp.where(place >= value, value, start)
    other = lax.broadcasted_iota(jnp.int32, (size, last), 1)
    return jnp.where((other >= start) & (place >= other), scores, MASKED)


def chosen_gates(logits, names):
    lane = lax.broadcasted_iota(jnp.int32, logits.shape, 1)
    picked = [
        jnp.sum(jnp.where(name == lane, logits, 0.0), axis=1, keepdims=True) for name in names
    ]
    top = jnp.maximum(picked[0], picked[1])
    expo = [jnp.exp(value - top) for value in picked]
    total = expo[0] + expo[1]
    return [value / total for value in expo]


def front_kernel(sharers, *refs):
    (
        resid, gain, router_t, w_query, w_key, w_value, w_out, cosines, sines,
        marks, mark_rows, gain_two, router_two_t, lengths, dealt,
        normed_t, cosine, sine, factor, logits, gates, gate_local, query, keys, values, heads, log_total,
        hidden, factor_two, logits_two, gates_two, sent_rows, lines,
        grads_back, grads_out, inbox_grads,
        normed_two, grads_here, grads_slots,
        deal_send, deal_land, load_sem,
    ), refs = refs[:42], refs[42:]
    place = Place()
    spread = Spread(place, grads_slots, inbox_grads, refs[:6], True, sharers)
    exchange = Exchange(place, refs[6:10])
    collect = Collect(place, refs[10:])
    tokens, columns = query.shape
    width = hidden.shape[1]
    groups = place.groups
    capacity = sent_rows.shape[1]
    experts_of = logits.shape[1]
    held = gate_local.shape[1]
    span = columns // held
    low = jnp.bfloat16
    parts = list(enumerate(bands(tokens)))
    place.meet(True, True)

    def deal_copy(step, index):
        peer = flip(place.expert, step, groups)
        return remote(
            dealt.at[peer],
            grads_back.at[index],
            deal_send.at[step],
            deal_land.at[step],
            place.device(peer, place.tensor),
        )

    for step in range(1, groups):
        deal_copy(step, place.expert).start()
    own = pltpu.make_async_copy(
        dealt.at[place.expert], grads_back.at[place.expert], deal_send.at[0]
    )
    own.start()
    router_high = router_t[...].astype(low)
    router_rest = (router_t[...] - router_high.astype(jnp.float32)).astype(low)
    columns_here = pl.ds(pl.multiple_of(place.tensor * width, 128), width)
    for _, (first, size) in parts:
        rows = slice(first, first + size)
        spot = lax.broadcasted_iota(jnp.int32, (size, 1), 0) + first
        start_cosine = jnp.broadcast_to(cosines[0:1, :], (size, HEAD))
        start_sine = jnp.broadcast_to(sines[0:1, :], (size, HEAD))
        for start in sequence_starts(lengths)[1:]:
            start_cosine = jnp.where(spot >= start, cosines[pl.ds(start, 1), :], start_cosine)
            start_sine = jnp.where(spot >= start, sines[pl.ds(start, 1), :], start_sine)
        lane = lax.broadcasted_iota(jnp.int32, (size, HEAD), 1)
        cosine[rows, :] = cosines[rows, :] * start_cosine + sines[rows, :] * start_sine
        turned = sines[rows, :] * start_cosine - cosines[rows, :] * start_sine
        sine[rows, :] = jnp.where(lane < HEAD // 2, -turned, turned)
        value = resid[rows, :].astype(jnp.float32)
        scale = lax.rsqrt(jnp.mean(value * value, axis=1, keepdims=True) + EPSILON)
        value = value * scale * gain[...]
        high = value.astype(low)
        rest = (value - high.astype(jnp.float32)).astype(low)
        factor[rows, :] = scale
        normed_t[:, rows] = high.T
        known = sum(
            dot_nt(left, right)
            for left, right in ((high, router_high), (high, router_rest), (rest, router_high))
        )
        logits[rows, :] = known
        names = [marks[rows, ROUTES + way : ROUTES + way + 1] for way in range(2)]
        pair = chosen_gates(known, names)
        for way in range(2):
            gates[rows, way : way + 1] = pair[way]
        for number in range(held):
            expert = place.tensor * held + number
            gate_local[rows, number : number + 1] = sum(
                jnp.where(name == expert, gate, 0.0) for name, gate in zip(names, pair)
            )
        values[rows, :] = jnp.dot(
            high, w_value[...], preferred_element_type=jnp.float32
        ).astype(low)
        for weight, out in ((w_query, query), (w_key, keys)):
            flat = jnp.dot(high, weight[...], preferred_element_type=jnp.float32)
            for head in range(columns // HEAD):
                column = slice(head * HEAD, (head + 1) * HEAD)
                part = flat[:, column]
                turned = pltpu.roll(part, HEAD // 2, 1)
                out[rows, column] = (part * cosine[rows, :] + turned * sine[rows, :]).astype(low)

    def selection(expert):
        number = lax.broadcasted_iota(jnp.int32, (capacity, tokens), 0) + expert * capacity
        return ((mark_rows[0:1, :] == number) | (mark_rows[1:2, :] == number)).astype(low)

    early = min(FRONT, groups)

    keep = pltpu.make_async_copy(grads_slots.at[0], grads_out, load_sem.at[groups])

    def take_grads():
        own.wait()
        bucket = grads_back.shape[1]
        for step in range(1, groups):
            deal_copy(step, flip(place.expert, step, groups)).wait_recv()
        fetches = [
            pltpu.make_async_copy(
                grads_back.at[group], grads_here.at[pl.ds(group * bucket, bucket)], load_sem.at[group]
            )
            for group in range(groups)
        ]
        for fetch in fetches:
            fetch.start()
        for fetch in fetches:
            fetch.wait()
        for expert in range(sent_rows.shape[0]):
            grads_slots[0, expert] = jnp.dot(
                selection(expert), grads_here[...], preferred_element_type=jnp.float32
            ).astype(low)
        keep.start()
        spread.start(min(AHEAD, early - 1))

    def tick(number):
        if number < early:
            spread.first(jnp.int32(number))
        if number + 1 + AHEAD < early:
            spread.send(jnp.int32(number + 1 + AHEAD))
        if 1 <= number <= early:
            spread.second(jnp.int32(number - 1))

    def attend_band(number, first, size):
        last = first + size
        rows = slice(first, last)
        for head in range(columns // HEAD):
            column = slice(head * HEAD, (head + 1) * HEAD)
            scores = masked_scores(query, keys, lengths, first, size, column)
            top = jnp.max(scores, axis=1, keepdims=True)
            expo = jnp.exp(scores - top)
            total = jnp.sum(expo, axis=1, keepdims=True)
            probs = (expo / total).astype(low)
            heads[rows, column] = jnp.dot(
                probs, values[:last, column], preferred_element_type=jnp.float32
            ).astype(low)
            log_total[rows, head : head + 1] = top + jnp.log(total)
        collect.free_stage(jnp.int32(number))
        for spot in range(place.spots):
            for core in range(2):
                start = (spot * 2 + core) * width
                total = None
                for expert in range(held):
                    inner = slice(expert * span, (expert + 1) * span)
                    term = gate_local[rows, expert : expert + 1] * jnp.dot(
                        heads[rows, inner],
                        w_out[inner, start : start + width],
                        preferred_element_type=jnp.float32,
                    )
                    total = term if total is None else total + term
                collect.stage[number % collect.slots, 0, spot, core] = total.astype(low)
        collect.first(jnp.int32(number))

    blank = jnp.zeros((128 - router_two_t.shape[0], width), jnp.float32)
    router_wide = jnp.concatenate([router_two_t[...], blank], axis=0)

    def measure(number, first, size):
        rows = slice(first, first + size)
        value = resid[rows, columns_here].astype(jnp.float32) + collect.third(jnp.int32(number))[0]
        hidden[rows, :] = value
        squares = jnp.sum(value * value, axis=1, keepdims=True)
        known = precise_dot(value * gain_two[...], router_wide, (1, 1))
        lane = lax.broadcasted_iota(jnp.int32, known.shape, 1)
        exchange.start(number, jnp.where(lane == SQUARES, squares, known))

    def conclude(number, first, size):
        rows = slice(first, first + size)
        total = exchange.total(number, size)
        scale = lax.rsqrt(total[:, SQUARES : SQUARES + 1] / (width * place.parts) + EPSILON)
        known = total[:, : logits_two.shape[1]] * scale
        factor_two[rows, :] = scale
        logits_two[rows, :] = known
        names = [marks[rows, ROUTES_TWO + way : ROUTES_TWO + way + 1] for way in range(2)]
        pair = chosen_gates(known, names)
        for way in range(2):
            gates_two[rows, way : way + 1] = pair[way]
        normed_two[rows, :] = (hidden[rows, :] * scale * gain_two[...]).astype(low)

    count = len(parts)
    for turn in range(count + 3):
        if turn < count:
            attend_band(turn, *parts[turn][1])
        if 2 <= turn < count + 2:
            measure(turn - 2, *parts[turn - 2][1])
        if 1 <= turn < count + 1:
            collect.second(jnp.int32(turn - 1))
        if turn >= 3:
            conclude(turn - 3, *parts[turn - 3][1])
        if turn == count:
            take_grads()
        if turn > count:
            tick(turn - count - 1)
    for expert in range(sent_rows.shape[0]):
        sent_rows[expert] = jnp.dot(
            selection(expert), normed_two[...], preferred_element_type=jnp.float32
        ).astype(low)
        wide = lines.shape[2]
        lane = lax.broadcasted_iota(jnp.int32, (tokens, wide), 1)
        number = jnp.where(lane < capacity, lane + expert * capacity, -1)
        line = sum(
            jnp.where(
                marks[:, SLOTS + way : SLOTS + way + 1] == number, gates_two[:, way : way + 1], 0.0
            )
            for way in range(2)
        )
        lines[expert] = jnp.broadcast_to(jnp.sum(line, axis=0, keepdims=True), lines.shape[1:])
    for number in range(2, early + 1):
        tick(number)
    keep.wait()
    for step in range(1, groups):
        deal_copy(step, place.expert).wait_send()
    for number in range(count):
        exchange.finish(number)
    collect.finish()

    def last(number, carry):
        spread.third(number)
        spread.finish(number)
        return carry

    lax.fori_loop(0, early, last, 0)


def front(
    resid, gain, router_t, weights, w_out, tables, marks, mark_rows, gain_two, router_two_t,
    lengths, dealt, capacity, sharers, collective,
):
    groups, parts = lax.axis_size("expert"), lax.axis_size("tensor")
    tokens, model_width = resid.shape
    columns = weights[0].shape[1]
    width = dealt.shape[2]
    experts_of = router_t.shape[0]
    held = columns // (QH * HEAD)
    slots_of = router_two_t.shape[0]
    low, full = jnp.bfloat16, jnp.float32
    block = jax.ShapeDtypeStruct((tokens, columns), low)
    wide = (capacity + 127) // 128 * 128
    inside = pl.BlockSpec(memory_space=pltpu.VMEM)
    anywhere = pl.BlockSpec(memory_space=pl.ANY)

    def column(count):
        return jax.ShapeDtypeStruct((tokens, count), full)

    pieces = len(bands(tokens))
    dma = pltpu.SemaphoreType.DMA
    return pl.pallas_call(
        functools.partial(front_kernel, sharers),
        out_shape=(
            jax.ShapeDtypeStruct((model_width, tokens), low),
            column(HEAD),
            column(HEAD),
            column(1),
            column(experts_of),
            column(2),
            column(held),
            block,
            block,
            block,
            block,
            column(columns // HEAD),
            column(width),
            column(1),
            column(slots_of),
            column(2),
            jax.ShapeDtypeStruct((slots_of, capacity, width), low),
            jax.ShapeDtypeStruct((slots_of, 8, wide), full),
            jax.ShapeDtypeStruct(dealt.shape, low),
            jax.ShapeDtypeStruct((slots_of, capacity, width), low),
            jax.ShapeDtypeStruct((1, groups, capacity, model_width), low),
        ),
        in_specs=[inside] * 13 + [pl.BlockSpec(memory_space=pltpu.SMEM), anywhere],
        out_specs=(inside,) * 18 + (anywhere,) * 3,
        scratch_shapes=[
            pltpu.VMEM((tokens, width), low),
            pltpu.VMEM((tokens, width), low),
            pltpu.VMEM((1, slots_of, capacity, width), low),
            dma((groups,)),
            dma((groups,)),
            dma((groups + 1,)),
        ]
        + Spread.scratch(groups, parts // 2)
        + Exchange.scratch(pieces, parts, tokens // pieces, 16)
        + Collect.scratch(pieces, 1, parts // 2, tokens // pieces, width, pieces),
        compiler_params=pltpu.CompilerParams(
            collective_id=collective, has_side_effects=True, vmem_limit_bytes=58 * MIB
        ),
        cost_estimate=lasting(60),
    )(
        resid, gain, router_t, *weights, w_out, *tables, marks, mark_rows, gain_two, router_two_t,
        lengths, dealt,
    )


def attend_back_kernel(
    grads, w_out, gates, heads, query, keys, values, log_total, cosine, sine, lengths,
    query_grad, key_grad, value_grad, gate_grad, gated_t,
    heads_grad, key_sum, value_sum,
):
    tokens, columns = query.shape
    low = jnp.bfloat16
    span = columns // gates.shape[1]
    scale = 1.0 / math.sqrt(HEAD)
    for first, size in bands(tokens):
        rows = slice(first, first + size)
        plain = dot_nt(grads[rows, :], w_out[...])
        for expert in range(gates.shape[1]):
            column = slice(expert * span, (expert + 1) * span)
            gate = gates[rows, expert : expert + 1]
            head = heads[rows, column].astype(jnp.float32)
            gate_grad[rows, expert : expert + 1] = jnp.sum(
                plain[:, column] * head, axis=1, keepdims=True
            )
            heads_grad[rows, column] = (plain[:, column] * gate).astype(low)
            gated_t[column, rows] = (head * gate).T.astype(low)

    def unturn(value, rows):
        turned = pltpu.roll(value * sine[rows, :], HEAD // 2, 1)
        return value * cosine[rows, :] + turned

    for head in range(columns // HEAD):
        column = slice(head * HEAD, (head + 1) * HEAD)
        for first, size in bands(tokens):
            last = first + size
            rows = slice(first, last)
            scores = masked_scores(query, keys, lengths, first, size, column)
            probs = jnp.exp(scores - log_total[rows, head : head + 1])
            value_part = dot_tn(probs.astype(low), heads_grad[rows, column])
            prob_grad = dot_nt(heads_grad[rows, column], values[:last, column])
            score_grad = (
                probs * (prob_grad - jnp.sum(probs * prob_grad, axis=1, keepdims=True))
            ).astype(low)
            query_grad[rows, column] = unturn(
                jnp.dot(score_grad, keys[:last, column], preferred_element_type=jnp.float32)
                * scale,
                rows,
            ).astype(low)
            key_part = dot_tn(score_grad, query[rows, column])
            if first:
                value_sum[:first, :] += value_part[:first]
                key_sum[:first, :] += key_part[:first]
            value_sum[rows, :] = value_part[first:]
            key_sum[rows, :] = key_part[first:]
        whole = slice(0, tokens)
        key_grad[:, column] = unturn(key_sum[...] * scale, whole).astype(low)
        value_grad[:, column] = value_sum[...].astype(low)


def attend_back(grads, w_out, gates, heads, query, keys, values, log_total, cosine, sine, lengths):
    tokens, model_width = grads.shape
    columns = query.shape[1]
    low, full = jnp.bfloat16, jnp.float32
    block = jax.ShapeDtypeStruct((tokens, columns), low)
    inside = pl.BlockSpec(memory_space=pltpu.VMEM)
    return pl.pallas_call(
        attend_back_kernel,
        out_shape=(
            block,
            block,
            block,
            jax.ShapeDtypeStruct(gates.shape, full),
            jax.ShapeDtypeStruct((columns, tokens), low),
        ),
        in_specs=[inside] * 10 + [pl.BlockSpec(memory_space=pltpu.SMEM)],
        out_specs=(inside,) * 5,
        scratch_shapes=[
            pltpu.VMEM((tokens, columns), low),
            pltpu.VMEM((tokens, HEAD), full),
            pltpu.VMEM((tokens, HEAD), full),
        ],
        compiler_params=pltpu.CompilerParams(vmem_limit_bytes=56 * MIB),
        cost_estimate=lasting(25),
    )(
        grads, w_out, gates, heads, query, keys, values, log_total, cosine, sine, lengths
    )


def body(
    tokens,
    out_grad,
    attn_gain,
    attn_router,
    w_query,
    w_key,
    w_value,
    w_out,
    mlp_gain,
    mlp_router,
    w_gate,
    w_up,
    w_down,
    deal,
    seq_lengths,
    attn_routes,
    mlp_routes,
    slot_order,
):
    tok_rows, model_width = tokens.shape
    group_count = lax.axis_size("expert")
    part_count = lax.axis_size("tensor")
    group_index = lax.axis_index("expert")
    part_index = lax.axis_index("tensor")
    bucket_rows = tok_rows // group_count
    col_width = model_width // part_count
    col_first = part_index * col_width
    low = jnp.bfloat16

    def own_cols(values):
        return lax.dynamic_slice_in_dim(values, col_first, col_width, values.ndim - 1)

    deal_rank = deal // tok_rows * bucket_rows + (deal % tok_rows - group_index * bucket_rows)
    row_ids = jnp.arange(tok_rows, dtype=jnp.int32)
    expert_count = mlp_router.shape[1]
    experts_of = attn_router.shape[1]
    sharers = group_count // expert_count
    capacity = 5 * tok_rows // (2 * expert_count)
    slots = expert_count * capacity
    pieces = 4
    orders = slot_order[0].reshape(tok_rows, 2)
    rows_in = jnp.concatenate([attn_routes.T, mlp_routes.T, orders.T, orders.T], axis=0)
    resid_low, dealt_grads, marks, mark_rows = deal_rows(
        tokens, out_grad, deal_rank[None], rows_in, capacity, expert_count, 0
    )
    resid_low = resid_low.reshape(tok_rows, model_width)
    gain_one, gain_two = own_cols(attn_gain), own_cols(mlp_gain)
    router_one, router_two = own_cols(attn_router.T), own_cols(mlp_router.T)
    (
        normed_t, cosine, sine, factor_one, attn_logits, attn_gates, gate_local, query, keys, values,
        heads_low, log_total, hidden, factor_two, mlp_logits, mlp_gates, slot_rows, gate_lines,
        grad_cols_low, slot_grads, early_grads,
    ) = front(
        resid_low,
        attn_gain[None],
        attn_router.T,
        (w_query, w_key, w_value),
        w_out,
        rotary_tables(tok_rows),
        marks,
        mark_rows,
        gain_two[None],
        router_two,
        seq_lengths,
        dealt_grads,
        capacity,
        sharers,
        1,
    )
    grad_cols_low = grad_cols_low.reshape(tok_rows, col_width)
    inbox, _, slot_grads, middle, gate_grad, up_grad, returned = experts(
        slot_rows,
        slot_grads,
        early_grads,
        gate_lines,
        w_gate[0],
        w_up[0],
        w_down[0],
        sharers,
        2,
    )
    if sharers > 1:
        returned = (
            jnp.sum(
                returned.reshape(2, expert_count, sharers, capacity, col_width).astype(jnp.float32),
                axis=2,
            )
        ).astype(low)
    back_mixed, hidden_grad, hidden_grad_low, mlp_router_grad, mlp_gain_grad = settle(
        returned.reshape(2, slots, col_width),
        marks,
        mlp_gates,
        mlp_logits,
        factor_two,
        hidden,
        grad_cols_low,
        gain_two[None],
        router_two,
        pieces,
        4,
    )
    back_mixed = back_mixed.reshape(tok_rows, col_width)
    hidden_grad_low = hidden_grad_low.reshape(tok_rows, model_width)
    query_pre_grad, key_pre_grad, value_pre_grad, local_gate_grad, gated_t = attend_back(
        hidden_grad_low,
        w_out,
        gate_local,
        heads_low,
        query,
        keys,
        values,
        log_total,
        cosine,
        sine,
        seq_lengths,
    )
    rows = inbox.reshape(-1, model_width)
    units = middle.shape[2]
    middle, gate_grad, up_grad = (
        jnp.pad(values.reshape(-1, units), ((0, 0), (0, -units % 128)))
        for values in (middle, gate_grad, up_grad)
    )
    *weight_grads, back_grad, small, gate_w_grad, up_w_grad, down_grad = closing(
        normed_t,
        (
            gain_one[None],
            factor_one,
            attn_gates,
            marks,
            attn_logits,
            local_gate_grad,
            router_one,
            mlp_gain_grad,
            mlp_router_grad,
        ),
        (query_pre_grad, key_pre_grad, value_pre_grad),
        gated_t,
        hidden_grad_low,
        hidden_grad,
        resid_low,
        (w_query, w_key, w_value),
        (rows, rows, middle),
        (gate_grad, up_grad, slot_grads.reshape(-1, model_width)),
        pieces,
        3,
    )
    back_grad = back_grad.reshape(tok_rows, col_width)
    weight_grads = [grad.astype(jnp.float32) for grad in weight_grads]
    deal_mask = (row_ids[:, None] == deal_rank[None, :]).astype(low)
    mixed, tokens_grad = (
        jnp.einsum("ri,rc->ic", deal_mask, back, preferred_element_type=jnp.float32).astype(low)
        for back in (back_mixed, back_grad)
    )
    small = small.transpose(1, 0, 2).reshape(-1, model_width)
    return (
        mixed,
        tokens_grad,
        small[0],
        small[1 : 1 + experts_of].T,
        weight_grads[0],
        weight_grads[1],
        weight_grads[2],
        weight_grads[3],
        small[1 + experts_of],
        small[2 + experts_of : 2 + experts_of + expert_count].T,
        gate_w_grad[None, :, :units].astype(jnp.float32),
        up_w_grad[None, :, :units].astype(jnp.float32),
        down_grad[None, :units].astype(jnp.float32),
    )


def solution(mesh):
    placed = (
        P("expert", None),
        P("expert", None),
        P(),
        P(),
        P(None, "tensor"),
        P(None, "tensor"),
        P(None, "tensor"),
        P("tensor", None),
        P(),
        P(),
        P("expert", None, "tensor"),
        P("expert", None, "tensor"),
        P("expert", "tensor", None),
        P("expert"),
        P("expert", None),
        P("expert", None),
        P("expert", None),
        P("expert", None),
    )
    return jax.shard_map(
        body,
        mesh=mesh,
        in_specs=placed,
        out_specs=(
            P("expert", "tensor"),
            P("expert", "tensor"),
            P(),
            P(),
            P(None, "tensor"),
            P(None, "tensor"),
            P(None, "tensor"),
            P("tensor", None),
            P(),
            P(),
            P("expert", None, "tensor"),
            P("expert", None, "tensor"),
            P("expert", "tensor", None),
        ),
        check_vma=False,
    )
```

```python
import functools
import math

import jax
import jax.numpy as jnp
import numpy as np
from jax import lax
from jax.experimental import pallas as pl
from jax.experimental.pallas import tpu as pltpu
from jax.sharding import PartitionSpec as P

HEAD = 128
QH = 2


EPSILON = 1e-06
MASKED = -1e30


def rotary_tables(tokens):
    frequency = np.exp(-math.log(10000.0) * np.arange(0, HEAD, 2, dtype=np.float32) / HEAD)
    angles = np.arange(tokens, dtype=np.float32)[:, None] * frequency.astype(np.float32)[None, :]
    angles = np.concatenate([angles, angles], axis=1).astype(np.float64)
    return jnp.asarray(np.cos(angles), jnp.float32), jnp.asarray(np.sin(angles), jnp.float32)


MESH = pl.DeviceIdType.MESH
MIB = 1 << 20
AHEAD_DEAL = 2
AHEAD = 2
FRONT = 3
SQUARES = 8
ROUTES, ROUTES_TWO, SLOTS = 0, 2, 4


def flip(number, other, count):
    total, bit = 0, 1
    while bit < count:
        total = total + lax.rem(lax.div(number, bit) + lax.div(other, bit), 2) * bit
        bit *= 2
    return total


def dot_nt(left, right):
    return lax.dot_general(
        left, right, (((1,), (1,)), ((), ())), preferred_element_type=jnp.float32
    )


class Place:
    def __init__(self):
        self.groups = lax.axis_size("expert")
        self.parts = lax.axis_size("tensor")
        self.spots = self.parts // 2
        self.expert = lax.axis_index("expert")
        self.tensor = lax.axis_index("tensor")
        self.spot = lax.div(self.tensor, 2)
        self.core = lax.rem(self.tensor, 2)

    def device(self, expert, tensor):
        return {"expert": expert, "tensor": tensor}

    def across(self, step):
        return lax.rem(self.spot + step, self.spots) * 2 + self.core

    def before(self, step):
        return lax.rem(self.spot + self.spots - step, self.spots) * 2 + self.core

    def meet(self, over_expert, whole_tensor=False):
        if whole_tensor:
            peers = [self.device(self.expert, self.along(step)) for step in range(1, self.parts)]
        else:
            peers = [self.device(self.expert, self.spot * 2 + 1 - self.core)]
            for step in range(1, self.spots):
                peers.append(self.device(self.expert, self.across(step)))
        if over_expert:
            for step in range(1, self.groups):
                peers.append(self.device(flip(self.expert, step, self.groups), self.tensor))
        barrier = pltpu.get_barrier_semaphore()
        for peer in peers:
            pl.semaphore_signal(barrier, inc=1, device_id=peer, device_id_type=MESH)
        pl.semaphore_wait(barrier, len(peers))

    def along(self, step):
        return lax.rem(self.tensor + step, self.parts)


def lasting(microseconds):
    return pl.CostEstimate(
        flops=0, bytes_accessed=int(microseconds * 3_000_000), transcendentals=0
    )


def remote(source, target, send, receive, device):
    return pltpu.make_async_remote_copy(
        src_ref=source,
        dst_ref=target,
        send_sem=send,
        recv_sem=receive,
        device_id=device,
        device_id_type=MESH,
    )


class Spread:
    @staticmethod
    def scratch(chunks, spots):
        return [
            pltpu.SemaphoreType.DMA((chunks,)),
            pltpu.SemaphoreType.DMA((chunks,)),
            pltpu.SemaphoreType.DMA((chunks, max(spots - 1, 1))),
            pltpu.SemaphoreType.DMA((chunks, max(spots - 1, 1))),
            pltpu.SemaphoreType.DMA((chunks, spots)),
            pltpu.SemaphoreType.DMA((chunks, spots)),
        ]

    def __init__(self, place, source, target, sems, over_expert, sharers=1, by_group=None):
        self.place, self.source, self.target = place, source, target
        self.by_group = over_expert if by_group is None else by_group
        self.first_send, self.first_land, self.side_send, self.side_land, self.core_send, self.core_land = sems
        self.over_expert, self.sharers = over_expert, sharers
        self.width = source.shape[3]
        self.chunks = target.shape[1]

    def owner(self, chunk):
        if not self.by_group:
            return chunk
        half, odd, pair = self.place.groups // 2, lax.rem(chunk, 2), lax.div(chunk, 2)
        even_way = jnp.minimum(chunk, 1) * half + pair
        odd_way = pair + (1 - jnp.minimum(pair, 1)) * half
        return flip(
            self.place.expert, odd * odd_way + (1 - odd) * even_way, self.place.groups
        )

    def spot_of(self, owner, tensor):
        first = pl.multiple_of(tensor * self.width, 128)
        return self.target.at[:, owner, :, pl.ds(first, self.width)]

    def block(self, owner):
        if self.sharers == 1:
            return self.source.at[:, owner]
        return self.source.at[:, lax.div(owner, self.sharers)]

    def send(self, chunk):
        place = self.place
        peer = self.owner(chunk)
        remote(
            self.block(peer),
            self.spot_of(place.expert, place.tensor),
            self.first_send.at[chunk],
            self.first_land.at[chunk],
            place.device(peer, place.tensor),
        ).start()

    def start(self, ahead):
        place = self.place
        own = self.owner(0)
        if not self.over_expert:
            return
        for chunk in range(1, min(ahead + 1, self.chunks)):
            self.send(chunk)
        copy = pltpu.make_async_copy(
            self.block(own), self.spot_of(own, place.tensor), self.first_send.at[0]
        )
        copy.start()
        copy.wait()

    def first(self, chunk):
        place = self.place
        owner = self.owner(chunk)
        mine = self.spot_of(owner, place.tensor)
        if self.over_expert:

            @pl.when(chunk > 0)
            def _():
                remote(
                    self.block(owner),
                    mine,
                    self.first_send.at[chunk],
                    self.first_land.at[chunk],
                    place.device(owner, place.tensor),
                ).wait_recv()

            held = mine
        else:
            pltpu.make_async_copy(self.block(owner), mine, self.first_send.at[chunk]).start()
            held = self.block(owner)
        for step in range(1, place.spots):
            remote(
                held,
                mine,
                self.side_send.at[chunk, step - 1],
                self.side_land.at[chunk, step - 1],
                place.device(place.expert, place.across(step)),
            ).start()
        remote(
            held,
            mine,
            self.core_send.at[chunk, 0],
            self.core_land.at[chunk, 0],
            place.device(place.expert, place.spot * 2 + 1 - place.core),
        ).start()

    def second(self, chunk):
        place = self.place
        owner = self.owner(chunk)
        for step in range(1, place.spots):
            came = self.spot_of(owner, place.before(step))
            remote(
                came,
                came,
                self.side_send.at[chunk, step - 1],
                self.side_land.at[chunk, step - 1],
                place.device(place.expert, place.across(step)),
            ).wait_recv()
            remote(
                came,
                came,
                self.core_send.at[chunk, step],
                self.core_land.at[chunk, step],
                place.device(place.expert, place.spot * 2 + 1 - place.core),
            ).start()

    def third(self, chunk):
        place = self.place
        owner = self.owner(chunk)
        flipped = 1 - 2 * place.core
        if not self.over_expert:
            mine = self.spot_of(owner, place.tensor)
            pltpu.make_async_copy(self.block(owner), mine, self.first_send.at[chunk]).wait()
        for step in range(place.spots):
            came = self.spot_of(owner, place.before(step) + flipped)
            remote(
                came,
                came,
                self.core_send.at[chunk, step],
                self.core_land.at[chunk, step],
                place.device(place.expert, place.spot * 2 + 1 - place.core),
            ).wait_recv()

    def finish(self, chunk):
        place = self.place
        owner = self.owner(chunk)
        mine = self.spot_of(owner, place.tensor)
        device = place.device(place.expert, place.tensor)
        if self.over_expert:

            @pl.when(chunk > 0)
            def _():
                remote(
                    self.block(owner),
                    mine,
                    self.first_send.at[chunk],
                    self.first_land.at[chunk],
                    device,
                ).wait_send()

        for step in range(1, place.spots):
            remote(
                mine,
                mine,
                self.side_send.at[chunk, step - 1],
                self.side_land.at[chunk, step - 1],
                device,
            ).wait_send()
        for step in range(place.spots):
            remote(
                mine, mine, self.core_send.at[chunk, step], self.core_land.at[chunk, step], device
            ).wait_send()


class Collect:
    @staticmethod
    def scratch(chunks, kinds, spots, rows, width, slots=2):
        return [
            pltpu.VMEM((slots, kinds, spots, 2, rows, width), jnp.bfloat16),
            pltpu.VMEM((slots, kinds, max(spots - 1, 1), rows, width), jnp.bfloat16),
            pltpu.VMEM((chunks, kinds, spots, rows, width), jnp.bfloat16),
            pltpu.VMEM((chunks, kinds, max(spots - 1, 1), rows, width), jnp.bfloat16),
            pltpu.SemaphoreType.DMA((chunks,)),
            pltpu.SemaphoreType.DMA((chunks,)),
            pltpu.SemaphoreType.DMA((chunks, max(spots - 1, 1))),
            pltpu.SemaphoreType.DMA((chunks, max(spots - 1, 1))),
        ]

    def __init__(self, place, refs):
        self.place = place
        self.stage, self.side, self.core_in, self.side_in = refs[:4]
        self.core_send, self.core_land, self.side_send, self.side_land = refs[4:]
        self.chunks = self.core_in.shape[0]
        self.slots = self.stage.shape[0]

    def core_copy(self, chunk):
        place = self.place
        return remote(
            self.stage.at[lax.rem(chunk, self.slots), :, :, 1 - place.core],
            self.core_in.at[chunk],
            self.core_send.at[chunk],
            self.core_land.at[chunk],
            place.device(place.expert, place.spot * 2 + 1 - place.core),
        )

    def side_copy(self, chunk, step):
        place = self.place
        return remote(
            self.side.at[lax.rem(chunk, self.slots), :, step - 1],
            self.side_in.at[chunk, :, step - 1],
            self.side_send.at[chunk, step - 1],
            self.side_land.at[chunk, step - 1],
            place.device(place.expert, place.across(step)),
        )

    def free_stage(self, chunk):
        @pl.when(chunk >= self.slots)
        def _():
            self.core_copy(chunk - self.slots).wait_send()

    def first(self, chunk):
        self.core_copy(chunk).start()

    def second(self, chunk):
        place = self.place
        slot = lax.rem(chunk, self.slots)
        self.core_copy(chunk).wait_recv()

        @pl.when(chunk >= self.slots)
        def _():
            for step in range(1, place.spots):
                self.side_copy(chunk - self.slots, step).wait_send()

        for step in range(1, place.spots):
            there = lax.rem(place.spot + step, place.spots)
            total = self.stage[slot, :, there, place.core].astype(jnp.float32) + self.core_in[
                chunk, :, there
            ].astype(jnp.float32)
            self.side[slot, :, step - 1] = total.astype(jnp.bfloat16)
            self.side_copy(chunk, step).start()

    def third(self, chunk):
        place = self.place
        slot = lax.rem(chunk, self.slots)
        total = self.stage[slot, :, place.spot, place.core].astype(jnp.float32) + self.core_in[
            chunk, :, place.spot
        ].astype(jnp.float32)
        for step in range(1, place.spots):
            self.side_copy(chunk, step).wait_recv()
            total = total + self.side_in[chunk, :, step - 1].astype(jnp.float32)
        return total

    def finish(self):
        for chunk in range(max(self.chunks - self.slots, 0), self.chunks):
            self.core_copy(chunk).wait_send()
            for step in range(1, self.place.spots):
                self.side_copy(chunk, step).wait_send()


def when(condition, action, *args):
    pl.when(condition)(functools.partial(action, *args))


def columns_of(rows):
    blank = jnp.zeros((128 - rows.shape[0], rows.shape[1]), jnp.float32)
    return jnp.concatenate([rows, blank], axis=0).T


def deal_kernel(
    capacity, experts_of, tokens, out_grad, ranks, rows_in,
    full, dealt_grads, marks, mark_rows,
    held, sending, slots, load_sem, *sems,
):
    place = Place()
    count, width = held.shape[1:]
    groups, bucket, _ = dealt_grads.shape
    low = jnp.bfloat16
    own = pl.ds(pl.multiple_of(place.tensor * width, 128), width)
    loads = [
        pltpu.make_async_copy(source.at[:, own], held.at[number], load_sem.at[number])
        for number, source in enumerate((tokens, out_grad))
    ]
    for load in loads:
        load.start()
    spread = Spread(place, sending, full, sems, True)
    place.meet(True)

    def dealt(number, group):
        rank = lax.broadcasted_iota(jnp.int32, (bucket, count), 0) + group * bucket
        chosen = (ranks[...] == rank).astype(low)
        return jnp.dot(chosen, held[number], preferred_element_type=jnp.float32).astype(low)

    loads[0].wait()
    for group in range(groups):
        sending[0, group] = dealt(0, group)
    spread.start(AHEAD_DEAL)

    def number_slots():
        rows = rows_in[...].astype(jnp.float32)
        columns = columns_of(rows)
        lane = lax.broadcasted_iota(jnp.int32, (count, 128), 1)
        found = jnp.zeros((count, 128), jnp.float32)
        for way in range(2):
            target = columns[:, ROUTES_TWO + way : ROUTES_TWO + way + 1]
            order = columns[:, 4 + way : 5 + way]
            position = jnp.zeros((count, 1), jnp.float32)
            for other in range(2):
                earlier = (rows[ROUTES_TWO + other : ROUTES_TWO + other + 1] == target) & (
                    rows[4 + other : 5 + other] < order
                )
                position = position + jnp.sum(
                    jnp.where(earlier, 1.0, 0.0), axis=1, keepdims=True
                )
            slot = jnp.where(
                position < capacity, target * capacity + position, experts_of * capacity
            )
            marks[:, SLOTS + way : SLOTS + way + 1] = slot.astype(jnp.int32)
            found = jnp.where(lane == way, slot, found)
        marks[:, :SLOTS] = columns[:, :SLOTS].astype(jnp.int32)
        slots[...] = found
        mark_rows[...] = slots[...].T[:8].astype(jnp.int32)

    def deal_grads():
        loads[1].wait()
        for group in range(groups):
            dealt_grads[group] = dealt(1, group)

    def step(turn, carry):
        when(turn < spread.chunks, spread.first, turn)
        when(turn + 1 + AHEAD_DEAL < spread.chunks, spread.send, turn + 1 + AHEAD_DEAL)
        when(turn >= 1, spread.second, turn - 1)
        when(turn == 1, deal_grads)
        when(turn == 2, number_slots)
        return carry

    lax.fori_loop(0, spread.chunks + 1, step, 0)

    def last(turn, carry):
        spread.third(turn)
        spread.finish(turn)
        return carry

    lax.fori_loop(0, spread.chunks, last, 0)


def deal_rows(tokens, out_grad, ranks, rows_in, capacity, experts_of, collective):
    groups, parts = lax.axis_size("expert"), lax.axis_size("tensor")
    count, model_width = tokens.shape
    width, bucket = model_width // parts, count // groups
    low = tokens.dtype
    inside = pl.BlockSpec(memory_space=pltpu.VMEM)
    anywhere = pl.BlockSpec(memory_space=pl.ANY)
    return pl.pallas_call(
        functools.partial(deal_kernel, capacity, experts_of),
        out_shape=(
            jax.ShapeDtypeStruct((1, groups, bucket, model_width), low),
            jax.ShapeDtypeStruct((groups, bucket, width), low),
            jax.ShapeDtypeStruct((count, 8), jnp.int32),
            jax.ShapeDtypeStruct((8, count), jnp.int32),
        ),
        in_specs=[anywhere] * 2 + [inside] * 2,
        out_specs=(anywhere,) + (inside,) * 3,
        scratch_shapes=[
            pltpu.VMEM((2, count, width), low),
            pltpu.VMEM((1, groups, bucket, width), low),
            pltpu.VMEM((count, 128), jnp.float32),
            pltpu.SemaphoreType.DMA((2,)),
        ]
        + Spread.scratch(groups, parts // 2),
        compiler_params=pltpu.CompilerParams(
            collective_id=collective, has_side_effects=True, vmem_limit_bytes=40 * MIB
        ),
        cost_estimate=lasting(35),
    )(tokens, out_grad, ranks, rows_in)


def experts_kernel(sharers, *refs):
    (
        source, source_grads, gates, gate_hbm, up_hbm, down_hbm, early_grads,
        inbox, inbox_grads, grads_out, middle_out, gate_out, up_out, returned,
        gate_w, up_w, down_w, rows, grads, middle, gate_g, up_g, closing, gates_in,
        load_sem, store_sem, back_send, back_land, mark_send, mark_land,
    ) = refs[:30]
    place = Place()
    spread = Spread(place, source, inbox, refs[30:36], True, sharers)
    spread_grads = Spread(place, source_grads, inbox_grads, refs[36:42], True, sharers)
    collect = Collect(place, refs[42:])
    chunks = spread.chunks
    width = source.shape[3]
    units = gate_w.shape[1]
    tile = 704 if units % 704 == 0 else units
    capacity = rows.shape[0]
    loads = [
        pltpu.make_async_copy(held, kept, load_sem.at[number])
        for number, (held, kept) in enumerate(
            ((gate_hbm, gate_w), (up_hbm, up_w), (down_hbm, down_w))
        )
    ]
    for load in loads:
        load.start()
    place.meet(True)

    def mark_copy(chunk):
        peer = spread.owner(chunk)
        return remote(
            gates.at[lax.div(peer, sharers)],
            gates_in.at[place.expert],
            mark_send.at[chunk],
            mark_land.at[chunk],
            place.device(peer, place.tensor),
        )

    def mark_landed(chunk):
        peer = spread.owner(chunk)
        return remote(
            gates.at[lax.div(peer, sharers)],
            gates_in.at[peer],
            mark_send.at[chunk],
            mark_land.at[chunk],
            place.device(peer, place.tensor),
        )

    spread.start(AHEAD)
    for chunk in range(1, chunks):
        mark_copy(chunk).start()
    own_mark = pltpu.make_async_copy(
        gates.at[lax.div(place.expert, sharers)], gates_in.at[place.expert], mark_send.at[0]
    )
    own_mark.start()
    own_mark.wait()
    early = min(FRONT, chunks)
    for chunk in range(early, min(AHEAD + 1, chunks)):
        spread_grads.send(chunk)

    def stores(owner):
        return [
            pltpu.make_async_copy(held, out.at[owner], store_sem.at[number])
            for number, (held, out) in enumerate(
                ((middle, middle_out), (gate_g, gate_out), (up_g, up_out), (grads, grads_out))
            )
        ]

    def fetches(owner):
        return [
            pltpu.make_async_copy(inbox.at[0, owner], rows, load_sem.at[3]),
            pltpu.make_async_copy(early_grads.at[0, owner], grads, load_sem.at[4]),
            pltpu.make_async_copy(inbox_grads.at[0, owner], grads, load_sem.at[4]),
        ]

    def work(chunk):
        owner = spread.owner(chunk)

        @pl.when(chunk == 0)
        def _():
            for load in loads:
                load.wait()

        @pl.when(chunk > 0)
        def _():
            for store in stores(spread.owner(chunk - 1)):
                store.wait()
            mark_landed(chunk).wait_recv()

        spread.third(chunk)
        when(chunk >= early, spread_grads.third, chunk)
        fetch, fetch_early, fetch_late = fetches(owner)
        fetch.start()
        when(chunk < early, fetch_early.start)
        when(chunk >= early, fetch_late.start)
        fetch.wait()
        fetch_early.wait()
        wide = gates_in.shape[2]
        line = jnp.broadcast_to(gates_in[owner][:1], (capacity, wide))
        here = lax.broadcasted_iota(jnp.int32, (capacity, wide), 0) == lax.broadcasted_iota(
            jnp.int32, (capacity, wide), 1
        )
        gate_column = jnp.sum(jnp.where(here, line, 0.0), axis=1, keepdims=True)
        grads[...] = (grads[...].astype(jnp.float32) * gate_column).astype(jnp.bfloat16)
        for first in range(0, units, tile):
            here = slice(first, first + tile)
            gate = jnp.dot(rows[...], gate_w[:, here], preferred_element_type=jnp.float32)
            up = jnp.dot(rows[...], up_w[:, here], preferred_element_type=jnp.float32)
            sig = jax.nn.sigmoid(gate)
            act = gate * sig
            middle[:, here] = (act * up).astype(jnp.bfloat16)
            grad = dot_nt(grads[...], down_w[here, :])
            gate_g[:, here] = (grad * up * sig * (1.0 + gate * (1.0 - sig))).astype(jnp.bfloat16)
            up_g[:, here] = (grad * act).astype(jnp.bfloat16)
        for store in stores(owner):
            store.start()
        made, fed = 2 * chunk, 2 * chunk + 1
        when(chunk >= 1, collect.second, made - 1)
        when(chunk >= 1, close, made - 2)
        collect.free_stage(made)
        for spot in range(place.spots):
            for core in range(2):
                first = (spot * 2 + core) * width
                here = slice(first, first + width)
                collect.stage[lax.rem(made, 4), 0, spot, core] = jnp.dot(
                    middle[...], down_w[:, here], preferred_element_type=jnp.float32
                ).astype(jnp.bfloat16)
        collect.first(made)
        collect.free_stage(fed)
        for spot in range(place.spots):
            for core in range(2):
                first = (spot * 2 + core) * width
                here = slice(first, first + width)
                collect.stage[lax.rem(fed, 4), 0, spot, core] = (
                    dot_nt(gate_g[...], gate_w[here, :]) + dot_nt(up_g[...], up_w[here, :])
                ).astype(jnp.bfloat16)
        collect.first(fed)
        collect.second(made)
        when(chunk >= 1, close, made - 1)

    def back_copy(item, owner=None):
        peer = spread.owner(lax.div(item, 2))
        return remote(
            closing.at[lax.rem(item, 4)],
            returned.at[lax.rem(item, 2), place.expert if owner is None else owner],
            back_send.at[item],
            back_land.at[item],
            place.device(peer, place.tensor),
        )

    def close(item):
        slot = lax.rem(item, 4)
        total = collect.third(item)[0]

        @pl.when(item >= 6)
        def _():
            back_copy(item - 4).wait_send()

        closing[slot] = total.astype(jnp.bfloat16)

        @pl.when(item >= 2)
        def _():
            back_copy(item).start()

        @pl.when(item < 2)
        def _():
            own = pltpu.make_async_copy(
                closing.at[slot],
                returned.at[lax.rem(item, 2), place.expert],
                back_send.at[item],
            )
            own.start()
            own.wait()

    def send_grads(chunk):
        when(chunk >= early, spread_grads.send, chunk)

    def step(turn, carry):
        now = turn - 2
        when(turn < chunks, spread.first, turn)
        when(turn + 1 + AHEAD < chunks, spread.send, turn + 1 + AHEAD)
        when((turn >= 1) & (turn <= chunks), spread.second, turn - 1)
        when((turn >= early - 1 - AHEAD) & (turn + 1 + AHEAD < chunks), send_grads, turn + 1 + AHEAD)
        when((turn >= early) & (turn < chunks), spread_grads.first, turn)
        when((turn > early) & (turn <= chunks), spread_grads.second, turn - 1)
        when(now >= 0, work, now)
        return carry

    lax.fori_loop(0, chunks + 2, step, 0)
    items = 2 * chunks
    collect.second(items - 1)
    close(items - 2)
    close(items - 1)

    def last(turn, carry):
        spread.finish(turn)
        when(turn >= early, spread_grads.finish, turn)

        @pl.when(turn > 0)
        def _():
            mark_copy(turn).wait_send()
            for item in (2 * turn, 2 * turn + 1):
                back_copy(item, spread.owner(turn)).wait_recv()

        return carry

    lax.fori_loop(0, chunks, last, 0)
    for store in stores(spread.owner(chunks - 1)):
        store.wait()
    for item in range(max(items - 4, 2), items):
        back_copy(item).wait_send()
    collect.finish()


def experts(source, source_grads, early_grads, gates, gate_w, up_w, down_w, sharers, collective):
    _, capacity, width = source.shape
    groups, parts = lax.axis_size("expert"), lax.axis_size("tensor")
    spots = parts // 2
    model_width, units = gate_w.shape
    low = jnp.bfloat16
    anywhere = pl.BlockSpec(memory_space=pl.ANY)
    hidden_rows = jax.ShapeDtypeStruct((groups, capacity, units), low)
    return pl.pallas_call(
        functools.partial(experts_kernel, sharers),
        out_shape=(
            jax.ShapeDtypeStruct((1, groups, capacity, model_width), low),
            jax.ShapeDtypeStruct((1, groups, capacity, model_width), low),
            jax.ShapeDtypeStruct((groups, capacity, model_width), low),
            hidden_rows,
            hidden_rows,
            hidden_rows,
            jax.ShapeDtypeStruct((2, groups, capacity, width), low),
        ),
        in_specs=[anywhere] * 7,
        out_specs=(anywhere,) * 7,
        scratch_shapes=[
            pltpu.VMEM((model_width, units), low),
            pltpu.VMEM((model_width, units), low),
            pltpu.VMEM((units, model_width), low),
            pltpu.VMEM((capacity, model_width), low),
            pltpu.VMEM((capacity, model_width), low),
            pltpu.VMEM((capacity, units), low),
            pltpu.VMEM((capacity, units), low),
            pltpu.VMEM((capacity, units), low),
            pltpu.VMEM((4, capacity, width), low),
            pltpu.VMEM((groups,) + gates.shape[1:], jnp.float32),
            pltpu.SemaphoreType.DMA((5,)),
            pltpu.SemaphoreType.DMA((4,)),
            pltpu.SemaphoreType.DMA((2 * groups,)),
            pltpu.SemaphoreType.DMA((2 * groups,)),
            pltpu.SemaphoreType.DMA((groups,)),
            pltpu.SemaphoreType.DMA((groups,)),
        ]
        + Spread.scratch(groups, spots)
        + Spread.scratch(groups, spots)
        + Collect.scratch(2 * groups, 1, spots, capacity, width, 4),
        compiler_params=pltpu.CompilerParams(
            collective_id=collective, has_side_effects=True, vmem_limit_bytes=60 * MIB
        ),
        cost_estimate=lasting(180),
    )(source[None], source_grads[None], gates, gate_w, up_w, down_w, early_grads)


class Return:
    @staticmethod
    def scratch(pieces, rows, width, groups):
        return [
            pltpu.VMEM((pieces, rows, width), jnp.bfloat16),
            pltpu.SemaphoreType.DMA((groups,)),
            pltpu.SemaphoreType.DMA((groups,)),
            pltpu.SemaphoreType.DMA,
        ]

    def __init__(self, place, back, refs):
        self.place, self.back = place, back
        self.ready, self.sent, self.landed, self.kept = refs
        self.bucket = back.shape[1]
        self.each = self.ready.shape[1] // self.bucket

    def block(self, piece, number):
        return self.ready.at[piece, pl.ds(number * self.bucket, self.bucket)]

    def copy(self, piece, number, index):
        target = piece * self.each + number
        return remote(
            self.block(piece, number),
            self.back.at[index],
            self.sent.at[target],
            self.landed.at[index],
            self.place.device(target, self.place.tensor),
        )

    def start(self, piece, values):
        place = self.place
        self.ready[piece] = values
        for number in range(self.each):
            target = piece * self.each + number

            @pl.when(target != place.expert)
            def _():
                self.copy(piece, number, place.expert).start()

            @pl.when(target == place.expert)
            def _():
                own = pltpu.make_async_copy(
                    self.block(piece, number), self.back.at[place.expert], self.kept
                )
                own.start()
                own.wait()

    def finish(self, piece):
        for number in range(self.each):
            target = piece * self.each + number

            @pl.when(target != self.place.expert)
            def _():
                self.copy(piece, number, self.place.expert).wait_send()
                self.copy(piece, number, target).wait_recv()


def pair_grad(gates, gate_grads, names, count):
    shared = gates[0] * gate_grads[0] + gates[1] * gate_grads[1]
    lane = lax.broadcasted_iota(jnp.int32, (gates[0].shape[0], count), 1)
    return sum(
        jnp.where(name == lane, gate * (grad - shared), 0.0)
        for gate, grad, name in zip(gates, gate_grads, names)
    )


def precise_dot(left, right, contract=(1, 0)):
    return lax.dot_general(
        left,
        right,
        (((contract[0],), (contract[1],)), ((), ())),
        precision=lax.Precision.HIGHEST,
        preferred_element_type=jnp.float32,
    )


class Exchange:
    @staticmethod
    def scratch(pieces, parts, rows, lanes):
        wide = (rows + 127) // 128 * 128
        return [
            pltpu.VMEM((pieces, lanes, wide), jnp.float32),
            pltpu.VMEM((pieces, parts - 1, lanes, wide), jnp.float32),
            pltpu.SemaphoreType.DMA((pieces, parts - 1)),
            pltpu.SemaphoreType.DMA((pieces, parts - 1)),
        ]

    def __init__(self, place, refs):
        self.place = place
        self.own, self.got, self.sent, self.landed = refs

    def copy(self, piece, step):
        return remote(
            self.own.at[piece],
            self.got.at[piece, step - 1],
            self.sent.at[piece, step - 1],
            self.landed.at[piece, step - 1],
            self.place.device(self.place.expert, self.place.along(step)),
        )

    def start(self, piece, values):
        _, lanes, wide = self.own.shape
        rows = values.shape[0]
        if rows < wide:
            blank = jnp.zeros((wide - rows, 128), jnp.float32)
            values = jnp.concatenate([values, blank], axis=0)
        self.own[piece] = values.T[:lanes]
        for step in range(1, self.place.parts):
            self.copy(piece, step).start()

    def total(self, piece, rows):
        _, lanes, wide = self.own.shape
        total = self.own[piece]
        for step in range(1, self.place.parts):
            self.copy(piece, step).wait_recv()
            total = total + self.got[piece, step - 1]
        blank = jnp.zeros((128 - lanes, wide), jnp.float32)
        return jnp.concatenate([total, blank], axis=0).T[:rows]

    def finish(self, piece):
        for step in range(1, self.place.parts):
            self.copy(piece, step).wait_send()


def closing_kernel(jobs, *refs):
    (
        normed_hbm, gain, factor, gates, marks, logits, gate_grads, router_t, gain_two, router_two,
        query_grad, key_grad, value_grad, gated_t, grads_hbm,
        hidden_hbm, resid_hbm, query_hbm, key_hbm, value_hbm,
    ), refs = refs[:20], refs[20:]
    grads = (query_grad, key_grad, value_grad)
    count = len(grads)
    lefts, rights, refs = refs[:3], refs[3:6], refs[6:]
    summed, back, small_out, products, refs = refs[:4], refs[4], refs[5], refs[6:9], refs[9:]
    (
        hold, hold_out, partial, small_own, small_got, small_sum,
        hidden, resid, w_query, w_key, w_value, right, left, product,
        ring_send, ring_land, small_send, small_land, last_send, last_land,
        own_sem, load_sem, job_sem, normed_t, hidden_grads, first_sem,
    ) = refs[:26]
    weights = (w_query, w_key, w_value)
    place = Place()
    exchange, of_gates = Exchange(place, refs[26:30]), Exchange(place, refs[30:34])
    giving = Return(place, back, refs[34:38])
    collect = Collect(place, refs[38:])
    first_loads = [
        pltpu.make_async_copy(normed_hbm, normed_t, first_sem.at[0]),
        pltpu.make_async_copy(grads_hbm, hidden_grads, first_sem.at[1]),
    ]
    for load in first_loads:
        load.start()
    groups, parts = place.groups, place.parts
    pieces, rows = collect.core_in.shape[0], collect.core_in.shape[3]
    width = hidden.shape[1]
    block = hold.shape[3]
    experts_of = logits.shape[1]
    own_columns = pl.ds(pl.multiple_of(place.tensor * width, 128), width)
    loads = [
        pltpu.make_async_copy(held, kept, load_sem.at[number])
        for number, (held, kept) in enumerate(
            (
                (query_hbm, w_query), (key_hbm, w_key), (value_hbm, w_value),
                (hidden_hbm, hidden), (resid_hbm.at[:, own_columns], resid),
            )
        )
    ]
    for load in loads:
        load.start()
    place.meet(True, True)

    parity, half = lax.rem(place.expert, 2), lax.div(place.expert, 2)
    at = half + parity * (groups - 1 - 2 * half)

    def member(spot):
        spot = lax.rem(spot + groups, groups)
        high = lax.div(spot, groups // 2)
        return (1 - high) * 2 * spot + high * (2 * (groups - 1 - spot) + 1)

    ways = ((0, 1), (1, -1))

    def first_row(way, sign, step):
        spot = lax.rem(at - sign * step + 2 * groups, groups)
        return pl.multiple_of((way * groups + spot) * block, block)

    def ring_copy(step, way, sign, number, source, target):
        return remote(
            source,
            target,
            ring_send.at[step, way, number],
            ring_land.at[step, way, number],
            place.device(member(at + sign), place.tensor),
        )

    out_rows, out_columns = hold_out.shape[2:]

    def first_column(sign, step):
        spot = lax.rem(at - sign * step + 2 * groups, groups)
        return pl.multiple_of(spot * out_columns, 128)

    def slot(step, way, number):
        if number == count:
            return hold_out.at[step, way]
        return hold.at[step, way, number]

    def spot_out(step, way, sign, number):
        if number == count:
            return summed[number].at[
                pl.ds(way * out_rows, out_rows), pl.ds(first_column(sign, step), out_columns)
            ]
        return summed[number].at[pl.ds(first_row(way, sign, step), block)]

    def own_part(step, way, sign, number):
        if number == count:
            return jnp.dot(
                gated_t[way * out_rows : (way + 1) * out_rows, :],
                hidden_grads[:, pl.ds(first_column(sign, step), out_columns)],
                preferred_element_type=jnp.float32,
            )
        return jnp.dot(
            normed_t[pl.ds(first_row(way, sign, step), block), :],
            grads[number][...],
            preferred_element_type=jnp.float32,
        )

    def ring(step):
        for number in range(count + 1):
            for way, sign in ways:

                @pl.when((step >= 1) & (step < groups))
                def _():
                    held = slot(step, way, number)
                    ring_copy(step - 1, way, sign, number, held, held).wait_recv()

                @pl.when(step >= groups)
                def _():
                    held = spot_out(step, way, sign, number)
                    ring_copy(step - 1, way, sign, number, held, held).wait_recv()

                @pl.when(step < groups)
                def _():
                    own = own_part(step, way, sign, number)
                    held = slot(step, way, number)

                    @pl.when(step == 0)
                    def _():
                        held[...] = own.astype(jnp.bfloat16)

                    @pl.when(step > 0)
                    def _():
                        held[...] = (own + held[...].astype(jnp.float32)).astype(jnp.bfloat16)

                @pl.when(step < groups - 1)
                def _():
                    ring_copy(
                        step, way, sign, number, slot(step, way, number), slot(step + 1, way, number)
                    ).start()

                @pl.when(step == groups - 1)
                def _():
                    held, there = slot(step, way, number), spot_out(step, way, sign, number)
                    ring_copy(step, way, sign, number, held, there).start()
                    pltpu.make_async_copy(held, there, own_sem.at[way, number]).start()

                @pl.when((step >= groups) & (step < 2 * groups - 2))
                def _():
                    held = spot_out(step, way, sign, number)
                    ring_copy(step, way, sign, number, held, held).start()

    def ring_finish(step, carry):
        for number in range(count + 1):
            for way, sign in ways:
                held = slot(0, way, number)
                ring_copy(step, way, sign, number, held, held).wait_send()
        return carry

    def band(piece):
        return pl.ds(pl.multiple_of(piece * rows, rows), rows)

    def project(piece):
        collect.free_stage(piece)
        side = lax.rem(piece, 2)
        for spot in range(place.spots):
            for core in range(2):
                first = (spot * 2 + core) * width
                part = None
                for grad, weight in zip(grads, weights):
                    term = dot_nt(grad[band(piece), :], weight[first : first + width, :])
                    part = term if part is None else part + term
                collect.stage[side, 0, spot, core] = part.astype(jnp.bfloat16)
        collect.first(piece)

    def scaled_of(piece):
        return resid[band(piece), :].astype(jnp.float32) * factor[band(piece), :]

    def tell(piece):
        lane = lax.broadcasted_iota(jnp.int32, (rows, 128), 1)
        values = jnp.zeros((rows, 128), jnp.float32)
        held = gate_grads.shape[1]
        for number in range(held):
            column = gate_grads[band(piece), number : number + 1]
            values = jnp.where(lane == place.tensor * held + number, column, values)
        of_gates.start(piece, values)

    def measure(piece):
        total = collect.third(piece)[0]
        partial[piece] = total
        inner = jnp.sum(total * scaled_of(piece) * gain[...], axis=1, keepdims=True)
        exchange.start(piece, jnp.broadcast_to(inner, (rows, 128)))

    def conclude(piece):
        here = band(piece)
        every = of_gates.total(piece, rows)[:, :experts_of]
        lane = lax.broadcasted_iota(jnp.int32, (rows, experts_of), 1)
        names = [marks[here, ROUTES + way : ROUTES + way + 1] for way in range(2)]
        logit_grad = pair_grad(
            [gates[here, way : way + 1] for way in range(2)],
            [
                jnp.sum(jnp.where(name == lane, every, 0.0), axis=1, keepdims=True)
                for name in names
            ],
            names,
            experts_of,
        )
        inner = exchange.total(piece, rows)[:, :1] + jnp.sum(
            logit_grad * logits[here, :], axis=1, keepdims=True
        )
        mean = inner / (width * parts)
        scaled = scaled_of(piece)
        grad = partial[piece] + precise_dot(logit_grad, router_t[...])
        small_own[0:1, :] += jnp.sum(grad * scaled, axis=0, keepdims=True)
        small_own[1 : 1 + experts_of, :] += precise_dot(logit_grad, scaled * gain[...], (0, 0))
        result = hidden[here, :] + factor[here, :] * (grad * gain[...] - scaled * mean)
        giving.start(piece, result.astype(jnp.bfloat16))

    def small_copy(step):
        return remote(
            small_own,
            small_got.at[step - 1],
            small_send.at[step - 1],
            small_land.at[step - 1],
            place.device(flip(place.expert, step, groups), place.tensor),
        )

    def last_copy(step, origin):
        return remote(
            small_sum,
            small_out.at[origin],
            last_send.at[step - 1],
            last_land.at[step - 1],
            place.device(place.expert, place.along(step)),
        )

    own_small = pltpu.make_async_copy(small_sum, small_out.at[place.tensor], own_sem.at[0, count + 1])

    def small_first():
        first = 1 + experts_of
        small_own[first : first + 1, :] = gain_two[...]
        small_own[first + 1 : first + 1 + router_two.shape[0], :] = router_two[...]
        for step in range(1, groups):
            small_copy(step).start()

    def small_second():
        total = small_own[...]
        for step in range(1, groups):
            small_copy(step).wait_recv()
            total = total + small_got[step - 1]
        small_sum[...] = total
        own_small.start()
        for step in range(1, parts):
            last_copy(step, place.tensor).start()

    small_own[...] = jnp.zeros_like(small_own)
    for load in first_loads:
        load.wait()
    turns = max(2 * groups - 1, pieces + 5)
    tiles = sum(job[0] for job in jobs)
    each_turn = -(-tiles // turns)

    def job_of(number, first, action):
        start = 0
        for index, (many, size, wide) in enumerate(jobs):
            when(
                (number >= start) & (number < start + many),
                functools.partial(action, index, size, wide),
                number - start,
            )
            start += many

    def right_copy(index, wide):
        return pltpu.make_async_copy(rights[index], right.at[:, pl.ds(0, wide)], job_sem.at[4])

    def left_copy(index, size, tile, side):
        first = pl.multiple_of(tile * size, 128)
        return pltpu.make_async_copy(
            lefts[index].at[:, pl.ds(first, size)],
            left.at[side, :, pl.ds(0, size)],
            job_sem.at[side],
        )

    def product_copy(index, size, wide, tile, side):
        first = pl.multiple_of(tile * size, 8)
        return pltpu.make_async_copy(
            product.at[side, pl.ds(0, size), pl.ds(0, wide)],
            products[index].at[pl.ds(first, size)],
            job_sem.at[2 + side],
        )

    def multiply(number):
        side = lax.rem(number, 2)

        def fetch_next(index, size, wide, tile):
            left_copy(index, size, tile, 1 - side).start()

        def stored(index, size, wide, tile):
            product_copy(index, size, wide, tile, side).wait()

        def work(index, size, wide, tile):
            @pl.when(tile == 0)
            def _():
                right_copy(index, wide).start()
                right_copy(index, wide).wait()

            left_copy(index, size, tile, side).wait()
            product[side, :size, :wide] = dot_tn(left[side, :, :size], right[:, :wide]).astype(
                jnp.bfloat16
            )
            product_copy(index, size, wide, tile, side).start()

        job_of(number + 1, None, fetch_next)
        job_of(number - 2, None, stored)
        job_of(number, None, work)

    left_copy(0, jobs[0][1], 0, 0).start()

    def turn_step(turn, carry):
        when(turn < 2 * groups - 1, ring, turn)

        @pl.when(turn == 0)
        def _():
            for load in loads:
                load.wait()

        when((turn >= 3) & (turn < pieces + 3), conclude, turn - 3)
        when((turn >= 2) & (turn < pieces + 2), measure, turn - 2)
        when((turn >= 1) & (turn < pieces + 1), collect.second, turn - 1)
        when(turn < pieces, project, turn)
        when(turn < pieces, tell, turn)
        when(turn == pieces + 3, small_first)
        when(turn == pieces + 4, small_second)
        lax.fori_loop(
            turn * each_turn,
            jnp.minimum((turn + 1) * each_turn, tiles),
            lambda number, held: (multiply(number), held)[1],
            0,
        )
        return carry

    lax.fori_loop(0, turns, turn_step, 0)
    for number in (tiles - 2, tiles - 1):
        index, tile = 0, number
        while tile >= jobs[index][0]:
            tile -= jobs[index][0]
            index += 1
        product_copy(index, jobs[index][1], jobs[index][2], tile, number % 2).wait()
    lax.fori_loop(0, 2 * groups - 2, ring_finish, 0)
    for number in range(count + 1):
        for way, sign in ways:
            pltpu.make_async_copy(
                slot(groups - 1, way, number),
                spot_out(groups - 1, way, sign, number),
                own_sem.at[way, number],
            ).wait()
    collect.finish()
    for step in range(1, groups):
        small_copy(step).wait_send()
    own_small.wait()
    for step in range(1, parts):
        origin = lax.rem(place.tensor + parts - step, parts)
        last_copy(step, place.tensor).wait_send()
        last_copy(step, origin).wait_recv()

    def settle(piece, carry):
        exchange.finish(piece)
        of_gates.finish(piece)
        giving.finish(piece)
        return carry

    lax.fori_loop(0, pieces, settle, 0)


def closing(
    normed_t, columns_in, grads, gated_t, hidden_grads, hidden, resid, weights,
    lefts, rights, pieces, collective,
):
    groups, parts = lax.axis_size("expert"), lax.axis_size("tensor")
    spots = parts // 2
    model_width, tokens = normed_t.shape
    columns = grads[0].shape[1]
    width = hidden.shape[1]
    count = len(grads)
    small = jax.ShapeDtypeStruct(
        ((2 + columns_in[4].shape[1] + columns_in[-1].shape[0] + 7) // 8 * 8, width), jnp.float32
    )
    rows = tokens // pieces
    block = model_width // (2 * groups)
    low, full = jnp.bfloat16, jnp.float32
    inside = pl.BlockSpec(memory_space=pltpu.VMEM)
    anywhere = pl.BlockSpec(memory_space=pl.ANY)
    dma = pltpu.SemaphoreType.DMA
    jobs = []
    for left, right in zip(lefts, rights):
        jobs.append((left.shape[1] // 128, 128, right.shape[1]))
    depth = lefts[0].shape[0]
    tile = max(job[1] for job in jobs)
    wide = max(job[2] for job in jobs)
    return pl.pallas_call(
        functools.partial(closing_kernel, tuple(jobs)),
        out_shape=(
            *(jax.ShapeDtypeStruct((model_width, columns), low) for _ in range(count)),
            jax.ShapeDtypeStruct((columns, model_width), low),
            jax.ShapeDtypeStruct((groups, tokens // groups, width), low),
            jax.ShapeDtypeStruct((parts,) + small.shape, full),
            *(
                jax.ShapeDtypeStruct((left.shape[1], right.shape[1]), low)
                for left, right in zip(lefts, rights)
            ),
        ),
        in_specs=[anywhere] + [inside] * 13 + [anywhere] * 12,
        out_specs=(anywhere,) * 9,
        scratch_shapes=[
            pltpu.VMEM((groups, 2, count, block, columns), low),
            pltpu.VMEM((groups, 2, columns // 2, model_width // groups), low),
            pltpu.VMEM((pieces, rows, width), full),
            pltpu.VMEM(small.shape, full),
            pltpu.VMEM((groups - 1,) + small.shape, full),
            pltpu.VMEM(small.shape, full),
            pltpu.VMEM((tokens, width), full),
            pltpu.VMEM((tokens, width), low),
            *(pltpu.VMEM(weight.shape, low) for weight in weights),
            pltpu.VMEM((depth, wide), low),
            pltpu.VMEM((2, depth, tile), low),
            pltpu.VMEM((2, tile, wide), low),
            dma((2 * groups - 2, 2, count + 1)),
            dma((2 * groups - 2, 2, count + 1)),
            dma((groups - 1,)),
            dma((groups - 1,)),
            dma((parts - 1,)),
            dma((parts - 1,)),
            dma((2, count + 2)),
            dma((5,)),
            dma((5,)),
            pltpu.VMEM(normed_t.shape, low),
            pltpu.VMEM(hidden_grads.shape, low),
            dma((2,)),
        ]
        + Exchange.scratch(pieces, parts, rows, 8)
        + Exchange.scratch(pieces, parts, rows, (columns_in[4].shape[1] + 7) // 8 * 8)
        + Return.scratch(pieces, rows, width, groups)
        + Collect.scratch(pieces, 1, spots, rows, width),
        compiler_params=pltpu.CompilerParams(
            collective_id=collective, has_side_effects=True, vmem_limit_bytes=60 * MIB
        ),
        cost_estimate=lasting(200),
    )(
        normed_t, *columns_in, *grads, gated_t, hidden_grads, hidden, resid, *weights,
        *lefts, *rights,
    )


def settle_kernel(
    came, marks, gates, logits, factor, hidden, grads, gain, router_t,
    back, hidden_grad, gathered, router_grad, gain_grad,
    row_grads, ready, *refs,
):
    place = Place()
    exchange = Exchange(place, refs[:4])
    giving = Return(place, back, refs[4:8])
    pieces, rows, width = row_grads.shape
    spread = Spread(place, ready, gathered, refs[8:], False)
    slots, experts_of = came.shape[1], logits.shape[1]
    low = jnp.bfloat16
    place.meet(True, True)
    router_grad[...] = jnp.zeros_like(router_grad)
    gain_grad[...] = jnp.zeros_like(gain_grad)

    def band(piece):
        return pl.ds(pl.multiple_of(piece * rows, rows), rows)

    def scaled_of(piece):
        return hidden[band(piece), :] * factor[band(piece), :]

    def gather(piece):
        here = band(piece)
        numbers = lax.broadcasted_iota(jnp.int32, (rows, slots), 1)
        chosen = [(marks[here, SLOTS + way : SLOTS + way + 1] == numbers).astype(low) for way in range(2)]
        result = hidden[here, :]
        grad = grads[here, :].astype(jnp.float32)
        lane = lax.broadcasted_iota(jnp.int32, (rows, 128), 1)
        stats = jnp.zeros((rows, 128), jnp.float32)
        for way in range(2):
            value = jnp.dot(chosen[way], came[0], preferred_element_type=jnp.float32)
            result = result + gates[here, way : way + 1] * value
            stats = jnp.where(lane == way, jnp.sum(value * grad, axis=1, keepdims=True), stats)
        total = jnp.dot(chosen[0] + chosen[1], came[1], preferred_element_type=jnp.float32)
        row_grads[piece] = total
        inner = jnp.sum(total * scaled_of(piece) * gain[...], axis=1, keepdims=True)
        exchange.start(piece, jnp.where(lane == 2, inner, stats))
        giving.start(piece, result.astype(low))

    def settle(piece):
        here = band(piece)
        stats = exchange.total(piece, rows)
        logit_grad = pair_grad(
            [gates[here, way : way + 1] for way in range(2)],
            [stats[:, way : way + 1] for way in range(2)],
            [marks[here, ROUTES_TWO + way : ROUTES_TWO + way + 1] for way in range(2)],
            experts_of,
        )
        mean = (
            stats[:, 2:3] + jnp.sum(logit_grad * logits[here, :], axis=1, keepdims=True)
        ) / (width * place.parts)
        scaled = scaled_of(piece)
        grad = row_grads[piece] + precise_dot(logit_grad, router_t[...])
        gain_grad[...] += jnp.sum(grad * scaled, axis=0, keepdims=True)
        router_grad[...] += precise_dot(logit_grad, scaled * gain[...], (0, 0))
        result = grads[here, :].astype(jnp.float32) + factor[here, :] * (
            grad * gain[...] - scaled * mean
        )
        hidden_grad[here, :] = result
        ready[0, piece] = result.astype(low)
        spread.first(piece)

    def step(turn, carry):
        when(turn < pieces, gather, turn)
        when((turn >= 2) & (turn <= pieces + 1), settle, turn - 2)
        when(turn >= 3, spread.second, turn - 3)
        return carry

    lax.fori_loop(0, pieces + 3, step, 0)

    def last(piece, carry):
        spread.third(piece)
        spread.finish(piece)
        exchange.finish(piece)
        giving.finish(piece)
        return carry

    lax.fori_loop(0, pieces, last, 0)


def settle(came, marks, gates, logits, factor, hidden, grads, gain, router_t, pieces, collective):
    groups, parts = lax.axis_size("expert"), lax.axis_size("tensor")
    tokens, width = hidden.shape
    rows = tokens // pieces
    low, full = jnp.bfloat16, jnp.float32
    inside = pl.BlockSpec(memory_space=pltpu.VMEM)
    anywhere = pl.BlockSpec(memory_space=pl.ANY)
    return pl.pallas_call(
        settle_kernel,
        out_shape=(
            jax.ShapeDtypeStruct((groups, tokens // groups, width), low),
            jax.ShapeDtypeStruct((tokens, width), full),
            jax.ShapeDtypeStruct((1, pieces, rows, width * parts), low),
            jax.ShapeDtypeStruct(router_t.shape, full),
            jax.ShapeDtypeStruct((1, width), full),
        ),
        in_specs=[inside] * 9,
        out_specs=(anywhere, inside, anywhere, inside, inside),
        scratch_shapes=[
            pltpu.VMEM((pieces, rows, width), full),
            pltpu.VMEM((1, pieces, rows, width), low),
        ]
        + Exchange.scratch(pieces, parts, rows, 8)
        + Return.scratch(pieces, rows, width, groups)
        + Spread.scratch(pieces, parts // 2),
        compiler_params=pltpu.CompilerParams(
            collective_id=collective, has_side_effects=True, vmem_limit_bytes=48 * MIB
        ),
        cost_estimate=lasting(30),
    )(came, marks, gates, logits, factor, hidden, grads, gain, router_t)


def dot_tn(left, right):
    return lax.dot_general(
        left, right, (((0,), (0,)), ((), ())), preferred_element_type=jnp.float32
    )


def bands(tokens):
    size = 256 if tokens % 256 == 0 else tokens
    return [(first, size) for first in range(0, tokens, size)]


def sequence_starts(lengths):
    starts = [0]
    for number in range(lengths.shape[1] - 1):
        starts.append(starts[-1] + lengths[0, number])
    return starts


def masked_scores(query, keys, lengths, first, size, column):
    last = first + size
    scores = dot_nt(query[first:last, column], keys[:last, column]) * (1.0 / math.sqrt(HEAD))
    place = lax.broadcasted_iota(jnp.int32, (size, 1), 0) + first
    start = jnp.zeros((size, 1), jnp.int32)
    for value in sequence_starts(lengths)[1:]:
        start = jnp.where(place >= value, value, start)
    other = lax.broadcasted_iota(jnp.int32, (size, last), 1)
    return jnp.where((other >= start) & (place >= other), scores, MASKED)


def chosen_gates(logits, names):
    lane = lax.broadcasted_iota(jnp.int32, logits.shape, 1)
    picked = [
        jnp.sum(jnp.where(name == lane, logits, 0.0), axis=1, keepdims=True) for name in names
    ]
    top = jnp.maximum(picked[0], picked[1])
    expo = [jnp.exp(value - top) for value in picked]
    total = expo[0] + expo[1]
    return [value / total for value in expo]


def front_kernel(sharers, *refs):
    (
        resid, gain, router_t, query_hbm, key_hbm, value_hbm, out_hbm, cosines, sines,
        marks, mark_rows, gain_two, router_two_t, lengths, dealt,
        normed_t, cosine, sine, factor, logits, gates, gate_local, query, keys, values, heads, log_total,
        hidden, factor_two, logits_two, gates_two, sent_rows, lines,
        grads_back, grads_out, inbox_grads,
        normed_two, grads_here, grads_slots, w_query, w_key, w_value, w_out,
        deal_send, deal_land, load_sem, weight_sem,
    ), refs = refs[:47], refs[47:]
    place = Place()
    weight_loads = [
        pltpu.make_async_copy(source, kept, weight_sem.at[number])
        for number, (source, kept) in enumerate(
            ((query_hbm, w_query), (key_hbm, w_key), (value_hbm, w_value), (out_hbm, w_out))
        )
    ]
    for load in weight_loads:
        load.start()
    spread = Spread(place, grads_slots, inbox_grads, refs[:6], True, sharers)
    exchange = Exchange(place, refs[6:10])
    collect = Collect(place, refs[10:])
    tokens, columns = query.shape
    width = hidden.shape[1]
    groups = place.groups
    capacity = sent_rows.shape[1]
    experts_of = logits.shape[1]
    held = gate_local.shape[1]
    span = columns // held
    low = jnp.bfloat16
    parts = list(enumerate(bands(tokens)))
    place.meet(True, True)

    def deal_copy(step, index):
        peer = flip(place.expert, step, groups)
        return remote(
            dealt.at[peer],
            grads_back.at[index],
            deal_send.at[step],
            deal_land.at[step],
            place.device(peer, place.tensor),
        )

    for step in range(1, groups):
        deal_copy(step, place.expert).start()
    own = pltpu.make_async_copy(
        dealt.at[place.expert], grads_back.at[place.expert], deal_send.at[0]
    )
    own.start()
    for load in weight_loads:
        load.wait()
    router_high = router_t[...].astype(low)
    router_rest = (router_t[...] - router_high.astype(jnp.float32)).astype(low)
    columns_here = pl.ds(pl.multiple_of(place.tensor * width, 128), width)
    for _, (first, size) in parts:
        rows = slice(first, first + size)
        spot = lax.broadcasted_iota(jnp.int32, (size, 1), 0) + first
        start_cosine = jnp.broadcast_to(cosines[0:1, :], (size, HEAD))
        start_sine = jnp.broadcast_to(sines[0:1, :], (size, HEAD))
        for start in sequence_starts(lengths)[1:]:
            start_cosine = jnp.where(spot >= start, cosines[pl.ds(start, 1), :], start_cosine)
            start_sine = jnp.where(spot >= start, sines[pl.ds(start, 1), :], start_sine)
        lane = lax.broadcasted_iota(jnp.int32, (size, HEAD), 1)
        cosine[rows, :] = cosines[rows, :] * start_cosine + sines[rows, :] * start_sine
        turned = sines[rows, :] * start_cosine - cosines[rows, :] * start_sine
        sine[rows, :] = jnp.where(lane < HEAD // 2, -turned, turned)
        value = resid[rows, :].astype(jnp.float32)
        scale = lax.rsqrt(jnp.mean(value * value, axis=1, keepdims=True) + EPSILON)
        value = value * scale * gain[...]
        high = value.astype(low)
        rest = (value - high.astype(jnp.float32)).astype(low)
        factor[rows, :] = scale
        normed_t[:, rows] = high.T
        known = sum(
            dot_nt(left, right)
            for left, right in ((high, router_high), (high, router_rest), (rest, router_high))
        )
        logits[rows, :] = known
        names = [marks[rows, ROUTES + way : ROUTES + way + 1] for way in range(2)]
        pair = chosen_gates(known, names)
        for way in range(2):
            gates[rows, way : way + 1] = pair[way]
        for number in range(held):
            expert = place.tensor * held + number
            gate_local[rows, number : number + 1] = sum(
                jnp.where(name == expert, gate, 0.0) for name, gate in zip(names, pair)
            )
        values[rows, :] = jnp.dot(
            high, w_value[...], preferred_element_type=jnp.float32
        ).astype(low)
        for weight, out in ((w_query, query), (w_key, keys)):
            flat = jnp.dot(high, weight[...], preferred_element_type=jnp.float32)
            for head in range(columns // HEAD):
                column = slice(head * HEAD, (head + 1) * HEAD)
                part = flat[:, column]
                turned = pltpu.roll(part, HEAD // 2, 1)
                out[rows, column] = (part * cosine[rows, :] + turned * sine[rows, :]).astype(low)

    def selection(expert):
        number = lax.broadcasted_iota(jnp.int32, (capacity, tokens), 0) + expert * capacity
        return ((mark_rows[0:1, :] == number) | (mark_rows[1:2, :] == number)).astype(low)

    early = min(FRONT, groups)

    keep = pltpu.make_async_copy(grads_slots.at[0], grads_out, load_sem.at[groups])

    def take_grads():
        own.wait()
        bucket = grads_back.shape[1]
        for step in range(1, groups):
            deal_copy(step, flip(place.expert, step, groups)).wait_recv()
        fetches = [
            pltpu.make_async_copy(
                grads_back.at[group], grads_here.at[pl.ds(group * bucket, bucket)], load_sem.at[group]
            )
            for group in range(groups)
        ]
        for fetch in fetches:
            fetch.start()
        for fetch in fetches:
            fetch.wait()
        for expert in range(sent_rows.shape[0]):
            grads_slots[0, expert] = jnp.dot(
                selection(expert), grads_here[...], preferred_element_type=jnp.float32
            ).astype(low)
        keep.start()
        spread.start(min(AHEAD, early - 1))

    def tick(number):
        if number < early:
            spread.first(jnp.int32(number))
        if number + 1 + AHEAD < early:
            spread.send(jnp.int32(number + 1 + AHEAD))
        if 1 <= number <= early:
            spread.second(jnp.int32(number - 1))

    def attend_band(number, first, size):
        last = first + size
        rows = slice(first, last)
        for head in range(columns // HEAD):
            column = slice(head * HEAD, (head + 1) * HEAD)
            scores = masked_scores(query, keys, lengths, first, size, column)
            top = jnp.max(scores, axis=1, keepdims=True)
            expo = jnp.exp(scores - top)
            total = jnp.sum(expo, axis=1, keepdims=True)
            probs = (expo / total).astype(low)
            heads[rows, column] = jnp.dot(
                probs, values[:last, column], preferred_element_type=jnp.float32
            ).astype(low)
            log_total[rows, head : head + 1] = top + jnp.log(total)
        collect.free_stage(jnp.int32(number))
        for spot in range(place.spots):
            for core in range(2):
                start = (spot * 2 + core) * width
                total = None
                for expert in range(held):
                    inner = slice(expert * span, (expert + 1) * span)
                    term = gate_local[rows, expert : expert + 1] * jnp.dot(
                        heads[rows, inner],
                        w_out[inner, start : start + width],
                        preferred_element_type=jnp.float32,
                    )
                    total = term if total is None else total + term
                collect.stage[number % collect.slots, 0, spot, core] = total.astype(low)
        collect.first(jnp.int32(number))

    blank = jnp.zeros((128 - router_two_t.shape[0], width), jnp.float32)
    router_wide = jnp.concatenate([router_two_t[...], blank], axis=0)

    def measure(number, first, size):
        rows = slice(first, first + size)
        value = resid[rows, columns_here].astype(jnp.float32) + collect.third(jnp.int32(number))[0]
        hidden[rows, :] = value
        squares = jnp.sum(value * value, axis=1, keepdims=True)
        known = precise_dot(value * gain_two[...], router_wide, (1, 1))
        lane = lax.broadcasted_iota(jnp.int32, known.shape, 1)
        exchange.start(number, jnp.where(lane == SQUARES, squares, known))

    def conclude(number, first, size):
        rows = slice(first, first + size)
        total = exchange.total(number, size)
        scale = lax.rsqrt(total[:, SQUARES : SQUARES + 1] / (width * place.parts) + EPSILON)
        known = total[:, : logits_two.shape[1]] * scale
        factor_two[rows, :] = scale
        logits_two[rows, :] = known
        names = [marks[rows, ROUTES_TWO + way : ROUTES_TWO + way + 1] for way in range(2)]
        pair = chosen_gates(known, names)
        for way in range(2):
            gates_two[rows, way : way + 1] = pair[way]
        normed_two[rows, :] = (hidden[rows, :] * scale * gain_two[...]).astype(low)

    count = len(parts)
    for turn in range(count + 3):
        if turn < count:
            attend_band(turn, *parts[turn][1])
        if 2 <= turn < count + 2:
            measure(turn - 2, *parts[turn - 2][1])
        if 1 <= turn < count + 1:
            collect.second(jnp.int32(turn - 1))
        if turn >= 3:
            conclude(turn - 3, *parts[turn - 3][1])
        if turn == count:
            take_grads()
        if turn > count:
            tick(turn - count - 1)
    for expert in range(sent_rows.shape[0]):
        sent_rows[expert] = jnp.dot(
            selection(expert), normed_two[...], preferred_element_type=jnp.float32
        ).astype(low)
        wide = lines.shape[2]
        lane = lax.broadcasted_iota(jnp.int32, (tokens, wide), 1)
        number = jnp.where(lane < capacity, lane + expert * capacity, -1)
        line = sum(
            jnp.where(
                marks[:, SLOTS + way : SLOTS + way + 1] == number, gates_two[:, way : way + 1], 0.0
            )
            for way in range(2)
        )
        lines[expert] = jnp.broadcast_to(jnp.sum(line, axis=0, keepdims=True), lines.shape[1:])
    for number in range(2, early + 1):
        tick(number)
    keep.wait()
    for step in range(1, groups):
        deal_copy(step, place.expert).wait_send()
    for number in range(count):
        exchange.finish(number)
    collect.finish()

    def last(number, carry):
        spread.third(number)
        spread.finish(number)
        return carry

    lax.fori_loop(0, early, last, 0)


def front(
    resid, gain, router_t, weights, w_out, tables, marks, mark_rows, gain_two, router_two_t,
    lengths, dealt, capacity, sharers, collective,
):
    groups, parts = lax.axis_size("expert"), lax.axis_size("tensor")
    tokens, model_width = resid.shape
    columns = weights[0].shape[1]
    width = dealt.shape[2]
    experts_of = router_t.shape[0]
    held = columns // (QH * HEAD)
    slots_of = router_two_t.shape[0]
    low, full = jnp.bfloat16, jnp.float32
    block = jax.ShapeDtypeStruct((tokens, columns), low)
    wide = (capacity + 127) // 128 * 128
    inside = pl.BlockSpec(memory_space=pltpu.VMEM)
    anywhere = pl.BlockSpec(memory_space=pl.ANY)

    def column(count):
        return jax.ShapeDtypeStruct((tokens, count), full)

    pieces = len(bands(tokens))
    dma = pltpu.SemaphoreType.DMA
    return pl.pallas_call(
        functools.partial(front_kernel, sharers),
        out_shape=(
            jax.ShapeDtypeStruct((model_width, tokens), low),
            column(HEAD),
            column(HEAD),
            column(1),
            column(experts_of),
            column(2),
            column(held),
            block,
            block,
            block,
            block,
            column(columns // HEAD),
            column(width),
            column(1),
            column(slots_of),
            column(2),
            jax.ShapeDtypeStruct((slots_of, capacity, width), low),
            jax.ShapeDtypeStruct((slots_of, 8, wide), full),
            jax.ShapeDtypeStruct(dealt.shape, low),
            jax.ShapeDtypeStruct((slots_of, capacity, width), low),
            jax.ShapeDtypeStruct((1, groups, capacity, model_width), low),
        ),
        in_specs=[inside] * 3
        + [anywhere] * 4
        + [inside] * 6
        + [pl.BlockSpec(memory_space=pltpu.SMEM), anywhere],
        out_specs=(inside,) * 18 + (anywhere,) * 3,
        scratch_shapes=[
            pltpu.VMEM((tokens, width), low),
            pltpu.VMEM((tokens, width), low),
            pltpu.VMEM((1, slots_of, capacity, width), low),
            *(pltpu.VMEM(weight.shape, low) for weight in (*weights, w_out)),
            dma((groups,)),
            dma((groups,)),
            dma((groups + 1,)),
            dma((4,)),
        ]
        + Spread.scratch(groups, parts // 2)
        + Exchange.scratch(pieces, parts, tokens // pieces, 16)
        + Collect.scratch(pieces, 1, parts // 2, tokens // pieces, width, pieces),
        compiler_params=pltpu.CompilerParams(
            collective_id=collective, has_side_effects=True, vmem_limit_bytes=58 * MIB
        ),
        cost_estimate=lasting(60),
    )(
        resid, gain, router_t, *weights, w_out, *tables, marks, mark_rows, gain_two, router_two_t,
        lengths, dealt,
    )


def attend_back_kernel(
    grads, w_out, gates, heads, query, keys, values, log_total, cosine, sine, lengths,
    query_grad, key_grad, value_grad, gate_grad, gated_t,
    heads_grad, key_sum, value_sum,
):
    tokens, columns = query.shape
    low = jnp.bfloat16
    span = columns // gates.shape[1]
    scale = 1.0 / math.sqrt(HEAD)
    for first, size in bands(tokens):
        rows = slice(first, first + size)
        plain = dot_nt(grads[rows, :], w_out[...])
        for expert in range(gates.shape[1]):
            column = slice(expert * span, (expert + 1) * span)
            gate = gates[rows, expert : expert + 1]
            head = heads[rows, column].astype(jnp.float32)
            gate_grad[rows, expert : expert + 1] = jnp.sum(
                plain[:, column] * head, axis=1, keepdims=True
            )
            heads_grad[rows, column] = (plain[:, column] * gate).astype(low)
            gated_t[column, rows] = (head * gate).T.astype(low)

    def unturn(value, rows):
        turned = pltpu.roll(value * sine[rows, :], HEAD // 2, 1)
        return value * cosine[rows, :] + turned

    for head in range(columns // HEAD):
        column = slice(head * HEAD, (head + 1) * HEAD)
        for first, size in bands(tokens):
            last = first + size
            rows = slice(first, last)
            scores = masked_scores(query, keys, lengths, first, size, column)
            probs = jnp.exp(scores - log_total[rows, head : head + 1])
            value_part = dot_tn(probs.astype(low), heads_grad[rows, column])
            prob_grad = dot_nt(heads_grad[rows, column], values[:last, column])
            score_grad = (
                probs * (prob_grad - jnp.sum(probs * prob_grad, axis=1, keepdims=True))
            ).astype(low)
            query_grad[rows, column] = unturn(
                jnp.dot(score_grad, keys[:last, column], preferred_element_type=jnp.float32)
                * scale,
                rows,
            ).astype(low)
            key_part = dot_tn(score_grad, query[rows, column])
            if first:
                value_sum[:first, :] += value_part[:first]
                key_sum[:first, :] += key_part[:first]
            value_sum[rows, :] = value_part[first:]
            key_sum[rows, :] = key_part[first:]
        whole = slice(0, tokens)
        key_grad[:, column] = unturn(key_sum[...] * scale, whole).astype(low)
        value_grad[:, column] = value_sum[...].astype(low)


def attend_back(grads, w_out, gates, heads, query, keys, values, log_total, cosine, sine, lengths):
    tokens, model_width = grads.shape
    columns = query.shape[1]
    low, full = jnp.bfloat16, jnp.float32
    block = jax.ShapeDtypeStruct((tokens, columns), low)
    inside = pl.BlockSpec(memory_space=pltpu.VMEM)
    return pl.pallas_call(
        attend_back_kernel,
        out_shape=(
            block,
            block,
            block,
            jax.ShapeDtypeStruct(gates.shape, full),
            jax.ShapeDtypeStruct((columns, tokens), low),
        ),
        in_specs=[inside] * 10 + [pl.BlockSpec(memory_space=pltpu.SMEM)],
        out_specs=(inside,) * 5,
        scratch_shapes=[
            pltpu.VMEM((tokens, columns), low),
            pltpu.VMEM((tokens, HEAD), full),
            pltpu.VMEM((tokens, HEAD), full),
        ],
        compiler_params=pltpu.CompilerParams(vmem_limit_bytes=56 * MIB),
        cost_estimate=lasting(25),
    )(
        grads, w_out, gates, heads, query, keys, values, log_total, cosine, sine, lengths
    )


def body(
    tokens,
    out_grad,
    attn_gain,
    attn_router,
    w_query,
    w_key,
    w_value,
    w_out,
    mlp_gain,
    mlp_router,
    w_gate,
    w_up,
    w_down,
    deal,
    seq_lengths,
    attn_routes,
    mlp_routes,
    slot_order,
):
    tok_rows, model_width = tokens.shape
    group_count = lax.axis_size("expert")
    part_count = lax.axis_size("tensor")
    group_index = lax.axis_index("expert")
    part_index = lax.axis_index("tensor")
    bucket_rows = tok_rows // group_count
    col_width = model_width // part_count
    col_first = part_index * col_width
    low = jnp.bfloat16

    def own_cols(values):
        return lax.dynamic_slice_in_dim(values, col_first, col_width, values.ndim - 1)

    deal_rank = deal // tok_rows * bucket_rows + (deal % tok_rows - group_index * bucket_rows)
    row_ids = jnp.arange(tok_rows, dtype=jnp.int32)
    expert_count = mlp_router.shape[1]
    experts_of = attn_router.shape[1]
    sharers = group_count // expert_count
    capacity = 5 * tok_rows // (2 * expert_count)
    slots = expert_count * capacity
    pieces = 4
    orders = slot_order[0].reshape(tok_rows, 2)
    rows_in = jnp.concatenate([attn_routes.T, mlp_routes.T, orders.T, orders.T], axis=0)
    resid_low, dealt_grads, marks, mark_rows = deal_rows(
        tokens, out_grad, deal_rank[None], rows_in, capacity, expert_count, 0
    )
    resid_low = resid_low.reshape(tok_rows, model_width)
    gain_one, gain_two = own_cols(attn_gain), own_cols(mlp_gain)
    router_one, router_two = own_cols(attn_router.T), own_cols(mlp_router.T)
    (
        normed_t, cosine, sine, factor_one, attn_logits, attn_gates, gate_local, query, keys, values,
        heads_low, log_total, hidden, factor_two, mlp_logits, mlp_gates, slot_rows, gate_lines,
        grad_cols_low, slot_grads, early_grads,
    ) = front(
        resid_low,
        attn_gain[None],
        attn_router.T,
        (w_query, w_key, w_value),
        w_out,
        rotary_tables(tok_rows),
        marks,
        mark_rows,
        gain_two[None],
        router_two,
        seq_lengths,
        dealt_grads,
        capacity,
        sharers,
        1,
    )
    grad_cols_low = grad_cols_low.reshape(tok_rows, col_width)
    inbox, _, slot_grads, middle, gate_grad, up_grad, returned = experts(
        slot_rows,
        slot_grads,
        early_grads,
        gate_lines,
        w_gate[0],
        w_up[0],
        w_down[0],
        sharers,
        2,
    )
    if sharers > 1:
        returned = (
            jnp.sum(
                returned.reshape(2, expert_count, sharers, capacity, col_width).astype(jnp.float32),
                axis=2,
            )
        ).astype(low)
    back_mixed, hidden_grad, hidden_grad_low, mlp_router_grad, mlp_gain_grad = settle(
        returned.reshape(2, slots, col_width),
        marks,
        mlp_gates,
        mlp_logits,
        factor_two,
        hidden,
        grad_cols_low,
        gain_two[None],
        router_two,
        pieces,
        4,
    )
    back_mixed = back_mixed.reshape(tok_rows, col_width)
    hidden_grad_low = hidden_grad_low.reshape(tok_rows, model_width)
    query_pre_grad, key_pre_grad, value_pre_grad, local_gate_grad, gated_t = attend_back(
        hidden_grad_low,
        w_out,
        gate_local,
        heads_low,
        query,
        keys,
        values,
        log_total,
        cosine,
        sine,
        seq_lengths,
    )
    rows = inbox.reshape(-1, model_width)
    units = middle.shape[2]
    middle, gate_grad, up_grad = (
        jnp.pad(values.reshape(-1, units), ((0, 0), (0, -units % 128)))
        for values in (middle, gate_grad, up_grad)
    )
    *weight_grads, back_grad, small, gate_w_grad, up_w_grad, down_grad = closing(
        normed_t,
        (
            gain_one[None],
            factor_one,
            attn_gates,
            marks,
            attn_logits,
            local_gate_grad,
            router_one,
            mlp_gain_grad,
            mlp_router_grad,
        ),
        (query_pre_grad, key_pre_grad, value_pre_grad),
        gated_t,
        hidden_grad_low,
        hidden_grad,
        resid_low,
        (w_query, w_key, w_value),
        (rows, rows, middle),
        (gate_grad, up_grad, slot_grads.reshape(-1, model_width)),
        pieces,
        3,
    )
    back_grad = back_grad.reshape(tok_rows, col_width)
    weight_grads = [grad.astype(jnp.float32) for grad in weight_grads]
    deal_mask = (row_ids[:, None] == deal_rank[None, :]).astype(low)
    mixed, tokens_grad = (
        jnp.einsum("ri,rc->ic", deal_mask, back, preferred_element_type=jnp.float32).astype(low)
        for back in (back_mixed, back_grad)
    )
    small = small.transpose(1, 0, 2).reshape(-1, model_width)
    return (
        mixed,
        tokens_grad,
        small[0],
        small[1 : 1 + experts_of].T,
        weight_grads[0],
        weight_grads[1],
        weight_grads[2],
        weight_grads[3],
        small[1 + experts_of],
        small[2 + experts_of : 2 + experts_of + expert_count].T,
        gate_w_grad[None, :, :units].astype(jnp.float32),
        up_w_grad[None, :, :units].astype(jnp.float32),
        down_grad[None, :units].astype(jnp.float32),
    )


def solution(mesh):
    placed = (
        P("expert", None),
        P("expert", None),
        P(),
        P(),
        P(None, "tensor"),
        P(None, "tensor"),
        P(None, "tensor"),
        P("tensor", None),
        P(),
        P(),
        P("expert", None, "tensor"),
        P("expert", None, "tensor"),
        P("expert", "tensor", None),
        P("expert"),
        P("expert", None),
        P("expert", None),
        P("expert", None),
        P("expert", None),
    )
    return jax.shard_map(
        body,
        mesh=mesh,
        in_specs=placed,
        out_specs=(
            P("expert", "tensor"),
            P("expert", "tensor"),
            P(),
            P(),
            P(None, "tensor"),
            P(None, "tensor"),
            P(None, "tensor"),
            P("tensor", None),
            P(),
            P(),
            P("expert", None, "tensor"),
            P("expert", None, "tensor"),
            P("expert", "tensor", None),
        ),
        check_vma=False,
    )
```

```python
import functools
import math

import jax
import jax.numpy as jnp
import numpy as np
from jax import lax
from jax.experimental import pallas as pl
from jax.experimental.pallas import tpu as pltpu
from jax.sharding import PartitionSpec as P

HEAD = 128
QH = 2


EPSILON = 1e-06
MASKED = -1e30


def rotary_tables(tokens):
    frequency = np.exp(-math.log(10000.0) * np.arange(0, HEAD, 2, dtype=np.float32) / HEAD)
    angles = np.arange(tokens, dtype=np.float32)[:, None] * frequency.astype(np.float32)[None, :]
    angles = np.concatenate([angles, angles], axis=1).astype(np.float64)
    return jnp.asarray(np.cos(angles), jnp.float32), jnp.asarray(np.sin(angles), jnp.float32)


MESH = pl.DeviceIdType.MESH
MIB = 1 << 20
AHEAD_DEAL = 2
AHEAD = 2
FRONT = 3
SQUARES = 8
ROUTES, ROUTES_TWO, SLOTS = 0, 2, 4


def flip(number, other, count):
    total, bit = 0, 1
    while bit < count:
        total = total + lax.rem(lax.div(number, bit) + lax.div(other, bit), 2) * bit
        bit *= 2
    return total


def dot_nt(left, right):
    return lax.dot_general(
        left, right, (((1,), (1,)), ((), ())), preferred_element_type=jnp.float32
    )


class Place:
    def __init__(self):
        self.groups = lax.axis_size("expert")
        self.parts = lax.axis_size("tensor")
        self.spots = self.parts // 2
        self.expert = lax.axis_index("expert")
        self.tensor = lax.axis_index("tensor")
        self.spot = lax.div(self.tensor, 2)
        self.core = lax.rem(self.tensor, 2)

    def device(self, expert, tensor):
        return {"expert": expert, "tensor": tensor}

    def across(self, step):
        return lax.rem(self.spot + step, self.spots) * 2 + self.core

    def before(self, step):
        return lax.rem(self.spot + self.spots - step, self.spots) * 2 + self.core

    def meet(self, over_expert, whole_tensor=False):
        if whole_tensor:
            peers = [self.device(self.expert, self.along(step)) for step in range(1, self.parts)]
        else:
            peers = [self.device(self.expert, self.spot * 2 + 1 - self.core)]
            for step in range(1, self.spots):
                peers.append(self.device(self.expert, self.across(step)))
        if over_expert:
            for step in range(1, self.groups):
                peers.append(self.device(flip(self.expert, step, self.groups), self.tensor))
        barrier = pltpu.get_barrier_semaphore()
        for peer in peers:
            pl.semaphore_signal(barrier, inc=1, device_id=peer, device_id_type=MESH)
        pl.semaphore_wait(barrier, len(peers))

    def along(self, step):
        return lax.rem(self.tensor + step, self.parts)


def lasting(microseconds):
    return pl.CostEstimate(
        flops=0, bytes_accessed=int(microseconds * 3_000_000), transcendentals=0
    )


def remote(source, target, send, receive, device):
    return pltpu.make_async_remote_copy(
        src_ref=source,
        dst_ref=target,
        send_sem=send,
        recv_sem=receive,
        device_id=device,
        device_id_type=MESH,
    )


class Spread:
    @staticmethod
    def scratch(chunks, spots):
        return [
            pltpu.SemaphoreType.DMA((chunks,)),
            pltpu.SemaphoreType.DMA((chunks,)),
            pltpu.SemaphoreType.DMA((chunks, max(spots - 1, 1))),
            pltpu.SemaphoreType.DMA((chunks, max(spots - 1, 1))),
            pltpu.SemaphoreType.DMA((chunks, spots)),
            pltpu.SemaphoreType.DMA((chunks, spots)),
        ]

    def __init__(self, place, source, target, sems, over_expert, sharers=1, by_group=None):
        self.place, self.source, self.target = place, source, target
        self.by_group = over_expert if by_group is None else by_group
        self.first_send, self.first_land, self.side_send, self.side_land, self.core_send, self.core_land = sems
        self.over_expert, self.sharers = over_expert, sharers
        self.width = source.shape[3]
        self.chunks = target.shape[1]

    def owner(self, chunk):
        if not self.by_group:
            return chunk
        half, odd, pair = self.place.groups // 2, lax.rem(chunk, 2), lax.div(chunk, 2)
        even_way = jnp.minimum(chunk, 1) * half + pair
        odd_way = pair + (1 - jnp.minimum(pair, 1)) * half
        return flip(
            self.place.expert, odd * odd_way + (1 - odd) * even_way, self.place.groups
        )

    def spot_of(self, owner, tensor):
        first = pl.multiple_of(tensor * self.width, 128)
        return self.target.at[:, owner, :, pl.ds(first, self.width)]

    def block(self, owner):
        if self.sharers == 1:
            return self.source.at[:, owner]
        return self.source.at[:, lax.div(owner, self.sharers)]

    def send(self, chunk):
        place = self.place
        peer = self.owner(chunk)
        remote(
            self.block(peer),
            self.spot_of(place.expert, place.tensor),
            self.first_send.at[chunk],
            self.first_land.at[chunk],
            place.device(peer, place.tensor),
        ).start()

    def start(self, ahead):
        place = self.place
        own = self.owner(0)
        if not self.over_expert:
            return
        for chunk in range(1, min(ahead + 1, self.chunks)):
            self.send(chunk)
        copy = pltpu.make_async_copy(
            self.block(own), self.spot_of(own, place.tensor), self.first_send.at[0]
        )
        copy.start()
        copy.wait()

    def first(self, chunk):
        place = self.place
        owner = self.owner(chunk)
        mine = self.spot_of(owner, place.tensor)
        if self.over_expert:

            @pl.when(chunk > 0)
            def _():
                remote(
                    self.block(owner),
                    mine,
                    self.first_send.at[chunk],
                    self.first_land.at[chunk],
                    place.device(owner, place.tensor),
                ).wait_recv()

            held = mine
        else:
            pltpu.make_async_copy(self.block(owner), mine, self.first_send.at[chunk]).start()
            held = self.block(owner)
        for step in range(1, place.spots):
            remote(
                held,
                mine,
                self.side_send.at[chunk, step - 1],
                self.side_land.at[chunk, step - 1],
                place.device(place.expert, place.across(step)),
            ).start()
        remote(
            held,
            mine,
            self.core_send.at[chunk, 0],
            self.core_land.at[chunk, 0],
            place.device(place.expert, place.spot * 2 + 1 - place.core),
        ).start()

    def second(self, chunk):
        place = self.place
        owner = self.owner(chunk)
        for step in range(1, place.spots):
            came = self.spot_of(owner, place.before(step))
            remote(
                came,
                came,
                self.side_send.at[chunk, step - 1],
                self.side_land.at[chunk, step - 1],
                place.device(place.expert, place.across(step)),
            ).wait_recv()
            remote(
                came,
                came,
                self.core_send.at[chunk, step],
                self.core_land.at[chunk, step],
                place.device(place.expert, place.spot * 2 + 1 - place.core),
            ).start()

    def third(self, chunk):
        place = self.place
        owner = self.owner(chunk)
        flipped = 1 - 2 * place.core
        if not self.over_expert:
            mine = self.spot_of(owner, place.tensor)
            pltpu.make_async_copy(self.block(owner), mine, self.first_send.at[chunk]).wait()
        for step in range(place.spots):
            came = self.spot_of(owner, place.before(step) + flipped)
            remote(
                came,
                came,
                self.core_send.at[chunk, step],
                self.core_land.at[chunk, step],
                place.device(place.expert, place.spot * 2 + 1 - place.core),
            ).wait_recv()

    def finish(self, chunk):
        place = self.place
        owner = self.owner(chunk)
        mine = self.spot_of(owner, place.tensor)
        device = place.device(place.expert, place.tensor)
        if self.over_expert:

            @pl.when(chunk > 0)
            def _():
                remote(
                    self.block(owner),
                    mine,
                    self.first_send.at[chunk],
                    self.first_land.at[chunk],
                    device,
                ).wait_send()

        for step in range(1, place.spots):
            remote(
                mine,
                mine,
                self.side_send.at[chunk, step - 1],
                self.side_land.at[chunk, step - 1],
                device,
            ).wait_send()
        for step in range(place.spots):
            remote(
                mine, mine, self.core_send.at[chunk, step], self.core_land.at[chunk, step], device
            ).wait_send()


class Collect:
    @staticmethod
    def scratch(chunks, kinds, spots, rows, width, slots=2):
        return [
            pltpu.VMEM((slots, kinds, spots, 2, rows, width), jnp.bfloat16),
            pltpu.VMEM((slots, kinds, max(spots - 1, 1), rows, width), jnp.bfloat16),
            pltpu.VMEM((chunks, kinds, spots, rows, width), jnp.bfloat16),
            pltpu.VMEM((chunks, kinds, max(spots - 1, 1), rows, width), jnp.bfloat16),
            pltpu.SemaphoreType.DMA((chunks,)),
            pltpu.SemaphoreType.DMA((chunks,)),
            pltpu.SemaphoreType.DMA((chunks, max(spots - 1, 1))),
            pltpu.SemaphoreType.DMA((chunks, max(spots - 1, 1))),
        ]

    def __init__(self, place, refs):
        self.place = place
        self.stage, self.side, self.core_in, self.side_in = refs[:4]
        self.core_send, self.core_land, self.side_send, self.side_land = refs[4:]
        self.chunks = self.core_in.shape[0]
        self.slots = self.stage.shape[0]

    def core_copy(self, chunk):
        place = self.place
        return remote(
            self.stage.at[lax.rem(chunk, self.slots), :, :, 1 - place.core],
            self.core_in.at[chunk],
            self.core_send.at[chunk],
            self.core_land.at[chunk],
            place.device(place.expert, place.spot * 2 + 1 - place.core),
        )

    def side_copy(self, chunk, step):
        place = self.place
        return remote(
            self.side.at[lax.rem(chunk, self.slots), :, step - 1],
            self.side_in.at[chunk, :, step - 1],
            self.side_send.at[chunk, step - 1],
            self.side_land.at[chunk, step - 1],
            place.device(place.expert, place.across(step)),
        )

    def free_stage(self, chunk):
        @pl.when(chunk >= self.slots)
        def _():
            self.core_copy(chunk - self.slots).wait_send()

    def first(self, chunk):
        self.core_copy(chunk).start()

    def second(self, chunk):
        place = self.place
        slot = lax.rem(chunk, self.slots)
        self.core_copy(chunk).wait_recv()

        @pl.when(chunk >= self.slots)
        def _():
            for step in range(1, place.spots):
                self.side_copy(chunk - self.slots, step).wait_send()

        for step in range(1, place.spots):
            there = lax.rem(place.spot + step, place.spots)
            total = self.stage[slot, :, there, place.core].astype(jnp.float32) + self.core_in[
                chunk, :, there
            ].astype(jnp.float32)
            self.side[slot, :, step - 1] = total.astype(jnp.bfloat16)
            self.side_copy(chunk, step).start()

    def third(self, chunk):
        place = self.place
        slot = lax.rem(chunk, self.slots)
        total = self.stage[slot, :, place.spot, place.core].astype(jnp.float32) + self.core_in[
            chunk, :, place.spot
        ].astype(jnp.float32)
        for step in range(1, place.spots):
            self.side_copy(chunk, step).wait_recv()
            total = total + self.side_in[chunk, :, step - 1].astype(jnp.float32)
        return total

    def finish(self):
        for chunk in range(max(self.chunks - self.slots, 0), self.chunks):
            self.core_copy(chunk).wait_send()
            for step in range(1, self.place.spots):
                self.side_copy(chunk, step).wait_send()


def when(condition, action, *args):
    pl.when(condition)(functools.partial(action, *args))


def columns_of(rows):
    blank = jnp.zeros((128 - rows.shape[0], rows.shape[1]), jnp.float32)
    return jnp.concatenate([rows, blank], axis=0).T


def deal_kernel(
    capacity, experts_of, tokens, out_grad, ranks, rows_in,
    full, dealt_grads, marks, mark_rows,
    held, sending, slots, load_sem, *sems,
):
    place = Place()
    count, width = held.shape[1:]
    groups, bucket, _ = dealt_grads.shape
    low = jnp.bfloat16
    own = pl.ds(pl.multiple_of(place.tensor * width, 128), width)
    loads = [
        pltpu.make_async_copy(source.at[:, own], held.at[number], load_sem.at[number])
        for number, source in enumerate((tokens, out_grad))
    ]
    for load in loads:
        load.start()
    spread = Spread(place, sending, full, sems, True)
    place.meet(True)

    def dealt(number, group):
        rank = lax.broadcasted_iota(jnp.int32, (bucket, count), 0) + group * bucket
        chosen = (ranks[...] == rank).astype(low)
        return jnp.dot(chosen, held[number], preferred_element_type=jnp.float32).astype(low)

    loads[0].wait()
    for group in range(groups):
        sending[0, group] = dealt(0, group)
    spread.start(AHEAD_DEAL)

    def number_slots():
        rows = rows_in[...].astype(jnp.float32)
        columns = columns_of(rows)
        lane = lax.broadcasted_iota(jnp.int32, (count, 128), 1)
        found = jnp.zeros((count, 128), jnp.float32)
        for way in range(2):
            target = columns[:, ROUTES_TWO + way : ROUTES_TWO + way + 1]
            order = columns[:, 4 + way : 5 + way]
            position = jnp.zeros((count, 1), jnp.float32)
            for other in range(2):
                earlier = (rows[ROUTES_TWO + other : ROUTES_TWO + other + 1] == target) & (
                    rows[4 + other : 5 + other] < order
                )
                position = position + jnp.sum(
                    jnp.where(earlier, 1.0, 0.0), axis=1, keepdims=True
                )
            slot = jnp.where(
                position < capacity, target * capacity + position, experts_of * capacity
            )
            marks[:, SLOTS + way : SLOTS + way + 1] = slot.astype(jnp.int32)
            found = jnp.where(lane == way, slot, found)
        marks[:, :SLOTS] = columns[:, :SLOTS].astype(jnp.int32)
        slots[...] = found
        mark_rows[...] = slots[...].T[:8].astype(jnp.int32)

    def deal_grads():
        loads[1].wait()
        for group in range(groups):
            dealt_grads[group] = dealt(1, group)

    def step(turn, carry):
        when(turn < spread.chunks, spread.first, turn)
        when(turn + 1 + AHEAD_DEAL < spread.chunks, spread.send, turn + 1 + AHEAD_DEAL)
        when(turn >= 1, spread.second, turn - 1)
        when(turn == 1, deal_grads)
        when(turn == 2, number_slots)
        return carry

    lax.fori_loop(0, spread.chunks + 1, step, 0)

    def last(turn, carry):
        spread.third(turn)
        spread.finish(turn)
        return carry

    lax.fori_loop(0, spread.chunks, last, 0)


def deal_rows(tokens, out_grad, ranks, rows_in, capacity, experts_of, collective):
    groups, parts = lax.axis_size("expert"), lax.axis_size("tensor")
    count, model_width = tokens.shape
    width, bucket = model_width // parts, count // groups
    low = tokens.dtype
    inside = pl.BlockSpec(memory_space=pltpu.VMEM)
    anywhere = pl.BlockSpec(memory_space=pl.ANY)
    return pl.pallas_call(
        functools.partial(deal_kernel, capacity, experts_of),
        out_shape=(
            jax.ShapeDtypeStruct((1, groups, bucket, model_width), low),
            jax.ShapeDtypeStruct((groups, bucket, width), low),
            jax.ShapeDtypeStruct((count, 8), jnp.int32),
            jax.ShapeDtypeStruct((8, count), jnp.int32),
        ),
        in_specs=[anywhere] * 2 + [inside] * 2,
        out_specs=(anywhere,) + (inside,) * 3,
        scratch_shapes=[
            pltpu.VMEM((2, count, width), low),
            pltpu.VMEM((1, groups, bucket, width), low),
            pltpu.VMEM((count, 128), jnp.float32),
            pltpu.SemaphoreType.DMA((2,)),
        ]
        + Spread.scratch(groups, parts // 2),
        compiler_params=pltpu.CompilerParams(
            collective_id=collective, has_side_effects=True, vmem_limit_bytes=40 * MIB
        ),
        cost_estimate=lasting(35),
    )(tokens, out_grad, ranks, rows_in)


def experts_kernel(sharers, *refs):
    (
        source, source_grads, gates, gate_hbm, up_hbm, down_hbm, early_grads,
        inbox, inbox_grads, grads_out, middle_out, gate_out, up_out, returned,
        gate_w, up_w, down_w, rows, grads, middle, gate_g, up_g, closing, gates_in,
        load_sem, store_sem, back_send, back_land, mark_send, mark_land,
    ) = refs[:30]
    place = Place()
    spread = Spread(place, source, inbox, refs[30:36], True, sharers)
    spread_grads = Spread(place, source_grads, inbox_grads, refs[36:42], True, sharers)
    collect = Collect(place, refs[42:])
    chunks = spread.chunks
    width = source.shape[3]
    units = gate_w.shape[1]
    tile = 704 if units % 704 == 0 else units
    capacity = rows.shape[0]
    loads = [
        pltpu.make_async_copy(held, kept, load_sem.at[number])
        for number, (held, kept) in enumerate(
            ((gate_hbm, gate_w), (up_hbm, up_w), (down_hbm, down_w))
        )
    ]
    for load in loads:
        load.start()
    place.meet(True)

    def mark_copy(chunk):
        peer = spread.owner(chunk)
        return remote(
            gates.at[lax.div(peer, sharers)],
            gates_in.at[place.expert],
            mark_send.at[chunk],
            mark_land.at[chunk],
            place.device(peer, place.tensor),
        )

    def mark_landed(chunk):
        peer = spread.owner(chunk)
        return remote(
            gates.at[lax.div(peer, sharers)],
            gates_in.at[peer],
            mark_send.at[chunk],
            mark_land.at[chunk],
            place.device(peer, place.tensor),
        )

    spread.start(AHEAD)
    for chunk in range(1, chunks):
        mark_copy(chunk).start()
    own_mark = pltpu.make_async_copy(
        gates.at[lax.div(place.expert, sharers)], gates_in.at[place.expert], mark_send.at[0]
    )
    own_mark.start()
    own_mark.wait()
    early = min(FRONT, chunks)
    for chunk in range(early, min(AHEAD + 1, chunks)):
        spread_grads.send(chunk)

    def stores(owner):
        return [
            pltpu.make_async_copy(held, out.at[owner], store_sem.at[number])
            for number, (held, out) in enumerate(
                ((middle, middle_out), (gate_g, gate_out), (up_g, up_out), (grads, grads_out))
            )
        ]

    def fetches(owner):
        return [
            pltpu.make_async_copy(inbox.at[0, owner], rows, load_sem.at[3]),
            pltpu.make_async_copy(early_grads.at[0, owner], grads, load_sem.at[4]),
            pltpu.make_async_copy(inbox_grads.at[0, owner], grads, load_sem.at[4]),
        ]

    def work(chunk):
        owner = spread.owner(chunk)

        @pl.when(chunk == 0)
        def _():
            for load in loads:
                load.wait()

        @pl.when(chunk > 0)
        def _():
            for store in stores(spread.owner(chunk - 1)):
                store.wait()
            mark_landed(chunk).wait_recv()

        spread.third(chunk)
        when(chunk >= early, spread_grads.third, chunk)
        fetch, fetch_early, fetch_late = fetches(owner)
        fetch.start()
        when(chunk < early, fetch_early.start)
        when(chunk >= early, fetch_late.start)
        fetch.wait()
        fetch_early.wait()
        wide = gates_in.shape[2]
        line = jnp.broadcast_to(gates_in[owner][:1], (capacity, wide))
        here = lax.broadcasted_iota(jnp.int32, (capacity, wide), 0) == lax.broadcasted_iota(
            jnp.int32, (capacity, wide), 1
        )
        gate_column = jnp.sum(jnp.where(here, line, 0.0), axis=1, keepdims=True)
        grads[...] = (grads[...].astype(jnp.float32) * gate_column).astype(jnp.bfloat16)
        for first in range(0, units, tile):
            here = slice(first, first + tile)
            gate = jnp.dot(rows[...], gate_w[:, here], preferred_element_type=jnp.float32)
            up = jnp.dot(rows[...], up_w[:, here], preferred_element_type=jnp.float32)
            sig = jax.nn.sigmoid(gate)
            act = gate * sig
            middle[:, here] = (act * up).astype(jnp.bfloat16)
            grad = dot_nt(grads[...], down_w[here, :])
            gate_g[:, here] = (grad * up * sig * (1.0 + gate * (1.0 - sig))).astype(jnp.bfloat16)
            up_g[:, here] = (grad * act).astype(jnp.bfloat16)
        for store in stores(owner):
            store.start()
        made, fed = 2 * chunk, 2 * chunk + 1
        when(chunk >= 1, collect.second, made - 1)
        when(chunk >= 1, close, made - 2)
        collect.free_stage(made)
        for spot in range(place.spots):
            for core in range(2):
                first = (spot * 2 + core) * width
                here = slice(first, first + width)
                collect.stage[lax.rem(made, 4), 0, spot, core] = jnp.dot(
                    middle[...], down_w[:, here], preferred_element_type=jnp.float32
                ).astype(jnp.bfloat16)
        collect.first(made)
        collect.free_stage(fed)
        for spot in range(place.spots):
            for core in range(2):
                first = (spot * 2 + core) * width
                here = slice(first, first + width)
                collect.stage[lax.rem(fed, 4), 0, spot, core] = (
                    dot_nt(gate_g[...], gate_w[here, :]) + dot_nt(up_g[...], up_w[here, :])
                ).astype(jnp.bfloat16)
        collect.first(fed)
        collect.second(made)
        when(chunk >= 1, close, made - 1)

    def back_copy(item, owner=None):
        peer = spread.owner(lax.div(item, 2))
        return remote(
            closing.at[lax.rem(item, 4)],
            returned.at[lax.rem(item, 2), place.expert if owner is None else owner],
            back_send.at[item],
            back_land.at[item],
            place.device(peer, place.tensor),
        )

    def close(item):
        slot = lax.rem(item, 4)
        total = collect.third(item)[0]

        @pl.when(item >= 6)
        def _():
            back_copy(item - 4).wait_send()

        closing[slot] = total.astype(jnp.bfloat16)

        @pl.when(item >= 2)
        def _():
            back_copy(item).start()

        @pl.when(item < 2)
        def _():
            own = pltpu.make_async_copy(
                closing.at[slot],
                returned.at[lax.rem(item, 2), place.expert],
                back_send.at[item],
            )
            own.start()
            own.wait()

    def send_grads(chunk):
        when(chunk >= early, spread_grads.send, chunk)

    def step(turn, carry):
        now = turn - 2
        when(turn < chunks, spread.first, turn)
        when(turn + 1 + AHEAD < chunks, spread.send, turn + 1 + AHEAD)
        when((turn >= 1) & (turn <= chunks), spread.second, turn - 1)
        when((turn >= early - 1 - AHEAD) & (turn + 1 + AHEAD < chunks), send_grads, turn + 1 + AHEAD)
        when((turn >= early) & (turn < chunks), spread_grads.first, turn)
        when((turn > early) & (turn <= chunks), spread_grads.second, turn - 1)
        when(now >= 0, work, now)
        return carry

    lax.fori_loop(0, chunks + 2, step, 0)
    items = 2 * chunks
    collect.second(items - 1)
    close(items - 2)
    close(items - 1)

    def last(turn, carry):
        spread.finish(turn)
        when(turn >= early, spread_grads.finish, turn)

        @pl.when(turn > 0)
        def _():
            mark_copy(turn).wait_send()
            for item in (2 * turn, 2 * turn + 1):
                back_copy(item, spread.owner(turn)).wait_recv()

        return carry

    lax.fori_loop(0, chunks, last, 0)
    for store in stores(spread.owner(chunks - 1)):
        store.wait()
    for item in range(max(items - 4, 2), items):
        back_copy(item).wait_send()
    collect.finish()


def experts(source, source_grads, early_grads, gates, gate_w, up_w, down_w, sharers, collective):
    _, capacity, width = source.shape
    groups, parts = lax.axis_size("expert"), lax.axis_size("tensor")
    spots = parts // 2
    model_width, units = gate_w.shape
    low = jnp.bfloat16
    anywhere = pl.BlockSpec(memory_space=pl.ANY)
    hidden_rows = jax.ShapeDtypeStruct((groups, capacity, units), low)
    return pl.pallas_call(
        functools.partial(experts_kernel, sharers),
        out_shape=(
            jax.ShapeDtypeStruct((1, groups, capacity, model_width), low),
            jax.ShapeDtypeStruct((1, groups, capacity, model_width), low),
            jax.ShapeDtypeStruct((groups, capacity, model_width), low),
            hidden_rows,
            hidden_rows,
            hidden_rows,
            jax.ShapeDtypeStruct((2, groups, capacity, width), low),
        ),
        in_specs=[anywhere] * 7,
        out_specs=(anywhere,) * 7,
        scratch_shapes=[
            pltpu.VMEM((model_width, units), low),
            pltpu.VMEM((model_width, units), low),
            pltpu.VMEM((units, model_width), low),
            pltpu.VMEM((capacity, model_width), low),
            pltpu.VMEM((capacity, model_width), low),
            pltpu.VMEM((capacity, units), low),
            pltpu.VMEM((capacity, units), low),
            pltpu.VMEM((capacity, units), low),
            pltpu.VMEM((4, capacity, width), low),
            pltpu.VMEM((groups,) + gates.shape[1:], jnp.float32),
            pltpu.SemaphoreType.DMA((5,)),
            pltpu.SemaphoreType.DMA((4,)),
            pltpu.SemaphoreType.DMA((2 * groups,)),
            pltpu.SemaphoreType.DMA((2 * groups,)),
            pltpu.SemaphoreType.DMA((groups,)),
            pltpu.SemaphoreType.DMA((groups,)),
        ]
        + Spread.scratch(groups, spots)
        + Spread.scratch(groups, spots)
        + Collect.scratch(2 * groups, 1, spots, capacity, width, 4),
        compiler_params=pltpu.CompilerParams(
            collective_id=collective, has_side_effects=True, vmem_limit_bytes=60 * MIB
        ),
        cost_estimate=lasting(180),
    )(source[None], source_grads[None], gates, gate_w, up_w, down_w, early_grads)


class Return:
    @staticmethod
    def scratch(pieces, rows, width, groups):
        return [
            pltpu.VMEM((pieces, rows, width), jnp.bfloat16),
            pltpu.SemaphoreType.DMA((groups,)),
            pltpu.SemaphoreType.DMA((groups,)),
            pltpu.SemaphoreType.DMA,
        ]

    def __init__(self, place, back, refs):
        self.place, self.back = place, back
        self.ready, self.sent, self.landed, self.kept = refs
        self.bucket = back.shape[1]
        self.each = self.ready.shape[1] // self.bucket

    def block(self, piece, number):
        return self.ready.at[piece, pl.ds(number * self.bucket, self.bucket)]

    def copy(self, piece, number, index):
        target = piece * self.each + number
        return remote(
            self.block(piece, number),
            self.back.at[index],
            self.sent.at[target],
            self.landed.at[index],
            self.place.device(target, self.place.tensor),
        )

    def start(self, piece, values):
        place = self.place
        self.ready[piece] = values
        for number in range(self.each):
            target = piece * self.each + number

            @pl.when(target != place.expert)
            def _():
                self.copy(piece, number, place.expert).start()

            @pl.when(target == place.expert)
            def _():
                own = pltpu.make_async_copy(
                    self.block(piece, number), self.back.at[place.expert], self.kept
                )
                own.start()
                own.wait()

    def finish(self, piece):
        for number in range(self.each):
            target = piece * self.each + number

            @pl.when(target != self.place.expert)
            def _():
                self.copy(piece, number, self.place.expert).wait_send()
                self.copy(piece, number, target).wait_recv()


def pair_grad(gates, gate_grads, names, count):
    shared = gates[0] * gate_grads[0] + gates[1] * gate_grads[1]
    lane = lax.broadcasted_iota(jnp.int32, (gates[0].shape[0], count), 1)
    return sum(
        jnp.where(name == lane, gate * (grad - shared), 0.0)
        for gate, grad, name in zip(gates, gate_grads, names)
    )


def precise_dot(left, right, contract=(1, 0)):
    return lax.dot_general(
        left,
        right,
        (((contract[0],), (contract[1],)), ((), ())),
        precision=lax.Precision.HIGHEST,
        preferred_element_type=jnp.float32,
    )


class Exchange:
    @staticmethod
    def scratch(pieces, parts, rows, lanes):
        wide = (rows + 127) // 128 * 128
        return [
            pltpu.VMEM((pieces, lanes, wide), jnp.float32),
            pltpu.VMEM((pieces, parts - 1, lanes, wide), jnp.float32),
            pltpu.SemaphoreType.DMA((pieces, parts - 1)),
            pltpu.SemaphoreType.DMA((pieces, parts - 1)),
        ]

    def __init__(self, place, refs):
        self.place = place
        self.own, self.got, self.sent, self.landed = refs

    def copy(self, piece, step):
        return remote(
            self.own.at[piece],
            self.got.at[piece, step - 1],
            self.sent.at[piece, step - 1],
            self.landed.at[piece, step - 1],
            self.place.device(self.place.expert, self.place.along(step)),
        )

    def start(self, piece, values):
        _, lanes, wide = self.own.shape
        rows = values.shape[0]
        if rows < wide:
            blank = jnp.zeros((wide - rows, 128), jnp.float32)
            values = jnp.concatenate([values, blank], axis=0)
        self.own[piece] = values.T[:lanes]
        for step in range(1, self.place.parts):
            self.copy(piece, step).start()

    def total(self, piece, rows):
        _, lanes, wide = self.own.shape
        total = self.own[piece]
        for step in range(1, self.place.parts):
            self.copy(piece, step).wait_recv()
            total = total + self.got[piece, step - 1]
        blank = jnp.zeros((128 - lanes, wide), jnp.float32)
        return jnp.concatenate([total, blank], axis=0).T[:rows]

    def finish(self, piece):
        for step in range(1, self.place.parts):
            self.copy(piece, step).wait_send()


def closing_kernel(jobs, *refs):
    (
        normed_hbm, gain, factor, gates, marks, logits, gate_grads, router_t, gain_two, router_two,
        query_grad, key_grad, value_grad, gated_t, grads_hbm,
        hidden_hbm, resid_hbm, query_hbm, key_hbm, value_hbm,
    ), refs = refs[:20], refs[20:]
    grads = (query_grad, key_grad, value_grad)
    count = len(grads)
    lefts, rights, refs = refs[:3], refs[3:6], refs[6:]
    summed, back, small_out, products, refs = refs[:4], refs[4], refs[5], refs[6:9], refs[9:]
    (
        hold, hold_out, partial, small_own, small_got, small_sum,
        hidden, resid, w_query, w_key, w_value, right, left, product,
        ring_send, ring_land, small_send, small_land, last_send, last_land,
        own_sem, load_sem, job_sem, normed_t, hidden_grads, first_sem,
    ) = refs[:26]
    weights = (w_query, w_key, w_value)
    place = Place()
    exchange, of_gates = Exchange(place, refs[26:30]), Exchange(place, refs[30:34])
    giving = Return(place, back, refs[34:38])
    collect = Collect(place, refs[38:])
    first_loads = [
        pltpu.make_async_copy(normed_hbm, normed_t, first_sem.at[0]),
        pltpu.make_async_copy(grads_hbm, hidden_grads, first_sem.at[1]),
    ]
    for load in first_loads:
        load.start()
    groups, parts = place.groups, place.parts
    pieces, rows = collect.core_in.shape[0], collect.core_in.shape[3]
    width = hidden.shape[1]
    block = hold.shape[3]
    experts_of = logits.shape[1]
    own_columns = pl.ds(pl.multiple_of(place.tensor * width, 128), width)
    loads = [
        pltpu.make_async_copy(held, kept, load_sem.at[number])
        for number, (held, kept) in enumerate(
            (
                (query_hbm, w_query), (key_hbm, w_key), (value_hbm, w_value),
                (hidden_hbm, hidden), (resid_hbm.at[:, own_columns], resid),
            )
        )
    ]
    for load in loads:
        load.start()
    place.meet(True, True)

    parity, half = lax.rem(place.expert, 2), lax.div(place.expert, 2)
    at = half + parity * (groups - 1 - 2 * half)

    def member(spot):
        spot = lax.rem(spot + groups, groups)
        high = lax.div(spot, groups // 2)
        return (1 - high) * 2 * spot + high * (2 * (groups - 1 - spot) + 1)

    ways = ((0, 1), (1, -1))

    def first_row(way, sign, step):
        spot = lax.rem(at - sign * step + 2 * groups, groups)
        return pl.multiple_of((way * groups + spot) * block, block)

    def ring_copy(step, way, sign, number, source, target):
        return remote(
            source,
            target,
            ring_send.at[step, way, number],
            ring_land.at[step, way, number],
            place.device(member(at + sign), place.tensor),
        )

    out_rows, out_columns = hold_out.shape[2:]

    def first_column(sign, step):
        spot = lax.rem(at - sign * step + 2 * groups, groups)
        return pl.multiple_of(spot * out_columns, 128)

    def slot(step, way, number):
        if number == count:
            return hold_out.at[step, way]
        return hold.at[step, way, number]

    def spot_out(step, way, sign, number):
        if number == count:
            return summed[number].at[
                pl.ds(way * out_rows, out_rows), pl.ds(first_column(sign, step), out_columns)
            ]
        return summed[number].at[pl.ds(first_row(way, sign, step), block)]

    def own_part(step, way, sign, number):
        if number == count:
            return jnp.dot(
                gated_t[way * out_rows : (way + 1) * out_rows, :],
                hidden_grads[:, pl.ds(first_column(sign, step), out_columns)],
                preferred_element_type=jnp.float32,
            )
        return jnp.dot(
            normed_t[pl.ds(first_row(way, sign, step), block), :],
            grads[number][...],
            preferred_element_type=jnp.float32,
        )

    def ring(step):
        for number in range(count + 1):
            for way, sign in ways:

                @pl.when((step >= 1) & (step < groups))
                def _():
                    held = slot(step, way, number)
                    ring_copy(step - 1, way, sign, number, held, held).wait_recv()

                @pl.when(step >= groups)
                def _():
                    held = spot_out(step, way, sign, number)
                    ring_copy(step - 1, way, sign, number, held, held).wait_recv()

                @pl.when(step < groups)
                def _():
                    own = own_part(step, way, sign, number)
                    held = slot(step, way, number)

                    @pl.when(step == 0)
                    def _():
                        held[...] = own.astype(jnp.bfloat16)

                    @pl.when(step > 0)
                    def _():
                        held[...] = (own + held[...].astype(jnp.float32)).astype(jnp.bfloat16)

                @pl.when(step < groups - 1)
                def _():
                    ring_copy(
                        step, way, sign, number, slot(step, way, number), slot(step + 1, way, number)
                    ).start()

                @pl.when(step == groups - 1)
                def _():
                    held, there = slot(step, way, number), spot_out(step, way, sign, number)
                    ring_copy(step, way, sign, number, held, there).start()
                    pltpu.make_async_copy(held, there, own_sem.at[way, number]).start()

                @pl.when((step >= groups) & (step < 2 * groups - 2))
                def _():
                    held = spot_out(step, way, sign, number)
                    ring_copy(step, way, sign, number, held, held).start()

    def ring_finish(step, carry):
        for number in range(count + 1):
            for way, sign in ways:
                held = slot(0, way, number)
                ring_copy(step, way, sign, number, held, held).wait_send()
        return carry

    def band(piece):
        return pl.ds(pl.multiple_of(piece * rows, rows), rows)

    def project(piece):
        collect.free_stage(piece)
        side = lax.rem(piece, 2)
        for spot in range(place.spots):
            for core in range(2):
                first = (spot * 2 + core) * width
                part = None
                for grad, weight in zip(grads, weights):
                    term = dot_nt(grad[band(piece), :], weight[first : first + width, :])
                    part = term if part is None else part + term
                collect.stage[side, 0, spot, core] = part.astype(jnp.bfloat16)
        collect.first(piece)

    def scaled_of(piece):
        return resid[band(piece), :].astype(jnp.float32) * factor[band(piece), :]

    def tell(piece):
        lane = lax.broadcasted_iota(jnp.int32, (rows, 128), 1)
        values = jnp.zeros((rows, 128), jnp.float32)
        held = gate_grads.shape[1]
        for number in range(held):
            column = gate_grads[band(piece), number : number + 1]
            values = jnp.where(lane == place.tensor * held + number, column, values)
        of_gates.start(piece, values)

    def measure(piece):
        total = collect.third(piece)[0]
        partial[piece] = total
        inner = jnp.sum(total * scaled_of(piece) * gain[...], axis=1, keepdims=True)
        exchange.start(piece, jnp.broadcast_to(inner, (rows, 128)))

    def conclude(piece):
        here = band(piece)
        every = of_gates.total(piece, rows)[:, :experts_of]
        lane = lax.broadcasted_iota(jnp.int32, (rows, experts_of), 1)
        names = [marks[here, ROUTES + way : ROUTES + way + 1] for way in range(2)]
        logit_grad = pair_grad(
            [gates[here, way : way + 1] for way in range(2)],
            [
                jnp.sum(jnp.where(name == lane, every, 0.0), axis=1, keepdims=True)
                for name in names
            ],
            names,
            experts_of,
        )
        inner = exchange.total(piece, rows)[:, :1] + jnp.sum(
            logit_grad * logits[here, :], axis=1, keepdims=True
        )
        mean = inner / (width * parts)
        scaled = scaled_of(piece)
        grad = partial[piece] + precise_dot(logit_grad, router_t[...])
        small_own[0:1, :] += jnp.sum(grad * scaled, axis=0, keepdims=True)
        small_own[1 : 1 + experts_of, :] += precise_dot(logit_grad, scaled * gain[...], (0, 0))
        result = hidden[here, :] + factor[here, :] * (grad * gain[...] - scaled * mean)
        giving.start(piece, result.astype(jnp.bfloat16))

    def small_copy(step):
        return remote(
            small_own,
            small_got.at[step - 1],
            small_send.at[step - 1],
            small_land.at[step - 1],
            place.device(flip(place.expert, step, groups), place.tensor),
        )

    def last_copy(step, origin):
        return remote(
            small_sum,
            small_out.at[origin],
            last_send.at[step - 1],
            last_land.at[step - 1],
            place.device(place.expert, place.along(step)),
        )

    own_small = pltpu.make_async_copy(small_sum, small_out.at[place.tensor], own_sem.at[0, count + 1])

    def small_first():
        first = 1 + experts_of
        small_own[first : first + 1, :] = gain_two[...]
        small_own[first + 1 : first + 1 + router_two.shape[0], :] = router_two[...]
        for step in range(1, groups):
            small_copy(step).start()

    def small_second():
        total = small_own[...]
        for step in range(1, groups):
            small_copy(step).wait_recv()
            total = total + small_got[step - 1]
        small_sum[...] = total
        own_small.start()
        for step in range(1, parts):
            last_copy(step, place.tensor).start()

    small_own[...] = jnp.zeros_like(small_own)
    for load in first_loads:
        load.wait()
    turns = max(2 * groups - 1, pieces + 5)
    tiles = sum(job[0] for job in jobs)
    each_turn = -(-tiles // turns)

    def job_of(number, first, action):
        start = 0
        for index, (many, size, wide) in enumerate(jobs):
            when(
                (number >= start) & (number < start + many),
                functools.partial(action, index, size, wide),
                number - start,
            )
            start += many

    def right_copy(index, wide):
        return pltpu.make_async_copy(rights[index], right.at[:, pl.ds(0, wide)], job_sem.at[4])

    def left_copy(index, size, tile, side):
        first = pl.multiple_of(tile * size, 128)
        return pltpu.make_async_copy(
            lefts[index].at[:, pl.ds(first, size)],
            left.at[side, :, pl.ds(0, size)],
            job_sem.at[side],
        )

    def product_copy(index, size, wide, tile, side):
        first = pl.multiple_of(tile * size, 8)
        return pltpu.make_async_copy(
            product.at[side, pl.ds(0, size), pl.ds(0, wide)],
            products[index].at[pl.ds(first, size)],
            job_sem.at[2 + side],
        )

    def multiply(number):
        side = lax.rem(number, 2)

        def fetch_next(index, size, wide, tile):
            left_copy(index, size, tile, 1 - side).start()

        def stored(index, size, wide, tile):
            product_copy(index, size, wide, tile, side).wait()

        def work(index, size, wide, tile):
            @pl.when(tile == 0)
            def _():
                right_copy(index, wide).start()
                right_copy(index, wide).wait()

            left_copy(index, size, tile, side).wait()
            product[side, :size, :wide] = dot_tn(left[side, :, :size], right[:, :wide]).astype(
                jnp.bfloat16
            )
            product_copy(index, size, wide, tile, side).start()

        job_of(number + 1, None, fetch_next)
        job_of(number - 2, None, stored)
        job_of(number, None, work)

    left_copy(0, jobs[0][1], 0, 0).start()

    def turn_step(turn, carry):
        when(turn < 2 * groups - 1, ring, turn)

        @pl.when(turn == 0)
        def _():
            for load in loads:
                load.wait()

        when((turn >= 3) & (turn < pieces + 3), conclude, turn - 3)
        when((turn >= 2) & (turn < pieces + 2), measure, turn - 2)
        when((turn >= 1) & (turn < pieces + 1), collect.second, turn - 1)
        when(turn < pieces, project, turn)
        when(turn < pieces, tell, turn)
        when(turn == pieces + 3, small_first)
        when(turn == pieces + 4, small_second)
        lax.fori_loop(
            turn * each_turn,
            jnp.minimum((turn + 1) * each_turn, tiles),
            lambda number, held: (multiply(number), held)[1],
            0,
        )
        return carry

    lax.fori_loop(0, turns, turn_step, 0)
    for number in (tiles - 2, tiles - 1):
        index, tile = 0, number
        while tile >= jobs[index][0]:
            tile -= jobs[index][0]
            index += 1
        product_copy(index, jobs[index][1], jobs[index][2], tile, number % 2).wait()
    lax.fori_loop(0, 2 * groups - 2, ring_finish, 0)
    for number in range(count + 1):
        for way, sign in ways:
            pltpu.make_async_copy(
                slot(groups - 1, way, number),
                spot_out(groups - 1, way, sign, number),
                own_sem.at[way, number],
            ).wait()
    collect.finish()
    for step in range(1, groups):
        small_copy(step).wait_send()
    own_small.wait()
    for step in range(1, parts):
        origin = lax.rem(place.tensor + parts - step, parts)
        last_copy(step, place.tensor).wait_send()
        last_copy(step, origin).wait_recv()

    def settle(piece, carry):
        exchange.finish(piece)
        of_gates.finish(piece)
        giving.finish(piece)
        return carry

    lax.fori_loop(0, pieces, settle, 0)


def closing(
    normed_t, columns_in, grads, gated_t, hidden_grads, hidden, resid, weights,
    lefts, rights, pieces, collective,
):
    groups, parts = lax.axis_size("expert"), lax.axis_size("tensor")
    spots = parts // 2
    model_width, tokens = normed_t.shape
    columns = grads[0].shape[1]
    width = hidden.shape[1]
    count = len(grads)
    small = jax.ShapeDtypeStruct(
        ((2 + columns_in[4].shape[1] + columns_in[-1].shape[0] + 7) // 8 * 8, width), jnp.float32
    )
    rows = tokens // pieces
    block = model_width // (2 * groups)
    low, full = jnp.bfloat16, jnp.float32
    inside = pl.BlockSpec(memory_space=pltpu.VMEM)
    anywhere = pl.BlockSpec(memory_space=pl.ANY)
    dma = pltpu.SemaphoreType.DMA
    jobs = []
    for left, right in zip(lefts, rights):
        jobs.append((left.shape[1] // 128, 128, right.shape[1]))
    depth = lefts[0].shape[0]
    tile = max(job[1] for job in jobs)
    wide = max(job[2] for job in jobs)
    return pl.pallas_call(
        functools.partial(closing_kernel, tuple(jobs)),
        out_shape=(
            *(jax.ShapeDtypeStruct((model_width, columns), low) for _ in range(count)),
            jax.ShapeDtypeStruct((columns, model_width), low),
            jax.ShapeDtypeStruct((groups, tokens // groups, width), low),
            jax.ShapeDtypeStruct((parts,) + small.shape, full),
            *(
                jax.ShapeDtypeStruct((left.shape[1], right.shape[1]), low)
                for left, right in zip(lefts, rights)
            ),
        ),
        in_specs=[anywhere] + [inside] * 13 + [anywhere] * 12,
        out_specs=(anywhere,) * 9,
        scratch_shapes=[
            pltpu.VMEM((groups, 2, count, block, columns), low),
            pltpu.VMEM((groups, 2, columns // 2, model_width // groups), low),
            pltpu.VMEM((pieces, rows, width), full),
            pltpu.VMEM(small.shape, full),
            pltpu.VMEM((groups - 1,) + small.shape, full),
            pltpu.VMEM(small.shape, full),
            pltpu.VMEM((tokens, width), full),
            pltpu.VMEM((tokens, width), low),
            *(pltpu.VMEM(weight.shape, low) for weight in weights),
            pltpu.VMEM((depth, wide), low),
            pltpu.VMEM((2, depth, tile), low),
            pltpu.VMEM((2, tile, wide), low),
            dma((2 * groups - 2, 2, count + 1)),
            dma((2 * groups - 2, 2, count + 1)),
            dma((groups - 1,)),
            dma((groups - 1,)),
            dma((parts - 1,)),
            dma((parts - 1,)),
            dma((2, count + 2)),
            dma((5,)),
            dma((5,)),
            pltpu.VMEM(normed_t.shape, low),
            pltpu.VMEM(hidden_grads.shape, low),
            dma((2,)),
        ]
        + Exchange.scratch(pieces, parts, rows, 8)
        + Exchange.scratch(pieces, parts, rows, (columns_in[4].shape[1] + 7) // 8 * 8)
        + Return.scratch(pieces, rows, width, groups)
        + Collect.scratch(pieces, 1, spots, rows, width),
        compiler_params=pltpu.CompilerParams(
            collective_id=collective, has_side_effects=True, vmem_limit_bytes=60 * MIB
        ),
        cost_estimate=lasting(200),
    )(
        normed_t, *columns_in, *grads, gated_t, hidden_grads, hidden, resid, *weights,
        *lefts, *rights,
    )


def settle_kernel(
    came, marks, gates, logits, factor, hidden, grads, gain, router_t,
    back, hidden_grad, gathered, router_grad, gain_grad,
    row_grads, ready, *refs,
):
    place = Place()
    exchange = Exchange(place, refs[:4])
    giving = Return(place, back, refs[4:8])
    pieces, rows, width = row_grads.shape
    spread = Spread(place, ready, gathered, refs[8:], False)
    slots, experts_of = came.shape[1], logits.shape[1]
    low = jnp.bfloat16
    place.meet(True, True)
    router_grad[...] = jnp.zeros_like(router_grad)
    gain_grad[...] = jnp.zeros_like(gain_grad)

    def band(piece):
        return pl.ds(pl.multiple_of(piece * rows, rows), rows)

    def scaled_of(piece):
        return hidden[band(piece), :] * factor[band(piece), :]

    def gather(piece):
        here = band(piece)
        numbers = lax.broadcasted_iota(jnp.int32, (rows, slots), 1)
        chosen = [(marks[here, SLOTS + way : SLOTS + way + 1] == numbers).astype(low) for way in range(2)]
        result = hidden[here, :]
        grad = grads[here, :].astype(jnp.float32)
        lane = lax.broadcasted_iota(jnp.int32, (rows, 128), 1)
        stats = jnp.zeros((rows, 128), jnp.float32)
        for way in range(2):
            value = jnp.dot(chosen[way], came[0], preferred_element_type=jnp.float32)
            result = result + gates[here, way : way + 1] * value
            stats = jnp.where(lane == way, jnp.sum(value * grad, axis=1, keepdims=True), stats)
        total = jnp.dot(chosen[0] + chosen[1], came[1], preferred_element_type=jnp.float32)
        row_grads[piece] = total
        inner = jnp.sum(total * scaled_of(piece) * gain[...], axis=1, keepdims=True)
        exchange.start(piece, jnp.where(lane == 2, inner, stats))
        giving.start(piece, result.astype(low))

    def settle(piece):
        here = band(piece)
        stats = exchange.total(piece, rows)
        logit_grad = pair_grad(
            [gates[here, way : way + 1] for way in range(2)],
            [stats[:, way : way + 1] for way in range(2)],
            [marks[here, ROUTES_TWO + way : ROUTES_TWO + way + 1] for way in range(2)],
            experts_of,
        )
        mean = (
            stats[:, 2:3] + jnp.sum(logit_grad * logits[here, :], axis=1, keepdims=True)
        ) / (width * place.parts)
        scaled = scaled_of(piece)
        grad = row_grads[piece] + precise_dot(logit_grad, router_t[...])
        gain_grad[...] += jnp.sum(grad * scaled, axis=0, keepdims=True)
        router_grad[...] += precise_dot(logit_grad, scaled * gain[...], (0, 0))
        result = grads[here, :].astype(jnp.float32) + factor[here, :] * (
            grad * gain[...] - scaled * mean
        )
        hidden_grad[here, :] = result
        ready[0, piece] = result.astype(low)
        spread.first(piece)

    def step(turn, carry):
        when(turn < pieces, gather, turn)
        when((turn >= 2) & (turn <= pieces + 1), settle, turn - 2)
        when(turn >= 3, spread.second, turn - 3)
        return carry

    lax.fori_loop(0, pieces + 3, step, 0)

    def last(piece, carry):
        spread.third(piece)
        spread.finish(piece)
        exchange.finish(piece)
        giving.finish(piece)
        return carry

    lax.fori_loop(0, pieces, last, 0)


def settle(came, marks, gates, logits, factor, hidden, grads, gain, router_t, pieces, collective):
    groups, parts = lax.axis_size("expert"), lax.axis_size("tensor")
    tokens, width = hidden.shape
    rows = tokens // pieces
    low, full = jnp.bfloat16, jnp.float32
    inside = pl.BlockSpec(memory_space=pltpu.VMEM)
    anywhere = pl.BlockSpec(memory_space=pl.ANY)
    return pl.pallas_call(
        settle_kernel,
        out_shape=(
            jax.ShapeDtypeStruct((groups, tokens // groups, width), low),
            jax.ShapeDtypeStruct((tokens, width), full),
            jax.ShapeDtypeStruct((1, pieces, rows, width * parts), low),
            jax.ShapeDtypeStruct(router_t.shape, full),
            jax.ShapeDtypeStruct((1, width), full),
        ),
        in_specs=[inside] * 9,
        out_specs=(anywhere, inside, anywhere, inside, inside),
        scratch_shapes=[
            pltpu.VMEM((pieces, rows, width), full),
            pltpu.VMEM((1, pieces, rows, width), low),
        ]
        + Exchange.scratch(pieces, parts, rows, 8)
        + Return.scratch(pieces, rows, width, groups)
        + Spread.scratch(pieces, parts // 2),
        compiler_params=pltpu.CompilerParams(
            collective_id=collective, has_side_effects=True, vmem_limit_bytes=48 * MIB
        ),
        cost_estimate=lasting(30),
    )(came, marks, gates, logits, factor, hidden, grads, gain, router_t)


def dot_tn(left, right):
    return lax.dot_general(
        left, right, (((0,), (0,)), ((), ())), preferred_element_type=jnp.float32
    )


def bands(tokens):
    size = 256 if tokens % 256 == 0 else tokens
    return [(first, size) for first in range(0, tokens, size)]


def sequence_starts(lengths):
    starts = [0]
    for number in range(lengths.shape[1] - 1):
        starts.append(starts[-1] + lengths[0, number])
    return starts


def masked_scores(query, keys, lengths, first, size, column):
    last = first + size
    scores = dot_nt(query[first:last, column], keys[:last, column]) * (1.0 / math.sqrt(HEAD))
    place = lax.broadcasted_iota(jnp.int32, (size, 1), 0) + first
    start = jnp.zeros((size, 1), jnp.int32)
    for value in sequence_starts(lengths)[1:]:
        start = jnp.where(place >= value, value, start)
    other = lax.broadcasted_iota(jnp.int32, (size, last), 1)
    return jnp.where((other >= start) & (place >= other), scores, MASKED)


def chosen_gates(logits, names):
    lane = lax.broadcasted_iota(jnp.int32, logits.shape, 1)
    picked = [
        jnp.sum(jnp.where(name == lane, logits, 0.0), axis=1, keepdims=True) for name in names
    ]
    top = jnp.maximum(picked[0], picked[1])
    expo = [jnp.exp(value - top) for value in picked]
    total = expo[0] + expo[1]
    return [value / total for value in expo]


def front_kernel(sharers, *refs):
    (
        resid, gain, router_t, query_hbm, key_hbm, value_hbm, out_hbm, cosines, sines,
        marks, mark_rows, gain_two, router_two_t, lengths, dealt,
        normed_t, cosine, sine, factor, logits, gates, gate_local, query, keys, values, heads, log_total,
        hidden, factor_two, logits_two, gates_two, sent_rows, lines,
        grads_back, grads_out, inbox_grads,
        normed_two, grads_here, grads_slots, w_query, w_key, w_value, w_out,
        deal_send, deal_land, load_sem, weight_sem,
    ), refs = refs[:47], refs[47:]
    place = Place()
    weight_loads = [
        pltpu.make_async_copy(source, kept, weight_sem.at[number])
        for number, (source, kept) in enumerate(
            ((query_hbm, w_query), (key_hbm, w_key), (value_hbm, w_value), (out_hbm, w_out))
        )
    ]
    for load in weight_loads:
        load.start()
    spread = Spread(place, grads_slots, inbox_grads, refs[:6], True, sharers)
    exchange = Exchange(place, refs[6:10])
    collect = Collect(place, refs[10:])
    tokens, columns = query.shape
    width = hidden.shape[1]
    groups = place.groups
    capacity = sent_rows.shape[1]
    experts_of = logits.shape[1]
    held = gate_local.shape[1]
    span = columns // held
    low = jnp.bfloat16
    parts = list(enumerate(bands(tokens)))
    place.meet(True, True)

    def deal_copy(step, index):
        peer = flip(place.expert, step, groups)
        return remote(
            dealt.at[peer],
            grads_back.at[index],
            deal_send.at[step],
            deal_land.at[step],
            place.device(peer, place.tensor),
        )

    for step in range(1, groups):
        deal_copy(step, place.expert).start()
    own = pltpu.make_async_copy(
        dealt.at[place.expert], grads_back.at[place.expert], deal_send.at[0]
    )
    own.start()
    for load in weight_loads:
        load.wait()
    router_high = router_t[...].astype(low)
    router_rest = (router_t[...] - router_high.astype(jnp.float32)).astype(low)
    columns_here = pl.ds(pl.multiple_of(place.tensor * width, 128), width)
    for _, (first, size) in parts:
        rows = slice(first, first + size)
        spot = lax.broadcasted_iota(jnp.int32, (size, 1), 0) + first
        start_cosine = jnp.broadcast_to(cosines[0:1, :], (size, HEAD))
        start_sine = jnp.broadcast_to(sines[0:1, :], (size, HEAD))
        for start in sequence_starts(lengths)[1:]:
            start_cosine = jnp.where(spot >= start, cosines[pl.ds(start, 1), :], start_cosine)
            start_sine = jnp.where(spot >= start, sines[pl.ds(start, 1), :], start_sine)
        lane = lax.broadcasted_iota(jnp.int32, (size, HEAD), 1)
        cosine[rows, :] = cosines[rows, :] * start_cosine + sines[rows, :] * start_sine
        turned = sines[rows, :] * start_cosine - cosines[rows, :] * start_sine
        sine[rows, :] = jnp.where(lane < HEAD // 2, -turned, turned)
        value = resid[rows, :].astype(jnp.float32)
        scale = lax.rsqrt(jnp.mean(value * value, axis=1, keepdims=True) + EPSILON)
        value = value * scale * gain[...]
        high = value.astype(low)
        rest = (value - high.astype(jnp.float32)).astype(low)
        factor[rows, :] = scale
        normed_t[:, rows] = high.T
        known = sum(
            dot_nt(left, right)
            for left, right in ((high, router_high), (high, router_rest), (rest, router_high))
        )
        logits[rows, :] = known
        names = [marks[rows, ROUTES + way : ROUTES + way + 1] for way in range(2)]
        pair = chosen_gates(known, names)
        for way in range(2):
            gates[rows, way : way + 1] = pair[way]
        for number in range(held):
            expert = place.tensor * held + number
            gate_local[rows, number : number + 1] = sum(
                jnp.where(name == expert, gate, 0.0) for name, gate in zip(names, pair)
            )
        values[rows, :] = jnp.dot(
            high, w_value[...], preferred_element_type=jnp.float32
        ).astype(low)
        for weight, out in ((w_query, query), (w_key, keys)):
            flat = jnp.dot(high, weight[...], preferred_element_type=jnp.float32)
            for head in range(columns // HEAD):
                column = slice(head * HEAD, (head + 1) * HEAD)
                part = flat[:, column]
                turned = pltpu.roll(part, HEAD // 2, 1)
                out[rows, column] = (part * cosine[rows, :] + turned * sine[rows, :]).astype(low)

    def selection(expert):
        number = lax.broadcasted_iota(jnp.int32, (capacity, tokens), 0) + expert * capacity
        return ((mark_rows[0:1, :] == number) | (mark_rows[1:2, :] == number)).astype(low)

    early = min(FRONT, groups)

    keep = pltpu.make_async_copy(grads_slots.at[0], grads_out, load_sem.at[groups])

    def take_grads():
        own.wait()
        bucket = grads_back.shape[1]
        for step in range(1, groups):
            deal_copy(step, flip(place.expert, step, groups)).wait_recv()
        fetches = [
            pltpu.make_async_copy(
                grads_back.at[group], grads_here.at[pl.ds(group * bucket, bucket)], load_sem.at[group]
            )
            for group in range(groups)
        ]
        for fetch in fetches:
            fetch.start()
        for fetch in fetches:
            fetch.wait()
        for expert in range(sent_rows.shape[0]):
            grads_slots[0, expert] = jnp.dot(
                selection(expert), grads_here[...], preferred_element_type=jnp.float32
            ).astype(low)
        keep.start()
        spread.start(min(AHEAD, early - 1))

    def tick(number):
        if number < early:
            spread.first(jnp.int32(number))
        if number + 1 + AHEAD < early:
            spread.send(jnp.int32(number + 1 + AHEAD))
        if 1 <= number <= early:
            spread.second(jnp.int32(number - 1))

    def attend_band(number, first, size):
        last = first + size
        rows = slice(first, last)
        for head in range(columns // HEAD):
            column = slice(head * HEAD, (head + 1) * HEAD)
            scores = masked_scores(query, keys, lengths, first, size, column)
            top = jnp.max(scores, axis=1, keepdims=True)
            expo = jnp.exp(scores - top)
            total = jnp.sum(expo, axis=1, keepdims=True)
            probs = (expo / total).astype(low)
            heads[rows, column] = jnp.dot(
                probs, values[:last, column], preferred_element_type=jnp.float32
            ).astype(low)
            log_total[rows, head : head + 1] = top + jnp.log(total)
        collect.free_stage(jnp.int32(number))
        for spot in range(place.spots):
            for core in range(2):
                start = (spot * 2 + core) * width
                total = None
                for expert in range(held):
                    inner = slice(expert * span, (expert + 1) * span)
                    term = gate_local[rows, expert : expert + 1] * jnp.dot(
                        heads[rows, inner],
                        w_out[inner, start : start + width],
                        preferred_element_type=jnp.float32,
                    )
                    total = term if total is None else total + term
                collect.stage[number % collect.slots, 0, spot, core] = total.astype(low)
        collect.first(jnp.int32(number))

    blank = jnp.zeros((128 - router_two_t.shape[0], width), jnp.float32)
    router_wide = jnp.concatenate([router_two_t[...], blank], axis=0)

    def measure(number, first, size):
        rows = slice(first, first + size)
        value = resid[rows, columns_here].astype(jnp.float32) + collect.third(jnp.int32(number))[0]
        hidden[rows, :] = value
        squares = jnp.sum(value * value, axis=1, keepdims=True)
        known = precise_dot(value * gain_two[...], router_wide, (1, 1))
        lane = lax.broadcasted_iota(jnp.int32, known.shape, 1)
        exchange.start(number, jnp.where(lane == SQUARES, squares, known))

    def conclude(number, first, size):
        rows = slice(first, first + size)
        total = exchange.total(number, size)
        scale = lax.rsqrt(total[:, SQUARES : SQUARES + 1] / (width * place.parts) + EPSILON)
        known = total[:, : logits_two.shape[1]] * scale
        factor_two[rows, :] = scale
        logits_two[rows, :] = known
        names = [marks[rows, ROUTES_TWO + way : ROUTES_TWO + way + 1] for way in range(2)]
        pair = chosen_gates(known, names)
        for way in range(2):
            gates_two[rows, way : way + 1] = pair[way]
        normed_two[rows, :] = (hidden[rows, :] * scale * gain_two[...]).astype(low)

    count = len(parts)
    for turn in range(count + 3):
        if turn < count:
            attend_band(turn, *parts[turn][1])
        if 2 <= turn < count + 2:
            measure(turn - 2, *parts[turn - 2][1])
        if 1 <= turn < count + 1:
            collect.second(jnp.int32(turn - 1))
        if turn >= 3:
            conclude(turn - 3, *parts[turn - 3][1])
        if turn == count:
            take_grads()
        if turn > count:
            tick(turn - count - 1)
    for expert in range(sent_rows.shape[0]):
        sent_rows[expert] = jnp.dot(
            selection(expert), normed_two[...], preferred_element_type=jnp.float32
        ).astype(low)
        wide = lines.shape[2]
        lane = lax.broadcasted_iota(jnp.int32, (tokens, wide), 1)
        number = jnp.where(lane < capacity, lane + expert * capacity, -1)
        line = sum(
            jnp.where(
                marks[:, SLOTS + way : SLOTS + way + 1] == number, gates_two[:, way : way + 1], 0.0
            )
            for way in range(2)
        )
        lines[expert] = jnp.broadcast_to(jnp.sum(line, axis=0, keepdims=True), lines.shape[1:])
    for number in range(2, early + 1):
        tick(number)
    keep.wait()
    for step in range(1, groups):
        deal_copy(step, place.expert).wait_send()
    for number in range(count):
        exchange.finish(number)
    collect.finish()

    def last(number, carry):
        spread.third(number)
        spread.finish(number)
        return carry

    lax.fori_loop(0, early, last, 0)


def front(
    resid, gain, router_t, weights, w_out, tables, marks, mark_rows, gain_two, router_two_t,
    lengths, dealt, capacity, sharers, collective,
):
    groups, parts = lax.axis_size("expert"), lax.axis_size("tensor")
    tokens, model_width = resid.shape
    columns = weights[0].shape[1]
    width = dealt.shape[2]
    experts_of = router_t.shape[0]
    held = columns // (QH * HEAD)
    slots_of = router_two_t.shape[0]
    low, full = jnp.bfloat16, jnp.float32
    block = jax.ShapeDtypeStruct((tokens, columns), low)
    wide = (capacity + 127) // 128 * 128
    inside = pl.BlockSpec(memory_space=pltpu.VMEM)
    anywhere = pl.BlockSpec(memory_space=pl.ANY)

    def column(count):
        return jax.ShapeDtypeStruct((tokens, count), full)

    pieces = len(bands(tokens))
    dma = pltpu.SemaphoreType.DMA
    return pl.pallas_call(
        functools.partial(front_kernel, sharers),
        out_shape=(
            jax.ShapeDtypeStruct((model_width, tokens), low),
            column(HEAD),
            column(HEAD),
            column(1),
            column(experts_of),
            column(2),
            column(held),
            block,
            block,
            block,
            block,
            column(columns // HEAD),
            column(width),
            column(1),
            column(slots_of),
            column(2),
            jax.ShapeDtypeStruct((slots_of, capacity, width), low),
            jax.ShapeDtypeStruct((slots_of, 8, wide), full),
            jax.ShapeDtypeStruct(dealt.shape, low),
            jax.ShapeDtypeStruct((slots_of, capacity, width), low),
            jax.ShapeDtypeStruct((1, groups, capacity, model_width), low),
        ),
        in_specs=[inside] * 3
        + [anywhere] * 4
        + [inside] * 6
        + [pl.BlockSpec(memory_space=pltpu.SMEM), anywhere],
        out_specs=(inside,) * 18 + (anywhere,) * 3,
        scratch_shapes=[
            pltpu.VMEM((tokens, width), low),
            pltpu.VMEM((tokens, width), low),
            pltpu.VMEM((1, slots_of, capacity, width), low),
            *(pltpu.VMEM(weight.shape, low) for weight in (*weights, w_out)),
            dma((groups,)),
            dma((groups,)),
            dma((groups + 1,)),
            dma((4,)),
        ]
        + Spread.scratch(groups, parts // 2)
        + Exchange.scratch(pieces, parts, tokens // pieces, 16)
        + Collect.scratch(pieces, 1, parts // 2, tokens // pieces, width, pieces),
        compiler_params=pltpu.CompilerParams(
            collective_id=collective, has_side_effects=True, vmem_limit_bytes=58 * MIB
        ),
        cost_estimate=lasting(60),
    )(
        resid, gain, router_t, *weights, w_out, *tables, marks, mark_rows, gain_two, router_two_t,
        lengths, dealt,
    )


def attend_back_kernel(
    grads, w_out, gates, heads, query, keys, values, log_total, cosine, sine, lengths,
    query_grad, key_grad, value_grad, gate_grad, gated_t,
    heads_grad, key_sum, value_sum,
):
    tokens, columns = query.shape
    low = jnp.bfloat16
    span = columns // gates.shape[1]
    scale = 1.0 / math.sqrt(HEAD)
    for first, size in bands(tokens):
        rows = slice(first, first + size)
        plain = dot_nt(grads[rows, :], w_out[...])
        for expert in range(gates.shape[1]):
            column = slice(expert * span, (expert + 1) * span)
            gate = gates[rows, expert : expert + 1]
            head = heads[rows, column].astype(jnp.float32)
            gate_grad[rows, expert : expert + 1] = jnp.sum(
                plain[:, column] * head, axis=1, keepdims=True
            )
            heads_grad[rows, column] = (plain[:, column] * gate).astype(low)
            gated_t[column, rows] = (head * gate).T.astype(low)

    def unturn(value, rows):
        turned = pltpu.roll(value * sine[rows, :], HEAD // 2, 1)
        return value * cosine[rows, :] + turned

    for head in range(columns // HEAD):
        column = slice(head * HEAD, (head + 1) * HEAD)
        for first, size in bands(tokens):
            last = first + size
            rows = slice(first, last)
            scores = masked_scores(query, keys, lengths, first, size, column)
            probs = jnp.exp(scores - log_total[rows, head : head + 1])
            value_part = dot_tn(probs.astype(low), heads_grad[rows, column])
            prob_grad = dot_nt(heads_grad[rows, column], values[:last, column])
            score_grad = (
                probs * (prob_grad - jnp.sum(probs * prob_grad, axis=1, keepdims=True))
            ).astype(low)
            query_grad[rows, column] = unturn(
                jnp.dot(score_grad, keys[:last, column], preferred_element_type=jnp.float32)
                * scale,
                rows,
            ).astype(low)
            key_part = dot_tn(score_grad, query[rows, column])
            if first:
                value_sum[:first, :] += value_part[:first]
                key_sum[:first, :] += key_part[:first]
            value_sum[rows, :] = value_part[first:]
            key_sum[rows, :] = key_part[first:]
        whole = slice(0, tokens)
        key_grad[:, column] = unturn(key_sum[...] * scale, whole).astype(low)
        value_grad[:, column] = value_sum[...].astype(low)


def attend_back(grads, w_out, gates, heads, query, keys, values, log_total, cosine, sine, lengths):
    tokens, model_width = grads.shape
    columns = query.shape[1]
    low, full = jnp.bfloat16, jnp.float32
    block = jax.ShapeDtypeStruct((tokens, columns), low)
    inside = pl.BlockSpec(memory_space=pltpu.VMEM)
    return pl.pallas_call(
        attend_back_kernel,
        out_shape=(
            block,
            block,
            block,
            jax.ShapeDtypeStruct(gates.shape, full),
            jax.ShapeDtypeStruct((columns, tokens), low),
        ),
        in_specs=[inside] * 10 + [pl.BlockSpec(memory_space=pltpu.SMEM)],
        out_specs=(inside,) * 5,
        scratch_shapes=[
            pltpu.VMEM((tokens, columns), low),
            pltpu.VMEM((tokens, HEAD), full),
            pltpu.VMEM((tokens, HEAD), full),
        ],
        compiler_params=pltpu.CompilerParams(vmem_limit_bytes=56 * MIB),
        cost_estimate=lasting(25),
    )(
        grads, w_out, gates, heads, query, keys, values, log_total, cosine, sine, lengths
    )


def body(
    tokens,
    out_grad,
    attn_gain,
    attn_router,
    w_query,
    w_key,
    w_value,
    w_out,
    mlp_gain,
    mlp_router,
    w_gate,
    w_up,
    w_down,
    deal,
    seq_lengths,
    attn_routes,
    mlp_routes,
    slot_order,
):
    tok_rows, model_width = tokens.shape
    group_count = lax.axis_size("expert")
    part_count = lax.axis_size("tensor")
    group_index = lax.axis_index("expert")
    part_index = lax.axis_index("tensor")
    bucket_rows = tok_rows // group_count
    col_width = model_width // part_count
    col_first = part_index * col_width
    low = jnp.bfloat16

    def own_cols(values):
        return lax.dynamic_slice_in_dim(values, col_first, col_width, values.ndim - 1)

    deal_rank = deal // tok_rows * bucket_rows + (deal % tok_rows - group_index * bucket_rows)
    row_ids = jnp.arange(tok_rows, dtype=jnp.int32)
    expert_count = mlp_router.shape[1]
    experts_of = attn_router.shape[1]
    sharers = group_count // expert_count
    capacity = 5 * tok_rows // (2 * expert_count)
    slots = expert_count * capacity
    pieces = 8
    orders = slot_order[0].reshape(tok_rows, 2)
    rows_in = jnp.concatenate([attn_routes.T, mlp_routes.T, orders.T, orders.T], axis=0)
    resid_low, dealt_grads, marks, mark_rows = deal_rows(
        tokens, out_grad, deal_rank[None], rows_in, capacity, expert_count, 0
    )
    resid_low = resid_low.reshape(tok_rows, model_width)
    gain_one, gain_two = own_cols(attn_gain), own_cols(mlp_gain)
    router_one, router_two = own_cols(attn_router.T), own_cols(mlp_router.T)
    (
        normed_t, cosine, sine, factor_one, attn_logits, attn_gates, gate_local, query, keys, values,
        heads_low, log_total, hidden, factor_two, mlp_logits, mlp_gates, slot_rows, gate_lines,
        grad_cols_low, slot_grads, early_grads,
    ) = front(
        resid_low,
        attn_gain[None],
        attn_router.T,
        (w_query, w_key, w_value),
        w_out,
        rotary_tables(tok_rows),
        marks,
        mark_rows,
        gain_two[None],
        router_two,
        seq_lengths,
        dealt_grads,
        capacity,
        sharers,
        1,
    )
    grad_cols_low = grad_cols_low.reshape(tok_rows, col_width)
    inbox, _, slot_grads, middle, gate_grad, up_grad, returned = experts(
        slot_rows,
        slot_grads,
        early_grads,
        gate_lines,
        w_gate[0],
        w_up[0],
        w_down[0],
        sharers,
        2,
    )
    if sharers > 1:
        returned = (
            jnp.sum(
                returned.reshape(2, expert_count, sharers, capacity, col_width).astype(jnp.float32),
                axis=2,
            )
        ).astype(low)
    back_mixed, hidden_grad, hidden_grad_low, mlp_router_grad, mlp_gain_grad = settle(
        returned.reshape(2, slots, col_width),
        marks,
        mlp_gates,
        mlp_logits,
        factor_two,
        hidden,
        grad_cols_low,
        gain_two[None],
        router_two,
        pieces,
        4,
    )
    back_mixed = back_mixed.reshape(tok_rows, col_width)
    hidden_grad_low = hidden_grad_low.reshape(tok_rows, model_width)
    query_pre_grad, key_pre_grad, value_pre_grad, local_gate_grad, gated_t = attend_back(
        hidden_grad_low,
        w_out,
        gate_local,
        heads_low,
        query,
        keys,
        values,
        log_total,
        cosine,
        sine,
        seq_lengths,
    )
    rows = inbox.reshape(-1, model_width)
    units = middle.shape[2]
    middle, gate_grad, up_grad = (
        jnp.pad(values.reshape(-1, units), ((0, 0), (0, -units % 128)))
        for values in (middle, gate_grad, up_grad)
    )
    *weight_grads, back_grad, small, gate_w_grad, up_w_grad, down_grad = closing(
        normed_t,
        (
            gain_one[None],
            factor_one,
            attn_gates,
            marks,
            attn_logits,
            local_gate_grad,
            router_one,
            mlp_gain_grad,
            mlp_router_grad,
        ),
        (query_pre_grad, key_pre_grad, value_pre_grad),
        gated_t,
        hidden_grad_low,
        hidden_grad,
        resid_low,
        (w_query, w_key, w_value),
        (rows, rows, middle),
        (gate_grad, up_grad, slot_grads.reshape(-1, model_width)),
        pieces,
        3,
    )
    back_grad = back_grad.reshape(tok_rows, col_width)
    weight_grads = [grad.astype(jnp.float32) for grad in weight_grads]
    deal_mask = (row_ids[:, None] == deal_rank[None, :]).astype(low)
    mixed, tokens_grad = (
        jnp.einsum("ri,rc->ic", deal_mask, back, preferred_element_type=jnp.float32).astype(low)
        for back in (back_mixed, back_grad)
    )
    small = small.transpose(1, 0, 2).reshape(-1, model_width)
    return (
        mixed,
        tokens_grad,
        small[0],
        small[1 : 1 + experts_of].T,
        weight_grads[0],
        weight_grads[1],
        weight_grads[2],
        weight_grads[3],
        small[1 + experts_of],
        small[2 + experts_of : 2 + experts_of + expert_count].T,
        gate_w_grad[None, :, :units].astype(jnp.float32),
        up_w_grad[None, :, :units].astype(jnp.float32),
        down_grad[None, :units].astype(jnp.float32),
    )


def solution(mesh):
    placed = (
        P("expert", None),
        P("expert", None),
        P(),
        P(),
        P(None, "tensor"),
        P(None, "tensor"),
        P(None, "tensor"),
        P("tensor", None),
        P(),
        P(),
        P("expert", None, "tensor"),
        P("expert", None, "tensor"),
        P("expert", "tensor", None),
        P("expert"),
        P("expert", None),
        P("expert", None),
        P("expert", None),
        P("expert", None),
    )
    return jax.shard_map(
        body,
        mesh=mesh,
        in_specs=placed,
        out_specs=(
            P("expert", "tensor"),
            P("expert", "tensor"),
            P(),
            P(),
            P(None, "tensor"),
            P(None, "tensor"),
            P(None, "tensor"),
            P("tensor", None),
            P(),
            P(),
            P("expert", None, "tensor"),
            P("expert", None, "tensor"),
            P("expert", "tensor", None),
        ),
        check_vma=False,
    )
```
